128 devices in a mesh: section: 2 (over core), seq: 16 (over y, x), wshard: 4 (over z).
Axes of the slice: x: 4, y: 4, z: 4, core: 2. Of those that a mesh axis runs over, the one named last changes fastest.
Arguments:
- inputs: float32 [2, 4, 2048, 1024], P(None, 'wshard', 'seq'), may hold values from -6 to 6
- cotangent: float32 [2, 4, 2048, 1024], P(None, 'wshard', 'seq'), may hold values from -6 to 6
- segments: int32 [2, 4, 2048], P(None, 'wshard'), may hold values from 0 to 8, as said below
- norm_gains: float32 [2, 2, 1024], P('section'), may hold values from 0.5 to 1.5
- attend_in: bfloat16 [2, 1024, 3072], P('section', 'wshard'), may hold values from -0.1875 to 0.1875
- attend_out: bfloat16 [2, 1024, 1024], P('section', 'wshard'), may hold values from -2 to 2
- hidden_in: bfloat16 [2, 1024, 5248], P('section', 'wshard'), may hold values from -0.1875 to 0.1875
- hidden_out: bfloat16 [2, 2624, 1024], P('section', 'wshard'), may hold values from -0.125 to 0.125
Outputs:
- section_outputs: float32 [2, 2, 4, 2048, 1024], P('section', None, 'wshard', 'seq')
- section_input_grads: float32 [2, 2, 4, 2048, 1024], P('section', None, 'wshard', 'seq')
- attend_in_grad: float32 [2, 1024, 3072], P('section', ('seq', 'wshard'))
- attend_out_grad: float32 [2, 1024, 1024], P('section', ('seq', 'wshard'))
- hidden_in_grad: float32 [2, 1024, 5248], P('section', ('seq', 'wshard'))
- hidden_out_grad: float32 [2, 2624, 1024], P('section', ('seq', 'wshard'))
- gain_grads: float32 [2, 2, 1024], P('section', None, ('seq', 'wshard'))
The draws below stay inside these ranges and needn't reach their ends.
Inputs may be any that keep to these rules, and one draw needn't show every extreme that they name: Segment numbers start at 0 at the start of each sequence, never fall along it and rise by at most one from token to token; a sequence holds at most 9 segments.
All inputs are finite; a program needn't handle non-finite values.
Results may differ from the reference program's by a relative error of at most 0.025.
Values may be sent and summed in bfloat16 or wider, within the bound.
No kernel may reach another device: no remote copies, remote signals or barrier semaphores. Data moves between devices by JAX's collectives and lax.ppermute only.
A program may use at most 192 MiB of HBM per device.

```python
import math
import jax
import jax.numpy as jnp
from jax import lax

D = 1024
HEADS = 16
HEAD_DIM = 64
FF = 2624
WINDOW = 128
MB = 2
HALO = 64
SEQ_LEN = 2048
SEQS = 4


def draw_segments(key, part):
    key = jax.random.fold_in(key, 11)
    flag_key, whole_key = jax.random.split(key)
    start_count = SEQ_LEN // (2 * WINDOW)
    places = jnp.arange(SEQ_LEN - 1, dtype=jnp.int32)
    scores = jax.random.randint(flag_key, (MB, SEQS, SEQ_LEN - 1), 0, 1 << 16) * SEQ_LEN + places
    order = jnp.argsort(scores, axis=2, stable=True)
    chosen = (order[:, :, :start_count] + 1).astype(jnp.int32)
    positions = jnp.arange(SEQ_LEN, dtype=jnp.int32)
    starts = jnp.any(chosen[:, :, :, None] == positions[None, None, None, :], axis=2).astype(jnp.int32)
    single = jax.random.randint(whole_key, (SEQS,), 0, MB)
    keeping = (jnp.arange(MB)[:, None] != single[None, :]).astype(jnp.int32)
    starts = starts * keeping[:, :, None]
    return jnp.cumsum(starts, axis=2).astype(jnp.int32)


def level_of(key, shape, shards, least, high):
    level, own = 1.0, jax.random.fold_in(key, 6)
    for axis_at, blocks in shards:
        heights = jnp.exp(jax.random.uniform(jax.random.fold_in(own, axis_at), (blocks,), jnp.float32, least / len(shards), high / len(shards)))
        level = level * jnp.repeat(heights, shape[axis_at] // blocks).reshape([-1 if axis == axis_at else 1 for axis in range(len(shape))])
    return level


def gaussian(stream_key, extent, spread, reach, shards=(), held_as=jnp.bfloat16):
    result = spread * jax.random.normal(stream_key, extent, jnp.float32)
    if shards:
        result = result * level_of(stream_key, extent, shards, -0.22, 0.18)
    return jnp.clip(result, -reach, reach).astype(held_as)


def setup_inputs(seed: int = 0) -> dict:
    key_list = jax.random.split(jax.random.key(seed), 9)
    inputs = gaussian(key_list[0], (MB, SEQS, SEQ_LEN, D), 1.0, 6.0, ((1, 4), (2, 16)), jnp.float32)
    cotangent = gaussian(key_list[1], (MB, SEQS, SEQ_LEN, D), 1.0, 6.0, ((1, 4), (2, 16)), jnp.float32)
    segments = draw_segments(jax.random.fold_in(key_list[8], 71), 0)
    norm_gains = jnp.clip(1.0 + 0.1 * jax.random.normal(key_list[3], (2, 2, D), jnp.float32), 0.5, 1.5)
    attend_in = gaussian(key_list[4], (2, D, 3 * D), D ** -0.5, 0.1875, ((0, 2), (1, 4)))
    attend_out = gaussian(key_list[5], (2, D, D), (D // WINDOW) ** -0.5, 2.0, ((0, 2), (1, 4)))
    hidden_in = gaussian(key_list[6], (2, D, 2 * FF), D ** -0.5, 0.1875, ((0, 2), (1, 4)))
    hidden_out = gaussian(key_list[7], (2, FF, D), FF ** -0.5, 0.125, ((0, 2), (1, 4)))
    return {"inputs": inputs, "cotangent": cotangent, "segments": segments, "norm_gains": norm_gains, "attend_in": attend_in, "attend_out": attend_out, "hidden_in": hidden_in, "hidden_out": hidden_out}


norm_eps = 1e-05
root_half = 1.0 / math.sqrt(2.0)

@jax.custom_vjp
def low(v):
    return lax.optimization_barrier(v.astype(jnp.bfloat16)).astype(jnp.float32)

@jax.custom_vjp
def low_back(v):
    return v

def low_keep(v):
    return (low(v), None)

def low_pass(kept, grad):
    return (grad,)

def back_keep(v):
    return (v, None)

def back_low(kept, grad):
    return (low(grad),)
low.defvjp(low_keep, low_pass)
low_back.defvjp(back_keep, back_low)

def matmul(left_rows, right_rows):
    return jnp.dot(left_rows, right_rows, precision=lax.Precision.HIGHEST)

def layer_norm(rows_in):
    centred = rows_in - lax.optimization_barrier(jnp.mean(rows_in, axis=1, keepdims=True))
    return centred * lax.rsqrt(lax.optimization_barrier(jnp.mean(centred * centred, axis=1, keepdims=True)) + norm_eps)

def attention(queries, keys_in, values_in, segment_row):
    length = queries.shape[0]
    block_rows = math.gcd(length, 512)
    block_count = length // block_rows
    key_span = block_rows + 2 * HALO
    keys_pad = jnp.pad(keys_in, ((HALO, HALO), (0, 0)))
    values_pad = jnp.pad(values_in, ((HALO, HALO), (0, 0)))
    segment_pad = jnp.pad(segment_row, (HALO, HALO), constant_values=-1)
    score_scale = 1.0 / math.sqrt(HEAD_DIM)

    @jax.checkpoint
    def one_block(block_index):
        first_row = (block_index * block_rows).astype(jnp.int32)
        query_heads = lax.dynamic_slice_in_dim(queries, first_row, block_rows, 0).reshape(block_rows, HEADS, HEAD_DIM)
        key_heads = lax.dynamic_slice_in_dim(keys_pad, first_row, key_span, 0).reshape(key_span, HEADS, HEAD_DIM)
        value_heads = lax.dynamic_slice_in_dim(values_pad, first_row, key_span, 0).reshape(key_span, HEADS, HEAD_DIM)
        query_seg = lax.dynamic_slice_in_dim(segment_row, first_row, block_rows, 0)
        key_seg = lax.dynamic_slice_in_dim(segment_pad, first_row, key_span, 0)
        query_pos = jnp.arange(block_rows)[:, None]
        key_pos = jnp.arange(key_span)[None, :] - HALO
        allowed = (jnp.abs(query_pos - key_pos) <= HALO) & (query_seg[:, None] == key_seg[None, :])
        scores = low_back(jnp.einsum('qhd,khd->hqk', query_heads, key_heads, precision=lax.Precision.HIGHEST) * score_scale)
        scores = jnp.where(allowed[None], scores, -1e+30)
        row_max = lax.optimization_barrier(jnp.max(scores, axis=2, keepdims=True))
        exponent = jnp.where(allowed[None], jnp.exp(scores - row_max), 0.0)
        probs = exponent / lax.optimization_barrier(jnp.sum(exponent, axis=2, keepdims=True))
        mixed = jnp.einsum('hqk,khd->qhd', low(probs), value_heads, precision=lax.Precision.HIGHEST)
        return mixed.reshape(block_rows, HEADS * HEAD_DIM)
    blocks = lax.map(one_block, jnp.arange(block_count, dtype=jnp.int32))
    return blocks.reshape(length, HEADS * HEAD_DIM)

def layer(rows_in, gain_pair, attend_w, attend_o, hidden_w, hidden_o, segment_row):
    model_width = rows_in.shape[1]
    act_in = low(layer_norm(rows_in) * gain_pair[0])
    qkv = low(low_back(matmul(act_in, attend_w)))
    mixed = attention(qkv[:, :model_width], qkv[:, model_width:2 * model_width], qkv[:, 2 * model_width:], segment_row)
    mixed = low(low_back(mixed))
    middle = rows_in + low_back(matmul(mixed, attend_o))
    act_mid = low(layer_norm(middle) * gain_pair[1])
    hidden = low_back(matmul(act_mid, hidden_w))
    gate_part = hidden[:, :FF]
    product = low(gate_part * 0.5 * (1.0 + lax.erf(gate_part * root_half)) * hidden[:, FF:])
    return middle + low_back(matmul(product, hidden_o))

def reference(inputs, cotangent, segments, norm_gains, attend_in, attend_out, hidden_in, hidden_out):
    mats = [m.astype(jnp.float32) for m in (attend_in, attend_out, hidden_in, hidden_out)]
    seq_total = MB * SEQS
    flat_inputs = inputs.reshape(seq_total, SEQ_LEN, D)
    flat_cot = cotangent.reshape(seq_total, SEQ_LEN, D)
    flat_seg = segments.reshape(seq_total, SEQ_LEN)

    def one_sequence(totals, item):
        rows_in, grad_rows, segment_row = item

        def run(layer_in, gain_pair, attend_w, attend_o, hidden_w, hidden_o):
            return layer(layer_in, gain_pair, attend_w, attend_o, hidden_w, hidden_o, segment_row)
        middle, back_first = jax.vjp(run, rows_in, norm_gains[0], mats[0][0], mats[1][0], mats[2][0], mats[3][0])
        final, back_second = jax.vjp(run, middle, norm_gains[1], mats[0][1], mats[1][1], mats[2][1], mats[3][1])
        second = back_second(grad_rows)
        first = back_first(second[0])
        totals = tuple((total + jnp.stack([early, late]) for total, early, late in zip(totals, first[1:], second[1:])))
        return (totals, (middle, final, first[0], second[0]))
    start_totals = (jnp.zeros_like(norm_gains), jnp.zeros_like(mats[0]), jnp.zeros_like(mats[1]), jnp.zeros_like(mats[2]), jnp.zeros_like(mats[3]))
    totals, (mids, finals, grad_first, grad_second) = lax.scan(one_sequence, start_totals, (flat_inputs, flat_cot, flat_seg))
    out_shape = (MB, SEQS, SEQ_LEN, D)
    section_outputs = jnp.stack([mids.reshape(out_shape), finals.reshape(out_shape)])
    section_input_grads = jnp.stack([grad_first.reshape(out_shape), grad_second.reshape(out_shape)])
    return (section_outputs, section_input_grads, totals[1], totals[2], totals[3], totals[4], totals[0])
```

```python
import math

import jax
import jax.numpy as jnp
from jax import lax
from jax.experimental import pallas as pl
from jax.experimental.pallas import tpu as pltpu
from jax.sharding import PartitionSpec as P

HEADS = 16
HEAD_DIM = 64
FF = 2624
HALO = 64
SEQ_DEV = 16
W_DEV = 4
PAD_ROWS = 48

norm_eps = 1e-05
root_half = 1.0 / math.sqrt(2.0)
root_two_pi = 1.0 / math.sqrt(2.0 * math.pi)
score_scale = 1.0 / math.sqrt(HEAD_DIM)

SWAP = [(0, 1), (1, 0)]


def swapped(array):
    return lax.ppermute(array, "section", SWAP)


def norm_parts(rows_in):
    centred = rows_in - jnp.mean(rows_in, axis=1, keepdims=True)
    factor = lax.rsqrt(jnp.mean(centred * centred, axis=1, keepdims=True) + norm_eps)
    return (centred * factor, factor)


def norm_back(grad_norm, normed, factor):
    inner = jnp.mean(grad_norm, axis=1, keepdims=True)
    along = jnp.mean(grad_norm * normed, axis=1, keepdims=True)
    return factor * (grad_norm - inner - normed * along)


def matmul(left, right):
    return jnp.dot(left, right, preferred_element_type=jnp.float32)


def matmul_t(left, right):
    return lax.dot_general(
        left, right, (((1,), (1,)), ((), ())), preferred_element_type=jnp.float32
    )


def inner_rows(left, right):
    return lax.dot_general(
        left, right, (((0,), (0,)), ((), ())), preferred_element_type=jnp.float32
    )


def column_halves(array, on_first):
    even = jnp.concatenate([array[:, 256 * k : 256 * k + 128] for k in range(4)], axis=1)
    odd = jnp.concatenate([array[:, 256 * k + 128 : 256 * k + 256] for k in range(4)], axis=1)
    return (jnp.where(on_first, even, odd), jnp.where(on_first, odd, even))


def from_halves(own, other, on_first):
    even = jnp.where(on_first, own, other)
    odd = jnp.where(on_first, other, own)
    parts = []
    for k in range(4):
        parts += [even[:, 128 * k : 128 * k + 128], odd[:, 128 * k : 128 * k + 128]]
    return jnp.concatenate(parts, axis=1)


def window_allowed(query_seg, key_seg):
    rows, keys = (query_seg.shape[0], key_seg.shape[1])
    offset = lax.broadcasted_iota(jnp.int32, (rows, keys), 1) - lax.broadcasted_iota(
        jnp.int32, (rows, keys), 0
    )
    return (offset >= 0) & (offset <= 2 * HALO) & (query_seg == key_seg)


def attend_kernel(query_seg, key_seg, qkv, mixed, log_total):
    allowed = window_allowed(query_seg[...], key_seg[...])
    width = HEADS * HEAD_DIM
    rows = mixed.shape[0]
    for head in range(HEADS):
        at = head * HEAD_DIM
        q = qkv[HALO : HALO + rows, at : at + HEAD_DIM]
        k = qkv[:, width + at : width + at + HEAD_DIM]
        v = qkv[:, 2 * width + at : 2 * width + at + HEAD_DIM]
        scores = jnp.where(allowed, matmul_t(q, k) * score_scale, -1e30)
        row_max = jnp.max(scores, axis=1, keepdims=True)
        exponent = jnp.exp(scores - row_max)
        total = jnp.sum(exponent, axis=1, keepdims=True)
        probs = (exponent * (1.0 / total)).astype(jnp.bfloat16)
        mixed[:, at : at + HEAD_DIM] = matmul(probs, v).astype(jnp.bfloat16)
        log_total[:, at : at + HEAD_DIM] = jnp.broadcast_to(
            row_max + jnp.log(total), (rows, HEAD_DIM)
        )


def attend_back_kernel(
    query_seg, key_seg, qkv, log_total, grad_mixed, grad_query, own, before, after
):
    allowed = window_allowed(query_seg[...], key_seg[...])
    width = HEADS * HEAD_DIM
    rows = grad_mixed.shape[0]
    for head in range(HEADS):
        at = head * HEAD_DIM
        q = qkv[HALO : HALO + rows, at : at + HEAD_DIM]
        k = qkv[:, width + at : width + at + HEAD_DIM]
        v = qkv[:, 2 * width + at : 2 * width + at + HEAD_DIM]
        grad = grad_mixed[:, at : at + HEAD_DIM]
        scores = jnp.where(allowed, matmul_t(q, k) * score_scale, -1e30)
        probs = jnp.exp(scores - log_total[:, at : at + 1])
        grad_probs = matmul_t(grad, v)
        inner = jnp.sum(probs * grad_probs, axis=1, keepdims=True)
        grad_scores = (probs * (grad_probs - inner)).astype(jnp.bfloat16)
        grad_query[:, at : at + HEAD_DIM] = (matmul(grad_scores, k) * score_scale).astype(
            jnp.bfloat16
        )
        for place, piece in (
            (at, inner_rows(grad_scores, q) * score_scale),
            (width + at, inner_rows(probs.astype(jnp.bfloat16), grad)),
        ):
            columns = slice(place, place + HEAD_DIM)
            before[:, columns] = piece[:HALO].astype(jnp.bfloat16)
            own[:, columns] = piece[HALO : HALO + rows]
            after[:, columns] = piece[HALO + rows :].astype(jnp.bfloat16)


params = pltpu.CompilerParams(vmem_limit_bytes=40 * 1024 * 1024)


def attend(query_seg, key_seg, qkv):
    rows, width = (query_seg.shape[0], HEADS * HEAD_DIM)
    return pl.pallas_call(
        attend_kernel,
        out_shape=(
            jax.ShapeDtypeStruct((rows, width), jnp.bfloat16),
            jax.ShapeDtypeStruct((rows, width), jnp.float32),
        ),
        compiler_params=params,
        name="attend",
    )(query_seg, key_seg, qkv)


def attend_back(query_seg, key_seg, qkv, log_total, grad_mixed):
    rows, width = (query_seg.shape[0], HEADS * HEAD_DIM)
    return pl.pallas_call(
        attend_back_kernel,
        out_shape=(
            jax.ShapeDtypeStruct((rows, width), jnp.bfloat16),
            jax.ShapeDtypeStruct((rows, 2 * width), jnp.float32),
            jax.ShapeDtypeStruct((HALO, 2 * width), jnp.bfloat16),
            jax.ShapeDtypeStruct((HALO, 2 * width), jnp.bfloat16),
        ),
        compiler_params=params,
        name="attend_back",
    )(query_seg, key_seg, qkv, log_total, grad_mixed)


def to_next(array):
    return lax.ppermute(array, "seq", [(i, i + 1) for i in range(SEQ_DEV - 1)])


def to_previous(array):
    return lax.ppermute(array, "seq", [(i + 1, i) for i in range(SEQ_DEV - 1)])


def split_normal(gate):
    cumulative = 0.5 * (1.0 + lax.erf(gate * root_half))
    return cumulative


def layer_forward(rows_in, gain_pair, weights, segs, on_first):
    (attn_own, attn_other), (hidden_own, hidden_other), (down_own, down_other) = weights
    width = rows_in.shape[1]
    normed1, factor1 = norm_parts(rows_in)
    act_in = (normed1 * gain_pair[0]).astype(jnp.bfloat16)
    before = to_next(act_in[act_in.shape[0] - HALO :])
    after = to_previous(act_in[:HALO])
    extended = jnp.concatenate([before, act_in, after], axis=0)
    own, other = column_halves(extended, on_first)
    qkv = (
        matmul(own, attn_own[:, : 3 * width]) + matmul(other, attn_other[:, : 3 * width])
    ).astype(jnp.bfloat16)
    mixed, log_total = attend(*segs, qkv)
    own, other = column_halves(mixed, on_first)
    middle = (
        rows_in + matmul(own, attn_own[:, 3 * width :]) + matmul(other, attn_other[:, 3 * width :])
    )
    normed2, factor2 = norm_parts(middle)
    act_mid = (normed2 * gain_pair[1]).astype(jnp.bfloat16)
    own, other = column_halves(act_mid, on_first)
    hidden = matmul(own, hidden_own) + matmul(other, hidden_other)
    gate, up = (hidden[:, :FF], hidden[:, FF:])
    product = (gate * split_normal(gate) * up).astype(jnp.bfloat16)
    mine, theirs = (matmul(product, down_own), matmul(product, down_other))
    output = middle + jnp.concatenate(
        [jnp.where(on_first, mine, theirs), jnp.where(on_first, theirs, mine)], axis=1
    )
    kept = (normed1, factor1, act_in, qkv, log_total, mixed, normed2, factor2, act_mid, hidden, product)
    return (output, kept)


def padded_rows(product):
    pieces = product.reshape(product.shape[0], SEQ_DEV * W_DEV, FF // (SEQ_DEV * W_DEV))
    pieces = jnp.pad(pieces, ((0, 0), (0, 0), (0, PAD_ROWS - pieces.shape[2])))
    return pieces.reshape(product.shape[0], SEQ_DEV * W_DEV * PAD_ROWS)


def seq_sum(total):
    return lax.psum_scatter(total, "seq", scatter_dimension=0, tiled=True)


def half_exchange(arrays, on_first):
    keep, give = ([], [])
    for low, high in arrays:
        keep.append(jnp.where(on_first, low, high))
        give.append(jnp.where(on_first, high, low))
    widths = [g.shape[1] for g in give]
    got = swapped(jnp.concatenate(give, axis=1))
    outs, at = ([], 0)
    for mine, w in zip(keep, widths):
        outs.append(jnp.concatenate([mine, got[:, at : at + w]], axis=0))
        at += w
    return outs


def layer_backward(grad_out, kept, gain_pair, weights, segs, on_first):
    (attn_own, attn_other), (hidden_own, hidden_other), (down_own, down_other) = weights
    (normed1, factor1, act_in, qkv, log_total, mixed, normed2, factor2, act_mid, hidden, product) = kept
    rows, width = normed1.shape
    acts = jnp.concatenate([act_in, mixed, act_mid, padded_rows(product)], axis=1)
    acts = jnp.concatenate([acts, swapped(acts)], axis=0)
    both_in = acts[:, :width]
    both_mixed = acts[:, width : 2 * width]
    both_mid = acts[:, 2 * width : 3 * width]
    both_product = acts[:, 3 * width :]
    half = width // 2
    grad_branch = grad_out.astype(jnp.bfloat16)
    low, high = (grad_branch[:, :half], grad_branch[:, half:])
    grad_product = matmul_t(jnp.where(on_first, low, high), down_own) + matmul_t(
        jnp.where(on_first, high, low), down_other
    )
    gate, up = (hidden[:, :FF], hidden[:, FF:])
    cumulative = split_normal(gate)
    derivative = cumulative + gate * jnp.exp(-0.5 * gate * gate) * root_two_pi
    grad_gate = (grad_product * up * derivative).astype(jnp.bfloat16)
    grad_up = (grad_product * gate * cumulative).astype(jnp.bfloat16)
    branch_half, hidden_half = half_exchange(((low, high), (grad_gate, grad_up)), on_first)
    down_sum = seq_sum(inner_rows(both_product, branch_half).astype(jnp.bfloat16))
    hidden_sum = seq_sum(inner_rows(both_mid, hidden_half).astype(jnp.bfloat16))
    mine, theirs = [
        matmul_t(grad_gate, w[:, :FF]) + matmul_t(grad_up, w[:, FF:])
        for w in (hidden_own, hidden_other)
    ]
    grad_norm2 = from_halves(mine, theirs, on_first)
    gain_mid = jnp.sum(normed2 * grad_norm2, axis=0)
    grad_middle = grad_out + norm_back(grad_norm2 * gain_pair[1], normed2, factor2)
    grad_attn = grad_middle.astype(jnp.bfloat16)
    mine, theirs = [matmul_t(grad_attn, w[:, 3 * width :]) for w in (attn_own, attn_other)]
    grad_mixed = from_halves(mine, theirs, on_first).astype(jnp.bfloat16)
    grad_query, grad_own, grad_before, grad_after = attend_back(*segs, qkv, log_total, grad_mixed)
    from_previous = to_next(grad_after).astype(jnp.float32)
    from_next = to_previous(grad_before).astype(jnp.float32)
    grad_pairs = grad_own + jnp.concatenate([from_previous, from_next], axis=0)
    grad_qkv = jnp.concatenate([grad_query, grad_pairs.astype(jnp.bfloat16)], axis=1)
    qkv_half, attn_half = half_exchange(
        (
            (grad_qkv[:, : 3 * half], grad_qkv[:, 3 * half :]),
            (grad_attn[:, :half], grad_attn[:, half:]),
        ),
        on_first,
    )
    mine, theirs = [matmul_t(grad_qkv, w[:, : 3 * width]) for w in (attn_own, attn_other)]
    grad_norm1 = from_halves(mine, theirs, on_first)
    gain_first = jnp.sum(normed1 * grad_norm1, axis=0)
    grad_inputs = grad_middle + norm_back(grad_norm1 * gain_pair[0], normed1, factor1)
    gains = jnp.stack([gain_first, gain_mid]).astype(jnp.bfloat16)
    gain_columns = jnp.pad(gains, ((0, 126), (0, 0))).T
    late = jnp.concatenate(
        [
            inner_rows(both_in, qkv_half).astype(jnp.bfloat16),
            inner_rows(both_mixed, attn_half).astype(jnp.bfloat16),
            gain_columns,
        ],
        axis=1,
    )
    late_sum = seq_sum(late)
    return (grad_inputs, (late_sum, hidden_sum, down_sum))


def summed_over_w(block, place):
    rows = block.shape[0] // W_DEV
    total = lax.dynamic_slice_in_dim(block, place * rows, rows).astype(jnp.float32)
    for step in range(1, W_DEV):
        part = lax.dynamic_slice_in_dim(block, lax.rem(place + step, W_DEV) * rows, rows)
        got = lax.ppermute(part, "wshard", [(j, (j + step) % W_DEV) for j in range(W_DEV)])
        total = total + got.astype(jnp.float32)
    return total


def per_device(
    inputs, cotangent, segments, norm_gains, attend_in, attend_out, hidden_in, hidden_out
):
    on_first = lax.axis_index("section") == 0
    core = lax.axis_index("section")
    seq_place = lax.axis_index("seq")
    w_place = lax.axis_index("wshard")

    def by_core(first, second):
        return jnp.where(on_first, first, second)

    def sections(own, got):
        return (by_core(own, got), by_core(got, own))

    row_weights = jnp.concatenate([attend_in[0], attend_out[0], hidden_in[0]], axis=1)
    slice_rows = row_weights.shape[0] // (2 * SEQ_DEV)

    def row_slice(which):
        return lax.dynamic_slice_in_dim(
            row_weights, (which * SEQ_DEV + seq_place) * slice_rows, slice_rows
        )

    row_pieces = sections(row_slice(core), swapped(row_slice(1 - core)))
    half = hidden_out.shape[2] // 2
    low, high = (hidden_out[0, :, :half], hidden_out[0, :, half:])
    down_pieces = sections(by_core(low, high), swapped(by_core(high, low)))
    gains_other = swapped(norm_gains[0])
    gain_pairs = sections(norm_gains[0], gains_other)
    attn_width = attend_in.shape[2] + attend_out.shape[2]

    def gathered(piece, axes):
        own = lax.all_gather(piece, axes, axis=0, tiled=True)
        return (own, swapped(own))

    def weights_of(section):
        return (
            gathered(row_pieces[section][:, :attn_width], ("wshard", "seq")),
            gathered(row_pieces[section][:, attn_width:], ("wshard", "seq")),
            gathered(down_pieces[section], "wshard"),
        )

    weights = (weights_of(0), weights_of(1))
    rows_in = by_core(inputs[0, 0], inputs[1, 0])
    row_count = rows_in.shape[0]
    segment_row = by_core(segments[0, 0], segments[1, 0])
    padded = jnp.pad(segment_row, (HALO, HALO), constant_values=-1)
    first_row = seq_place * row_count
    segs = (
        lax.dynamic_slice_in_dim(segment_row, first_row, row_count)[:, None],
        lax.dynamic_slice_in_dim(padded, first_row, row_count + 2 * HALO)[None, :],
    )
    middle, kept0 = layer_forward(rows_in, gain_pairs[0], weights[0], segs, on_first)
    final, kept1 = layer_forward(middle, gain_pairs[1], weights[1], segs, on_first)
    upstream = by_core(cotangent[0, 0], cotangent[1, 0])
    grads1, sums1 = layer_backward(upstream, kept1, gain_pairs[1], weights[1], segs, on_first)
    grads0, sums0 = layer_backward(grads1, kept0, gain_pairs[0], weights[0], segs, on_first)

    def placed(first, second):
        mine, give = (by_core(first, second), by_core(second, first))
        got = swapped(give)
        return jnp.stack([by_core(mine, got), by_core(got, mine)])[None, :, None]

    section_outputs = placed(middle, final)
    section_input_grads = placed(grads0, grads1)

    def both_halves(first, second):
        mine, got = (by_core(first, second), swapped(by_core(second, first)))
        return (by_core(mine, got), by_core(got, mine))

    rows_first, rows_second = both_halves(
        *[jnp.concatenate([sums[0], sums[1]], axis=1) for sums in (sums0, sums1)]
    )
    width = rows_in.shape[1]
    attn_half, out_half = (3 * width // 2, width // 2)
    cuts = (0, attn_half, attn_half + out_half, attn_half + out_half + 128)
    pieces = [
        [rows[:, cuts[k] : (cuts + (rows.shape[1],))[k + 1]] for k in range(4)]
        for rows in (rows_first, rows_second)
    ]
    gain_part = pieces[0][2].astype(jnp.float32) + pieces[1][2].astype(jnp.float32)
    row_block = jnp.concatenate(
        [
            pieces[0][0],
            pieces[1][0],
            pieces[0][1],
            pieces[1][1],
            pieces[0][3],
            pieces[1][3],
            gain_part.astype(jnp.bfloat16),
        ],
        axis=1,
    )
    row_total = summed_over_w(row_block, w_place)
    down_block = jnp.concatenate(both_halves(sums0[2], sums1[2]), axis=1)
    down_total = summed_over_w(down_block, w_place)[: FF // (SEQ_DEV * W_DEV)]
    qkv_rows = row_total[:, : 3 * width]
    attn_rows = row_total[:, 3 * width : 4 * width]
    hidden_rows = row_total[:, 4 * width : 4 * width + 2 * FF]
    gain_rows = row_total[:, 4 * width + 2 * FF :][:, :2].T
    return (
        section_outputs,
        section_input_grads,
        qkv_rows[None],
        attn_rows[None],
        hidden_rows[None],
        down_total[None],
        gain_rows[None],
    )


def solution(mesh):
    placed = (
        P(None, "wshard", "seq", None),
        P(None, "wshard", "seq", None),
        P(None, "wshard", None),
        P("section", None, None),
        P("section", "wshard", None),
        P("section", "wshard", None),
        P("section", "wshard", None),
        P("section", "wshard", None),
    )
    return jax.shard_map(
        per_device,
        mesh=mesh,
        in_specs=placed,
        out_specs=(
            P("section", None, "wshard", "seq", None),
            P("section", None, "wshard", "seq", None),
            P("section", ("seq", "wshard"), None),
            P("section", ("seq", "wshard"), None),
            P("section", ("seq", "wshard"), None),
            P("section", ("seq", "wshard"), None),
            P("section", None, ("seq", "wshard")),
        ),
        check_vma=False,
    )
```

```python
import math

import jax
import jax.numpy as jnp
from jax import lax
from jax.experimental import pallas as pl
from jax.experimental.pallas import tpu as pltpu
from jax.sharding import PartitionSpec as P

HEADS = 16
HEAD_DIM = 64
FF = 2624
HALO = 64
FF_PAD = 2688
SEQ_DEV = 16
W_DEV = 4
PAD_ROWS = 48
BLOCK = 256
GRAD_PAD = 2816

norm_eps = 1e-05
root_half = 1.0 / math.sqrt(2.0)
root_two_pi = 1.0 / math.sqrt(2.0 * math.pi)
score_scale = 1.0 / math.sqrt(HEAD_DIM)

SWAP = [(0, 1), (1, 0)]


def swapped(array):
    return lax.ppermute(array, "section", SWAP)


def norm_parts(rows_in):
    centred = rows_in - jnp.mean(rows_in, axis=1, keepdims=True)
    factor = lax.rsqrt(jnp.mean(centred * centred, axis=1, keepdims=True) + norm_eps)
    return (centred * factor, factor)


def norm_back(grad_norm, normed, factor):
    inner = jnp.mean(grad_norm, axis=1, keepdims=True)
    along = jnp.mean(grad_norm * normed, axis=1, keepdims=True)
    return factor * (grad_norm - inner - normed * along)


def matmul(left, right):
    return jnp.dot(left, right, preferred_element_type=jnp.float32)


def matmul_t(left, right):
    return lax.dot_general(
        left, right, (((1,), (1,)), ((), ())), preferred_element_type=jnp.float32
    )


def inner_rows(left, right):
    return lax.dot_general(
        left, right, (((0,), (0,)), ((), ())), preferred_element_type=jnp.float32
    )


def column_halves(array, on_first):
    even = jnp.concatenate([array[:, 256 * k : 256 * k + 128] for k in range(4)], axis=1)
    odd = jnp.concatenate([array[:, 256 * k + 128 : 256 * k + 256] for k in range(4)], axis=1)
    return (jnp.where(on_first, even, odd), jnp.where(on_first, odd, even))


def from_halves(own, other, on_first):
    even = jnp.where(on_first, own, other)
    odd = jnp.where(on_first, other, own)
    parts = []
    for k in range(4):
        parts += [even[:, 128 * k : 128 * k + 128], odd[:, 128 * k : 128 * k + 128]]
    return jnp.concatenate(parts, axis=1)


def window_allowed(query_seg, key_seg):
    rows, keys = (query_seg.shape[0], key_seg.shape[1])
    offset = lax.broadcasted_iota(jnp.int32, (rows, keys), 1) - lax.broadcasted_iota(
        jnp.int32, (rows, keys), 0
    )
    return (offset >= 0) & (offset <= 2 * HALO) & (query_seg == key_seg)


def attend_kernel(query_seg, key_seg, qkv, mixed, log_total):
    allowed = window_allowed(query_seg[...], key_seg[...])
    width = HEADS * HEAD_DIM
    rows = mixed.shape[0]
    for head in range(HEADS):
        at = head * HEAD_DIM
        q = qkv[HALO : HALO + rows, at : at + HEAD_DIM]
        k = qkv[:, width + at : width + at + HEAD_DIM]
        v = qkv[:, 2 * width + at : 2 * width + at + HEAD_DIM]
        scores = jnp.where(allowed, matmul_t(q, k) * score_scale, -1e30)
        row_max = jnp.max(scores, axis=1, keepdims=True)
        exponent = jnp.exp(scores - row_max)
        total = jnp.sum(exponent, axis=1, keepdims=True)
        probs = (exponent * (1.0 / total)).astype(jnp.bfloat16)
        mixed[:, at : at + HEAD_DIM] = matmul(probs, v).astype(jnp.bfloat16)
        log_total[:, at : at + HEAD_DIM] = jnp.broadcast_to(
            row_max + jnp.log(total), (rows, HEAD_DIM)
        )


def attend_back_kernel(
    query_seg, key_seg, qkv, log_total, grad_mixed, grad_query, own, before, after
):
    allowed = window_allowed(query_seg[...], key_seg[...])
    width = HEADS * HEAD_DIM
    rows = grad_mixed.shape[0]
    for head in range(HEADS):
        at = head * HEAD_DIM
        q = qkv[HALO : HALO + rows, at : at + HEAD_DIM]
        k = qkv[:, width + at : width + at + HEAD_DIM]
        v = qkv[:, 2 * width + at : 2 * width + at + HEAD_DIM]
        grad = grad_mixed[:, at : at + HEAD_DIM]
        scores = jnp.where(allowed, matmul_t(q, k) * score_scale, -1e30)
        probs = jnp.exp(scores - log_total[:, at : at + 1])
        grad_probs = matmul_t(grad, v)
        inner = jnp.sum(probs * grad_probs, axis=1, keepdims=True)
        grad_scores = (probs * (grad_probs - inner)).astype(jnp.bfloat16)
        grad_query[:, at : at + HEAD_DIM] = (matmul(grad_scores, k) * score_scale).astype(
            jnp.bfloat16
        )
        for place, piece in (
            (at, inner_rows(grad_scores, q) * score_scale),
            (width + at, inner_rows(probs.astype(jnp.bfloat16), grad)),
        ):
            columns = slice(place, place + HEAD_DIM)
            before[:, columns] = piece[:HALO].astype(jnp.bfloat16)
            own[:, columns] = piece[HALO : HALO + rows]
            after[:, columns] = piece[HALO + rows :].astype(jnp.bfloat16)


params = pltpu.CompilerParams(vmem_limit_bytes=40 * 1024 * 1024)


def attend(query_seg, key_seg, qkv):
    rows, width = (query_seg.shape[0], HEADS * HEAD_DIM)
    return pl.pallas_call(
        attend_kernel,
        out_shape=(
            jax.ShapeDtypeStruct((rows, width), jnp.bfloat16),
            jax.ShapeDtypeStruct((rows, width), jnp.float32),
        ),
        compiler_params=params,
        name="attend",
    )(query_seg, key_seg, qkv)


def attend_back(query_seg, key_seg, qkv, log_total, grad_mixed):
    rows, width = (query_seg.shape[0], HEADS * HEAD_DIM)
    return pl.pallas_call(
        attend_back_kernel,
        out_shape=(
            jax.ShapeDtypeStruct((rows, width), jnp.bfloat16),
            jax.ShapeDtypeStruct((rows, 2 * width), jnp.float32),
            jax.ShapeDtypeStruct((HALO, 2 * width), jnp.bfloat16),
            jax.ShapeDtypeStruct((HALO, 2 * width), jnp.bfloat16),
        ),
        compiler_params=params,
        name="attend_back",
    )(query_seg, key_seg, qkv, log_total, grad_mixed)


def to_next(array):
    return lax.ppermute(array, "seq", [(i, i + 1) for i in range(SEQ_DEV - 1)])


def to_previous(array):
    return lax.ppermute(array, "seq", [(i + 1, i) for i in range(SEQ_DEV - 1)])


def split_normal(gate):
    cumulative = 0.5 * (1.0 + lax.erf(gate * root_half))
    return cumulative


def layer_forward(rows_in, gain_pair, weights, segs, on_first):
    (attn_own, attn_other), (hidden_own, hidden_other), (down_own, down_other) = weights
    width = rows_in.shape[1]
    normed1, factor1 = norm_parts(rows_in)
    act_in = (normed1 * gain_pair[0]).astype(jnp.bfloat16)
    before = to_next(act_in[act_in.shape[0] - HALO :])
    after = to_previous(act_in[:HALO])
    extended = jnp.concatenate([before, act_in, after], axis=0)
    own, other = column_halves(extended, on_first)
    qkv = (
        matmul(own, attn_own[:, : 3 * width]) + matmul(other, attn_other[:, : 3 * width])
    ).astype(jnp.bfloat16)
    mixed, log_total = attend(*segs, qkv)
    own, other = column_halves(mixed, on_first)
    middle = (
        rows_in + matmul(own, attn_own[:, 3 * width :]) + matmul(other, attn_other[:, 3 * width :])
    )
    normed2, factor2 = norm_parts(middle)
    act_mid = (normed2 * gain_pair[1]).astype(jnp.bfloat16)
    own, other = column_halves(act_mid, on_first)
    hidden = matmul(own, hidden_own) + matmul(other, hidden_other)
    gate, up = (hidden[:, :FF_PAD], hidden[:, FF_PAD:])
    product = (gate * split_normal(gate) * up).astype(jnp.bfloat16)
    mine, theirs = (matmul(product, down_own), matmul(product, down_other))
    output = middle + jnp.concatenate(
        [jnp.where(on_first, mine, theirs), jnp.where(on_first, theirs, mine)], axis=1
    )
    acts = jnp.concatenate([jnp.stack([act_in, mixed, act_mid]), row_groups(product)], axis=0)
    kept = (normed1, factor1, qkv, log_total, normed2, factor2, hidden, acts, swapped(acts))
    return (output, kept)


def row_groups(product):
    devices, groups = (SEQ_DEV * W_DEV, PAD_ROWS // 16)
    pieces = product[:, :FF].reshape(product.shape[0], devices, FF // devices)
    pieces = jnp.pad(pieces, ((0, 0), (0, 0), (0, PAD_ROWS - pieces.shape[2])))
    pieces = pieces.reshape(product.shape[0], devices, groups, 16).transpose(2, 0, 1, 3)
    return pieces.reshape(groups, product.shape[0], devices * 16)


def seq_sum(total):
    return lax.psum_scatter(total, "seq", scatter_dimension=0, tiled=True)


def weight_grad_kernel(
    act_index, grad_index, act_mine, act_got, grad_mine, grad_got, gains, out, turned, rows
):
    step = pl.program_id(0)
    count = act_mine.shape[1]

    @pl.when((step == 0) | (act_index[step] != act_index[jnp.maximum(step - 1, 0)]))
    def _():
        turned[:, :count] = act_mine[0].T
        turned[:, count:] = act_got[0].T

    rows[:count] = grad_mine[...]
    rows[count:] = grad_got[...]
    out[...] = matmul(turned[...], rows[...]).astype(jnp.bfloat16)

    @pl.when(step == (2048 + GRAD_PAD) // BLOCK - 1)
    def _():
        out[:, BLOCK - gains.shape[1] :] = gains[...]


def weight_grads(act_mine, act_got, grad_mine, grad_got, gains):
    count, width = act_mine.shape[1:]
    sizes = (1536 // BLOCK, 512 // BLOCK, GRAD_PAD // BLOCK) + (512 // BLOCK,) * 3
    acts, grads, at = ([], [], 0)
    for member, blocks in enumerate(sizes):
        first = at if member < 3 else sum(sizes[:3])
        acts += [member] * blocks
        grads += list(range(first, first + blocks))
        at += blocks
    act_spec = pl.BlockSpec((1, count, width), lambda n, a, g: (a[n], 0, 0))
    grad_spec = pl.BlockSpec((count, BLOCK), lambda n, a, g: (0, g[n]))
    return pl.pallas_call(
        weight_grad_kernel,
        grid_spec=pltpu.PrefetchScalarGridSpec(
            num_scalar_prefetch=2,
            grid=(len(acts),),
            in_specs=[
                act_spec,
                act_spec,
                grad_spec,
                grad_spec,
                pl.BlockSpec((width, 128), lambda n, a, g: (0, 0)),
            ],
            out_specs=pl.BlockSpec((width, BLOCK), lambda n, a, g: (0, n)),
            scratch_shapes=[
                pltpu.VMEM((width, 2 * count), jnp.bfloat16),
                pltpu.VMEM((2 * count, BLOCK), jnp.bfloat16),
            ],
        ),
        out_shape=jax.ShapeDtypeStruct((width, len(acts) * BLOCK), jnp.bfloat16),
        compiler_params=params,
        name="weight_grads",
    )(jnp.array(acts, jnp.int32), jnp.array(grads, jnp.int32), act_mine, act_got, grad_mine, grad_got, gains)


def layer_backward(grad_out, kept, gain_pair, weights, segs, on_first):
    (attn_own, attn_other), (hidden_own, hidden_other), (down_own, down_other) = weights
    (normed1, factor1, qkv, log_total, normed2, factor2, hidden, acts, acts_got) = kept
    rows, width = normed1.shape
    half = width // 2
    grad_branch = grad_out.astype(jnp.bfloat16)
    low, high = (grad_branch[:, :half], grad_branch[:, half:])
    branch_own, branch_other = (jnp.where(on_first, low, high), jnp.where(on_first, high, low))
    grad_product = matmul_t(branch_own, down_own) + matmul_t(branch_other, down_other)
    gate, up = (hidden[:, :FF_PAD], hidden[:, FF_PAD:])
    cumulative = split_normal(gate)
    derivative = cumulative + gate * jnp.exp(-0.5 * gate * gate) * root_two_pi
    grad_gate = (grad_product * up * derivative).astype(jnp.bfloat16)
    grad_up = (grad_product * gate * cumulative).astype(jnp.bfloat16)
    grad_hidden = jnp.concatenate([grad_gate, grad_up], axis=1)
    mine, theirs = [matmul_t(grad_hidden, w) for w in (hidden_own, hidden_other)]
    grad_norm2 = from_halves(mine, theirs, on_first)
    gain_mid = jnp.sum(normed2 * grad_norm2, axis=0)
    grad_middle = grad_out + norm_back(grad_norm2 * gain_pair[1], normed2, factor2)
    grad_attn = grad_middle.astype(jnp.bfloat16)
    mine, theirs = [matmul_t(grad_attn, w[:, 3 * width :]) for w in (attn_own, attn_other)]
    grad_mixed = from_halves(mine, theirs, on_first).astype(jnp.bfloat16)
    grad_query, grad_own, grad_before, grad_after = attend_back(*segs, qkv, log_total, grad_mixed)
    from_previous = to_next(grad_after).astype(jnp.float32)
    from_next = to_previous(grad_before).astype(jnp.float32)
    grad_pairs = grad_own + jnp.concatenate([from_previous, from_next], axis=0)
    grad_qkv = jnp.concatenate([grad_query, grad_pairs.astype(jnp.bfloat16)], axis=1)
    halves = (
        (grad_qkv[:, : 3 * half], grad_qkv[:, 3 * half :]),
        (grad_attn[:, :half], grad_attn[:, half:]),
        (grad_gate, grad_up),
        (jnp.zeros((rows, GRAD_PAD - FF_PAD), jnp.bfloat16),) * 2,
        (low, high),
    )
    first, second = [jnp.concatenate([h[k] for h in halves], axis=1) for k in range(2)]
    grad_mine = jnp.where(on_first, first, second)
    grad_got = swapped(jnp.where(on_first, second, first))
    mine, theirs = [matmul_t(grad_qkv, w[:, : 3 * width]) for w in (attn_own, attn_other)]
    grad_norm1 = from_halves(mine, theirs, on_first)
    gain_first = jnp.sum(normed1 * grad_norm1, axis=0)
    grad_inputs = grad_middle + norm_back(grad_norm1 * gain_pair[0], normed1, factor1)
    gains = jnp.stack([gain_first, gain_mid])
    gain_columns = jnp.pad(gains, ((0, 126), (0, 0))).T.astype(jnp.bfloat16)
    return (grad_inputs, seq_sum(weight_grads(acts, acts_got, grad_mine, grad_got, gain_columns)))


def summed_over_w(block, place):
    rows = block.shape[0] // W_DEV
    total = lax.dynamic_slice_in_dim(block, place * rows, rows).astype(jnp.float32)
    for step in range(1, W_DEV):
        part = lax.dynamic_slice_in_dim(block, lax.rem(place + step, W_DEV) * rows, rows)
        got = lax.ppermute(part, "wshard", [(j, (j + step) % W_DEV) for j in range(W_DEV)])
        total = total + got.astype(jnp.float32)
    return total


def per_device(
    inputs, cotangent, segments, norm_gains, attend_in, attend_out, hidden_in, hidden_out
):
    on_first = lax.axis_index("section") == 0
    core = lax.axis_index("section")
    seq_place = lax.axis_index("seq")
    w_place = lax.axis_index("wshard")

    def by_core(first, second):
        return jnp.where(on_first, first, second)

    def sections(own, got):
        return (by_core(own, got), by_core(got, own))

    pad = jnp.zeros((hidden_in.shape[1], FF_PAD - FF), jnp.bfloat16)
    row_weights = jnp.concatenate(
        [attend_in[0], attend_out[0], hidden_in[0, :, :FF], pad, hidden_in[0, :, FF:], pad], axis=1
    )
    slice_rows = row_weights.shape[0] // (2 * SEQ_DEV)

    def row_slice(which):
        return lax.dynamic_slice_in_dim(
            row_weights, (which * SEQ_DEV + seq_place) * slice_rows, slice_rows
        )

    row_pieces = sections(row_slice(core), swapped(row_slice(1 - core)))
    all_own = lax.all_gather(
        jnp.concatenate(row_pieces, axis=1), ("wshard", "seq"), axis=0, tiled=True
    )
    half = hidden_out.shape[2] // 2
    low, high = (hidden_out[0, :, :half], hidden_out[0, :, half:])
    down_piece = jnp.concatenate(sections(by_core(low, high), swapped(by_core(high, low))), axis=1)
    down_pieces = [down_piece]
    for step in range(1, W_DEV):
        down_pieces.append(
            lax.ppermute(down_piece, "wshard", [(j, (j + step) % W_DEV) for j in range(W_DEV)])
        )
    gains_other = swapped(norm_gains[0])
    gain_pairs = sections(norm_gains[0], gains_other)
    attn_width = attend_in.shape[2] + attend_out.shape[2]

    def both(own):
        return (own, swapped(own))

    def weights_of(section):
        at, rows = (section * row_weights.shape[1], down_piece.shape[0])
        down_own = jnp.zeros((FF_PAD, half), jnp.bfloat16)
        for step, piece in enumerate(down_pieces):
            down_own = lax.dynamic_update_slice_in_dim(
                down_own,
                piece[:, section * half : (section + 1) * half],
                lax.rem(w_place + W_DEV - step, W_DEV) * rows,
                0,
            )
        return (
            both(all_own[:, at : at + attn_width]),
            both(all_own[:, at + attn_width : at + row_weights.shape[1]]),
            both(down_own),
        )

    weights = (weights_of(0), weights_of(1))
    rows_in = by_core(inputs[0, 0], inputs[1, 0])
    row_count = rows_in.shape[0]
    segment_row = by_core(segments[0, 0], segments[1, 0])
    padded = jnp.pad(segment_row, (HALO, HALO), constant_values=-1)
    first_row = seq_place * row_count
    segs = (
        lax.dynamic_slice_in_dim(segment_row, first_row, row_count)[:, None],
        lax.dynamic_slice_in_dim(padded, first_row, row_count + 2 * HALO)[None, :],
    )
    middle, kept0 = layer_forward(rows_in, gain_pairs[0], weights[0], segs, on_first)
    final, kept1 = layer_forward(middle, gain_pairs[1], weights[1], segs, on_first)
    upstream = by_core(cotangent[0, 0], cotangent[1, 0])
    grads1, sums1 = layer_backward(upstream, kept1, gain_pairs[1], weights[1], segs, on_first)
    grads0, sums0 = layer_backward(grads1, kept0, gain_pairs[0], weights[0], segs, on_first)

    def placed(first, second):
        mine, give = (by_core(first, second), by_core(second, first))
        got = swapped(give)
        return jnp.stack([by_core(mine, got), by_core(got, mine)])[None, :, None]

    section_outputs = placed(middle, final)
    section_input_grads = placed(grads0, grads1)

    totals = [summed_over_w(sums, w_place) for sums in (sums0, sums1)]
    mine, got = (by_core(*totals), swapped(by_core(totals[1], totals[0])))
    low, high = (by_core(mine, got), by_core(got, mine))
    width = rows_in.shape[1]
    attn_end, hidden_at = (3 * width // 2, 2 * width)
    down_at = hidden_at + GRAD_PAD
    qkv_rows = jnp.concatenate([low[:, :attn_end], high[:, :attn_end]], axis=1)
    attn_rows = jnp.concatenate([low[:, attn_end:hidden_at], high[:, attn_end:hidden_at]], axis=1)
    hidden_rows = jnp.concatenate(
        [low[:, hidden_at : hidden_at + FF], high[:, hidden_at : hidden_at + FF]], axis=1
    )
    gain_rows = (low + high)[:, down_at - 128 : down_at - 126].T
    down_total = jnp.concatenate(
        [
            jnp.concatenate(
                [h[:, at : at + width // 2] for h in (low, high)], axis=1
            )
            for at in range(down_at, low.shape[1], width // 2)
        ],
        axis=0,
    )[: FF // (SEQ_DEV * W_DEV)]
    return (
        section_outputs,
        section_input_grads,
        qkv_rows[None],
        attn_rows[None],
        hidden_rows[None],
        down_total[None],
        gain_rows[None],
    )


def solution(mesh):
    placed = (
        P(None, "wshard", "seq", None),
        P(None, "wshard", "seq", None),
        P(None, "wshard", None),
        P("section", None, None),
        P("section", "wshard", None),
        P("section", "wshard", None),
        P("section", "wshard", None),
        P("section", "wshard", None),
    )
    return jax.shard_map(
        per_device,
        mesh=mesh,
        in_specs=placed,
        out_specs=(
            P("section", None, "wshard", "seq", None),
            P("section", None, "wshard", "seq", None),
            P("section", ("seq", "wshard"), None),
            P("section", ("seq", "wshard"), None),
            P("section", ("seq", "wshard"), None),
            P("section", ("seq", "wshard"), None),
            P("section", None, ("seq", "wshard")),
        ),
        check_vma=False,
    )
```

```python
import math

import jax
import jax.numpy as jnp
from jax import lax
from jax.experimental import pallas as pl
from jax.experimental.pallas import tpu as pltpu
from jax.sharding import PartitionSpec as P

HEADS = 16
HEAD_DIM = 64
FF = 2624
HALO = 64
FF_PAD = 2688
SEQ_DEV = 16
W_DEV = 4
PAD_ROWS = 48
GRAD_PAD = 2816
HIDDEN_BLOCK = 384
QKV_BLOCK = 768

norm_eps = 1e-05
root_half = 1.0 / math.sqrt(2.0)
root_two_pi = 1.0 / math.sqrt(2.0 * math.pi)
score_scale = 1.0 / math.sqrt(HEAD_DIM)

SWAP = [(0, 1), (1, 0)]


def swapped(array):
    return lax.ppermute(array, "section", SWAP)


def norm_parts(rows_in):
    centred = rows_in - jnp.mean(rows_in, axis=1, keepdims=True)
    factor = lax.rsqrt(jnp.mean(centred * centred, axis=1, keepdims=True) + norm_eps)
    return (centred * factor, factor)


def norm_back(grad_norm, normed, factor):
    inner = jnp.mean(grad_norm, axis=1, keepdims=True)
    along = jnp.mean(grad_norm * normed, axis=1, keepdims=True)
    return factor * (grad_norm - inner - normed * along)


def matmul(left, right):
    return jnp.dot(left, right, preferred_element_type=jnp.float32)


def matmul_t(left, right):
    return lax.dot_general(
        left, right, (((1,), (1,)), ((), ())), preferred_element_type=jnp.float32
    )


def inner_rows(left, right):
    return lax.dot_general(
        left, right, (((0,), (0,)), ((), ())), preferred_element_type=jnp.float32
    )


def column_halves(array, on_first):
    even = jnp.concatenate([array[:, 256 * k : 256 * k + 128] for k in range(4)], axis=1)
    odd = jnp.concatenate([array[:, 256 * k + 128 : 256 * k + 256] for k in range(4)], axis=1)
    return (jnp.where(on_first, even, odd), jnp.where(on_first, odd, even))


def from_halves(own, other, on_first):
    even = jnp.where(on_first, own, other)
    odd = jnp.where(on_first, other, own)
    parts = []
    for k in range(4):
        parts += [even[:, 128 * k : 128 * k + 128], odd[:, 128 * k : 128 * k + 128]]
    return jnp.concatenate(parts, axis=1)


def window_allowed(query_seg, key_seg):
    rows, keys = (query_seg.shape[0], key_seg.shape[1])
    offset = lax.broadcasted_iota(jnp.int32, (rows, keys), 1) - lax.broadcasted_iota(
        jnp.int32, (rows, keys), 0
    )
    return (offset >= 0) & (offset <= 2 * HALO) & (query_seg == key_seg)


def attend_kernel(query_seg, key_seg, qkv, mixed, log_total):
    allowed = window_allowed(query_seg[...], key_seg[...])
    width = HEADS * HEAD_DIM
    rows = mixed.shape[0]
    for head in range(HEADS):
        at = head * HEAD_DIM
        q = qkv[HALO : HALO + rows, at : at + HEAD_DIM]
        k = qkv[:, width + at : width + at + HEAD_DIM]
        v = qkv[:, 2 * width + at : 2 * width + at + HEAD_DIM]
        scores = jnp.where(allowed, matmul_t(q, k) * score_scale, -1e30)
        row_max = jnp.max(scores, axis=1, keepdims=True)
        exponent = jnp.exp(scores - row_max)
        total = jnp.sum(exponent, axis=1, keepdims=True)
        probs = (exponent * (1.0 / total)).astype(jnp.bfloat16)
        mixed[:, at : at + HEAD_DIM] = matmul(probs, v).astype(jnp.bfloat16)
        log_total[:, at : at + HEAD_DIM] = jnp.broadcast_to(
            row_max + jnp.log(total), (rows, HEAD_DIM)
        )


def attend_back_kernel(
    query_seg, key_seg, qkv, log_total, grad_mixed, grad_query, own, before, after
):
    allowed = window_allowed(query_seg[...], key_seg[...])
    width = HEADS * HEAD_DIM
    rows = grad_mixed.shape[0]
    for head in range(HEADS):
        at = head * HEAD_DIM
        q = qkv[HALO : HALO + rows, at : at + HEAD_DIM]
        k = qkv[:, width + at : width + at + HEAD_DIM]
        v = qkv[:, 2 * width + at : 2 * width + at + HEAD_DIM]
        grad = grad_mixed[:, at : at + HEAD_DIM]
        scores = jnp.where(allowed, matmul_t(q, k) * score_scale, -1e30)
        probs = jnp.exp(scores - log_total[:, at : at + 1])
        grad_probs = matmul_t(grad, v)
        inner = jnp.sum(probs * grad_probs, axis=1, keepdims=True)
        grad_scores = (probs * (grad_probs - inner)).astype(jnp.bfloat16)
        grad_query[:, at : at + HEAD_DIM] = (matmul(grad_scores, k) * score_scale).astype(
            jnp.bfloat16
        )
        for place, piece in (
            (at, inner_rows(grad_scores, q) * score_scale),
            (width + at, inner_rows(probs.astype(jnp.bfloat16), grad)),
        ):
            columns = slice(place, place + HEAD_DIM)
            before[:, columns] = piece[:HALO].astype(jnp.bfloat16)
            own[:, columns] = piece[HALO : HALO + rows]
            after[:, columns] = piece[HALO + rows :].astype(jnp.bfloat16)


params = pltpu.CompilerParams(vmem_limit_bytes=40 * 1024 * 1024)


def attend(query_seg, key_seg, qkv):
    rows, width = (query_seg.shape[0], HEADS * HEAD_DIM)
    return pl.pallas_call(
        attend_kernel,
        out_shape=(
            jax.ShapeDtypeStruct((rows, width), jnp.bfloat16),
            jax.ShapeDtypeStruct((rows, width), jnp.float32),
        ),
        compiler_params=params,
        name="attend",
    )(query_seg, key_seg, qkv)


def attend_back(query_seg, key_seg, qkv, log_total, grad_mixed):
    rows, width = (query_seg.shape[0], HEADS * HEAD_DIM)
    return pl.pallas_call(
        attend_back_kernel,
        out_shape=(
            jax.ShapeDtypeStruct((rows, width), jnp.bfloat16),
            jax.ShapeDtypeStruct((rows, 2 * width), jnp.float32),
            jax.ShapeDtypeStruct((HALO, 2 * width), jnp.bfloat16),
            jax.ShapeDtypeStruct((HALO, 2 * width), jnp.bfloat16),
        ),
        compiler_params=params,
        name="attend_back",
    )(query_seg, key_seg, qkv, log_total, grad_mixed)


def to_next(array):
    return lax.ppermute(array, "seq", [(i, i + 1) for i in range(SEQ_DEV - 1)])


def to_previous(array):
    return lax.ppermute(array, "seq", [(i + 1, i) for i in range(SEQ_DEV - 1)])


def split_normal(gate):
    cumulative = 0.5 * (1.0 + lax.erf(gate * root_half))
    return cumulative


def grid_call(kernel, name, scalars, grid, in_specs, out_specs, out_shape, scratch, args):
    return pl.pallas_call(
        kernel,
        grid_spec=pltpu.PrefetchScalarGridSpec(
            num_scalar_prefetch=len(scalars),
            grid=grid,
            in_specs=in_specs,
            out_specs=out_specs,
            scratch_shapes=scratch,
        ),
        out_shape=out_shape,
        compiler_params=params,
        name=name,
    )(*scalars, *args)


def whole(array):
    return pl.BlockSpec(array.shape, lambda n, *_: (0,) * array.ndim)


def columns_at(rows, block, first):
    return pl.BlockSpec((rows, block), lambda n, *_: (0, first + n))


def rows_at(block, columns):
    return pl.BlockSpec((block, columns), lambda n, *_: (n, 0))


def add_to(step, total, value):
    @pl.when(step == 0)
    def _():
        total[...] = value

    @pl.when(step > 0)
    def _():
        total[...] += value


def store_halves(out, own, other, on_first):
    for k in range(4):
        block = slice(128 * k, 128 * k + 128)
        out[:, 256 * k : 256 * k + 128] = jnp.where(on_first, own[:, block], other[:, block])
        out[:, 256 * k + 128 : 256 * k + 256] = jnp.where(on_first, other[:, block], own[:, block])


def qkv_kernel(own, other, weight_own, weight_other, out):
    out[...] = (
        matmul(own[...], weight_own[...]) + matmul(other[...], weight_other[...])
    ).astype(jnp.bfloat16)


def qkv_of(own, other, weights):
    (w_own, at_own), (w_other, at_other) = weights["qkv"]
    width = 3 * HEADS * HEAD_DIM
    depth = own.shape[1]
    return grid_call(
        qkv_kernel,
        "qkv",
        (),
        (width // QKV_BLOCK,),
        [
            whole(own),
            whole(other),
            columns_at(depth, QKV_BLOCK, at_own // QKV_BLOCK),
            columns_at(depth, QKV_BLOCK, at_other // QKV_BLOCK),
        ],
        columns_at(own.shape[0], QKV_BLOCK, 0),
        jax.ShapeDtypeStruct((own.shape[0], width), jnp.bfloat16),
        [],
        (own, other, w_own, w_other),
    )


def qkv_back_kernel(first, grad, weight_own, weight_other, out, total_own, total_other):
    step = pl.program_id(0)
    add_to(step, total_own, matmul_t(grad[...], weight_own[...]))
    add_to(step, total_other, matmul_t(grad[...], weight_other[...]))

    @pl.when(step == pl.num_programs(0) - 1)
    def _():
        store_halves(out, total_own[...], total_other[...], first[0] == 1)


def qkv_back(first, grad, weights):
    (w_own, at_own), (w_other, at_other) = weights["qkv"]
    rows, width = grad.shape
    depth = w_own.shape[0]
    return grid_call(
        qkv_back_kernel,
        "qkv_back",
        (first,),
        (width // QKV_BLOCK,),
        [
            columns_at(rows, QKV_BLOCK, 0),
            columns_at(depth, QKV_BLOCK, at_own // QKV_BLOCK),
            columns_at(depth, QKV_BLOCK, at_other // QKV_BLOCK),
        ],
        pl.BlockSpec((rows, 2 * depth), lambda n, *_: (0, 0)),
        jax.ShapeDtypeStruct((rows, 2 * depth), jnp.float32),
        [pltpu.VMEM((rows, depth), jnp.float32)] * 2,
        (grad, w_own, w_other),
    )


def hidden_kernel(
    first, own, other, gate_own, gate_other, up_own, up_other, down_own, down_other, middle,
    gate_out, up_out, product_out, out, total_own, total_other,
):
    step = pl.program_id(0)
    gate = matmul(own[...], gate_own[...]) + matmul(other[...], gate_other[...])
    up = matmul(own[...], up_own[...]) + matmul(other[...], up_other[...])
    product = (gate * split_normal(gate) * up).astype(jnp.bfloat16)
    gate_out[...] = gate
    up_out[...] = up
    product_out[...] = product
    add_to(step, total_own, matmul(product, down_own[...]))
    add_to(step, total_other, matmul(product, down_other[...]))

    @pl.when(step == pl.num_programs(0) - 1)
    def _():
        half = total_own.shape[1]
        mine, theirs, on_first = (total_own[...], total_other[...], first[0] == 1)
        out[:, :half] = middle[:, :half] + jnp.where(on_first, mine, theirs)
        out[:, half:] = middle[:, half:] + jnp.where(on_first, theirs, mine)


def hidden_specs(weights, depth):
    specs, arrays = ([], [])
    for part in ("gate", "up"):
        for array, at in weights[part]:
            specs.append(columns_at(depth, HIDDEN_BLOCK, at // HIDDEN_BLOCK))
            arrays.append(array)
    for array in weights["down"]:
        specs.append(rows_at(HIDDEN_BLOCK, array.shape[1]))
        arrays.append(array)
    return (specs, arrays)


def hidden_forward(first, own, other, middle, weights):
    rows, depth = own.shape
    width = middle.shape[1]
    specs, arrays = hidden_specs(weights, depth)
    piece = columns_at(rows, HIDDEN_BLOCK, 0)
    return grid_call(
        hidden_kernel,
        "hidden",
        (first,),
        (FF_PAD // HIDDEN_BLOCK,),
        [whole(own), whole(other), *specs, whole(middle)],
        (piece, piece, piece, whole(middle)),
        (
            jax.ShapeDtypeStruct((rows, FF_PAD), jnp.float32),
            jax.ShapeDtypeStruct((rows, FF_PAD), jnp.float32),
            jax.ShapeDtypeStruct((rows, FF_PAD), jnp.bfloat16),
            jax.ShapeDtypeStruct((rows, width), jnp.float32),
        ),
        [pltpu.VMEM((rows, width // 2), jnp.float32)] * 2,
        (own, other, *arrays, middle),
    )


def hidden_back_kernel(
    first, grad_own, grad_other, gate_in, up_in, gate_own, gate_other, up_own, up_other, down_own,
    down_other, grad_gate_out, grad_up_out, out, total_own, total_other,
):
    step = pl.program_id(0)
    gate, up = (gate_in[...], up_in[...])
    grad_product = matmul_t(grad_own[...], down_own[...]) + matmul_t(
        grad_other[...], down_other[...]
    )
    cumulative = split_normal(gate)
    derivative = cumulative + gate * jnp.exp(-0.5 * gate * gate) * root_two_pi
    grad_gate = (grad_product * up * derivative).astype(jnp.bfloat16)
    grad_up = (grad_product * gate * cumulative).astype(jnp.bfloat16)
    grad_gate_out[...] = grad_gate
    grad_up_out[...] = grad_up
    add_to(step, total_own, matmul_t(grad_gate, gate_own[...]) + matmul_t(grad_up, up_own[...]))
    add_to(
        step, total_other, matmul_t(grad_gate, gate_other[...]) + matmul_t(grad_up, up_other[...])
    )

    @pl.when(step == pl.num_programs(0) - 1)
    def _():
        store_halves(out, total_own[...], total_other[...], first[0] == 1)


def hidden_back(first, grad_own, grad_other, gate, up, weights):
    rows, half = grad_own.shape
    depth = half
    specs, arrays = hidden_specs(weights, depth)
    piece = columns_at(rows, HIDDEN_BLOCK, 0)
    return grid_call(
        hidden_back_kernel,
        "hidden_back",
        (first,),
        (FF_PAD // HIDDEN_BLOCK,),
        [whole(grad_own), whole(grad_other), piece, piece, *specs],
        (piece, piece, pl.BlockSpec((rows, 2 * depth), lambda n, *_: (0, 0))),
        (
            jax.ShapeDtypeStruct((rows, FF_PAD), jnp.bfloat16),
            jax.ShapeDtypeStruct((rows, FF_PAD), jnp.bfloat16),
            jax.ShapeDtypeStruct((rows, 2 * depth), jnp.float32),
        ),
        [pltpu.VMEM((rows, depth), jnp.float32)] * 2,
        (grad_own, grad_other, gate, up, *arrays),
    )


def layer_forward(rows_in, gain_pair, weights, segs, on_first, first):
    normed1, factor1 = norm_parts(rows_in)
    act_in = (normed1 * gain_pair[0]).astype(jnp.bfloat16)
    before = to_next(act_in[act_in.shape[0] - HALO :])
    after = to_previous(act_in[:HALO])
    extended = jnp.concatenate([before, act_in, after], axis=0)
    qkv = qkv_of(*column_halves(extended, on_first), weights)
    mixed, log_total = attend(*segs, qkv)
    own, other = column_halves(mixed, on_first)
    middle = rows_in + matmul(own, weights["out"][0]) + matmul(other, weights["out"][1])
    normed2, factor2 = norm_parts(middle)
    act_mid = (normed2 * gain_pair[1]).astype(jnp.bfloat16)
    own, other = column_halves(act_mid, on_first)
    gate, up, product, output = hidden_forward(first, own, other, middle, weights)
    acts = jnp.concatenate([jnp.stack([act_in, mixed, act_mid]), row_groups(product)], axis=0)
    kept = (normed1, factor1, qkv, log_total, normed2, factor2, gate, up, acts, swapped(acts))
    return (output, kept)


def row_groups(product):
    devices, groups = (SEQ_DEV * W_DEV, PAD_ROWS // 16)
    pieces = product[:, :FF].reshape(product.shape[0], devices, FF // devices)
    pieces = jnp.pad(pieces, ((0, 0), (0, 0), (0, PAD_ROWS - pieces.shape[2])))
    pieces = pieces.reshape(product.shape[0], devices, groups, 16).transpose(2, 0, 1, 3)
    return pieces.reshape(groups, product.shape[0], devices * 16)


def seq_sum(total):
    return lax.psum_scatter(total, "seq", scatter_dimension=0, tiled=True)


GRAD_WIDTHS = (1536, 512, GRAD_PAD, 512, 512, 512)


def weight_grad_kernel(act_mine, act_got, grad_mine, grad_got, gains, out, grads):
    count = act_mine.shape[1]

    @pl.when(pl.program_id(0) == 0)
    def _():
        grads[:count] = grad_mine[...]
        grads[count:] = grad_got[...]

    at = 0
    for member, width in enumerate(GRAD_WIDTHS):
        acts = jnp.concatenate([act_mine[member], act_got[member]], axis=0)
        place = at if member < 3 else sum(GRAD_WIDTHS[:3])
        for part in range(0, width, 512):
            size = min(512, width - part)
            out[:, at + part : at + part + size] = inner_rows(
                acts, grads[:, place + part : place + part + size]
            ).astype(jnp.bfloat16)
        at += width
    end = sum(GRAD_WIDTHS[:3])
    out[:, end - gains.shape[1] : end] = gains[...]


def weight_grads(act_mine, act_got, grad_mine, grad_got, gains):
    members, count, width = act_mine.shape
    block = 256
    acts = pl.BlockSpec((members, count, block), lambda n: (0, 0, n))
    return grid_call(
        weight_grad_kernel,
        "weight_grads",
        (),
        (width // block,),
        [acts, acts, whole(grad_mine), whole(grad_got), rows_at(block, gains.shape[1])],
        rows_at(block, sum(GRAD_WIDTHS)),
        jax.ShapeDtypeStruct((width, sum(GRAD_WIDTHS)), jnp.bfloat16),
        [pltpu.VMEM((2 * count, grad_mine.shape[1]), jnp.bfloat16)],
        (act_mine, act_got, grad_mine, grad_got, gains),
    )


def layer_backward(grad_out, kept, gain_pair, weights, segs, on_first, first):
    (normed1, factor1, qkv, log_total, normed2, factor2, gate, up, acts, acts_got) = kept
    rows, width = normed1.shape
    half = width // 2
    grad_branch = grad_out.astype(jnp.bfloat16)
    low, high = (grad_branch[:, :half], grad_branch[:, half:])
    branch_own, branch_other = (jnp.where(on_first, low, high), jnp.where(on_first, high, low))
    grad_gate, grad_up, grad_norm2 = hidden_back(
        first, branch_own, branch_other, gate, up, weights
    )
    gain_mid = jnp.sum(normed2 * grad_norm2, axis=0)
    grad_middle = grad_out + norm_back(grad_norm2 * gain_pair[1], normed2, factor2)
    grad_attn = grad_middle.astype(jnp.bfloat16)
    mine, theirs = [matmul_t(grad_attn, w) for w in weights["out"]]
    grad_mixed = from_halves(mine, theirs, on_first).astype(jnp.bfloat16)
    grad_query, grad_own, grad_before, grad_after = attend_back(*segs, qkv, log_total, grad_mixed)
    from_previous = to_next(grad_after).astype(jnp.float32)
    from_next = to_previous(grad_before).astype(jnp.float32)
    grad_pairs = grad_own + jnp.concatenate([from_previous, from_next], axis=0)
    grad_qkv = jnp.concatenate([grad_query, grad_pairs.astype(jnp.bfloat16)], axis=1)
    halves = (
        (grad_qkv[:, : 3 * half], grad_qkv[:, 3 * half :]),
        (grad_attn[:, :half], grad_attn[:, half:]),
        (grad_gate, grad_up),
        (jnp.zeros((rows, GRAD_PAD - FF_PAD), jnp.bfloat16),) * 2,
        (low, high),
    )
    first_half, second_half = [jnp.concatenate([h[k] for h in halves], axis=1) for k in range(2)]
    grad_mine = jnp.where(on_first, first_half, second_half)
    grad_got = swapped(jnp.where(on_first, second_half, first_half))
    grad_norm1 = qkv_back(first, grad_qkv, weights)
    gain_first = jnp.sum(normed1 * grad_norm1, axis=0)
    grad_inputs = grad_middle + norm_back(grad_norm1 * gain_pair[0], normed1, factor1)
    gains = jnp.stack([gain_first, gain_mid])
    gain_columns = jnp.pad(gains, ((0, 126), (0, 0))).T.astype(jnp.bfloat16)
    return (grad_inputs, seq_sum(weight_grads(acts, acts_got, grad_mine, grad_got, gain_columns)))


def summed_over_w(block, place):
    rows = block.shape[0] // W_DEV
    total = lax.dynamic_slice_in_dim(block, place * rows, rows).astype(jnp.float32)
    for step in range(1, W_DEV):
        part = lax.dynamic_slice_in_dim(block, lax.rem(place + step, W_DEV) * rows, rows)
        got = lax.ppermute(part, "wshard", [(j, (j + step) % W_DEV) for j in range(W_DEV)])
        total = total + got.astype(jnp.float32)
    return total


def per_device(
    inputs, cotangent, segments, norm_gains, attend_in, attend_out, hidden_in, hidden_out
):
    on_first = lax.axis_index("section") == 0
    core = lax.axis_index("section")
    seq_place = lax.axis_index("seq")
    w_place = lax.axis_index("wshard")

    def by_core(first, second):
        return jnp.where(on_first, first, second)

    def sections(own, got):
        return (by_core(own, got), by_core(got, own))

    slice_rows = attend_in.shape[1] // (2 * SEQ_DEV)
    pad = jnp.zeros((slice_rows, FF_PAD - FF), jnp.bfloat16)
    width = inputs.shape[3]

    def row_slice(which):
        at = (which * SEQ_DEV + seq_place) * slice_rows
        hidden, qkv, out = [
            lax.dynamic_slice_in_dim(w[0], at, slice_rows)
            for w in (hidden_in, attend_in, attend_out)
        ]
        return jnp.concatenate([hidden[:, :FF], pad, hidden[:, FF:], pad, qkv, out], axis=1)

    row_pieces = sections(row_slice(core), swapped(row_slice(1 - core)))
    up_at, qkv_at, out_at = (FF_PAD, 2 * FF_PAD, 2 * FF_PAD + 3 * width)
    all_own = lax.all_gather(
        jnp.concatenate(
            [piece[:, :out_at] for piece in row_pieces] + [piece[:, out_at:] for piece in row_pieces],
            axis=1,
        ),
        ("wshard", "seq"),
        axis=0,
        tiled=True,
    )
    half = hidden_out.shape[2] // 2
    low, high = (hidden_out[0, :, :half], hidden_out[0, :, half:])
    down_piece = jnp.concatenate(sections(by_core(low, high), swapped(by_core(high, low))), axis=1)
    w_up = [(j, (j + 1) % W_DEV) for j in range(W_DEV)]
    w_down = [(j, i) for i, j in w_up]
    below = lax.ppermute(down_piece, "wshard", w_up)
    above = lax.ppermute(down_piece, "wshard", w_down)
    far = (
        lax.ppermute(below[:, :half], "wshard", w_up),
        lax.ppermute(above[:, half:], "wshard", w_down),
    )
    gain_pairs = sections(norm_gains[0], swapped(norm_gains[0]))
    piece_rows = down_piece.shape[0]

    def down_of(section):
        columns = slice(section * half, (section + 1) * half)
        own = jnp.zeros((FF_PAD, half), jnp.bfloat16)
        for step, piece in (
            (0, down_piece[:, columns]),
            (1, above[:, columns]),
            (2, far[section]),
            (3, below[:, columns]),
        ):
            own = lax.dynamic_update_slice_in_dim(
                own, piece, lax.rem(w_place + step, W_DEV) * piece_rows, 0
            )
        return (own, swapped(own))

    first_qkv = swapped(all_own[:, qkv_at:out_at])
    first_out = swapped(all_own[:, 2 * out_at : 2 * out_at + width])
    first_hidden = swapped(all_own[:, :qkv_at])
    all_other = swapped(all_own)
    out_own = [all_own[:, 2 * out_at + k * width : 2 * out_at + (k + 1) * width] for k in (0, 1)]
    weights = (
        {
            "qkv": ((all_own, qkv_at), (first_qkv, 0)),
            "gate": ((all_own, 0), (first_hidden, 0)),
            "up": ((all_own, up_at), (first_hidden, up_at)),
            "out": (out_own[0], first_out),
            "down": down_of(0),
        },
        {
            "qkv": ((all_own, out_at + qkv_at), (all_other, out_at + qkv_at)),
            "gate": ((all_own, out_at), (all_other, out_at)),
            "up": ((all_own, out_at + up_at), (all_other, out_at + up_at)),
            "out": (out_own[1], all_other[:, 2 * out_at + width :]),
            "down": down_of(1),
        },
    )
    first = on_first.astype(jnp.int32)[None]
    rows_in = by_core(inputs[0, 0], inputs[1, 0])
    row_count = rows_in.shape[0]
    segment_row = by_core(segments[0, 0], segments[1, 0])
    padded = jnp.pad(segment_row, (HALO, HALO), constant_values=-1)
    first_row = seq_place * row_count
    segs = (
        lax.dynamic_slice_in_dim(segment_row, first_row, row_count)[:, None],
        lax.dynamic_slice_in_dim(padded, first_row, row_count + 2 * HALO)[None, :],
    )
    middle, kept0 = layer_forward(rows_in, gain_pairs[0], weights[0], segs, on_first, first)
    final, kept1 = layer_forward(middle, gain_pairs[1], weights[1], segs, on_first, first)
    upstream = by_core(cotangent[0, 0], cotangent[1, 0])
    grads1, sums1 = layer_backward(upstream, kept1, gain_pairs[1], weights[1], segs, on_first, first)
    grads0, sums0 = layer_backward(grads1, kept0, gain_pairs[0], weights[0], segs, on_first, first)

    def placed(first, second):
        mine, give = (by_core(first, second), by_core(second, first))
        got = swapped(give)
        return jnp.stack([by_core(mine, got), by_core(got, mine)])[None, :, None]

    section_outputs = placed(middle, final)
    section_input_grads = placed(grads0, grads1)

    totals = [summed_over_w(sums, w_place) for sums in (sums0, sums1)]
    mine, got = (by_core(*totals), swapped(by_core(totals[1], totals[0])))
    low, high = (by_core(mine, got), by_core(got, mine))
    attn_end, hidden_at = (3 * width // 2, 2 * width)
    down_at = hidden_at + GRAD_PAD
    qkv_rows = jnp.concatenate([low[:, :attn_end], high[:, :attn_end]], axis=1)
    attn_rows = jnp.concatenate([low[:, attn_end:hidden_at], high[:, attn_end:hidden_at]], axis=1)
    hidden_rows = jnp.concatenate(
        [low[:, hidden_at : hidden_at + FF], high[:, hidden_at : hidden_at + FF]], axis=1
    )
    gain_rows = (low + high)[:, down_at - 128 : down_at - 126].T
    down_total = jnp.concatenate(
        [
            jnp.concatenate(
                [h[:, at : at + width // 2] for h in (low, high)], axis=1
            )
            for at in range(down_at, low.shape[1], width // 2)
        ],
        axis=0,
    )[: FF // (SEQ_DEV * W_DEV)]
    return (
        section_outputs,
        section_input_grads,
        qkv_rows[None],
        attn_rows[None],
        hidden_rows[None],
        down_total[None],
        gain_rows[None],
    )


def solution(mesh):
    placed = (
        P(None, "wshard", "seq", None),
        P(None, "wshard", "seq", None),
        P(None, "wshard", None),
        P("section", None, None),
        P("section", "wshard", None),
        P("section", "wshard", None),
        P("section", "wshard", None),
        P("section", "wshard", None),
    )
    return jax.shard_map(
        per_device,
        mesh=mesh,
        in_specs=placed,
        out_specs=(
            P("section", None, "wshard", "seq", None),
            P("section", None, "wshard", "seq", None),
            P("section", ("seq", "wshard"), None),
            P("section", ("seq", "wshard"), None),
            P("section", ("seq", "wshard"), None),
            P("section", ("seq", "wshard"), None),
            P("section", None, ("seq", "wshard")),
        ),
        check_vma=False,
    )
```

```python
import math

import jax
import jax.numpy as jnp
from jax import lax
from jax.experimental import pallas as pl
from jax.experimental.pallas import tpu as pltpu
from jax.sharding import PartitionSpec as P

HEADS = 16
HEAD_DIM = 64
FF = 2624
HALO = 64
FF_PAD = 2688
SEQ_DEV = 16
W_DEV = 4
PAD_ROWS = 48
GRAD_PAD = 2816
HIDDEN_BLOCK = 896
QKV_BLOCK = 1536

norm_eps = 1e-05
root_half = 1.0 / math.sqrt(2.0)
root_two_pi = 1.0 / math.sqrt(2.0 * math.pi)
score_scale = 1.0 / math.sqrt(HEAD_DIM)

SWAP = [(0, 1), (1, 0)]


def swapped(array):
    return lax.ppermute(array, "section", SWAP)


def norm_parts(rows_in):
    centred = rows_in - jnp.mean(rows_in, axis=1, keepdims=True)
    factor = lax.rsqrt(jnp.mean(centred * centred, axis=1, keepdims=True) + norm_eps)
    return (centred * factor, factor)


def norm_back(grad_norm, normed, factor):
    inner = jnp.mean(grad_norm, axis=1, keepdims=True)
    along = jnp.mean(grad_norm * normed, axis=1, keepdims=True)
    return factor * (grad_norm - inner - normed * along)


def matmul(left, right):
    return jnp.dot(left, right, preferred_element_type=jnp.float32)


def matmul_t(left, right):
    return lax.dot_general(
        left, right, (((1,), (1,)), ((), ())), preferred_element_type=jnp.float32
    )


def inner_rows(left, right):
    return lax.dot_general(
        left, right, (((0,), (0,)), ((), ())), preferred_element_type=jnp.float32
    )


def column_halves(array, on_first):
    even = jnp.concatenate([array[:, 256 * k : 256 * k + 128] for k in range(4)], axis=1)
    odd = jnp.concatenate([array[:, 256 * k + 128 : 256 * k + 256] for k in range(4)], axis=1)
    return (jnp.where(on_first, even, odd), jnp.where(on_first, odd, even))


def from_halves(own, other, on_first):
    even = jnp.where(on_first, own, other)
    odd = jnp.where(on_first, other, own)
    parts = []
    for k in range(4):
        parts += [even[:, 128 * k : 128 * k + 128], odd[:, 128 * k : 128 * k + 128]]
    return jnp.concatenate(parts, axis=1)


def window_allowed(query_seg, key_seg):
    rows, keys = (query_seg.shape[0], key_seg.shape[1])
    offset = lax.broadcasted_iota(jnp.int32, (rows, keys), 1) - lax.broadcasted_iota(
        jnp.int32, (rows, keys), 0
    )
    return (offset >= 0) & (offset <= 2 * HALO) & (query_seg == key_seg)


def attend_kernel(query_seg, key_seg, qkv, *refs):
    mixed, log_total = refs[-2:]
    allowed = window_allowed(query_seg[...], key_seg[...])
    width = HEADS * HEAD_DIM
    rows = mixed.shape[0]
    for head in range(HEADS):
        at = head * HEAD_DIM
        q = qkv[HALO : HALO + rows, at : at + HEAD_DIM]
        k = qkv[:, width + at : width + at + HEAD_DIM]
        v = qkv[:, 2 * width + at : 2 * width + at + HEAD_DIM]
        scores = jnp.where(allowed, matmul_t(q, k) * score_scale, -1e30)
        row_max = jnp.max(scores, axis=1, keepdims=True)
        exponent = jnp.exp(scores - row_max)
        total = jnp.sum(exponent, axis=1, keepdims=True)
        probs = (exponent * (1.0 / total)).astype(jnp.bfloat16)
        mixed[:, at : at + HEAD_DIM] = matmul(probs, v).astype(jnp.bfloat16)
        log_total[:, at : at + HEAD_DIM] = jnp.broadcast_to(
            row_max + jnp.log(total), (rows, HEAD_DIM)
        )


def attend_back_kernel(
    query_seg, key_seg, qkv, log_total, grad_mixed, grad_query, own, before, after
):
    allowed = window_allowed(query_seg[...], key_seg[...])
    width = HEADS * HEAD_DIM
    rows = grad_mixed.shape[0]
    for head in range(HEADS):
        at = head * HEAD_DIM
        q = qkv[HALO : HALO + rows, at : at + HEAD_DIM]
        k = qkv[:, width + at : width + at + HEAD_DIM]
        v = qkv[:, 2 * width + at : 2 * width + at + HEAD_DIM]
        grad = grad_mixed[:, at : at + HEAD_DIM]
        scores = jnp.where(allowed, matmul_t(q, k) * score_scale, -1e30)
        probs = jnp.exp(scores - log_total[:, at : at + 1])
        grad_probs = matmul_t(grad, v)
        inner = jnp.sum(probs * grad_probs, axis=1, keepdims=True)
        grad_scores = (probs * (grad_probs - inner)).astype(jnp.bfloat16)
        grad_query[:, at : at + HEAD_DIM] = (matmul(grad_scores, k) * score_scale).astype(
            jnp.bfloat16
        )
        for place, piece in (
            (at, inner_rows(grad_scores, q) * score_scale),
            (width + at, inner_rows(probs.astype(jnp.bfloat16), grad)),
        ):
            columns = slice(place, place + HEAD_DIM)
            before[:, columns] = piece[:HALO].astype(jnp.bfloat16)
            own[:, columns] = piece[HALO : HALO + rows]
            after[:, columns] = piece[HALO + rows :].astype(jnp.bfloat16)


params = pltpu.CompilerParams(vmem_limit_bytes=40 * 1024 * 1024)


def attend(query_seg, key_seg, qkv, ready):
    rows, width = (query_seg.shape[0], HEADS * HEAD_DIM)
    return pl.pallas_call(
        attend_kernel,
        out_shape=(
            jax.ShapeDtypeStruct((rows, width), jnp.bfloat16),
            jax.ShapeDtypeStruct((rows, width), jnp.float32),
        ),
        in_specs=[pl.BlockSpec(memory_space=pltpu.VMEM)] * 3
        + [pl.BlockSpec(memory_space=pl.ANY)] * len(ready),
        compiler_params=params,
        name="attend",
    )(query_seg, key_seg, qkv, *ready)


def attend_back(query_seg, key_seg, qkv, log_total, grad_mixed):
    rows, width = (query_seg.shape[0], HEADS * HEAD_DIM)
    return pl.pallas_call(
        attend_back_kernel,
        out_shape=(
            jax.ShapeDtypeStruct((rows, width), jnp.bfloat16),
            jax.ShapeDtypeStruct((rows, 2 * width), jnp.float32),
            jax.ShapeDtypeStruct((HALO, 2 * width), jnp.bfloat16),
            jax.ShapeDtypeStruct((HALO, 2 * width), jnp.bfloat16),
        ),
        compiler_params=params,
        name="attend_back",
    )(query_seg, key_seg, qkv, log_total, grad_mixed)


def to_next(array):
    return lax.ppermute(array, "seq", [(i, i + 1) for i in range(SEQ_DEV - 1)])


def to_previous(array):
    return lax.ppermute(array, "seq", [(i + 1, i) for i in range(SEQ_DEV - 1)])


def split_normal(gate):
    cumulative = 0.5 * (1.0 + lax.erf(gate * root_half))
    return cumulative


def grid_call(kernel, name, scalars, grid, in_specs, out_specs, out_shape, scratch, args):
    return pl.pallas_call(
        kernel,
        grid_spec=pltpu.PrefetchScalarGridSpec(
            num_scalar_prefetch=len(scalars),
            grid=grid,
            in_specs=in_specs,
            out_specs=out_specs,
            scratch_shapes=scratch,
        ),
        out_shape=out_shape,
        compiler_params=params,
        name=name,
    )(*scalars, *args)


def whole(array):
    return pl.BlockSpec(array.shape, lambda n, *_: (0,) * array.ndim)


def columns_at(rows, block, first):
    return pl.BlockSpec((rows, block), lambda n, *_: (0, first + n))


def rows_at(block, columns):
    return pl.BlockSpec((block, columns), lambda n, *_: (n, 0))


def add_to(step, total, value):
    @pl.when(step == 0)
    def _():
        total[...] = value

    @pl.when(step > 0)
    def _():
        total[...] += value


def store_halves(out, own, other, on_first):
    for k in range(4):
        block = slice(128 * k, 128 * k + 128)
        out[:, 256 * k : 256 * k + 128] = jnp.where(on_first, own[:, block], other[:, block])
        out[:, 256 * k + 128 : 256 * k + 256] = jnp.where(on_first, other[:, block], own[:, block])


def qkv_kernel(own, other, weight_own, weight_other, out):
    out[...] = (
        matmul(own[...], weight_own[...]) + matmul(other[...], weight_other[...])
    ).astype(jnp.bfloat16)


def qkv_of(own, other, weights):
    (w_own, at_own), (w_other, at_other) = weights["qkv"]
    width = 3 * HEADS * HEAD_DIM
    depth = own.shape[1]
    return grid_call(
        qkv_kernel,
        "qkv",
        (),
        (width // QKV_BLOCK,),
        [
            whole(own),
            whole(other),
            columns_at(depth, QKV_BLOCK, at_own // QKV_BLOCK),
            columns_at(depth, QKV_BLOCK, at_other // QKV_BLOCK),
        ],
        columns_at(own.shape[0], QKV_BLOCK, 0),
        jax.ShapeDtypeStruct((own.shape[0], width), jnp.bfloat16),
        [],
        (own, other, w_own, w_other),
    )


def qkv_back_kernel(first, grad, weight_own, weight_other, out, total_own, total_other):
    step = pl.program_id(0)
    add_to(step, total_own, matmul_t(grad[...], weight_own[...]))
    add_to(step, total_other, matmul_t(grad[...], weight_other[...]))

    @pl.when(step == pl.num_programs(0) - 1)
    def _():
        store_halves(out, total_own[...], total_other[...], first[0] == 1)


def qkv_back(first, grad, weights):
    (w_own, at_own), (w_other, at_other) = weights["qkv"]
    rows, width = grad.shape
    depth = w_own.shape[0]
    return grid_call(
        qkv_back_kernel,
        "qkv_back",
        (first,),
        (width // QKV_BLOCK,),
        [
            columns_at(rows, QKV_BLOCK, 0),
            columns_at(depth, QKV_BLOCK, at_own // QKV_BLOCK),
            columns_at(depth, QKV_BLOCK, at_other // QKV_BLOCK),
        ],
        pl.BlockSpec((rows, 2 * depth), lambda n, *_: (0, 0)),
        jax.ShapeDtypeStruct((rows, 2 * depth), jnp.float32),
        [pltpu.VMEM((rows, depth), jnp.float32)] * 2,
        (grad, w_own, w_other),
    )


def hidden_kernel(
    first, own, other, gate_own, gate_other, up_own, up_other, down_own, down_other, middle,
    gate_out, up_out, product_out, out, total_own, total_other,
):
    step = pl.program_id(0)
    gate = matmul(own[...], gate_own[...]) + matmul(other[...], gate_other[...])
    up = matmul(own[...], up_own[...]) + matmul(other[...], up_other[...])
    product = (gate * split_normal(gate) * up).astype(jnp.bfloat16)
    gate_out[...] = gate
    up_out[...] = up
    product_out[...] = product
    add_to(step, total_own, matmul(product, down_own[...]))
    add_to(step, total_other, matmul(product, down_other[...]))

    @pl.when(step == pl.num_programs(0) - 1)
    def _():
        half = total_own.shape[1]
        mine, theirs, on_first = (total_own[...], total_other[...], first[0] == 1)
        out[:, :half] = middle[:, :half] + jnp.where(on_first, mine, theirs)
        out[:, half:] = middle[:, half:] + jnp.where(on_first, theirs, mine)


def hidden_specs(weights, depth):
    specs, arrays = ([], [])
    for part in ("gate", "up"):
        for array, at in weights[part]:
            specs.append(columns_at(depth, HIDDEN_BLOCK, at // HIDDEN_BLOCK))
            arrays.append(array)
    for array in weights["down"]:
        specs.append(rows_at(HIDDEN_BLOCK, array.shape[1]))
        arrays.append(array)
    return (specs, arrays)


def hidden_forward(first, own, other, middle, weights):
    rows, depth = own.shape
    width = middle.shape[1]
    specs, arrays = hidden_specs(weights, depth)
    piece = columns_at(rows, HIDDEN_BLOCK, 0)
    return grid_call(
        hidden_kernel,
        "hidden",
        (first,),
        (FF_PAD // HIDDEN_BLOCK,),
        [whole(own), whole(other), *specs, whole(middle)],
        (piece, piece, piece, whole(middle)),
        (
            jax.ShapeDtypeStruct((rows, FF_PAD), jnp.float32),
            jax.ShapeDtypeStruct((rows, FF_PAD), jnp.float32),
            jax.ShapeDtypeStruct((rows, FF_PAD), jnp.bfloat16),
            jax.ShapeDtypeStruct((rows, width), jnp.float32),
        ),
        [pltpu.VMEM((rows, width // 2), jnp.float32)] * 2,
        (own, other, *arrays, middle),
    )


def hidden_back_kernel(
    first, grad_own, grad_other, gate_in, up_in, gate_own, gate_other, up_own, up_other, down_own,
    down_other, grad_gate_out, grad_up_out, out, total_own, total_other,
):
    step = pl.program_id(0)
    gate, up = (gate_in[...], up_in[...])
    grad_product = matmul_t(grad_own[...], down_own[...]) + matmul_t(
        grad_other[...], down_other[...]
    )
    cumulative = split_normal(gate)
    derivative = cumulative + gate * jnp.exp(-0.5 * gate * gate) * root_two_pi
    grad_gate = (grad_product * up * derivative).astype(jnp.bfloat16)
    grad_up = (grad_product * gate * cumulative).astype(jnp.bfloat16)
    grad_gate_out[...] = grad_gate
    grad_up_out[...] = grad_up
    add_to(step, total_own, matmul_t(grad_gate, gate_own[...]) + matmul_t(grad_up, up_own[...]))
    add_to(
        step, total_other, matmul_t(grad_gate, gate_other[...]) + matmul_t(grad_up, up_other[...])
    )

    @pl.when(step == pl.num_programs(0) - 1)
    def _():
        store_halves(out, total_own[...], total_other[...], first[0] == 1)


def hidden_back(first, grad_own, grad_other, gate, up, weights):
    rows, half = grad_own.shape
    depth = half
    specs, arrays = hidden_specs(weights, depth)
    piece = columns_at(rows, HIDDEN_BLOCK, 0)
    return grid_call(
        hidden_back_kernel,
        "hidden_back",
        (first,),
        (FF_PAD // HIDDEN_BLOCK,),
        [whole(grad_own), whole(grad_other), piece, piece, *specs],
        (piece, piece, pl.BlockSpec((rows, 2 * depth), lambda n, *_: (0, 0))),
        (
            jax.ShapeDtypeStruct((rows, FF_PAD), jnp.bfloat16),
            jax.ShapeDtypeStruct((rows, FF_PAD), jnp.bfloat16),
            jax.ShapeDtypeStruct((rows, 2 * depth), jnp.float32),
        ),
        [pltpu.VMEM((rows, depth), jnp.float32)] * 2,
        (grad_own, grad_other, gate, up, *arrays),
    )


def layer_forward(rows_in, gain_pair, weights, segs, on_first, first, later=(), ready=()):
    normed1, factor1 = norm_parts(rows_in)
    act_in = (normed1 * gain_pair[0]).astype(jnp.bfloat16)
    before = to_next(act_in[act_in.shape[0] - HALO :])
    after = to_previous(act_in[:HALO])
    extended = jnp.concatenate([before, act_in, after], axis=0)
    qkv = qkv_of(*column_halves(extended, on_first), weights)
    mixed, log_total = attend(*segs, qkv, ready)
    mixed, *later = lax.optimization_barrier((mixed, *later))
    own, other = column_halves(mixed, on_first)
    middle = rows_in + matmul(own, weights["out"][0]) + matmul(other, weights["out"][1])
    normed2, factor2 = norm_parts(middle)
    act_mid = (normed2 * gain_pair[1]).astype(jnp.bfloat16)
    own, other = column_halves(act_mid, on_first)
    gate, up, product, output = hidden_forward(first, own, other, middle, weights)
    acts = (jnp.stack([act_in, mixed, act_mid]), product)
    got = tuple(swapped(act) for act in acts)
    kept = (normed1, factor1, qkv, log_total, normed2, factor2, gate, up, acts, got)
    return (output, kept, later)


def seq_sum(total):
    return lax.psum_scatter(total, "seq", scatter_dimension=0, tiled=True)


GRAD_WIDTHS = (1536, 512, GRAD_PAD)
ROW_PIECE = FF // (SEQ_DEV * W_DEV)


def weight_grad_kernel(
    act_mine, act_got, product_mine, product_got, grad_mine, grad_got, gains, out,
    grads, down, groups,
):
    count, block = (act_mine.shape[1], act_mine.shape[2])
    step = pl.program_id(0)
    end = sum(GRAD_WIDTHS)

    @pl.when(step == 0)
    def _():
        grads[:count] = grad_mine[...]
        grads[count:] = grad_got[...]
        for at in range(0, FF_PAD, 896):
            product = jnp.concatenate(
                [product_mine[:, at : at + 896], product_got[:, at : at + 896]], axis=0
            )
            down[at : at + 896] = inner_rows(product, grads[:, end:])
        width = down.shape[1]
        for piece in range(SEQ_DEV * W_DEV):
            for group in range(PAD_ROWS // 16):
                rows = piece * ROW_PIECE + group * 16
                groups[16 * piece : 16 * piece + 16, group * width : (group + 1) * width] = down[
                    rows : rows + 16
                ].astype(jnp.bfloat16)

    at = 0
    for member, width in enumerate(GRAD_WIDTHS):
        acts = jnp.concatenate([act_mine[member], act_got[member]], axis=0)
        for part in range(at, at + width, 512):
            size = min(512, at + width - part)
            out[:, part : part + size] = inner_rows(acts, grads[:, part : part + size]).astype(
                jnp.bfloat16
            )
        at += width
    out[:, end - gains.shape[1] : end] = gains[...]
    out[:, end:] = groups[pl.ds(pl.multiple_of(step * block, block), block)]


def weight_grads(acts, acts_got, grad_mine, grad_got, gains):
    members, count, width = acts[0].shape
    block = 256
    half = grad_mine.shape[1] - sum(GRAD_WIDTHS)
    groups = half * PAD_ROWS // 16
    act_spec = pl.BlockSpec((members, count, block), lambda n: (0, 0, n))
    product_spec = whole(acts[1])
    return grid_call(
        weight_grad_kernel,
        "weight_grads",
        (),
        (width // block,),
        [
            act_spec,
            act_spec,
            product_spec,
            product_spec,
            whole(grad_mine),
            whole(grad_got),
            rows_at(block, gains.shape[1]),
        ],
        rows_at(block, sum(GRAD_WIDTHS) + groups),
        jax.ShapeDtypeStruct((width, sum(GRAD_WIDTHS) + groups), jnp.bfloat16),
        [
            pltpu.VMEM((2 * count, grad_mine.shape[1]), jnp.bfloat16),
            pltpu.VMEM((FF_PAD, half), jnp.float32),
            pltpu.VMEM((width, groups), jnp.bfloat16),
        ],
        (acts[0], acts_got[0], acts[1], acts_got[1], grad_mine, grad_got, gains),
    )


def layer_backward(grad_out, kept, gain_pair, weights, segs, on_first, first):
    (normed1, factor1, qkv, log_total, normed2, factor2, gate, up, acts, got) = kept
    rows, width = normed1.shape
    half = width // 2
    grad_branch = grad_out.astype(jnp.bfloat16)
    low, high = (grad_branch[:, :half], grad_branch[:, half:])
    branch_own, branch_other = (jnp.where(on_first, low, high), jnp.where(on_first, high, low))
    grad_gate, grad_up, grad_norm2 = hidden_back(
        first, branch_own, branch_other, gate, up, weights
    )
    gain_mid = jnp.sum(normed2 * grad_norm2, axis=0)
    grad_middle = grad_out + norm_back(grad_norm2 * gain_pair[1], normed2, factor2)
    grad_attn = grad_middle.astype(jnp.bfloat16)
    mine, theirs = [matmul_t(grad_attn, w) for w in weights["out"]]
    grad_mixed = from_halves(mine, theirs, on_first).astype(jnp.bfloat16)
    grad_query, grad_own, grad_before, grad_after = attend_back(*segs, qkv, log_total, grad_mixed)
    from_previous = to_next(grad_after).astype(jnp.float32)
    from_next = to_previous(grad_before).astype(jnp.float32)
    grad_pairs = grad_own + jnp.concatenate([from_previous, from_next], axis=0)
    grad_qkv = jnp.concatenate([grad_query, grad_pairs.astype(jnp.bfloat16)], axis=1)
    halves = (
        (grad_qkv[:, : 3 * half], grad_qkv[:, 3 * half :]),
        (grad_attn[:, :half], grad_attn[:, half:]),
        (grad_gate, grad_up),
        (jnp.zeros((rows, GRAD_PAD - FF_PAD), jnp.bfloat16),) * 2,
        (low, high),
    )
    first_half, second_half = [jnp.concatenate([h[k] for h in halves], axis=1) for k in range(2)]
    grad_mine = jnp.where(on_first, first_half, second_half)
    grad_got = swapped(jnp.where(on_first, second_half, first_half))
    grad_norm1 = qkv_back(first, grad_qkv, weights)
    gain_first = jnp.sum(normed1 * grad_norm1, axis=0)
    grad_inputs = grad_middle + norm_back(grad_norm1 * gain_pair[0], normed1, factor1)
    gains = jnp.stack([gain_first, gain_mid])
    gain_columns = jnp.pad(gains, ((0, 126), (0, 0))).T.astype(jnp.bfloat16)
    sums = seq_sum(weight_grads(acts, got, grad_mine, grad_got, gain_columns))
    return (grad_inputs, sums)


def summed_over_w(block, place):
    rows = block.shape[0] // W_DEV
    total = lax.dynamic_slice_in_dim(block, place * rows, rows).astype(jnp.float32)
    for step in range(1, W_DEV):
        part = lax.dynamic_slice_in_dim(block, lax.rem(place + step, W_DEV) * rows, rows)
        got = lax.ppermute(part, "wshard", [(j, (j + step) % W_DEV) for j in range(W_DEV)])
        total = total + got.astype(jnp.float32)
    return total


def per_device(
    inputs, cotangent, segments, norm_gains, attend_in, attend_out, hidden_in, hidden_out
):
    on_first = lax.axis_index("section") == 0
    core = lax.axis_index("section")
    seq_place = lax.axis_index("seq")
    w_place = lax.axis_index("wshard")

    def by_core(first, second):
        return jnp.where(on_first, first, second)

    def sections(own, got):
        return (by_core(own, got), by_core(got, own))

    slice_rows = attend_in.shape[1] // (2 * SEQ_DEV)
    pad = jnp.zeros((slice_rows, FF_PAD - FF), jnp.bfloat16)
    width = inputs.shape[3]

    def row_slice(which):
        at = (which * SEQ_DEV + seq_place) * slice_rows
        hidden, qkv, out = [
            lax.dynamic_slice_in_dim(w[0], at, slice_rows)
            for w in (hidden_in, attend_in, attend_out)
        ]
        return jnp.concatenate([hidden[:, :FF], pad, hidden[:, FF:], pad, qkv, out], axis=1)

    def in_order(first, second):
        ends = (0, 2 * FF_PAD, 2 * FF_PAD + 3 * width, 2 * FF_PAD + 4 * width)
        return jnp.concatenate(
            [piece[:, a:b] for a, b in zip(ends, ends[1:]) for piece in (first, second)], axis=1
        )

    row_pieces = sections(row_slice(core), swapped(row_slice(1 - core)))
    hidden_width, qkv_width = (2 * FF_PAD, 3 * width)
    qkv_at = 2 * hidden_width
    out_at = qkv_at + 2 * qkv_width
    all_own = lax.all_gather(in_order(*row_pieces), ("wshard", "seq"), axis=0, tiled=True)
    half = hidden_out.shape[2] // 2
    low, high = (hidden_out[0, :, :half], hidden_out[0, :, half:])
    down_piece = jnp.concatenate(sections(by_core(low, high), swapped(by_core(high, low))), axis=1)
    w_up = [(j, (j + 1) % W_DEV) for j in range(W_DEV)]
    w_down = [(j, i) for i, j in w_up]
    below = lax.ppermute(down_piece, "wshard", w_up)
    above = lax.ppermute(down_piece, "wshard", w_down)
    far = (
        lax.ppermute(below[:, :half], "wshard", w_up),
        lax.ppermute(above[:, half:], "wshard", w_down),
    )
    gain_pairs = sections(norm_gains[0], swapped(norm_gains[0]))
    piece_rows = down_piece.shape[0]

    def down_of(section):
        columns = slice(section * half, (section + 1) * half)
        own = jnp.zeros((FF_PAD, half), jnp.bfloat16)
        for step, piece in (
            (0, down_piece[:, columns]),
            (1, above[:, columns]),
            (2, far[section]),
            (3, below[:, columns]),
        ):
            own = lax.dynamic_update_slice_in_dim(
                own, piece, lax.rem(w_place + step, W_DEV) * piece_rows, 0
            )
        return own

    all_own, *down_own = lax.optimization_barrier((all_own, down_of(0), down_of(1)))
    first_qkv = swapped(all_own[:, qkv_at : qkv_at + qkv_width])
    first_out = swapped(all_own[:, out_at : out_at + width])
    first_hidden = swapped(all_own[:, :hidden_width])
    out_own = [all_own[:, out_at + k * width : out_at + (k + 1) * width] for k in (0, 1)]
    first_weights = {
        "qkv": ((all_own, qkv_at), (first_qkv, 0)),
        "gate": ((all_own, 0), (first_hidden, 0)),
        "up": ((all_own, FF_PAD), (first_hidden, FF_PAD)),
        "out": (all_own[:, out_at : out_at + width], first_out),
        "down": (down_own[0], swapped(down_own[0])),
    }

    def second_weights(all_late):
        all_other = swapped(all_late)
        return {
            "qkv": ((all_own, qkv_at + qkv_width), (all_other, qkv_at + qkv_width)),
            "gate": ((all_own, hidden_width), (all_other, hidden_width)),
            "up": ((all_own, hidden_width + FF_PAD), (all_other, hidden_width + FF_PAD)),
            "out": (all_own[:, out_at + width :], all_other[:, out_at + width :]),
            "down": (down_own[1], swapped(down_own[1])),
        }

    first = on_first.astype(jnp.int32)[None]
    rows_in = by_core(inputs[0, 0], inputs[1, 0])
    row_count = rows_in.shape[0]
    segment_row = by_core(segments[0, 0], segments[1, 0])
    padded = jnp.pad(segment_row, (HALO, HALO), constant_values=-1)
    first_row = seq_place * row_count
    segs = (
        lax.dynamic_slice_in_dim(segment_row, first_row, row_count)[:, None],
        lax.dynamic_slice_in_dim(padded, first_row, row_count + 2 * HALO)[None, :],
    )
    middle, kept0, (all_late,) = layer_forward(
        rows_in, gain_pairs[0], first_weights, segs, on_first, first, (all_own,), (first_hidden, first_out)
    )
    weights = (first_weights, second_weights(all_late))
    final, kept1, _ = layer_forward(middle, gain_pairs[1], weights[1], segs, on_first, first)
    upstream = by_core(cotangent[0, 0], cotangent[1, 0])
    grads1, sums1 = layer_backward(upstream, kept1, gain_pairs[1], weights[1], segs, on_first, first)
    grads0, sums0 = layer_backward(grads1, kept0, gain_pairs[0], weights[0], segs, on_first, first)

    def placed(first, second):
        mine, give = (by_core(first, second), by_core(second, first))
        got = swapped(give)
        return jnp.stack([by_core(mine, got), by_core(got, mine)])[None, :, None]

    section_outputs = placed(middle, final)
    section_input_grads = placed(grads0, grads1)

    totals = [summed_over_w(sums, w_place) for sums in (sums0, sums1)]
    mine, got = (by_core(*totals), swapped(by_core(totals[1], totals[0])))
    low, high = (by_core(mine, got), by_core(got, mine))
    attn_end, hidden_at = (3 * width // 2, 2 * width)
    down_at = hidden_at + GRAD_PAD
    qkv_rows = jnp.concatenate([low[:, :attn_end], high[:, :attn_end]], axis=1)
    attn_rows = jnp.concatenate([low[:, attn_end:hidden_at], high[:, attn_end:hidden_at]], axis=1)
    hidden_rows = jnp.concatenate(
        [low[:, hidden_at : hidden_at + FF], high[:, hidden_at : hidden_at + FF]], axis=1
    )
    gain_rows = (low + high)[:, down_at - 128 : down_at - 126].T
    down_total = jnp.concatenate(
        [
            jnp.concatenate(
                [h[:, at : at + width // 2] for h in (low, high)], axis=1
            )
            for at in range(down_at, low.shape[1], width // 2)
        ],
        axis=0,
    )[: FF // (SEQ_DEV * W_DEV)]
    return (
        section_outputs,
        section_input_grads,
        qkv_rows[None],
        attn_rows[None],
        hidden_rows[None],
        down_total[None],
        gain_rows[None],
    )


def solution(mesh):
    placed = (
        P(None, "wshard", "seq", None),
        P(None, "wshard", "seq", None),
        P(None, "wshard", None),
        P("section", None, None),
        P("section", "wshard", None),
        P("section", "wshard", None),
        P("section", "wshard", None),
        P("section", "wshard", None),
    )
    return jax.shard_map(
        per_device,
        mesh=mesh,
        in_specs=placed,
        out_specs=(
            P("section", None, "wshard", "seq", None),
            P("section", None, "wshard", "seq", None),
            P("section", ("seq", "wshard"), None),
            P("section", ("seq", "wshard"), None),
            P("section", ("seq", "wshard"), None),
            P("section", ("seq", "wshard"), None),
            P("section", None, ("seq", "wshard")),
        ),
        check_vma=False,
    )
```

```python
import math

import jax
import jax.numpy as jnp
from jax import lax
from jax.experimental import pallas as pl
from jax.experimental.pallas import tpu as pltpu
from jax.sharding import PartitionSpec as P

HEADS = 16
HEAD_DIM = 64
FF = 2624
HALO = 64
FF_PAD = 2688
SEQ_DEV = 16
W_DEV = 4
PAD_ROWS = 48
GRAD_PAD = 2816
HIDDEN_BLOCK = 896
QKV_BLOCK = 1536

norm_eps = 1e-05
root_half = 1.0 / math.sqrt(2.0)
root_two_pi = 1.0 / math.sqrt(2.0 * math.pi)
score_scale = 1.0 / math.sqrt(HEAD_DIM)

SWAP = [(0, 1), (1, 0)]


def swapped(array):
    return lax.ppermute(array, "section", SWAP)


def norm_parts(rows_in):
    centred = rows_in - jnp.mean(rows_in, axis=1, keepdims=True)
    factor = lax.rsqrt(jnp.mean(centred * centred, axis=1, keepdims=True) + norm_eps)
    return (centred * factor, factor)


def norm_back(grad_norm, normed, factor):
    inner = jnp.mean(grad_norm, axis=1, keepdims=True)
    along = jnp.mean(grad_norm * normed, axis=1, keepdims=True)
    return factor * (grad_norm - inner - normed * along)


def matmul(left, right):
    return jnp.dot(left, right, preferred_element_type=jnp.float32)


def matmul_t(left, right):
    return lax.dot_general(
        left, right, (((1,), (1,)), ((), ())), preferred_element_type=jnp.float32
    )


def inner_rows(left, right):
    return lax.dot_general(
        left, right, (((0,), (0,)), ((), ())), preferred_element_type=jnp.float32
    )


def column_halves(array, on_first):
    even = jnp.concatenate([array[:, 256 * k : 256 * k + 128] for k in range(4)], axis=1)
    odd = jnp.concatenate([array[:, 256 * k + 128 : 256 * k + 256] for k in range(4)], axis=1)
    return (jnp.where(on_first, even, odd), jnp.where(on_first, odd, even))


def from_halves(own, other, on_first):
    even = jnp.where(on_first, own, other)
    odd = jnp.where(on_first, other, own)
    parts = []
    for k in range(4):
        parts += [even[:, 128 * k : 128 * k + 128], odd[:, 128 * k : 128 * k + 128]]
    return jnp.concatenate(parts, axis=1)


def window_allowed(query_seg, key_seg):
    rows, keys = (query_seg.shape[0], key_seg.shape[1])
    offset = lax.broadcasted_iota(jnp.int32, (rows, keys), 1) - lax.broadcasted_iota(
        jnp.int32, (rows, keys), 0
    )
    return (offset >= 0) & (offset <= 2 * HALO) & (query_seg == key_seg)


def attend_kernel(query_seg, key_seg, qkv, *refs):
    mixed, log_total = refs[-2:]
    allowed = window_allowed(query_seg[...], key_seg[...])
    width = HEADS * HEAD_DIM
    rows = mixed.shape[0]
    for head in range(HEADS):
        at = head * HEAD_DIM
        q = qkv[HALO : HALO + rows, at : at + HEAD_DIM]
        k = qkv[:, width + at : width + at + HEAD_DIM]
        v = qkv[:, 2 * width + at : 2 * width + at + HEAD_DIM]
        scores = jnp.where(allowed, matmul_t(q, k) * score_scale, -1e30)
        row_max = jnp.max(scores, axis=1, keepdims=True)
        exponent = jnp.exp(scores - row_max)
        total = jnp.sum(exponent, axis=1, keepdims=True)
        probs = (exponent * (1.0 / total)).astype(jnp.bfloat16)
        mixed[:, at : at + HEAD_DIM] = matmul(probs, v).astype(jnp.bfloat16)
        log_total[:, at : at + HEAD_DIM] = jnp.broadcast_to(
            row_max + jnp.log(total), (rows, HEAD_DIM)
        )


def attend_back_kernel(
    query_seg, key_seg, qkv, log_total, grad_mixed, grad_query, own, before, after
):
    allowed = window_allowed(query_seg[...], key_seg[...])
    width = HEADS * HEAD_DIM
    rows = grad_mixed.shape[0]
    for head in range(HEADS):
        at = head * HEAD_DIM
        q = qkv[HALO : HALO + rows, at : at + HEAD_DIM]
        k = qkv[:, width + at : width + at + HEAD_DIM]
        v = qkv[:, 2 * width + at : 2 * width + at + HEAD_DIM]
        grad = grad_mixed[:, at : at + HEAD_DIM]
        scores = jnp.where(allowed, matmul_t(q, k) * score_scale, -1e30)
        probs = jnp.exp(scores - log_total[:, at : at + 1])
        grad_probs = matmul_t(grad, v)
        inner = jnp.sum(probs * grad_probs, axis=1, keepdims=True)
        grad_scores = (probs * (grad_probs - inner)).astype(jnp.bfloat16)
        grad_query[:, at : at + HEAD_DIM] = (matmul(grad_scores, k) * score_scale).astype(
            jnp.bfloat16
        )
        for place, piece in (
            (at, inner_rows(grad_scores, q) * score_scale),
            (width + at, inner_rows(probs.astype(jnp.bfloat16), grad)),
        ):
            columns = slice(place, place + HEAD_DIM)
            before[:, columns] = piece[:HALO].astype(jnp.bfloat16)
            own[:, columns] = piece[HALO : HALO + rows]
            after[:, columns] = piece[HALO + rows :].astype(jnp.bfloat16)


params = pltpu.CompilerParams(vmem_limit_bytes=40 * 1024 * 1024)


def attend(query_seg, key_seg, qkv, ready):
    rows, width = (query_seg.shape[0], HEADS * HEAD_DIM)
    return pl.pallas_call(
        attend_kernel,
        out_shape=(
            jax.ShapeDtypeStruct((rows, width), jnp.bfloat16),
            jax.ShapeDtypeStruct((rows, width), jnp.float32),
        ),
        in_specs=[pl.BlockSpec(memory_space=pltpu.VMEM)] * 3
        + [pl.BlockSpec(memory_space=pl.ANY)] * len(ready),
        compiler_params=params,
        name="attend",
    )(query_seg, key_seg, qkv, *ready)


def attend_back(query_seg, key_seg, qkv, log_total, grad_mixed):
    rows, width = (query_seg.shape[0], HEADS * HEAD_DIM)
    return pl.pallas_call(
        attend_back_kernel,
        out_shape=(
            jax.ShapeDtypeStruct((rows, width), jnp.bfloat16),
            jax.ShapeDtypeStruct((rows, 2 * width), jnp.float32),
            jax.ShapeDtypeStruct((HALO, 2 * width), jnp.bfloat16),
            jax.ShapeDtypeStruct((HALO, 2 * width), jnp.bfloat16),
        ),
        compiler_params=params,
        name="attend_back",
    )(query_seg, key_seg, qkv, log_total, grad_mixed)


def to_next(array):
    return lax.ppermute(array, "seq", [(i, i + 1) for i in range(SEQ_DEV - 1)])


def to_previous(array):
    return lax.ppermute(array, "seq", [(i + 1, i) for i in range(SEQ_DEV - 1)])


def split_normal(gate):
    cumulative = 0.5 * (1.0 + lax.erf(gate * root_half))
    return cumulative


def grid_call(kernel, name, scalars, grid, in_specs, out_specs, out_shape, scratch, args):
    return pl.pallas_call(
        kernel,
        grid_spec=pltpu.PrefetchScalarGridSpec(
            num_scalar_prefetch=len(scalars),
            grid=grid,
            in_specs=in_specs,
            out_specs=out_specs,
            scratch_shapes=scratch,
        ),
        out_shape=out_shape,
        compiler_params=params,
        name=name,
    )(*scalars, *args)


def whole(array):
    return pl.BlockSpec(array.shape, lambda n, *_: (0,) * array.ndim)


def columns_at(rows, block, first):
    return pl.BlockSpec((rows, block), lambda n, *_: (0, first + n))


def rows_at(block, columns):
    return pl.BlockSpec((block, columns), lambda n, *_: (n, 0))


def add_to(step, total, value):
    @pl.when(step == 0)
    def _():
        total[...] = value

    @pl.when(step > 0)
    def _():
        total[...] += value


def store_halves(out, own, other, on_first):
    for k in range(4):
        block = slice(128 * k, 128 * k + 128)
        out[:, 256 * k : 256 * k + 128] = jnp.where(on_first, own[:, block], other[:, block])
        out[:, 256 * k + 128 : 256 * k + 256] = jnp.where(on_first, other[:, block], own[:, block])


def qkv_kernel(own, other, weight_own, weight_other, out):
    out[...] = (
        matmul(own[...], weight_own[...]) + matmul(other[...], weight_other[...])
    ).astype(jnp.bfloat16)


def qkv_of(own, other, weights):
    (w_own, at_own), (w_other, at_other) = weights["qkv"]
    width = 3 * HEADS * HEAD_DIM
    depth = own.shape[1]
    return grid_call(
        qkv_kernel,
        "qkv",
        (),
        (width // QKV_BLOCK,),
        [
            whole(own),
            whole(other),
            columns_at(depth, QKV_BLOCK, at_own // QKV_BLOCK),
            columns_at(depth, QKV_BLOCK, at_other // QKV_BLOCK),
        ],
        columns_at(own.shape[0], QKV_BLOCK, 0),
        jax.ShapeDtypeStruct((own.shape[0], width), jnp.bfloat16),
        [],
        (own, other, w_own, w_other),
    )


def qkv_back_kernel(first, grad, weight_own, weight_other, out, total_own, total_other):
    step = pl.program_id(0)
    add_to(step, total_own, matmul_t(grad[...], weight_own[...]))
    add_to(step, total_other, matmul_t(grad[...], weight_other[...]))

    @pl.when(step == pl.num_programs(0) - 1)
    def _():
        store_halves(out, total_own[...], total_other[...], first[0] == 1)


def qkv_back(first, grad, weights):
    (w_own, at_own), (w_other, at_other) = weights["qkv"]
    rows, width = grad.shape
    depth = w_own.shape[0]
    return grid_call(
        qkv_back_kernel,
        "qkv_back",
        (first,),
        (width // QKV_BLOCK,),
        [
            columns_at(rows, QKV_BLOCK, 0),
            columns_at(depth, QKV_BLOCK, at_own // QKV_BLOCK),
            columns_at(depth, QKV_BLOCK, at_other // QKV_BLOCK),
        ],
        pl.BlockSpec((rows, 2 * depth), lambda n, *_: (0, 0)),
        jax.ShapeDtypeStruct((rows, 2 * depth), jnp.float32),
        [pltpu.VMEM((rows, depth), jnp.float32)] * 2,
        (grad, w_own, w_other),
    )


def hidden_kernel(
    first, own, other, gate_own, gate_other, up_own, up_other, down_own, down_other, middle,
    gate_out, up_out, product_out, out, total_own, total_other,
):
    step = pl.program_id(0)
    gate = matmul(own[...], gate_own[...]) + matmul(other[...], gate_other[...])
    up = matmul(own[...], up_own[...]) + matmul(other[...], up_other[...])
    product = (gate * split_normal(gate) * up).astype(jnp.bfloat16)
    gate_out[...] = gate
    up_out[...] = up
    product_out[...] = product
    add_to(step, total_own, matmul(product, down_own[...]))
    add_to(step, total_other, matmul(product, down_other[...]))

    @pl.when(step == pl.num_programs(0) - 1)
    def _():
        half = total_own.shape[1]
        mine, theirs, on_first = (total_own[...], total_other[...], first[0] == 1)
        out[:, :half] = middle[:, :half] + jnp.where(on_first, mine, theirs)
        out[:, half:] = middle[:, half:] + jnp.where(on_first, theirs, mine)


def hidden_specs(weights, depth):
    specs, arrays = ([], [])
    for part in ("gate", "up"):
        for array, at in weights[part]:
            specs.append(columns_at(depth, HIDDEN_BLOCK, at // HIDDEN_BLOCK))
            arrays.append(array)
    for array in weights["down"]:
        specs.append(rows_at(HIDDEN_BLOCK, array.shape[1]))
        arrays.append(array)
    return (specs, arrays)


def hidden_forward(first, own, other, middle, weights):
    rows, depth = own.shape
    width = middle.shape[1]
    specs, arrays = hidden_specs(weights, depth)
    piece = columns_at(rows, HIDDEN_BLOCK, 0)
    return grid_call(
        hidden_kernel,
        "hidden",
        (first,),
        (FF_PAD // HIDDEN_BLOCK,),
        [whole(own), whole(other), *specs, whole(middle)],
        (piece, piece, piece, whole(middle)),
        (
            jax.ShapeDtypeStruct((rows, FF_PAD), jnp.float32),
            jax.ShapeDtypeStruct((rows, FF_PAD), jnp.float32),
            jax.ShapeDtypeStruct((rows, FF_PAD), jnp.bfloat16),
            jax.ShapeDtypeStruct((rows, width), jnp.float32),
        ),
        [pltpu.VMEM((rows, width // 2), jnp.float32)] * 2,
        (own, other, *arrays, middle),
    )


def hidden_back_kernel(
    first, grad_own, grad_other, gate_in, up_in, gate_own, gate_other, up_own, up_other, down_own,
    down_other, grad_gate_out, grad_up_out, out, total_own, total_other,
):
    step = pl.program_id(0)
    gate, up = (gate_in[...], up_in[...])
    grad_product = matmul_t(grad_own[...], down_own[...]) + matmul_t(
        grad_other[...], down_other[...]
    )
    cumulative = split_normal(gate)
    derivative = cumulative + gate * jnp.exp(-0.5 * gate * gate) * root_two_pi
    grad_gate = (grad_product * up * derivative).astype(jnp.bfloat16)
    grad_up = (grad_product * gate * cumulative).astype(jnp.bfloat16)
    grad_gate_out[...] = grad_gate
    grad_up_out[...] = grad_up
    add_to(step, total_own, matmul_t(grad_gate, gate_own[...]) + matmul_t(grad_up, up_own[...]))
    add_to(
        step, total_other, matmul_t(grad_gate, gate_other[...]) + matmul_t(grad_up, up_other[...])
    )

    @pl.when(step == pl.num_programs(0) - 1)
    def _():
        store_halves(out, total_own[...], total_other[...], first[0] == 1)


def hidden_back(first, grad_own, grad_other, gate, up, weights):
    rows, half = grad_own.shape
    depth = half
    specs, arrays = hidden_specs(weights, depth)
    piece = columns_at(rows, HIDDEN_BLOCK, 0)
    return grid_call(
        hidden_back_kernel,
        "hidden_back",
        (first,),
        (FF_PAD // HIDDEN_BLOCK,),
        [whole(grad_own), whole(grad_other), piece, piece, *specs],
        (piece, piece, pl.BlockSpec((rows, 2 * depth), lambda n, *_: (0, 0))),
        (
            jax.ShapeDtypeStruct((rows, FF_PAD), jnp.bfloat16),
            jax.ShapeDtypeStruct((rows, FF_PAD), jnp.bfloat16),
            jax.ShapeDtypeStruct((rows, 2 * depth), jnp.float32),
        ),
        [pltpu.VMEM((rows, depth), jnp.float32)] * 2,
        (grad_own, grad_other, gate, up, *arrays),
    )


def attention_input(rows_in, gain):
    normed, factor = norm_parts(rows_in)
    act_in = (normed * gain).astype(jnp.bfloat16)
    before = to_next(act_in[act_in.shape[0] - HALO :])
    after = to_previous(act_in[:HALO])
    return (normed, factor, act_in, jnp.concatenate([before, act_in, after], axis=0))


def layer_forward(rows_in, entry, gain_pair, weights, segs, on_first, first, later=(), ready=()):
    normed1, factor1, act_in, extended = entry
    qkv = qkv_of(*column_halves(extended, on_first), weights)
    mixed, log_total = attend(*segs, qkv, ready)
    mixed, *later = lax.optimization_barrier((mixed, *later))
    own, other = column_halves(mixed, on_first)
    middle = rows_in + matmul(own, weights["out"][0]) + matmul(other, weights["out"][1])
    normed2, factor2 = norm_parts(middle)
    act_mid = (normed2 * gain_pair[1]).astype(jnp.bfloat16)
    own, other = column_halves(act_mid, on_first)
    gate, up, product, output = hidden_forward(first, own, other, middle, weights)
    acts = (jnp.stack([act_in, mixed, act_mid]), product)
    got = tuple(swapped(act) for act in acts)
    kept = (normed1, factor1, qkv, log_total, normed2, factor2, gate, up, acts, got)
    return (output, kept, later)


def seq_sum(total):
    return lax.psum_scatter(total, "seq", scatter_dimension=0, tiled=True)


GRAD_WIDTHS = (1536, 512, GRAD_PAD)
ROW_PIECE = FF // (SEQ_DEV * W_DEV)


def weight_grad_kernel(
    act_mine, act_got, product_mine, product_got, grad_mine, grad_got, gains, out,
    grads, down, groups,
):
    count, block = (act_mine.shape[1], act_mine.shape[2])
    step = pl.program_id(0)
    end = sum(GRAD_WIDTHS)

    @pl.when(step == 0)
    def _():
        grads[:count] = grad_mine[...]
        grads[count:] = grad_got[...]
        for at in range(0, FF_PAD, 896):
            product = jnp.concatenate(
                [product_mine[:, at : at + 896], product_got[:, at : at + 896]], axis=0
            )
            down[at : at + 896] = inner_rows(product, grads[:, end:])
        width = down.shape[1]
        for piece in range(SEQ_DEV * W_DEV):
            for group in range(PAD_ROWS // 16):
                rows = piece * ROW_PIECE + group * 16
                groups[16 * piece : 16 * piece + 16, group * width : (group + 1) * width] = down[
                    rows : rows + 16
                ].astype(jnp.bfloat16)

    at = 0
    for member, width in enumerate(GRAD_WIDTHS):
        acts = jnp.concatenate([act_mine[member], act_got[member]], axis=0)
        for part in range(at, at + width, 512):
            size = min(512, at + width - part)
            out[:, part : part + size] = inner_rows(acts, grads[:, part : part + size]).astype(
                jnp.bfloat16
            )
        at += width
    out[:, end - gains.shape[1] : end] = gains[...]
    out[:, end:] = groups[pl.ds(pl.multiple_of(step * block, block), block)]


def weight_grads(acts, acts_got, grad_mine, grad_got, gains):
    members, count, width = acts[0].shape
    block = 256
    half = grad_mine.shape[1] - sum(GRAD_WIDTHS)
    groups = half * PAD_ROWS // 16
    act_spec = pl.BlockSpec((members, count, block), lambda n: (0, 0, n))
    product_spec = whole(acts[1])
    return grid_call(
        weight_grad_kernel,
        "weight_grads",
        (),
        (width // block,),
        [
            act_spec,
            act_spec,
            product_spec,
            product_spec,
            whole(grad_mine),
            whole(grad_got),
            rows_at(block, gains.shape[1]),
        ],
        rows_at(block, sum(GRAD_WIDTHS) + groups),
        jax.ShapeDtypeStruct((width, sum(GRAD_WIDTHS) + groups), jnp.bfloat16),
        [
            pltpu.VMEM((2 * count, grad_mine.shape[1]), jnp.bfloat16),
            pltpu.VMEM((FF_PAD, half), jnp.float32),
            pltpu.VMEM((width, groups), jnp.bfloat16),
        ],
        (acts[0], acts_got[0], acts[1], acts_got[1], grad_mine, grad_got, gains),
    )


def layer_backward(grad_out, kept, gain_pair, weights, segs, on_first, first, earlier_gains):
    (normed1, factor1, qkv, log_total, normed2, factor2, gate, up, acts, got) = kept
    rows, width = normed1.shape
    half = width // 2
    grad_branch = grad_out.astype(jnp.bfloat16)
    low, high = (grad_branch[:, :half], grad_branch[:, half:])
    branch_own, branch_other = (jnp.where(on_first, low, high), jnp.where(on_first, high, low))
    grad_gate, grad_up, grad_norm2 = hidden_back(
        first, branch_own, branch_other, gate, up, weights
    )
    gain_mid = jnp.sum(normed2 * grad_norm2, axis=0)
    grad_middle = grad_out + norm_back(grad_norm2 * gain_pair[1], normed2, factor2)
    grad_attn = grad_middle.astype(jnp.bfloat16)
    mine, theirs = [matmul_t(grad_attn, w) for w in weights["out"]]
    grad_mixed = from_halves(mine, theirs, on_first).astype(jnp.bfloat16)
    grad_query, grad_own, grad_before, grad_after = attend_back(*segs, qkv, log_total, grad_mixed)
    from_previous = to_next(grad_after).astype(jnp.float32)
    from_next = to_previous(grad_before).astype(jnp.float32)
    grad_pairs = grad_own + jnp.concatenate([from_previous, from_next], axis=0)
    grad_qkv = jnp.concatenate([grad_query, grad_pairs.astype(jnp.bfloat16)], axis=1)
    halves = (
        (grad_qkv[:, : 3 * half], grad_qkv[:, 3 * half :]),
        (grad_attn[:, :half], grad_attn[:, half:]),
        (grad_gate, grad_up),
        (jnp.zeros((rows, GRAD_PAD - FF_PAD), jnp.bfloat16),) * 2,
        (low, high),
    )
    first_half, second_half = [jnp.concatenate([h[k] for h in halves], axis=1) for k in range(2)]
    grad_mine = jnp.where(on_first, first_half, second_half)
    grad_got = swapped(jnp.where(on_first, second_half, first_half))
    grad_norm1 = qkv_back(first, grad_qkv, weights)
    gain_first = jnp.sum(normed1 * grad_norm1, axis=0)
    grad_inputs = grad_middle + norm_back(grad_norm1 * gain_pair[0], normed1, factor1)
    gains = jnp.stack([gain_first, gain_mid])
    gains = jnp.concatenate([gains, earlier_gains], axis=0)
    columns = jnp.pad(gains, ((0, 128 - gains.shape[0]), (0, 0))).T.astype(jnp.bfloat16)
    if earlier_gains.shape[0] == 0:
        columns = jnp.zeros(columns.shape, columns.dtype)
    sums = seq_sum(weight_grads(acts, got, grad_mine, grad_got, columns))
    return (grad_inputs, sums, gains)


def summed_over_w(block, place):
    rows = block.shape[0] // W_DEV
    total = lax.dynamic_slice_in_dim(block, place * rows, rows).astype(jnp.float32)
    for step in range(1, W_DEV):
        part = lax.dynamic_slice_in_dim(block, lax.rem(place + step, W_DEV) * rows, rows)
        got = lax.ppermute(part, "wshard", [(j, (j + step) % W_DEV) for j in range(W_DEV)])
        total = total + got.astype(jnp.float32)
    return total


def per_device(
    inputs, cotangent, segments, norm_gains, attend_in, attend_out, hidden_in, hidden_out
):
    on_first = lax.axis_index("section") == 0
    core = lax.axis_index("section")
    seq_place = lax.axis_index("seq")
    w_place = lax.axis_index("wshard")

    def by_core(first, second):
        return jnp.where(on_first, first, second)

    def sections(own, got):
        return (by_core(own, got), by_core(got, own))

    slice_rows = attend_in.shape[1] // (2 * SEQ_DEV)
    pad = jnp.zeros((slice_rows, FF_PAD - FF), jnp.bfloat16)
    width = inputs.shape[3]

    def row_slice(which):
        at = (which * SEQ_DEV + seq_place) * slice_rows
        hidden, qkv, out = [
            lax.dynamic_slice_in_dim(w[0], at, slice_rows)
            for w in (hidden_in, attend_in, attend_out)
        ]
        return jnp.concatenate([hidden[:, :FF], pad, hidden[:, FF:], pad, qkv, out], axis=1)

    def in_order(first, second):
        ends = (0, 2 * FF_PAD, 2 * FF_PAD + 3 * width, 2 * FF_PAD + 4 * width)
        return jnp.concatenate(
            [piece[:, a:b] for a, b in zip(ends, ends[1:]) for piece in (first, second)], axis=1
        )

    row_pieces = sections(row_slice(core), swapped(row_slice(1 - core)))
    hidden_width, qkv_width = (2 * FF_PAD, 3 * width)
    qkv_at = 2 * hidden_width
    out_at = qkv_at + 2 * qkv_width
    all_own = lax.all_gather(in_order(*row_pieces), ("wshard", "seq"), axis=0, tiled=True)
    half = hidden_out.shape[2] // 2
    low, high = (hidden_out[0, :, :half], hidden_out[0, :, half:])
    down_piece = jnp.concatenate(sections(by_core(low, high), swapped(by_core(high, low))), axis=1)
    w_up = [(j, (j + 1) % W_DEV) for j in range(W_DEV)]
    w_down = [(j, i) for i, j in w_up]
    below = lax.ppermute(down_piece, "wshard", w_up)
    above = lax.ppermute(down_piece, "wshard", w_down)
    far = (
        lax.ppermute(below[:, :half], "wshard", w_up),
        lax.ppermute(above[:, half:], "wshard", w_down),
    )
    gain_pairs = sections(norm_gains[0], swapped(norm_gains[0]))
    piece_rows = down_piece.shape[0]

    def down_of(section):
        columns = slice(section * half, (section + 1) * half)
        own = jnp.zeros((FF_PAD, half), jnp.bfloat16)
        for step, piece in (
            (0, down_piece[:, columns]),
            (1, above[:, columns]),
            (2, far[section]),
            (3, below[:, columns]),
        ):
            own = lax.dynamic_update_slice_in_dim(
                own, piece, lax.rem(w_place + step, W_DEV) * piece_rows, 0
            )
        return own

    rows_in = by_core(inputs[0, 0], inputs[1, 0])
    row_count = rows_in.shape[0]
    segment_row = by_core(segments[0, 0], segments[1, 0])
    padded = jnp.pad(segment_row, (HALO, HALO), constant_values=-1)
    first_row = seq_place * row_count
    segs = (
        lax.dynamic_slice_in_dim(segment_row, first_row, row_count)[:, None],
        lax.dynamic_slice_in_dim(padded, first_row, row_count + 2 * HALO)[None, :],
    )
    entry = attention_input(rows_in, gain_pairs[0][0])
    down_own = (down_of(0), down_of(1))
    all_own, down_own, down_other, entry, gain_pairs, segs = lax.optimization_barrier(
        (all_own, down_own, tuple(swapped(d) for d in down_own), entry, gain_pairs, segs)
    )
    qkv_piece, all_own = lax.optimization_barrier(
        (all_own[:, qkv_at : qkv_at + qkv_width], all_own)
    )
    first_qkv = swapped(qkv_piece)
    first_out = swapped(all_own[:, out_at : out_at + width])
    first_hidden = swapped(all_own[:, :hidden_width])
    first_weights = {
        "qkv": ((all_own, qkv_at), (first_qkv, 0)),
        "gate": ((all_own, 0), (first_hidden, 0)),
        "up": ((all_own, FF_PAD), (first_hidden, FF_PAD)),
        "out": (all_own[:, out_at : out_at + width], first_out),
        "down": (down_own[0], down_other[0]),
    }

    def second_weights(all_late):
        all_other = swapped(all_late)
        return {
            "qkv": ((all_own, qkv_at + qkv_width), (all_other, qkv_at + qkv_width)),
            "gate": ((all_own, hidden_width), (all_other, hidden_width)),
            "up": ((all_own, hidden_width + FF_PAD), (all_other, hidden_width + FF_PAD)),
            "out": (all_own[:, out_at + width :], all_other[:, out_at + width :]),
            "down": (down_own[1], down_other[1]),
        }

    first = on_first.astype(jnp.int32)[None]
    middle, kept0, (all_late,) = layer_forward(
        rows_in, entry, gain_pairs[0], first_weights, segs, on_first, first,
        (all_own,), (first_hidden, first_out),
    )
    weights = (first_weights, second_weights(all_late))
    entry = attention_input(middle, gain_pairs[1][0])
    final, kept1, _ = layer_forward(
        middle, entry, gain_pairs[1], weights[1], segs, on_first, first
    )
    upstream = by_core(cotangent[0, 0], cotangent[1, 0])
    no_gains = jnp.zeros((0, width), jnp.float32)
    grads1, sums1, gains1 = layer_backward(
        upstream, kept1, gain_pairs[1], weights[1], segs, on_first, first, no_gains
    )
    grads0, sums0, _ = layer_backward(
        grads1, kept0, gain_pairs[0], weights[0], segs, on_first, first, gains1
    )

    def placed(first, second):
        mine, give = (by_core(first, second), by_core(second, first))
        got = swapped(give)
        return jnp.stack([by_core(mine, got), by_core(got, mine)])[None, :, None]

    section_outputs = placed(middle, final)
    section_input_grads = placed(grads0, grads1)

    totals = [summed_over_w(sums, w_place) for sums in (sums0, sums1)]
    mine, got = (by_core(*totals), swapped(by_core(totals[1], totals[0])))
    low, high = (by_core(mine, got), by_core(got, mine))
    attn_end, hidden_at = (3 * width // 2, 2 * width)
    down_at = hidden_at + GRAD_PAD
    qkv_rows = jnp.concatenate([low[:, :attn_end], high[:, :attn_end]], axis=1)
    attn_rows = jnp.concatenate([low[:, attn_end:hidden_at], high[:, attn_end:hidden_at]], axis=1)
    hidden_rows = jnp.concatenate(
        [low[:, hidden_at : hidden_at + FF], high[:, hidden_at : hidden_at + FF]], axis=1
    )
    gain_part = totals[0][:, down_at - 128 : down_at]
    gain_part = gain_part + swapped(gain_part)
    gain_rows = by_core(gain_part[:, :2], gain_part[:, 2:4]).T
    down_total = jnp.concatenate(
        [
            jnp.concatenate(
                [h[:, at : at + width // 2] for h in (low, high)], axis=1
            )
            for at in range(down_at, low.shape[1], width // 2)
        ],
        axis=0,
    )[: FF // (SEQ_DEV * W_DEV)]
    return (
        section_outputs,
        section_input_grads,
        qkv_rows[None],
        attn_rows[None],
        hidden_rows[None],
        down_total[None],
        gain_rows[None],
    )


def solution(mesh):
    placed = (
        P(None, "wshard", "seq", None),
        P(None, "wshard", "seq", None),
        P(None, "wshard", None),
        P("section", None, None),
        P("section", "wshard", None),
        P("section", "wshard", None),
        P("section", "wshard", None),
        P("section", "wshard", None),
    )
    return jax.shard_map(
        per_device,
        mesh=mesh,
        in_specs=placed,
        out_specs=(
            P("section", None, "wshard", "seq", None),
            P("section", None, "wshard", "seq", None),
            P("section", ("seq", "wshard"), None),
            P("section", ("seq", "wshard"), None),
            P("section", ("seq", "wshard"), None),
            P("section", ("seq", "wshard"), None),
            P("section", None, ("seq", "wshard")),
        ),
        check_vma=False,
    )
```

```python
import math

import jax
import jax.numpy as jnp
from jax import lax
from jax.experimental import pallas as pl
from jax.experimental.pallas import tpu as pltpu
from jax.sharding import PartitionSpec as P

HEADS = 16
HEAD_DIM = 64
FF = 2624
HALO = 64
FF_PAD = 2688
SEQ_DEV = 16
W_DEV = 4
PAD_ROWS = 48
HIDDEN_BLOCK = 896
QKV_BLOCK = 1536

norm_eps = 1e-05
root_half = 1.0 / math.sqrt(2.0)
root_two_pi = 1.0 / math.sqrt(2.0 * math.pi)
score_scale = 1.0 / math.sqrt(HEAD_DIM)

SWAP = [(0, 1), (1, 0)]


def swapped(array):
    return lax.ppermute(array, "section", SWAP)


def norm_parts(rows_in):
    centred = rows_in - jnp.mean(rows_in, axis=1, keepdims=True)
    factor = lax.rsqrt(jnp.mean(centred * centred, axis=1, keepdims=True) + norm_eps)
    return (centred * factor, factor)


def norm_back(grad_norm, normed, factor):
    inner = jnp.mean(grad_norm, axis=1, keepdims=True)
    along = jnp.mean(grad_norm * normed, axis=1, keepdims=True)
    return factor * (grad_norm - inner - normed * along)


def matmul(left, right):
    return jnp.dot(left, right, preferred_element_type=jnp.float32)


def matmul_t(left, right):
    return lax.dot_general(
        left, right, (((1,), (1,)), ((), ())), preferred_element_type=jnp.float32
    )


def inner_rows(left, right):
    return lax.dot_general(
        left, right, (((0,), (0,)), ((), ())), preferred_element_type=jnp.float32
    )


def column_halves(array, on_first):
    even = jnp.concatenate([array[:, 256 * k : 256 * k + 128] for k in range(4)], axis=1)
    odd = jnp.concatenate([array[:, 256 * k + 128 : 256 * k + 256] for k in range(4)], axis=1)
    return (jnp.where(on_first, even, odd), jnp.where(on_first, odd, even))


def from_halves(own, other, on_first):
    even = jnp.where(on_first, own, other)
    odd = jnp.where(on_first, other, own)
    parts = []
    for k in range(4):
        parts += [even[:, 128 * k : 128 * k + 128], odd[:, 128 * k : 128 * k + 128]]
    return jnp.concatenate(parts, axis=1)


def window_allowed(query_seg, key_seg):
    rows, keys = (query_seg.shape[0], key_seg.shape[1])
    offset = lax.broadcasted_iota(jnp.int32, (rows, keys), 1) - lax.broadcasted_iota(
        jnp.int32, (rows, keys), 0
    )
    return (offset >= 0) & (offset <= 2 * HALO) & (query_seg == key_seg)


def attend_kernel(query_seg, key_seg, qkv, *refs):
    mixed, log_total = refs[-2:]
    allowed = window_allowed(query_seg[...], key_seg[...])
    width = HEADS * HEAD_DIM
    rows = mixed.shape[0]
    for head in range(HEADS):
        at = head * HEAD_DIM
        q = qkv[HALO : HALO + rows, at : at + HEAD_DIM]
        k = qkv[:, width + at : width + at + HEAD_DIM]
        v = qkv[:, 2 * width + at : 2 * width + at + HEAD_DIM]
        scores = jnp.where(allowed, matmul_t(q, k) * score_scale, -1e30)
        row_max = jnp.max(scores, axis=1, keepdims=True)
        exponent = jnp.exp(scores - row_max)
        total = jnp.sum(exponent, axis=1, keepdims=True)
        probs = (exponent * (1.0 / total)).astype(jnp.bfloat16)
        mixed[:, at : at + HEAD_DIM] = matmul(probs, v).astype(jnp.bfloat16)
        log_total[:, at : at + HEAD_DIM] = jnp.broadcast_to(
            row_max + jnp.log(total), (rows, HEAD_DIM)
        )


def attend_back_kernel(
    query_seg, key_seg, qkv, log_total, grad_mixed, grad_query, own, before, after
):
    allowed = window_allowed(query_seg[...], key_seg[...])
    width = HEADS * HEAD_DIM
    rows = grad_mixed.shape[0]
    for head in range(HEADS):
        at = head * HEAD_DIM
        q = qkv[HALO : HALO + rows, at : at + HEAD_DIM]
        k = qkv[:, width + at : width + at + HEAD_DIM]
        v = qkv[:, 2 * width + at : 2 * width + at + HEAD_DIM]
        grad = grad_mixed[:, at : at + HEAD_DIM]
        scores = jnp.where(allowed, matmul_t(q, k) * score_scale, -1e30)
        probs = jnp.exp(scores - log_total[:, at : at + 1])
        grad_probs = matmul_t(grad, v)
        inner = jnp.sum(probs * grad_probs, axis=1, keepdims=True)
        grad_scores = (probs * (grad_probs - inner)).astype(jnp.bfloat16)
        grad_query[:, at : at + HEAD_DIM] = (matmul(grad_scores, k) * score_scale).astype(
            jnp.bfloat16
        )
        for place, piece in (
            (at, inner_rows(grad_scores, q) * score_scale),
            (width + at, inner_rows(probs.astype(jnp.bfloat16), grad)),
        ):
            columns = slice(place, place + HEAD_DIM)
            before[:, columns] = piece[:HALO].astype(jnp.bfloat16)
            own[:, columns] = piece[HALO : HALO + rows]
            after[:, columns] = piece[HALO + rows :].astype(jnp.bfloat16)


params = pltpu.CompilerParams(vmem_limit_bytes=40 * 1024 * 1024)


def attend(query_seg, key_seg, qkv, ready):
    rows, width = (query_seg.shape[0], HEADS * HEAD_DIM)
    return pl.pallas_call(
        attend_kernel,
        out_shape=(
            jax.ShapeDtypeStruct((rows, width), jnp.bfloat16),
            jax.ShapeDtypeStruct((rows, width), jnp.float32),
        ),
        in_specs=[pl.BlockSpec(memory_space=pltpu.VMEM)] * 3
        + [pl.BlockSpec(memory_space=pl.ANY)] * len(ready),
        compiler_params=params,
        name="attend",
    )(query_seg, key_seg, qkv, *ready)


def attend_back(query_seg, key_seg, qkv, log_total, grad_mixed):
    rows, width = (query_seg.shape[0], HEADS * HEAD_DIM)
    return pl.pallas_call(
        attend_back_kernel,
        out_shape=(
            jax.ShapeDtypeStruct((rows, width), jnp.bfloat16),
            jax.ShapeDtypeStruct((rows, 2 * width), jnp.float32),
            jax.ShapeDtypeStruct((HALO, 2 * width), jnp.bfloat16),
            jax.ShapeDtypeStruct((HALO, 2 * width), jnp.bfloat16),
        ),
        compiler_params=params,
        name="attend_back",
    )(query_seg, key_seg, qkv, log_total, grad_mixed)


def to_next(array):
    return lax.ppermute(array, "seq", [(i, i + 1) for i in range(SEQ_DEV - 1)])


def to_previous(array):
    return lax.ppermute(array, "seq", [(i + 1, i) for i in range(SEQ_DEV - 1)])


def split_normal(gate):
    cumulative = 0.5 * (1.0 + lax.erf(gate * root_half))
    return cumulative


def grid_call(kernel, name, scalars, grid, in_specs, out_specs, out_shape, scratch, args, aliases=None):
    return pl.pallas_call(
        kernel,
        grid_spec=pltpu.PrefetchScalarGridSpec(
            num_scalar_prefetch=len(scalars),
            grid=grid,
            in_specs=in_specs,
            out_specs=out_specs,
            scratch_shapes=scratch,
        ),
        out_shape=out_shape,
        input_output_aliases=aliases or {},
        compiler_params=params,
        name=name,
    )(*scalars, *args)


def whole(array):
    return pl.BlockSpec(array.shape, lambda n, *_: (0,) * array.ndim)


def columns_at(rows, block, first):
    return pl.BlockSpec((rows, block), lambda n, *_: (0, first + n))


def rows_at(block, columns):
    return pl.BlockSpec((block, columns), lambda n, *_: (n, 0))


def add_to(step, total, value):
    @pl.when(step == 0)
    def _():
        total[...] = value

    @pl.when(step > 0)
    def _():
        total[...] += value


def store_halves(out, own, other, on_first):
    for k in range(4):
        block = slice(128 * k, 128 * k + 128)
        out[:, 256 * k : 256 * k + 128] = jnp.where(on_first, own[:, block], other[:, block])
        out[:, 256 * k + 128 : 256 * k + 256] = jnp.where(on_first, other[:, block], own[:, block])


def qkv_kernel(own, other, weight_own, weight_other, out):
    out[...] = (
        matmul(own[...], weight_own[...]) + matmul(other[...], weight_other[...])
    ).astype(jnp.bfloat16)


def qkv_of(own, other, weights):
    (w_own, at_own), (w_other, at_other) = weights["qkv"]
    width = 3 * HEADS * HEAD_DIM
    depth = own.shape[1]
    return grid_call(
        qkv_kernel,
        "qkv",
        (),
        (width // QKV_BLOCK,),
        [
            whole(own),
            whole(other),
            columns_at(depth, QKV_BLOCK, at_own // QKV_BLOCK),
            columns_at(depth, QKV_BLOCK, at_other // QKV_BLOCK),
        ],
        columns_at(own.shape[0], QKV_BLOCK, 0),
        jax.ShapeDtypeStruct((own.shape[0], width), jnp.bfloat16),
        [],
        (own, other, w_own, w_other),
    )


def qkv_back_kernel(first, grad, weight_own, weight_other, out, total_own, total_other):
    step = pl.program_id(0)
    add_to(step, total_own, matmul_t(grad[...], weight_own[...]))
    add_to(step, total_other, matmul_t(grad[...], weight_other[...]))

    @pl.when(step == pl.num_programs(0) - 1)
    def _():
        store_halves(out, total_own[...], total_other[...], first[0] == 1)


def qkv_back(first, grad, weights):
    (w_own, at_own), (w_other, at_other) = weights["qkv"]
    rows, width = grad.shape
    depth = w_own.shape[0]
    return grid_call(
        qkv_back_kernel,
        "qkv_back",
        (first,),
        (width // QKV_BLOCK,),
        [
            columns_at(rows, QKV_BLOCK, 0),
            columns_at(depth, QKV_BLOCK, at_own // QKV_BLOCK),
            columns_at(depth, QKV_BLOCK, at_other // QKV_BLOCK),
        ],
        pl.BlockSpec((rows, 2 * depth), lambda n, *_: (0, 0)),
        jax.ShapeDtypeStruct((rows, 2 * depth), jnp.float32),
        [pltpu.VMEM((rows, depth), jnp.float32)] * 2,
        (grad, w_own, w_other),
    )


def hidden_kernel(
    first, own, other, gate_own, gate_other, up_own, up_other, down_own, down_other, middle,
    gate_out, up_out, product_out, out, total_own, total_other,
):
    step = pl.program_id(0)
    gate = matmul(own[...], gate_own[...]) + matmul(other[...], gate_other[...])
    up = matmul(own[...], up_own[...]) + matmul(other[...], up_other[...])
    product = (gate * split_normal(gate) * up).astype(jnp.bfloat16)
    gate_out[...] = gate
    up_out[...] = up
    product_out[...] = product
    add_to(step, total_own, matmul(product, down_own[...]))
    add_to(step, total_other, matmul(product, down_other[...]))

    @pl.when(step == pl.num_programs(0) - 1)
    def _():
        half = total_own.shape[1]
        mine, theirs, on_first = (total_own[...], total_other[...], first[0] == 1)
        out[:, :half] = middle[:, :half] + jnp.where(on_first, mine, theirs)
        out[:, half:] = middle[:, half:] + jnp.where(on_first, theirs, mine)


def hidden_specs(weights, depth):
    specs, arrays = ([], [])
    for part in ("gate", "up"):
        for array, at in weights[part]:
            specs.append(columns_at(depth, HIDDEN_BLOCK, at // HIDDEN_BLOCK))
            arrays.append(array)
    for array in weights["down"]:
        specs.append(rows_at(HIDDEN_BLOCK, array.shape[1]))
        arrays.append(array)
    return (specs, arrays)


def hidden_forward(first, own, other, middle, weights):
    rows, depth = own.shape
    width = middle.shape[1]
    specs, arrays = hidden_specs(weights, depth)
    piece = columns_at(rows, HIDDEN_BLOCK, 0)
    return grid_call(
        hidden_kernel,
        "hidden",
        (first,),
        (FF_PAD // HIDDEN_BLOCK,),
        [whole(own), whole(other), *specs, whole(middle)],
        (piece, piece, piece, whole(middle)),
        (
            jax.ShapeDtypeStruct((rows, FF_PAD), jnp.float32),
            jax.ShapeDtypeStruct((rows, FF_PAD), jnp.float32),
            jax.ShapeDtypeStruct((rows, FF_PAD), jnp.bfloat16),
            jax.ShapeDtypeStruct((rows, width), jnp.float32),
        ),
        [pltpu.VMEM((rows, width // 2), jnp.float32)] * 2,
        (own, other, *arrays, middle),
    )


def hidden_back_kernel(
    first, grad_own, grad_other, gate_in, up_in, gate_own, gate_other, up_own, up_other, down_own,
    down_other, grad_gate_out, grad_up_out, out, total_own, total_other,
):
    step = pl.program_id(0)
    gate, up = (gate_in[...], up_in[...])
    grad_product = matmul_t(grad_own[...], down_own[...]) + matmul_t(
        grad_other[...], down_other[...]
    )
    cumulative = split_normal(gate)
    derivative = cumulative + gate * jnp.exp(-0.5 * gate * gate) * root_two_pi
    grad_gate = (grad_product * up * derivative).astype(jnp.bfloat16)
    grad_up = (grad_product * gate * cumulative).astype(jnp.bfloat16)
    grad_gate_out[...] = grad_gate
    grad_up_out[...] = grad_up
    add_to(step, total_own, matmul_t(grad_gate, gate_own[...]) + matmul_t(grad_up, up_own[...]))
    add_to(
        step, total_other, matmul_t(grad_gate, gate_other[...]) + matmul_t(grad_up, up_other[...])
    )

    @pl.when(step == pl.num_programs(0) - 1)
    def _():
        store_halves(out, total_own[...], total_other[...], first[0] == 1)


def hidden_back(first, grad_own, grad_other, gate, up, weights):
    rows, half = grad_own.shape
    depth = half
    specs, arrays = hidden_specs(weights, depth)
    piece = columns_at(rows, HIDDEN_BLOCK, 0)
    return grid_call(
        hidden_back_kernel,
        "hidden_back",
        (first,),
        (FF_PAD // HIDDEN_BLOCK,),
        [whole(grad_own), whole(grad_other), piece, piece, *specs],
        (piece, piece, pl.BlockSpec((rows, 2 * depth), lambda n, *_: (0, 0))),
        (
            jax.ShapeDtypeStruct((rows, FF_PAD), jnp.bfloat16),
            jax.ShapeDtypeStruct((rows, FF_PAD), jnp.bfloat16),
            jax.ShapeDtypeStruct((rows, 2 * depth), jnp.float32),
        ),
        [pltpu.VMEM((rows, depth), jnp.float32)] * 2,
        (grad_own, grad_other, gate, up, *arrays),
    )


def attention_input(rows_in, gain):
    normed, factor = norm_parts(rows_in)
    act_in = (normed * gain).astype(jnp.bfloat16)
    before = to_next(act_in[act_in.shape[0] - HALO :])
    after = to_previous(act_in[:HALO])
    return (normed, factor, act_in, jnp.concatenate([before, act_in, after], axis=0))


def layer_forward(rows_in, entry, gain_pair, weights, segs, on_first, first, later=(), ready=()):
    normed1, factor1, act_in, extended = entry
    qkv = qkv_of(*column_halves(extended, on_first), weights)
    mixed, log_total = attend(*segs, qkv, ready)
    mixed, *later = lax.optimization_barrier((mixed, *later))
    own, other = column_halves(mixed, on_first)
    middle = rows_in + matmul(own, weights["out"][0]) + matmul(other, weights["out"][1])
    normed2, factor2 = norm_parts(middle)
    act_mid = (normed2 * gain_pair[1]).astype(jnp.bfloat16)
    own, other = column_halves(act_mid, on_first)
    gate, up, product, output = hidden_forward(first, own, other, middle, weights)
    acts = (jnp.stack([act_in, mixed, act_mid]), product)
    got = tuple(swapped(act) for act in acts)
    kept = (normed1, factor1, qkv, log_total, normed2, factor2, gate, up, acts, got)
    return (output, kept, later)


def seq_sum(total):
    return lax.psum_scatter(total, "seq", scatter_dimension=0, tiled=True)


ROW_PIECE = FF // (SEQ_DEV * W_DEV)
ROW_GROUPS = PAD_ROWS // 16


def weight_grads(name, items, grads, total, product=None, gains=None, base=None):
    count, width = items[0][0].shape[1:]
    block = 256
    in_specs, args = ([], [])
    for acts, got, member, *_ in items:
        for array in (acts, got):
            in_specs.append(pl.BlockSpec((1, count, block), lambda n, m=member: (m, 0, n)))
            args.append(array)
    for pair in grads:
        in_specs += [whole(array) for array in pair]
        args += list(pair)
    scratch = [pltpu.VMEM((2 * count, pair[0].shape[1]), jnp.bfloat16) for pair in grads]
    if product is not None:
        in_specs += [whole(array) for array in product[:2]]
        args += list(product[:2])
        half = grads[product[2]][0].shape[1] - product[3]
        scratch += [
            pltpu.VMEM((FF_PAD, half), jnp.float32),
            pltpu.VMEM((width, ROW_GROUPS * half), jnp.bfloat16),
        ]
    if gains is not None:
        in_specs.append(rows_at(block, gains[0].shape[1]))
        args.append(gains[0])
    aliases = {}
    columns = total
    if base is not None:
        aliases = {len(args): 0}
        in_specs.append(pl.BlockSpec(memory_space=pl.ANY))
        args.append(base)
        columns = gains[1] + gains[0].shape[1]

    def kernel(*refs):
        act_refs = refs[: 2 * len(items)]
        grad_refs = refs[2 * len(items) : 2 * (len(items) + len(grads))]
        rest = refs[2 * (len(items) + len(grads)) : len(args)]
        out = refs[len(args)]
        rows = refs[len(args) + 1 :]
        step = pl.program_id(0)

        @pl.when(step == 0)
        def _():
            for k in range(len(grads)):
                rows[k][:count] = grad_refs[2 * k][...]
                rows[k][count:] = grad_refs[2 * k + 1][...]
            if product is not None:
                down, groups = rows[-2:]
                for at in range(0, FF_PAD, 896):
                    part = jnp.concatenate([r[:, at : at + 896] for r in rest[:2]], axis=0)
                    down[at : at + 896] = inner_rows(part, rows[product[2]][:, product[3] :])
                for piece in range(SEQ_DEV * W_DEV):
                    for group in range(ROW_GROUPS):
                        first_row = piece * ROW_PIECE + group * 16
                        groups[
                            16 * piece : 16 * piece + 16, group * half : (group + 1) * half
                        ] = down[first_row : first_row + 16].astype(jnp.bfloat16)

        for k, (_, _, _, which, at, size, place) in enumerate(items):
            acts = jnp.concatenate([act_refs[2 * k][0], act_refs[2 * k + 1][0]], axis=0)
            for part in range(0, size, 512):
                wide = min(512, size - part)
                out[:, place + part : place + part + wide] = inner_rows(
                    acts, rows[which][:, at + part : at + part + wide]
                ).astype(jnp.bfloat16)
        if product is not None:
            place = product[4]
            out[:, place : place + ROW_GROUPS * half] = rows[-1][
                pl.ds(pl.multiple_of(step * block, block), block)
            ]
        if gains is not None:
            out[:, gains[1] : gains[1] + gains[0].shape[1]] = rest[0][...]

    return grid_call(
        kernel,
        name,
        (),
        (width // block,),
        in_specs,
        rows_at(block, columns),
        jax.ShapeDtypeStruct((width, total), jnp.bfloat16),
        scratch,
        args,
        aliases,
    )


def core_halves(pairs, on_first):
    low, high = [jnp.concatenate([p[k] for p in pairs], axis=1) for k in range(2)]
    return (jnp.where(on_first, low, high), swapped(jnp.where(on_first, high, low)))


def layer_backward(grad_out, kept, gain_pair, weights, segs, on_first, first):
    (normed1, factor1, qkv, log_total, normed2, factor2, gate, up, acts, got) = kept
    rows, width = normed1.shape
    half = width // 2
    grad_branch = grad_out.astype(jnp.bfloat16)
    low, high = (grad_branch[:, :half], grad_branch[:, half:])
    branch_own, branch_other = (jnp.where(on_first, low, high), jnp.where(on_first, high, low))
    grad_gate, grad_up, grad_norm2 = hidden_back(
        first, branch_own, branch_other, gate, up, weights
    )
    hidden_pair = core_halves(((grad_gate, grad_up), (low, high)), on_first)
    gain_mid = jnp.sum(normed2 * grad_norm2, axis=0)
    grad_middle = grad_out + norm_back(grad_norm2 * gain_pair[1], normed2, factor2)
    grad_attn = grad_middle.astype(jnp.bfloat16)
    mine, theirs = [matmul_t(grad_attn, w) for w in weights["out"]]
    grad_mixed = from_halves(mine, theirs, on_first).astype(jnp.bfloat16)
    grad_query, grad_own, grad_before, grad_after = attend_back(*segs, qkv, log_total, grad_mixed)
    from_previous = to_next(grad_after).astype(jnp.float32)
    from_next = to_previous(grad_before).astype(jnp.float32)
    grad_pairs = grad_own + jnp.concatenate([from_previous, from_next], axis=0)
    grad_qkv = jnp.concatenate([grad_query, grad_pairs.astype(jnp.bfloat16)], axis=1)
    attn_pair = core_halves(
        (
            (grad_qkv[:, : 3 * half], grad_qkv[:, 3 * half :]),
            (grad_attn[:, :half], grad_attn[:, half:]),
        ),
        on_first,
    )
    grad_norm1 = qkv_back(first, grad_qkv, weights)
    gain_first = jnp.sum(normed1 * grad_norm1, axis=0)
    grad_inputs = grad_middle + norm_back(grad_norm1 * gain_pair[0], normed1, factor1)
    gains = jnp.stack([gain_first, gain_mid])
    return (grad_inputs, hidden_pair, attn_pair, gains)


def summed_over_w(block, place):
    rows = block.shape[0] // W_DEV
    total = lax.dynamic_slice_in_dim(block, place * rows, rows).astype(jnp.float32)
    for step in range(1, W_DEV):
        part = lax.dynamic_slice_in_dim(block, lax.rem(place + step, W_DEV) * rows, rows)
        got = lax.ppermute(part, "wshard", [(j, (j + step) % W_DEV) for j in range(W_DEV)])
        total = total + got.astype(jnp.float32)
    return total


def per_device(
    inputs, cotangent, segments, norm_gains, attend_in, attend_out, hidden_in, hidden_out
):
    on_first = lax.axis_index("section") == 0
    core = lax.axis_index("section")
    seq_place = lax.axis_index("seq")
    w_place = lax.axis_index("wshard")

    def by_core(first, second):
        return jnp.where(on_first, first, second)

    def sections(own, got):
        return (by_core(own, got), by_core(got, own))

    slice_rows = attend_in.shape[1] // (2 * SEQ_DEV)
    pad = jnp.zeros((slice_rows, FF_PAD - FF), jnp.bfloat16)
    width = inputs.shape[3]

    def row_slice(which):
        at = (which * SEQ_DEV + seq_place) * slice_rows
        hidden, qkv, out = [
            lax.dynamic_slice_in_dim(w[0], at, slice_rows)
            for w in (hidden_in, attend_in, attend_out)
        ]
        return jnp.concatenate([hidden[:, :FF], pad, hidden[:, FF:], pad, qkv, out], axis=1)

    def in_order(first, second):
        ends = (0, 2 * FF_PAD, 2 * FF_PAD + 3 * width, 2 * FF_PAD + 4 * width)
        return jnp.concatenate(
            [piece[:, a:b] for a, b in zip(ends, ends[1:]) for piece in (first, second)], axis=1
        )

    row_pieces = sections(row_slice(core), swapped(row_slice(1 - core)))
    hidden_width, qkv_width = (2 * FF_PAD, 3 * width)
    qkv_at = 2 * hidden_width
    out_at = qkv_at + 2 * qkv_width
    all_own = lax.all_gather(in_order(*row_pieces), ("wshard", "seq"), axis=0, tiled=True)
    half = hidden_out.shape[2] // 2
    low, high = (hidden_out[0, :, :half], hidden_out[0, :, half:])
    down_piece = jnp.concatenate(sections(by_core(low, high), swapped(by_core(high, low))), axis=1)
    w_up = [(j, (j + 1) % W_DEV) for j in range(W_DEV)]
    w_down = [(j, i) for i, j in w_up]
    below = lax.ppermute(down_piece, "wshard", w_up)
    above = lax.ppermute(down_piece, "wshard", w_down)
    far = (
        lax.ppermute(below[:, :half], "wshard", w_up),
        lax.ppermute(above[:, half:], "wshard", w_down),
    )
    gain_pairs = sections(norm_gains[0], swapped(norm_gains[0]))
    piece_rows = down_piece.shape[0]

    def down_of(section):
        columns = slice(section * half, (section + 1) * half)
        own = jnp.zeros((FF_PAD, half), jnp.bfloat16)
        for step, piece in (
            (0, down_piece[:, columns]),
            (1, above[:, columns]),
            (2, far[section]),
            (3, below[:, columns]),
        ):
            own = lax.dynamic_update_slice_in_dim(
                own, piece, lax.rem(w_place + step, W_DEV) * piece_rows, 0
            )
        return own

    rows_in = by_core(inputs[0, 0], inputs[1, 0])
    row_count = rows_in.shape[0]
    segment_row = by_core(segments[0, 0], segments[1, 0])
    padded = jnp.pad(segment_row, (HALO, HALO), constant_values=-1)
    first_row = seq_place * row_count
    segs = (
        lax.dynamic_slice_in_dim(segment_row, first_row, row_count)[:, None],
        lax.dynamic_slice_in_dim(padded, first_row, row_count + 2 * HALO)[None, :],
    )
    entry = attention_input(rows_in, gain_pairs[0][0])
    down_own = (down_of(0), down_of(1))
    all_own, down_own, down_other, entry, gain_pairs, segs = lax.optimization_barrier(
        (all_own, down_own, tuple(swapped(d) for d in down_own), entry, gain_pairs, segs)
    )
    first_qkv, all_own = lax.optimization_barrier(
        (swapped(all_own[:, qkv_at : qkv_at + qkv_width]), all_own)
    )
    first_out = swapped(all_own[:, out_at : out_at + width])
    first_hidden = swapped(all_own[:, :hidden_width])
    first_weights = {
        "qkv": ((all_own, qkv_at), (first_qkv, 0)),
        "gate": ((all_own, 0), (first_hidden, 0)),
        "up": ((all_own, FF_PAD), (first_hidden, FF_PAD)),
        "out": (all_own[:, out_at : out_at + width], first_out),
        "down": (down_own[0], down_other[0]),
    }

    def second_weights(all_late):
        all_other = swapped(all_late)
        return {
            "qkv": ((all_own, qkv_at + qkv_width), (all_other, qkv_at + qkv_width)),
            "gate": ((all_own, hidden_width), (all_other, hidden_width)),
            "up": ((all_own, hidden_width + FF_PAD), (all_other, hidden_width + FF_PAD)),
            "out": (all_own[:, out_at + width :], all_other[:, out_at + width :]),
            "down": (down_own[1], down_other[1]),
        }

    first = on_first.astype(jnp.int32)[None]
    middle, kept0, (all_late,) = layer_forward(
        rows_in, entry, gain_pairs[0], first_weights, segs, on_first, first,
        (all_own,), (first_hidden, first_out),
    )
    weights = (first_weights, second_weights(all_late))
    entry = attention_input(middle, gain_pairs[1][0])
    final, kept1, _ = layer_forward(
        middle, entry, gain_pairs[1], weights[1], segs, on_first, first
    )
    upstream = by_core(cotangent[0, 0], cotangent[1, 0])
    attn_cols, out_cols, down_cols = (qkv_width // 2, half, ROW_GROUPS * half)
    hidden_end = FF_PAD + down_cols
    second_at = attn_cols + out_cols + 128
    hidden_at = second_at + attn_cols + out_cols
    total = hidden_at + hidden_end

    def attn_items(kept, which, at):
        acts, got = (kept[-2][0], kept[-1][0])
        return [
            (acts, got, 0, which, 0, attn_cols, at),
            (acts, got, 1, which, attn_cols, out_cols, at + attn_cols),
        ]

    def hidden_items(kept, which, at):
        acts, got = (kept[-2], kept[-1])
        return (
            [(acts[0], got[0], 2, which, 0, FF_PAD, at)],
            (acts[1], got[1], which, FF_PAD, at + FF_PAD),
        )

    grads1, hidden_pair1, attn_pair1, gains1 = layer_backward(
        upstream, kept1, gain_pairs[1], weights[1], segs, on_first, first
    )
    items, product = hidden_items(kept1, 0, 0)
    early = seq_sum(weight_grads("hidden_grads", items, [hidden_pair1], hidden_end, product))
    grads0, hidden_pair0, attn_pair0, gains0 = layer_backward(
        grads1, kept0, gain_pairs[0], weights[0], segs, on_first, first
    )
    items, product = hidden_items(kept0, 1, hidden_at)
    base = weight_grads(
        "joint_grads",
        attn_items(kept1, 0, second_at) + items,
        [attn_pair1, hidden_pair0],
        total,
        product,
    )
    gains = jnp.concatenate([gains0, gains1], axis=0)
    gains = jnp.pad(gains, ((0, 128 - gains.shape[0]), (0, 0))).T.astype(jnp.bfloat16)
    late = seq_sum(
        weight_grads(
            "attn_grads",
            attn_items(kept0, 0, 0),
            [attn_pair0],
            total,
            None,
            (gains, attn_cols + out_cols),
            base,
        )
    )

    def placed(first, second):
        mine, give = (by_core(first, second), by_core(second, first))
        got = swapped(give)
        return jnp.stack([by_core(mine, got), by_core(got, mine)])[None, :, None]

    section_outputs = placed(middle, final)
    section_input_grads = placed(grads0, grads1)

    early_total, late_total = (summed_over_w(early, w_place), summed_over_w(late, w_place))
    gain_at = attn_cols + out_cols
    of_first = jnp.concatenate([late_total[:, :second_at], late_total[:, hidden_at:]], axis=1)
    of_second = jnp.concatenate(
        [late_total[:, second_at:hidden_at], late_total[:, gain_at:second_at], early_total], axis=1
    )
    mine, got = (by_core(of_first, of_second), swapped(by_core(of_second, of_first)))
    low, high = (by_core(mine, got), by_core(got, mine))
    qkv_rows = jnp.concatenate([low[:, :attn_cols], high[:, :attn_cols]], axis=1)
    attn_rows = jnp.concatenate([low[:, attn_cols:gain_at], high[:, attn_cols:gain_at]], axis=1)
    gain_part = (low + high)[:, gain_at:second_at]
    gain_rows = by_core(gain_part[:, :2], gain_part[:, 2:4]).T
    hidden_rows = jnp.concatenate(
        [low[:, second_at : second_at + FF], high[:, second_at : second_at + FF]], axis=1
    )
    down_total = jnp.concatenate(
        [
            jnp.concatenate([h[:, at : at + half] for h in (low, high)], axis=1)
            for at in range(second_at + FF_PAD, low.shape[1], half)
        ],
        axis=0,
    )[:ROW_PIECE]
    return (
        section_outputs,
        section_input_grads,
        qkv_rows[None],
        attn_rows[None],
        hidden_rows[None],
        down_total[None],
        gain_rows[None],
    )


def solution(mesh):
    placed = (
        P(None, "wshard", "seq", None),
        P(None, "wshard", "seq", None),
        P(None, "wshard", None),
        P("section", None, None),
        P("section", "wshard", None),
        P("section", "wshard", None),
        P("section", "wshard", None),
        P("section", "wshard", None),
    )
    return jax.shard_map(
        per_device,
        mesh=mesh,
        in_specs=placed,
        out_specs=(
            P("section", None, "wshard", "seq", None),
            P("section", None, "wshard", "seq", None),
            P("section", ("seq", "wshard"), None),
            P("section", ("seq", "wshard"), None),
            P("section", ("seq", "wshard"), None),
            P("section", ("seq", "wshard"), None),
            P("section", None, ("seq", "wshard")),
        ),
        check_vma=False,
    )
```

```python
import math

import jax
import jax.numpy as jnp
from jax import lax
from jax.experimental import pallas as pl
from jax.experimental.pallas import tpu as pltpu
from jax.sharding import PartitionSpec as P

HEADS = 16
HEAD_DIM = 64
FF = 2624
HALO = 64
FF_PAD = 2688
SEQ_DEV = 16
W_DEV = 4
PAD_ROWS = 48
HIDDEN_BLOCK = 896
QKV_BLOCK = 1536

norm_eps = 1e-05
root_half = 1.0 / math.sqrt(2.0)
root_two_pi = 1.0 / math.sqrt(2.0 * math.pi)
score_scale = 1.0 / math.sqrt(HEAD_DIM)

SWAP = [(0, 1), (1, 0)]


def swapped(array):
    return lax.ppermute(array, "section", SWAP)


def norm_parts(rows_in):
    centred = rows_in - jnp.mean(rows_in, axis=1, keepdims=True)
    factor = lax.rsqrt(jnp.mean(centred * centred, axis=1, keepdims=True) + norm_eps)
    return (centred * factor, factor)


def norm_back(grad_norm, normed, factor):
    inner = jnp.mean(grad_norm, axis=1, keepdims=True)
    along = jnp.mean(grad_norm * normed, axis=1, keepdims=True)
    return factor * (grad_norm - inner - normed * along)


def matmul(left, right):
    return jnp.dot(left, right, preferred_element_type=jnp.float32)


def matmul_t(left, right):
    return lax.dot_general(
        left, right, (((1,), (1,)), ((), ())), preferred_element_type=jnp.float32
    )


def inner_rows(left, right):
    return lax.dot_general(
        left, right, (((0,), (0,)), ((), ())), preferred_element_type=jnp.float32
    )


def column_halves(array, on_first):
    even = jnp.concatenate([array[:, 256 * k : 256 * k + 128] for k in range(4)], axis=1)
    odd = jnp.concatenate([array[:, 256 * k + 128 : 256 * k + 256] for k in range(4)], axis=1)
    return (jnp.where(on_first, even, odd), jnp.where(on_first, odd, even))


def from_halves(own, other, on_first):
    even = jnp.where(on_first, own, other)
    odd = jnp.where(on_first, other, own)
    parts = []
    for k in range(4):
        parts += [even[:, 128 * k : 128 * k + 128], odd[:, 128 * k : 128 * k + 128]]
    return jnp.concatenate(parts, axis=1)


def window_allowed(query_seg, key_seg):
    rows, keys = (query_seg.shape[0], key_seg.shape[1])
    offset = lax.broadcasted_iota(jnp.int32, (rows, keys), 1) - lax.broadcasted_iota(
        jnp.int32, (rows, keys), 0
    )
    return (offset >= 0) & (offset <= 2 * HALO) & (query_seg == key_seg)


def attend_kernel(query_seg, key_seg, qkv, *refs):
    mixed, log_total = refs[-2:]
    allowed = window_allowed(query_seg[...], key_seg[...])
    width = HEADS * HEAD_DIM
    rows = mixed.shape[0]
    for head in range(HEADS):
        at = head * HEAD_DIM
        q = qkv[HALO : HALO + rows, at : at + HEAD_DIM]
        k = qkv[:, width + at : width + at + HEAD_DIM]
        v = qkv[:, 2 * width + at : 2 * width + at + HEAD_DIM]
        scores = jnp.where(allowed, matmul_t(q, k) * score_scale, -1e30)
        row_max = jnp.max(scores, axis=1, keepdims=True)
        exponent = jnp.exp(scores - row_max)
        total = jnp.sum(exponent, axis=1, keepdims=True)
        probs = (exponent * (1.0 / total)).astype(jnp.bfloat16)
        mixed[:, at : at + HEAD_DIM] = matmul(probs, v).astype(jnp.bfloat16)
        log_total[:, at : at + HEAD_DIM] = jnp.broadcast_to(
            row_max + jnp.log(total), (rows, HEAD_DIM)
        )


def attend_back_kernel(query_seg, key_seg, qkv, log_total, grad_mixed, *refs):
    grad_query, own, before, after = refs[-4:]
    allowed = window_allowed(query_seg[...], key_seg[...])
    width = HEADS * HEAD_DIM
    rows = grad_mixed.shape[0]
    for head in range(HEADS):
        at = head * HEAD_DIM
        q = qkv[HALO : HALO + rows, at : at + HEAD_DIM]
        k = qkv[:, width + at : width + at + HEAD_DIM]
        v = qkv[:, 2 * width + at : 2 * width + at + HEAD_DIM]
        grad = grad_mixed[:, at : at + HEAD_DIM]
        scores = jnp.where(allowed, matmul_t(q, k) * score_scale, -1e30)
        probs = jnp.exp(scores - log_total[:, at : at + 1])
        grad_probs = matmul_t(grad, v)
        inner = jnp.sum(probs * grad_probs, axis=1, keepdims=True)
        grad_scores = (probs * (grad_probs - inner)).astype(jnp.bfloat16)
        grad_query[:, at : at + HEAD_DIM] = (matmul(grad_scores, k) * score_scale).astype(
            jnp.bfloat16
        )
        for place, piece in (
            (at, inner_rows(grad_scores, q) * score_scale),
            (width + at, inner_rows(probs.astype(jnp.bfloat16), grad)),
        ):
            columns = slice(place, place + HEAD_DIM)
            before[:, columns] = piece[:HALO].astype(jnp.bfloat16)
            own[:, columns] = piece[HALO : HALO + rows]
            after[:, columns] = piece[HALO + rows :].astype(jnp.bfloat16)


params = pltpu.CompilerParams(vmem_limit_bytes=40 * 1024 * 1024)


def attend(query_seg, key_seg, qkv, ready):
    rows, width = (query_seg.shape[0], HEADS * HEAD_DIM)
    return pl.pallas_call(
        attend_kernel,
        out_shape=(
            jax.ShapeDtypeStruct((rows, width), jnp.bfloat16),
            jax.ShapeDtypeStruct((rows, width), jnp.float32),
        ),
        in_specs=[pl.BlockSpec(memory_space=pltpu.VMEM)] * 3
        + [pl.BlockSpec(memory_space=pl.ANY)] * len(ready),
        compiler_params=params,
        name="attend",
    )(query_seg, key_seg, qkv, *ready)


def attend_back(query_seg, key_seg, qkv, log_total, grad_mixed, ready):
    rows, width = (query_seg.shape[0], HEADS * HEAD_DIM)
    return pl.pallas_call(
        attend_back_kernel,
        out_shape=(
            jax.ShapeDtypeStruct((rows, width), jnp.bfloat16),
            jax.ShapeDtypeStruct((rows, 2 * width), jnp.float32),
            jax.ShapeDtypeStruct((HALO, 2 * width), jnp.bfloat16),
            jax.ShapeDtypeStruct((HALO, 2 * width), jnp.bfloat16),
        ),
        in_specs=[pl.BlockSpec(memory_space=pltpu.VMEM)] * 5
        + [pl.BlockSpec(memory_space=pl.ANY)] * len(ready),
        compiler_params=params,
        name="attend_back",
    )(query_seg, key_seg, qkv, log_total, grad_mixed, *ready)


def to_next(array):
    return lax.ppermute(array, "seq", [(i, i + 1) for i in range(SEQ_DEV - 1)])


def to_previous(array):
    return lax.ppermute(array, "seq", [(i + 1, i) for i in range(SEQ_DEV - 1)])


def split_normal(gate):
    cumulative = 0.5 * (1.0 + lax.erf(gate * root_half))
    return cumulative


def grid_call(kernel, name, scalars, grid, in_specs, out_specs, out_shape, scratch, args, aliases=None):
    return pl.pallas_call(
        kernel,
        grid_spec=pltpu.PrefetchScalarGridSpec(
            num_scalar_prefetch=len(scalars),
            grid=grid,
            in_specs=in_specs,
            out_specs=out_specs,
            scratch_shapes=scratch,
        ),
        out_shape=out_shape,
        input_output_aliases=aliases or {},
        compiler_params=params,
        name=name,
    )(*scalars, *args)


def whole(array):
    return pl.BlockSpec(array.shape, lambda n, *_: (0,) * array.ndim)


def columns_at(rows, block, first):
    return pl.BlockSpec((rows, block), lambda n, *_: (0, first + n))


def rows_at(block, columns):
    return pl.BlockSpec((block, columns), lambda n, *_: (n, 0))


def add_to(step, total, value):
    @pl.when(step == 0)
    def _():
        total[...] = value

    @pl.when(step > 0)
    def _():
        total[...] += value


def store_halves(out, own, other, on_first):
    for k in range(4):
        block = slice(128 * k, 128 * k + 128)
        out[:, 256 * k : 256 * k + 128] = jnp.where(on_first, own[:, block], other[:, block])
        out[:, 256 * k + 128 : 256 * k + 256] = jnp.where(on_first, other[:, block], own[:, block])


def qkv_kernel(own, other, weight_own, weight_other, out):
    out[...] = (
        matmul(own[...], weight_own[...]) + matmul(other[...], weight_other[...])
    ).astype(jnp.bfloat16)


def qkv_of(own, other, weights):
    (w_own, at_own), (w_other, at_other) = weights["qkv"]
    width = 3 * HEADS * HEAD_DIM
    depth = own.shape[1]
    return grid_call(
        qkv_kernel,
        "qkv",
        (),
        (width // QKV_BLOCK,),
        [
            whole(own),
            whole(other),
            columns_at(depth, QKV_BLOCK, at_own // QKV_BLOCK),
            columns_at(depth, QKV_BLOCK, at_other // QKV_BLOCK),
        ],
        columns_at(own.shape[0], QKV_BLOCK, 0),
        jax.ShapeDtypeStruct((own.shape[0], width), jnp.bfloat16),
        [],
        (own, other, w_own, w_other),
    )


def qkv_back_kernel(first, grad, weight_own, weight_other, out, total_own, total_other):
    step = pl.program_id(0)
    add_to(step, total_own, matmul_t(grad[...], weight_own[...]))
    add_to(step, total_other, matmul_t(grad[...], weight_other[...]))

    @pl.when(step == pl.num_programs(0) - 1)
    def _():
        store_halves(out, total_own[...], total_other[...], first[0] == 1)


def qkv_back(first, grad, weights):
    (w_own, at_own), (w_other, at_other) = weights["qkv"]
    rows, width = grad.shape
    depth = w_own.shape[0]
    return grid_call(
        qkv_back_kernel,
        "qkv_back",
        (first,),
        (width // QKV_BLOCK,),
        [
            columns_at(rows, QKV_BLOCK, 0),
            columns_at(depth, QKV_BLOCK, at_own // QKV_BLOCK),
            columns_at(depth, QKV_BLOCK, at_other // QKV_BLOCK),
        ],
        pl.BlockSpec((rows, 2 * depth), lambda n, *_: (0, 0)),
        jax.ShapeDtypeStruct((rows, 2 * depth), jnp.float32),
        [pltpu.VMEM((rows, depth), jnp.float32)] * 2,
        (grad, w_own, w_other),
    )


def hidden_kernel(
    first, own, other, gate_own, gate_other, up_own, up_other, down_own, down_other, middle,
    gate_out, up_out, product_out, out, total_own, total_other,
):
    step = pl.program_id(0)
    gate = matmul(own[...], gate_own[...]) + matmul(other[...], gate_other[...])
    up = matmul(own[...], up_own[...]) + matmul(other[...], up_other[...])
    product = (gate * split_normal(gate) * up).astype(jnp.bfloat16)
    gate_out[...] = gate
    up_out[...] = up
    product_out[...] = product
    add_to(step, total_own, matmul(product, down_own[...]))
    add_to(step, total_other, matmul(product, down_other[...]))

    @pl.when(step == pl.num_programs(0) - 1)
    def _():
        half = total_own.shape[1]
        mine, theirs, on_first = (total_own[...], total_other[...], first[0] == 1)
        out[:, :half] = middle[:, :half] + jnp.where(on_first, mine, theirs)
        out[:, half:] = middle[:, half:] + jnp.where(on_first, theirs, mine)


def hidden_specs(weights, depth):
    specs, arrays = ([], [])
    for part in ("gate", "up"):
        for array, at in weights[part]:
            specs.append(columns_at(depth, HIDDEN_BLOCK, at // HIDDEN_BLOCK))
            arrays.append(array)
    for array in weights["down"]:
        specs.append(rows_at(HIDDEN_BLOCK, array.shape[1]))
        arrays.append(array)
    return (specs, arrays)


def hidden_forward(first, own, other, middle, weights):
    rows, depth = own.shape
    width = middle.shape[1]
    specs, arrays = hidden_specs(weights, depth)
    piece = columns_at(rows, HIDDEN_BLOCK, 0)
    return grid_call(
        hidden_kernel,
        "hidden",
        (first,),
        (FF_PAD // HIDDEN_BLOCK,),
        [whole(own), whole(other), *specs, whole(middle)],
        (piece, piece, piece, whole(middle)),
        (
            jax.ShapeDtypeStruct((rows, FF_PAD), jnp.float32),
            jax.ShapeDtypeStruct((rows, FF_PAD), jnp.float32),
            jax.ShapeDtypeStruct((rows, FF_PAD), jnp.bfloat16),
            jax.ShapeDtypeStruct((rows, width), jnp.float32),
        ),
        [pltpu.VMEM((rows, width // 2), jnp.float32)] * 2,
        (own, other, *arrays, middle),
    )


def hidden_back_kernel(
    first, grad_own, grad_other, gate_in, up_in, gate_own, gate_other, up_own, up_other, down_own,
    down_other, grad_gate_out, grad_up_out, out, total_own, total_other,
):
    step = pl.program_id(0)
    gate, up = (gate_in[...], up_in[...])
    grad_product = matmul_t(grad_own[...], down_own[...]) + matmul_t(
        grad_other[...], down_other[...]
    )
    cumulative = split_normal(gate)
    derivative = cumulative + gate * jnp.exp(-0.5 * gate * gate) * root_two_pi
    grad_gate = (grad_product * up * derivative).astype(jnp.bfloat16)
    grad_up = (grad_product * gate * cumulative).astype(jnp.bfloat16)
    grad_gate_out[...] = grad_gate
    grad_up_out[...] = grad_up
    add_to(step, total_own, matmul_t(grad_gate, gate_own[...]) + matmul_t(grad_up, up_own[...]))
    add_to(
        step, total_other, matmul_t(grad_gate, gate_other[...]) + matmul_t(grad_up, up_other[...])
    )

    @pl.when(step == pl.num_programs(0) - 1)
    def _():
        store_halves(out, total_own[...], total_other[...], first[0] == 1)


def hidden_back(first, grad_own, grad_other, gate, up, weights):
    rows, half = grad_own.shape
    depth = half
    specs, arrays = hidden_specs(weights, depth)
    piece = columns_at(rows, HIDDEN_BLOCK, 0)
    return grid_call(
        hidden_back_kernel,
        "hidden_back",
        (first,),
        (FF_PAD // HIDDEN_BLOCK,),
        [whole(grad_own), whole(grad_other), piece, piece, *specs],
        (piece, piece, pl.BlockSpec((rows, 2 * depth), lambda n, *_: (0, 0))),
        (
            jax.ShapeDtypeStruct((rows, FF_PAD), jnp.bfloat16),
            jax.ShapeDtypeStruct((rows, FF_PAD), jnp.bfloat16),
            jax.ShapeDtypeStruct((rows, 2 * depth), jnp.float32),
        ),
        [pltpu.VMEM((rows, depth), jnp.float32)] * 2,
        (grad_own, grad_other, gate, up, *arrays),
    )


def attention_input(rows_in, gain):
    normed, factor = norm_parts(rows_in)
    act_in = (normed * gain).astype(jnp.bfloat16)
    before = to_next(act_in[act_in.shape[0] - HALO :])
    after = to_previous(act_in[:HALO])
    return (normed, factor, act_in, jnp.concatenate([before, act_in, after], axis=0))


def layer_forward(rows_in, entry, gain_pair, weights, segs, on_first, first, later=(), ready=()):
    normed1, factor1, act_in, extended = entry
    qkv = qkv_of(*column_halves(extended, on_first), weights)
    mixed, log_total = attend(*segs, qkv, ready)
    mixed, *later = lax.optimization_barrier((mixed, *later))
    own, other = column_halves(mixed, on_first)
    middle = rows_in + matmul(own, weights["out"][0]) + matmul(other, weights["out"][1])
    normed2, factor2 = norm_parts(middle)
    act_mid = (normed2 * gain_pair[1]).astype(jnp.bfloat16)
    own, other = column_halves(act_mid, on_first)
    gate, up, product, output = hidden_forward(first, own, other, middle, weights)
    acts = (jnp.stack([act_in, mixed, act_mid]), product)
    got = tuple(swapped(act) for act in acts)
    kept = (normed1, factor1, qkv, log_total, normed2, factor2, gate, up, acts, got)
    return (output, kept, later)


def seq_sum(total):
    return lax.psum_scatter(total, "seq", scatter_dimension=0, tiled=True)


ROW_PIECE = FF // (SEQ_DEV * W_DEV)
ROW_GROUPS = PAD_ROWS // 16


def weight_grads(name, items, grads, total, product=None, gains=None, base=None):
    count, width = items[0][0].shape[1:]
    block = 256
    in_specs, args = ([], [])
    for acts, got, member, *_ in items:
        for array in (acts, got):
            in_specs.append(pl.BlockSpec((1, count, block), lambda n, m=member: (m, 0, n)))
            args.append(array)
    for pair in grads:
        in_specs += [whole(array) for array in pair]
        args += list(pair)
    scratch = [pltpu.VMEM((2 * count, pair[0].shape[1]), jnp.bfloat16) for pair in grads]
    if product is not None:
        in_specs += [whole(array) for array in product[:2]]
        args += list(product[:2])
        half = grads[product[2]][0].shape[1] - product[3]
        scratch += [
            pltpu.VMEM((FF_PAD, half), jnp.float32),
            pltpu.VMEM((width, ROW_GROUPS * half), jnp.bfloat16),
        ]
    if gains is not None:
        in_specs.append(rows_at(block, gains[0].shape[1]))
        args.append(gains[0])
    aliases = {}
    columns = total
    if base is not None:
        aliases = {len(args): 0}
        in_specs.append(pl.BlockSpec(memory_space=pl.ANY))
        args.append(base)
        columns = gains[1] + gains[0].shape[1]

    def kernel(*refs):
        act_refs = refs[: 2 * len(items)]
        grad_refs = refs[2 * len(items) : 2 * (len(items) + len(grads))]
        rest = refs[2 * (len(items) + len(grads)) : len(args)]
        out = refs[len(args)]
        rows = refs[len(args) + 1 :]
        step = pl.program_id(0)

        @pl.when(step == 0)
        def _():
            for k in range(len(grads)):
                rows[k][:count] = grad_refs[2 * k][...]
                rows[k][count:] = grad_refs[2 * k + 1][...]
            if product is not None:
                down, groups = rows[-2:]
                for at in range(0, FF_PAD, 896):
                    part = jnp.concatenate([r[:, at : at + 896] for r in rest[:2]], axis=0)
                    down[at : at + 896] = inner_rows(part, rows[product[2]][:, product[3] :])
                for piece in range(SEQ_DEV * W_DEV):
                    for group in range(ROW_GROUPS):
                        first_row = piece * ROW_PIECE + group * 16
                        groups[
                            16 * piece : 16 * piece + 16, group * half : (group + 1) * half
                        ] = down[first_row : first_row + 16].astype(jnp.bfloat16)

        for k, (_, _, _, which, at, size, place) in enumerate(items):
            acts = jnp.concatenate([act_refs[2 * k][0], act_refs[2 * k + 1][0]], axis=0)
            for part in range(0, size, 512):
                wide = min(512, size - part)
                out[:, place + part : place + part + wide] = inner_rows(
                    acts, rows[which][:, at + part : at + part + wide]
                ).astype(jnp.bfloat16)
        if product is not None:
            place = product[4]
            out[:, place : place + ROW_GROUPS * half] = rows[-1][
                pl.ds(pl.multiple_of(step * block, block), block)
            ]
        if gains is not None:
            out[:, gains[1] : gains[1] + gains[0].shape[1]] = rest[0][...]

    return grid_call(
        kernel,
        name,
        (),
        (width // block,),
        in_specs,
        rows_at(block, columns),
        jax.ShapeDtypeStruct((width, total), jnp.bfloat16),
        scratch,
        args,
        aliases,
    )


def core_halves(pairs, on_first):
    low, high = [jnp.concatenate([p[k] for p in pairs], axis=1) for k in range(2)]
    return (jnp.where(on_first, low, high), swapped(jnp.where(on_first, high, low)))


def layer_backward(grad_out, kept, gain_pair, weights, segs, on_first, first, ready_of):
    (normed1, factor1, qkv, log_total, normed2, factor2, gate, up, _, _) = kept
    rows, width = normed1.shape
    half = width // 2
    grad_branch = grad_out.astype(jnp.bfloat16)
    low, high = (grad_branch[:, :half], grad_branch[:, half:])
    branch_own, branch_other = (jnp.where(on_first, low, high), jnp.where(on_first, high, low))
    grad_gate, grad_up, grad_norm2 = hidden_back(
        first, branch_own, branch_other, gate, up, weights
    )
    hidden_pair = core_halves(((grad_gate, grad_up), (low, high)), on_first)
    gain_mid = jnp.sum(normed2 * grad_norm2, axis=0)
    grad_middle = grad_out + norm_back(grad_norm2 * gain_pair[1], normed2, factor2)
    grad_attn = grad_middle.astype(jnp.bfloat16)
    mine, theirs = [matmul_t(grad_attn, w) for w in weights["out"]]
    grad_mixed = from_halves(mine, theirs, on_first).astype(jnp.bfloat16)
    grad_query, grad_own, grad_before, grad_after = attend_back(
        *segs, qkv, log_total, grad_mixed, ready_of(hidden_pair)
    )
    from_previous = to_next(grad_after).astype(jnp.float32)
    from_next = to_previous(grad_before).astype(jnp.float32)
    grad_pairs = grad_own + jnp.concatenate([from_previous, from_next], axis=0)
    grad_qkv = jnp.concatenate([grad_query, grad_pairs.astype(jnp.bfloat16)], axis=1)
    attn_pair = core_halves(
        (
            (grad_qkv[:, : 3 * half], grad_qkv[:, 3 * half :]),
            (grad_attn[:, :half], grad_attn[:, half:]),
        ),
        on_first,
    )
    grad_norm1 = qkv_back(first, grad_qkv, weights)
    gain_first = jnp.sum(normed1 * grad_norm1, axis=0)
    grad_inputs = grad_middle + norm_back(grad_norm1 * gain_pair[0], normed1, factor1)
    gains = jnp.stack([gain_first, gain_mid])
    return (grad_inputs, hidden_pair, attn_pair, gains)


def summed_over_w(block, place):
    rows = block.shape[0] // W_DEV
    total = lax.dynamic_slice_in_dim(block, place * rows, rows).astype(jnp.float32)
    for step in range(1, W_DEV):
        part = lax.dynamic_slice_in_dim(block, lax.rem(place + step, W_DEV) * rows, rows)
        got = lax.ppermute(part, "wshard", [(j, (j + step) % W_DEV) for j in range(W_DEV)])
        total = total + got.astype(jnp.float32)
    return total


def summed_by_steps(block, seq_place, w_place):
    side = 4
    columns = block.shape[1]

    def phase(parts, axis, at, place, route):
        size = parts.shape[at]

        def part(step):
            return lax.dynamic_index_in_dim(parts, lax.rem(place + step, size), at, keepdims=False)

        total = part(0).astype(jnp.float32)
        for step in range(1, size):
            total = total + lax.ppermute(part(step), axis, route(step)).astype(jnp.float32)
        return total

    total = phase(
        block.reshape(SEQ_DEV, W_DEV, 16, columns),
        "wshard",
        1,
        w_place,
        lambda step: [(j, (j + step) % W_DEV) for j in range(W_DEV)],
    )
    total = phase(
        total.astype(jnp.bfloat16).reshape(side, side, 16, columns),
        "seq",
        1,
        lax.rem(seq_place, side),
        lambda step: [
            (side * y + x, side * y + (x + step) % side) for y in range(side) for x in range(side)
        ],
    )
    return phase(
        total.astype(jnp.bfloat16),
        "seq",
        0,
        seq_place // side,
        lambda step: [
            (side * y + x, side * ((y + step) % side) + x) for y in range(side) for x in range(side)
        ],
    )


def per_device(
    inputs, cotangent, segments, norm_gains, attend_in, attend_out, hidden_in, hidden_out
):
    on_first = lax.axis_index("section") == 0
    core = lax.axis_index("section")
    seq_place = lax.axis_index("seq")
    w_place = lax.axis_index("wshard")

    def by_core(first, second):
        return jnp.where(on_first, first, second)

    def sections(own, got):
        return (by_core(own, got), by_core(got, own))

    slice_rows = attend_in.shape[1] // (2 * SEQ_DEV)
    pad = jnp.zeros((slice_rows, FF_PAD - FF), jnp.bfloat16)
    width = inputs.shape[3]

    def row_slice(which):
        at = (which * SEQ_DEV + seq_place) * slice_rows
        hidden, qkv, out = [
            lax.dynamic_slice_in_dim(w[0], at, slice_rows)
            for w in (hidden_in, attend_in, attend_out)
        ]
        return jnp.concatenate([hidden[:, :FF], pad, hidden[:, FF:], pad, qkv, out], axis=1)

    def in_order(first, second):
        ends = (0, 2 * FF_PAD, 2 * FF_PAD + 3 * width, 2 * FF_PAD + 4 * width)
        return jnp.concatenate(
            [piece[:, a:b] for a, b in zip(ends, ends[1:]) for piece in (first, second)], axis=1
        )

    row_pieces = sections(row_slice(core), swapped(row_slice(1 - core)))
    hidden_width, qkv_width = (2 * FF_PAD, 3 * width)
    qkv_at = 2 * hidden_width
    out_at = qkv_at + 2 * qkv_width
    all_own = lax.all_gather(in_order(*row_pieces), ("wshard", "seq"), axis=0, tiled=True)
    half = hidden_out.shape[2] // 2
    low, high = (hidden_out[0, :, :half], hidden_out[0, :, half:])
    down_piece = jnp.concatenate(sections(by_core(low, high), swapped(by_core(high, low))), axis=1)
    w_up = [(j, (j + 1) % W_DEV) for j in range(W_DEV)]
    w_down = [(j, i) for i, j in w_up]
    below = lax.ppermute(down_piece, "wshard", w_up)
    above = lax.ppermute(down_piece, "wshard", w_down)
    far = (
        lax.ppermute(below[:, :half], "wshard", w_up),
        lax.ppermute(above[:, half:], "wshard", w_down),
    )
    gain_pairs = sections(norm_gains[0], swapped(norm_gains[0]))
    piece_rows = down_piece.shape[0]

    def down_of(section):
        columns = slice(section * half, (section + 1) * half)
        own = jnp.zeros((FF_PAD, half), jnp.bfloat16)
        for step, piece in (
            (0, down_piece[:, columns]),
            (1, above[:, columns]),
            (2, far[section]),
            (3, below[:, columns]),
        ):
            own = lax.dynamic_update_slice_in_dim(
                own, piece, lax.rem(w_place + step, W_DEV) * piece_rows, 0
            )
        return own

    rows_in = by_core(inputs[0, 0], inputs[1, 0])
    row_count = rows_in.shape[0]
    segment_row = by_core(segments[0, 0], segments[1, 0])
    padded = jnp.pad(segment_row, (HALO, HALO), constant_values=-1)
    first_row = seq_place * row_count
    segs = (
        lax.dynamic_slice_in_dim(segment_row, first_row, row_count)[:, None],
        lax.dynamic_slice_in_dim(padded, first_row, row_count + 2 * HALO)[None, :],
    )
    entry = attention_input(rows_in, gain_pairs[0][0])
    down_own = (down_of(0), down_of(1))
    all_own, down_own, down_other, entry, gain_pairs, segs = lax.optimization_barrier(
        (all_own, down_own, tuple(swapped(d) for d in down_own), entry, gain_pairs, segs)
    )
    first_qkv, all_own = lax.optimization_barrier(
        (swapped(all_own[:, qkv_at : qkv_at + qkv_width]), all_own)
    )
    first_out = swapped(all_own[:, out_at : out_at + width])
    first_hidden = swapped(all_own[:, :hidden_width])
    first_weights = {
        "qkv": ((all_own, qkv_at), (first_qkv, 0)),
        "gate": ((all_own, 0), (first_hidden, 0)),
        "up": ((all_own, FF_PAD), (first_hidden, FF_PAD)),
        "out": (all_own[:, out_at : out_at + width], first_out),
        "down": (down_own[0], down_other[0]),
    }

    def second_weights(all_late):
        all_other = swapped(all_late)
        return {
            "qkv": ((all_own, qkv_at + qkv_width), (all_other, qkv_at + qkv_width)),
            "gate": ((all_own, hidden_width), (all_other, hidden_width)),
            "up": ((all_own, hidden_width + FF_PAD), (all_other, hidden_width + FF_PAD)),
            "out": (all_own[:, out_at + width :], all_other[:, out_at + width :]),
            "down": (down_own[1], down_other[1]),
        }

    first = on_first.astype(jnp.int32)[None]
    middle, kept0, (all_late,) = layer_forward(
        rows_in, entry, gain_pairs[0], first_weights, segs, on_first, first,
        (all_own,), (first_hidden, first_out),
    )
    weights = (first_weights, second_weights(all_late))
    entry = attention_input(middle, gain_pairs[1][0])
    final, kept1, _ = layer_forward(
        middle, entry, gain_pairs[1], weights[1], segs, on_first, first
    )
    upstream = by_core(cotangent[0, 0], cotangent[1, 0])
    attn_cols, out_cols, down_cols = (qkv_width // 2, half, ROW_GROUPS * half)
    hidden_end = FF_PAD + down_cols
    gain_at = attn_cols + out_cols
    second_at = gain_at + 128
    hidden_at = second_at + attn_cols
    total = hidden_at + FF_PAD

    def attn_items(kept, which, at):
        acts, got = (kept[-2][0], kept[-1][0])
        return [
            (acts, got, 0, which, 0, attn_cols, at),
            (acts, got, 1, which, attn_cols, out_cols, at + attn_cols),
        ]

    def hidden_items(kept, which, at, down_at):
        acts, got = (kept[-2], kept[-1])
        return (
            [(acts[0], got[0], 2, which, 0, FF_PAD, at)],
            (acts[1], got[1], which, FF_PAD, down_at),
        )

    early_grads = []

    def make_early(hidden_pair):
        items, product = hidden_items(kept1, 0, 0, FF_PAD)
        early_grads.append(weight_grads("hidden_grads", items, [hidden_pair], hidden_end, product))
        return early_grads

    grads1, _, attn_pair1, gains1 = layer_backward(
        upstream, kept1, gain_pairs[1], weights[1], segs, on_first, first, make_early
    )
    early = seq_sum(early_grads[0])
    grads0, hidden_pair0, attn_pair0, gains0 = layer_backward(
        grads1, kept0, gain_pairs[0], weights[0], segs, on_first, first,
        lambda hidden_pair: (hidden_pair[1], *kept0[-1]),
    )
    items, product = hidden_items(kept0, 1, hidden_at, out_cols)
    qkv_item, out_item = attn_items(kept1, 0, 0)
    pairs = [attn_pair1, hidden_pair0]
    side = weight_grads("side_grads", [out_item[:-1] + (0,)], pairs, out_cols + down_cols, product)
    side_total = summed_by_steps(side, seq_place, w_place)
    base = weight_grads("joint_grads", [qkv_item[:-1] + (second_at,)] + items, pairs, total)
    gains = jnp.concatenate([gains0, gains1], axis=0)
    gains = jnp.pad(gains, ((0, 128 - gains.shape[0]), (0, 0))).T.astype(jnp.bfloat16)
    late = seq_sum(
        weight_grads(
            "attn_grads",
            attn_items(kept0, 0, 0),
            [attn_pair0],
            total,
            None,
            (gains, gain_at),
            base,
        )
    )

    def placed(first, second):
        mine, give = (by_core(first, second), by_core(second, first))
        got = swapped(give)
        return jnp.stack([by_core(mine, got), by_core(got, mine)])[None, :, None]

    section_outputs = placed(middle, final)
    section_input_grads = placed(grads0, grads1)

    early_total, late_total = (summed_over_w(early, w_place), summed_over_w(late, w_place))
    of_first = jnp.concatenate(
        [late_total[:, :second_at], late_total[:, hidden_at:], side_total[:, out_cols:]], axis=1
    )
    of_second = jnp.concatenate(
        [
            late_total[:, second_at:hidden_at],
            side_total[:, :out_cols],
            late_total[:, gain_at:second_at],
            early_total,
        ],
        axis=1,
    )
    mine, got = (by_core(of_first, of_second), swapped(by_core(of_second, of_first)))
    low, high = (by_core(mine, got), by_core(got, mine))
    qkv_rows = jnp.concatenate([low[:, :attn_cols], high[:, :attn_cols]], axis=1)
    attn_rows = jnp.concatenate([low[:, attn_cols:gain_at], high[:, attn_cols:gain_at]], axis=1)
    gain_part = (low + high)[:, gain_at:second_at]
    gain_rows = by_core(gain_part[:, :2], gain_part[:, 2:4]).T
    hidden_rows = jnp.concatenate(
        [low[:, second_at : second_at + FF], high[:, second_at : second_at + FF]], axis=1
    )
    down_total = jnp.concatenate(
        [
            jnp.concatenate([h[:, at : at + half] for h in (low, high)], axis=1)
            for at in range(second_at + FF_PAD, low.shape[1], half)
        ],
        axis=0,
    )[:ROW_PIECE]
    return (
        section_outputs,
        section_input_grads,
        qkv_rows[None],
        attn_rows[None],
        hidden_rows[None],
        down_total[None],
        gain_rows[None],
    )


def solution(mesh):
    placed = (
        P(None, "wshard", "seq", None),
        P(None, "wshard", "seq", None),
        P(None, "wshard", None),
        P("section", None, None),
        P("section", "wshard", None),
        P("section", "wshard", None),
        P("section", "wshard", None),
        P("section", "wshard", None),
    )
    return jax.shard_map(
        per_device,
        mesh=mesh,
        in_specs=placed,
        out_specs=(
            P("section", None, "wshard", "seq", None),
            P("section", None, "wshard", "seq", None),
            P("section", ("seq", "wshard"), None),
            P("section", ("seq", "wshard"), None),
            P("section", ("seq", "wshard"), None),
            P("section", ("seq", "wshard"), None),
            P("section", None, ("seq", "wshard")),
        ),
        check_vma=False,
    )
```

```python
import math

import jax
import jax.numpy as jnp
from jax import lax
from jax.experimental import pallas as pl
from jax.experimental.pallas import tpu as pltpu
from jax.sharding import PartitionSpec as P

HEADS = 16
HEAD_DIM = 64
FF = 2624
HALO = 64
FF_PAD = 2688
SEQ_DEV = 16
W_DEV = 4
PAD_ROWS = 48
HIDDEN_BLOCK = 896
QKV_BLOCK = 768

norm_eps = 1e-05
root_half = 1.0 / math.sqrt(2.0)
root_two_pi = 1.0 / math.sqrt(2.0 * math.pi)
score_scale = 1.0 / math.sqrt(HEAD_DIM)

SWAP = [(0, 1), (1, 0)]


def swapped(array):
    return lax.ppermute(array, "section", SWAP)


def norm_parts(rows_in):
    centred = rows_in - jnp.mean(rows_in, axis=1, keepdims=True)
    factor = lax.rsqrt(jnp.mean(centred * centred, axis=1, keepdims=True) + norm_eps)
    return (centred * factor, factor)


def norm_back(grad_norm, normed, factor):
    inner = jnp.mean(grad_norm, axis=1, keepdims=True)
    along = jnp.mean(grad_norm * normed, axis=1, keepdims=True)
    return factor * (grad_norm - inner - normed * along)


def matmul(left, right):
    return jnp.dot(left, right, preferred_element_type=jnp.float32)


def matmul_t(left, right):
    return lax.dot_general(
        left, right, (((1,), (1,)), ((), ())), preferred_element_type=jnp.float32
    )


def inner_rows(left, right):
    return lax.dot_general(
        left, right, (((0,), (0,)), ((), ())), preferred_element_type=jnp.float32
    )


def column_halves(array, on_first):
    even = jnp.concatenate([array[:, 256 * k : 256 * k + 128] for k in range(4)], axis=1)
    odd = jnp.concatenate([array[:, 256 * k + 128 : 256 * k + 256] for k in range(4)], axis=1)
    return (jnp.where(on_first, even, odd), jnp.where(on_first, odd, even))


def from_halves(own, other, on_first):
    even = jnp.where(on_first, own, other)
    odd = jnp.where(on_first, other, own)
    parts = []
    for k in range(4):
        parts += [even[:, 128 * k : 128 * k + 128], odd[:, 128 * k : 128 * k + 128]]
    return jnp.concatenate(parts, axis=1)


def window_allowed(query_seg, key_seg):
    rows, keys = (query_seg.shape[0], key_seg.shape[1])
    offset = lax.broadcasted_iota(jnp.int32, (rows, keys), 1) - lax.broadcasted_iota(
        jnp.int32, (rows, keys), 0
    )
    return (offset >= 0) & (offset <= 2 * HALO) & (query_seg == key_seg)


def attend_kernel(query_seg, key_seg, qkv, mixed, log_total):
    allowed = window_allowed(query_seg[...], key_seg[...])
    width = HEADS * HEAD_DIM
    rows = mixed.shape[0]
    for head in range(HEADS):
        at = head * HEAD_DIM
        q = qkv[HALO : HALO + rows, at : at + HEAD_DIM]
        k = qkv[:, width + at : width + at + HEAD_DIM]
        v = qkv[:, 2 * width + at : 2 * width + at + HEAD_DIM]
        scores = jnp.where(allowed, matmul_t(q, k) * score_scale, -1e30)
        row_max = jnp.max(scores, axis=1, keepdims=True)
        exponent = jnp.exp(scores - row_max)
        total = jnp.sum(exponent, axis=1, keepdims=True)
        probs = (exponent * (1.0 / total)).astype(jnp.bfloat16)
        mixed[:, at : at + HEAD_DIM] = matmul(probs, v).astype(jnp.bfloat16)
        log_total[:, at : at + HEAD_DIM] = jnp.broadcast_to(
            row_max + jnp.log(total), (rows, HEAD_DIM)
        )


def attend_back_kernel(query_seg, key_seg, qkv, log_total, grad_mixed, *refs):
    grad_query, own, before, after = refs[-4:]
    allowed = window_allowed(query_seg[...], key_seg[...])
    width = HEADS * HEAD_DIM
    rows = grad_mixed.shape[0]
    for head in range(HEADS):
        at = head * HEAD_DIM
        q = qkv[HALO : HALO + rows, at : at + HEAD_DIM]
        k = qkv[:, width + at : width + at + HEAD_DIM]
        v = qkv[:, 2 * width + at : 2 * width + at + HEAD_DIM]
        grad = grad_mixed[:, at : at + HEAD_DIM]
        scores = jnp.where(allowed, matmul_t(q, k) * score_scale, -1e30)
        probs = jnp.exp(scores - log_total[:, at : at + 1])
        grad_probs = matmul_t(grad, v)
        inner = jnp.sum(probs * grad_probs, axis=1, keepdims=True)
        grad_scores = (probs * (grad_probs - inner)).astype(jnp.bfloat16)
        grad_query[:, at : at + HEAD_DIM] = (matmul(grad_scores, k) * score_scale).astype(
            jnp.bfloat16
        )
        for place, piece in (
            (at, inner_rows(grad_scores, q) * score_scale),
            (width + at, inner_rows(probs.astype(jnp.bfloat16), grad)),
        ):
            columns = slice(place, place + HEAD_DIM)
            before[:, columns] = piece[:HALO].astype(jnp.bfloat16)
            own[:, columns] = piece[HALO : HALO + rows]
            after[:, columns] = piece[HALO + rows :].astype(jnp.bfloat16)


params = pltpu.CompilerParams(vmem_limit_bytes=40 * 1024 * 1024)


def attend(query_seg, key_seg, qkv):
    rows, width = (query_seg.shape[0], HEADS * HEAD_DIM)
    return pl.pallas_call(
        attend_kernel,
        out_shape=(
            jax.ShapeDtypeStruct((rows, width), jnp.bfloat16),
            jax.ShapeDtypeStruct((rows, width), jnp.float32),
        ),
        compiler_params=params,
        name="attend",
    )(query_seg, key_seg, qkv)


def attend_back(query_seg, key_seg, qkv, log_total, grad_mixed, ready):
    rows, width = (query_seg.shape[0], HEADS * HEAD_DIM)
    return pl.pallas_call(
        attend_back_kernel,
        out_shape=(
            jax.ShapeDtypeStruct((rows, width), jnp.bfloat16),
            jax.ShapeDtypeStruct((rows, 2 * width), jnp.float32),
            jax.ShapeDtypeStruct((HALO, 2 * width), jnp.bfloat16),
            jax.ShapeDtypeStruct((HALO, 2 * width), jnp.bfloat16),
        ),
        in_specs=[pl.BlockSpec(memory_space=pltpu.VMEM)] * 5
        + [pl.BlockSpec(memory_space=pl.ANY)] * len(ready),
        compiler_params=params,
        name="attend_back",
    )(query_seg, key_seg, qkv, log_total, grad_mixed, *ready)


def to_next(array):
    return lax.ppermute(array, "seq", [(i, i + 1) for i in range(SEQ_DEV - 1)])


def to_previous(array):
    return lax.ppermute(array, "seq", [(i + 1, i) for i in range(SEQ_DEV - 1)])


def split_normal(gate):
    cumulative = 0.5 * (1.0 + lax.erf(gate * root_half))
    return cumulative


def grid_call(kernel, name, scalars, grid, in_specs, out_specs, out_shape, scratch, args, aliases=None):
    return pl.pallas_call(
        kernel,
        grid_spec=pltpu.PrefetchScalarGridSpec(
            num_scalar_prefetch=len(scalars),
            grid=grid,
            in_specs=in_specs,
            out_specs=out_specs,
            scratch_shapes=scratch,
        ),
        out_shape=out_shape,
        input_output_aliases=aliases or {},
        compiler_params=params,
        name=name,
    )(*scalars, *args)


def whole(array):
    return pl.BlockSpec(array.shape, lambda n, *_: (0,) * array.ndim)


def columns_at(rows, block, first):
    return pl.BlockSpec((rows, block), lambda n, *_: (0, first + n))


def rows_at(block, columns):
    return pl.BlockSpec((block, columns), lambda n, *_: (n, 0))


def add_to(step, total, value):
    @pl.when(step == 0)
    def _():
        total[...] = value

    @pl.when(step > 0)
    def _():
        total[...] += value


def store_halves(out, own, other, on_first):
    for k in range(4):
        block = slice(128 * k, 128 * k + 128)
        out[:, 256 * k : 256 * k + 128] = jnp.where(on_first, own[:, block], other[:, block])
        out[:, 256 * k + 128 : 256 * k + 256] = jnp.where(on_first, other[:, block], own[:, block])


def qkv_kernel(own, other, weight_own, weight_other, out):
    out[...] = (
        matmul(own[...], weight_own[...]) + matmul(other[...], weight_other[...])
    ).astype(jnp.bfloat16)


def qkv_of(own, other, weights):
    (w_own, at_own), (w_other, at_other) = weights["qkv"]
    width = 3 * HEADS * HEAD_DIM
    depth = own.shape[1]
    return grid_call(
        qkv_kernel,
        "qkv",
        (),
        (width // QKV_BLOCK,),
        [
            whole(own),
            whole(other),
            columns_at(depth, QKV_BLOCK, at_own // QKV_BLOCK),
            columns_at(depth, QKV_BLOCK, at_other // QKV_BLOCK),
        ],
        columns_at(own.shape[0], QKV_BLOCK, 0),
        jax.ShapeDtypeStruct((own.shape[0], width), jnp.bfloat16),
        [],
        (own, other, w_own, w_other),
    )


def qkv_back_kernel(first, grad, weight_own, weight_other, out, total_own, total_other):
    step = pl.program_id(0)
    add_to(step, total_own, matmul_t(grad[...], weight_own[...]))
    add_to(step, total_other, matmul_t(grad[...], weight_other[...]))

    @pl.when(step == pl.num_programs(0) - 1)
    def _():
        store_halves(out, total_own[...], total_other[...], first[0] == 1)


def qkv_back(first, grad, weights):
    (w_own, at_own), (w_other, at_other) = weights["qkv"]
    rows, width = grad.shape
    depth = w_own.shape[0]
    return grid_call(
        qkv_back_kernel,
        "qkv_back",
        (first,),
        (width // QKV_BLOCK,),
        [
            columns_at(rows, QKV_BLOCK, 0),
            columns_at(depth, QKV_BLOCK, at_own // QKV_BLOCK),
            columns_at(depth, QKV_BLOCK, at_other // QKV_BLOCK),
        ],
        pl.BlockSpec((rows, 2 * depth), lambda n, *_: (0, 0)),
        jax.ShapeDtypeStruct((rows, 2 * depth), jnp.float32),
        [pltpu.VMEM((rows, depth), jnp.float32)] * 2,
        (grad, w_own, w_other),
    )


def hidden_kernel(
    first, own, other, gate_own, gate_other, up_own, up_other, down_own, down_other, middle,
    gate_out, up_out, product_out, out, total_own, total_other,
):
    step = pl.program_id(0)
    gate = matmul(own[...], gate_own[...]) + matmul(other[...], gate_other[...])
    up = matmul(own[...], up_own[...]) + matmul(other[...], up_other[...])
    product = (gate * split_normal(gate) * up).astype(jnp.bfloat16)
    gate_out[...] = gate
    up_out[...] = up
    product_out[...] = product
    add_to(step, total_own, matmul(product, down_own[...]))
    add_to(step, total_other, matmul(product, down_other[...]))

    @pl.when(step == pl.num_programs(0) - 1)
    def _():
        half = total_own.shape[1]
        mine, theirs, on_first = (total_own[...], total_other[...], first[0] == 1)
        out[:, :half] = middle[:, :half] + jnp.where(on_first, mine, theirs)
        out[:, half:] = middle[:, half:] + jnp.where(on_first, theirs, mine)


def hidden_specs(weights, depth):
    specs, arrays = ([], [])
    for part in ("gate", "up"):
        for array, at in weights[part]:
            specs.append(columns_at(depth, HIDDEN_BLOCK, at // HIDDEN_BLOCK))
            arrays.append(array)
    for array in weights["down"]:
        specs.append(rows_at(HIDDEN_BLOCK, array.shape[1]))
        arrays.append(array)
    return (specs, arrays)


def hidden_forward(first, own, other, middle, weights):
    rows, depth = own.shape
    width = middle.shape[1]
    specs, arrays = hidden_specs(weights, depth)
    piece = columns_at(rows, HIDDEN_BLOCK, 0)
    return grid_call(
        hidden_kernel,
        "hidden",
        (first,),
        (FF_PAD // HIDDEN_BLOCK,),
        [whole(own), whole(other), *specs, whole(middle)],
        (piece, piece, piece, whole(middle)),
        (
            jax.ShapeDtypeStruct((rows, FF_PAD), jnp.float32),
            jax.ShapeDtypeStruct((rows, FF_PAD), jnp.float32),
            jax.ShapeDtypeStruct((rows, FF_PAD), jnp.bfloat16),
            jax.ShapeDtypeStruct((rows, width), jnp.float32),
        ),
        [pltpu.VMEM((rows, width // 2), jnp.float32)] * 2,
        (own, other, *arrays, middle),
    )


def hidden_back_kernel(
    first, grad_own, grad_other, gate_in, up_in, gate_own, gate_other, up_own, up_other, down_own,
    down_other, grad_gate_out, grad_up_out, out, total_own, total_other,
):
    step = pl.program_id(0)
    gate, up = (gate_in[...], up_in[...])
    grad_product = matmul_t(grad_own[...], down_own[...]) + matmul_t(
        grad_other[...], down_other[...]
    )
    cumulative = split_normal(gate)
    derivative = cumulative + gate * jnp.exp(-0.5 * gate * gate) * root_two_pi
    grad_gate = (grad_product * up * derivative).astype(jnp.bfloat16)
    grad_up = (grad_product * gate * cumulative).astype(jnp.bfloat16)
    grad_gate_out[...] = grad_gate
    grad_up_out[...] = grad_up
    add_to(step, total_own, matmul_t(grad_gate, gate_own[...]) + matmul_t(grad_up, up_own[...]))
    add_to(
        step, total_other, matmul_t(grad_gate, gate_other[...]) + matmul_t(grad_up, up_other[...])
    )

    @pl.when(step == pl.num_programs(0) - 1)
    def _():
        store_halves(out, total_own[...], total_other[...], first[0] == 1)


def hidden_back(first, grad_own, grad_other, gate, up, weights):
    rows, half = grad_own.shape
    depth = half
    specs, arrays = hidden_specs(weights, depth)
    piece = columns_at(rows, HIDDEN_BLOCK, 0)
    return grid_call(
        hidden_back_kernel,
        "hidden_back",
        (first,),
        (FF_PAD // HIDDEN_BLOCK,),
        [whole(grad_own), whole(grad_other), piece, piece, *specs],
        (piece, piece, pl.BlockSpec((rows, 2 * depth), lambda n, *_: (0, 0))),
        (
            jax.ShapeDtypeStruct((rows, FF_PAD), jnp.bfloat16),
            jax.ShapeDtypeStruct((rows, FF_PAD), jnp.bfloat16),
            jax.ShapeDtypeStruct((rows, 2 * depth), jnp.float32),
        ),
        [pltpu.VMEM((rows, depth), jnp.float32)] * 2,
        (grad_own, grad_other, gate, up, *arrays),
    )


def attention_input(rows_in, gain):
    normed, factor = norm_parts(rows_in)
    act_in = (normed * gain).astype(jnp.bfloat16)
    before = to_next(act_in[act_in.shape[0] - HALO :])
    after = to_previous(act_in[:HALO])
    return (normed, factor, act_in, jnp.concatenate([before, act_in, after], axis=0))


def layer_forward(rows_in, entry, gain_pair, weights, segs, on_first, first):
    normed1, factor1, act_in, extended = entry
    qkv = qkv_of(*column_halves(extended, on_first), weights)
    mixed, log_total = attend(*segs, qkv)
    own, other = column_halves(mixed, on_first)
    middle = rows_in + matmul(own, weights["out"][0]) + matmul(other, weights["out"][1])
    normed2, factor2 = norm_parts(middle)
    act_mid = (normed2 * gain_pair[1]).astype(jnp.bfloat16)
    own, other = column_halves(act_mid, on_first)
    gate, up, product, output = hidden_forward(first, own, other, middle, weights)
    acts = (jnp.stack([act_in, mixed, act_mid]), product)
    got = tuple(swapped(act) for act in acts)
    kept = (normed1, factor1, qkv, log_total, normed2, factor2, gate, up, acts, got)
    return (output, kept)


def seq_sum(total):
    return lax.psum_scatter(total, "seq", scatter_dimension=0, tiled=True)


ROW_PIECE = FF // (SEQ_DEV * W_DEV)
ROW_GROUPS = PAD_ROWS // 16


def weight_grads(name, items, grads, total, product=None, gains=None, base=None):
    count, width = items[0][0].shape[1:]
    block = 256
    in_specs, args = ([], [])
    for acts, got, member, *_ in items:
        for array in (acts, got):
            in_specs.append(pl.BlockSpec((1, count, block), lambda n, m=member: (m, 0, n)))
            args.append(array)
    for pair in grads:
        in_specs += [whole(array) for array in pair]
        args += list(pair)
    scratch = [pltpu.VMEM((2 * count, pair[0].shape[1]), jnp.bfloat16) for pair in grads]
    if product is not None:
        in_specs += [whole(array) for array in product[:2]]
        args += list(product[:2])
        half = grads[product[2]][0].shape[1] - product[3]
        scratch += [
            pltpu.VMEM((FF_PAD, half), jnp.float32),
            pltpu.VMEM((width, ROW_GROUPS * half), jnp.bfloat16),
        ]
    if gains is not None:
        in_specs.append(rows_at(block, gains[0].shape[1]))
        args.append(gains[0])
    aliases = {}
    columns = total
    if base is not None:
        aliases = {len(args): 0}
        in_specs.append(pl.BlockSpec(memory_space=pl.ANY))
        args.append(base)
        columns = gains[1] + gains[0].shape[1]

    def kernel(*refs):
        act_refs = refs[: 2 * len(items)]
        grad_refs = refs[2 * len(items) : 2 * (len(items) + len(grads))]
        rest = refs[2 * (len(items) + len(grads)) : len(args)]
        out = refs[len(args)]
        rows = refs[len(args) + 1 :]
        step = pl.program_id(0)

        @pl.when(step == 0)
        def _():
            for k in range(len(grads)):
                rows[k][:count] = grad_refs[2 * k][...]
                rows[k][count:] = grad_refs[2 * k + 1][...]
            if product is not None:
                down, groups = rows[-2:]
                for at in range(0, FF_PAD, 896):
                    part = jnp.concatenate([r[:, at : at + 896] for r in rest[:2]], axis=0)
                    down[at : at + 896] = inner_rows(part, rows[product[2]][:, product[3] :])
                for piece in range(SEQ_DEV * W_DEV):
                    for group in range(ROW_GROUPS):
                        first_row = piece * ROW_PIECE + group * 16
                        groups[
                            16 * piece : 16 * piece + 16, group * half : (group + 1) * half
                        ] = down[first_row : first_row + 16].astype(jnp.bfloat16)

        for k, (_, _, _, which, at, size, place) in enumerate(items):
            acts = jnp.concatenate([act_refs[2 * k][0], act_refs[2 * k + 1][0]], axis=0)
            for part in range(0, size, 512):
                wide = min(512, size - part)
                out[:, place + part : place + part + wide] = inner_rows(
                    acts, rows[which][:, at + part : at + part + wide]
                ).astype(jnp.bfloat16)
        if product is not None:
            place = product[4]
            out[:, place : place + ROW_GROUPS * half] = rows[-1][
                pl.ds(pl.multiple_of(step * block, block), block)
            ]
        if gains is not None:
            out[:, gains[1] : gains[1] + gains[0].shape[1]] = rest[0][...]

    return grid_call(
        kernel,
        name,
        (),
        (width // block,),
        in_specs,
        rows_at(block, columns),
        jax.ShapeDtypeStruct((width, total), jnp.bfloat16),
        scratch,
        args,
        aliases,
    )


def core_halves(pairs, on_first):
    low, high = [jnp.concatenate([p[k] for p in pairs], axis=1) for k in range(2)]
    return (jnp.where(on_first, low, high), swapped(jnp.where(on_first, high, low)))


def layer_backward(grad_out, kept, gain_pair, weights, segs, on_first, first, ready_of):
    (normed1, factor1, qkv, log_total, normed2, factor2, gate, up, _, _) = kept
    rows, width = normed1.shape
    half = width // 2
    grad_branch = grad_out.astype(jnp.bfloat16)
    low, high = (grad_branch[:, :half], grad_branch[:, half:])
    branch_own, branch_other = (jnp.where(on_first, low, high), jnp.where(on_first, high, low))
    grad_gate, grad_up, grad_norm2 = hidden_back(
        first, branch_own, branch_other, gate, up, weights
    )
    hidden_pair = core_halves(((grad_gate, grad_up), (low, high)), on_first)
    gain_mid = jnp.sum(normed2 * grad_norm2, axis=0)
    grad_middle = grad_out + norm_back(grad_norm2 * gain_pair[1], normed2, factor2)
    grad_attn = grad_middle.astype(jnp.bfloat16)
    mine, theirs = [matmul_t(grad_attn, w) for w in weights["out"]]
    grad_mixed = from_halves(mine, theirs, on_first).astype(jnp.bfloat16)
    grad_query, grad_own, grad_before, grad_after = attend_back(
        *segs, qkv, log_total, grad_mixed, ready_of(hidden_pair)
    )
    from_previous = to_next(grad_after).astype(jnp.float32)
    from_next = to_previous(grad_before).astype(jnp.float32)
    grad_pairs = grad_own + jnp.concatenate([from_previous, from_next], axis=0)
    grad_qkv = jnp.concatenate([grad_query, grad_pairs.astype(jnp.bfloat16)], axis=1)
    attn_pair = core_halves(
        (
            (grad_qkv[:, : 3 * half], grad_qkv[:, 3 * half :]),
            (grad_attn[:, :half], grad_attn[:, half:]),
        ),
        on_first,
    )
    grad_norm1 = qkv_back(first, grad_qkv, weights)
    gain_first = jnp.sum(normed1 * grad_norm1, axis=0)
    grad_inputs = grad_middle + norm_back(grad_norm1 * gain_pair[0], normed1, factor1)
    gains = jnp.stack([gain_first, gain_mid])
    return (grad_inputs, hidden_pair, attn_pair, gains)


def summed_over_w(block, place):
    rows = block.shape[0] // W_DEV
    total = lax.dynamic_slice_in_dim(block, place * rows, rows).astype(jnp.float32)
    for step in range(1, W_DEV):
        part = lax.dynamic_slice_in_dim(block, lax.rem(place + step, W_DEV) * rows, rows)
        got = lax.ppermute(part, "wshard", [(j, (j + step) % W_DEV) for j in range(W_DEV)])
        total = total + got.astype(jnp.float32)
    return total


def summed_by_steps(block, seq_place, w_place):
    side = 4
    columns = block.shape[1]

    def phase(parts, axis, at, place, route):
        size = parts.shape[at]

        def part(step):
            return lax.dynamic_index_in_dim(parts, lax.rem(place + step, size), at, keepdims=False)

        total = part(0).astype(jnp.float32)
        for step in range(1, size):
            total = total + lax.ppermute(part(step), axis, route(step)).astype(jnp.float32)
        return total

    total = phase(
        block.reshape(SEQ_DEV, W_DEV, 16, columns),
        "wshard",
        1,
        w_place,
        lambda step: [(j, (j + step) % W_DEV) for j in range(W_DEV)],
    )
    total = phase(
        total.astype(jnp.bfloat16).reshape(side, side, 16, columns),
        "seq",
        1,
        lax.rem(seq_place, side),
        lambda step: [
            (side * y + x, side * y + (x + step) % side) for y in range(side) for x in range(side)
        ],
    )
    return phase(
        total.astype(jnp.bfloat16),
        "seq",
        0,
        seq_place // side,
        lambda step: [
            (side * y + x, side * ((y + step) % side) + x) for y in range(side) for x in range(side)
        ],
    )


def per_device(
    inputs, cotangent, segments, norm_gains, attend_in, attend_out, hidden_in, hidden_out
):
    on_first = lax.axis_index("section") == 0
    core = lax.axis_index("section")
    seq_place = lax.axis_index("seq")
    w_place = lax.axis_index("wshard")

    def by_core(first, second):
        return jnp.where(on_first, first, second)

    def sections(own, got):
        return (by_core(own, got), by_core(got, own))

    slice_rows = attend_in.shape[1] // (2 * SEQ_DEV)
    pad = jnp.zeros((slice_rows, FF_PAD - FF), jnp.bfloat16)
    width = inputs.shape[3]

    def row_slice(which):
        at = (which * SEQ_DEV + seq_place) * slice_rows
        hidden, qkv, out = [
            lax.dynamic_slice_in_dim(w[0], at, slice_rows)
            for w in (hidden_in, attend_in, attend_out)
        ]
        return jnp.concatenate([hidden[:, :FF], pad, hidden[:, FF:], pad, qkv, out], axis=1)

    row_pieces = sections(row_slice(core), swapped(row_slice(1 - core)))
    hidden_width, qkv_width = (2 * FF_PAD, 3 * width)
    out_at = hidden_width + qkv_width

    def gathered(piece):
        return lax.all_gather(piece, ("wshard", "seq"), axis=0, tiled=True)

    first_own = gathered(row_pieces[0])
    half = hidden_out.shape[2] // 2
    low, high = (hidden_out[0, :, :half], hidden_out[0, :, half:])
    down_pieces = sections(by_core(low, high), swapped(by_core(high, low)))
    w_up = [(j, (j + 1) % W_DEV) for j in range(W_DEV)]
    w_down = [(j, i) for i, j in w_up]
    gain_pairs = sections(norm_gains[0], swapped(norm_gains[0]))

    def neighbours(piece):
        return (lax.ppermute(piece, "wshard", w_up), lax.ppermute(piece, "wshard", w_down))

    def down_of(piece, below, above):
        far = jnp.concatenate(
            [
                lax.ppermute(below[:, : half // 2], "wshard", w_up),
                lax.ppermute(above[:, half // 2 :], "wshard", w_down),
            ],
            axis=1,
        )
        own = jnp.zeros((FF_PAD, half), jnp.bfloat16)
        for step, part in enumerate((piece, above, far, below)):
            own = lax.dynamic_update_slice_in_dim(
                own, part, lax.rem(w_place + step, W_DEV) * piece.shape[0], 0
            )
        return (own, swapped(own))

    rows_in = by_core(inputs[0, 0], inputs[1, 0])
    row_count = rows_in.shape[0]
    segment_row = by_core(segments[0, 0], segments[1, 0])
    padded = jnp.pad(segment_row, (HALO, HALO), constant_values=-1)
    first_row = seq_place * row_count
    segs = (
        lax.dynamic_slice_in_dim(segment_row, first_row, row_count)[:, None],
        lax.dynamic_slice_in_dim(padded, first_row, row_count + 2 * HALO)[None, :],
    )
    entry = attention_input(rows_in, gain_pairs[0][0])
    row_piece, entry = lax.optimization_barrier((row_pieces[1], entry))
    second_own = gathered(row_piece)
    first_own, down_piece, first_down, entry, gain_pairs, segs = lax.optimization_barrier(
        (first_own, down_pieces[1], down_of(down_pieces[0], *neighbours(down_pieces[0])), entry, gain_pairs, segs)
    )
    near = neighbours(down_piece)

    def weights_of(own, other, qkv_other, out_other, down):
        return {
            "qkv": ((own, hidden_width), qkv_other),
            "gate": ((own, 0), (other, 0)),
            "up": ((own, FF_PAD), (other, FF_PAD)),
            "out": (own[:, out_at:], out_other),
            "down": down,
        }

    first = on_first.astype(jnp.int32)[None]
    other = swapped(first_own)
    first_weights = weights_of(
        first_own, other, (other, hidden_width), other[:, out_at:], first_down
    )
    middle, kept0 = layer_forward(
        rows_in, entry, gain_pairs[0], first_weights, segs, on_first, first
    )
    middle, near = lax.optimization_barrier((middle, near))
    second_own, second_down, entry = lax.optimization_barrier(
        (
            second_own, down_of(down_piece, *near), attention_input(middle, gain_pairs[1][0]),
        )
    )
    out_other = swapped(second_own[:, out_at:])
    qkv_other, second_own = lax.optimization_barrier(
        (swapped(second_own[:, hidden_width:out_at]), second_own)
    )
    weights = (
        first_weights,
        weights_of(second_own, swapped(second_own), (qkv_other, 0), out_other, second_down),
    )
    final, kept1 = layer_forward(middle, entry, gain_pairs[1], weights[1], segs, on_first, first)
    upstream = by_core(cotangent[0, 0], cotangent[1, 0])
    attn_cols, out_cols, down_cols = (qkv_width // 2, half, ROW_GROUPS * half)
    hidden_end = FF_PAD + down_cols
    gain_at = attn_cols + out_cols
    second_at = gain_at + 128
    hidden_at = second_at + attn_cols
    total = hidden_at + FF_PAD

    def attn_items(kept, which, at):
        acts, got = (kept[-2][0], kept[-1][0])
        return [
            (acts, got, 0, which, 0, attn_cols, at),
            (acts, got, 1, which, attn_cols, out_cols, at + attn_cols),
        ]

    def hidden_items(kept, which, at, down_at):
        acts, got = (kept[-2], kept[-1])
        return (
            [(acts[0], got[0], 2, which, 0, FF_PAD, at)],
            (acts[1], got[1], which, FF_PAD, down_at),
        )

    early_grads = []

    def make_early(hidden_pair):
        items, product = hidden_items(kept1, 0, 0, FF_PAD)
        early_grads.append(weight_grads("hidden_grads", items, [hidden_pair], hidden_end, product))
        return early_grads

    grads1, _, attn_pair1, gains1 = layer_backward(
        upstream, kept1, gain_pairs[1], weights[1], segs, on_first, first, make_early
    )
    early = seq_sum(early_grads[0])
    grads0, hidden_pair0, attn_pair0, gains0 = layer_backward(
        grads1, kept0, gain_pairs[0], weights[0], segs, on_first, first,
        lambda hidden_pair: (hidden_pair[1], *kept0[-1]),
    )
    items, product = hidden_items(kept0, 1, hidden_at, out_cols)
    qkv_item, out_item = attn_items(kept1, 0, 0)
    pairs = [attn_pair1, hidden_pair0]
    side = weight_grads("side_grads", [out_item[:-1] + (0,)], pairs, out_cols + down_cols, product)
    side_total = summed_by_steps(side, seq_place, w_place)
    base = weight_grads("joint_grads", [qkv_item[:-1] + (second_at,)] + items, pairs, total)
    gains = jnp.concatenate([gains0, gains1], axis=0)
    gains = jnp.pad(gains, ((0, 128 - gains.shape[0]), (0, 0))).T.astype(jnp.bfloat16)
    late = seq_sum(
        weight_grads(
            "attn_grads",
            attn_items(kept0, 0, 0),
            [attn_pair0],
            total,
            None,
            (gains, gain_at),
            base,
        )
    )

    def placed(first, second):
        mine, give = (by_core(first, second), by_core(second, first))
        got = swapped(give)
        return jnp.stack([by_core(mine, got), by_core(got, mine)])[None, :, None]

    section_outputs = placed(middle, final)
    section_input_grads = placed(grads0, grads1)

    early_total, late_total = (summed_over_w(early, w_place), summed_over_w(late, w_place))
    of_first = jnp.concatenate(
        [late_total[:, :second_at], late_total[:, hidden_at:], side_total[:, out_cols:]], axis=1
    )
    of_second = jnp.concatenate(
        [
            late_total[:, second_at:hidden_at],
            side_total[:, :out_cols],
            late_total[:, gain_at:second_at],
            early_total,
        ],
        axis=1,
    )
    mine, got = (by_core(of_first, of_second), swapped(by_core(of_second, of_first)))
    low, high = (by_core(mine, got), by_core(got, mine))
    qkv_rows = jnp.concatenate([low[:, :attn_cols], high[:, :attn_cols]], axis=1)
    attn_rows = jnp.concatenate([low[:, attn_cols:gain_at], high[:, attn_cols:gain_at]], axis=1)
    gain_part = (low + high)[:, gain_at:second_at]
    gain_rows = by_core(gain_part[:, :2], gain_part[:, 2:4]).T
    hidden_rows = jnp.concatenate(
        [low[:, second_at : second_at + FF], high[:, second_at : second_at + FF]], axis=1
    )
    down_total = jnp.concatenate(
        [
            jnp.concatenate([h[:, at : at + half] for h in (low, high)], axis=1)
            for at in range(second_at + FF_PAD, low.shape[1], half)
        ],
        axis=0,
    )[:ROW_PIECE]
    return (
        section_outputs,
        section_input_grads,
        qkv_rows[None],
        attn_rows[None],
        hidden_rows[None],
        down_total[None],
        gain_rows[None],
    )


def solution(mesh):
    placed = (
        P(None, "wshard", "seq", None),
        P(None, "wshard", "seq", None),
        P(None, "wshard", None),
        P("section", None, None),
        P("section", "wshard", None),
        P("section", "wshard", None),
        P("section", "wshard", None),
        P("section", "wshard", None),
    )
    return jax.shard_map(
        per_device,
        mesh=mesh,
        in_specs=placed,
        out_specs=(
            P("section", None, "wshard", "seq", None),
            P("section", None, "wshard", "seq", None),
            P("section", ("seq", "wshard"), None),
            P("section", ("seq", "wshard"), None),
            P("section", ("seq", "wshard"), None),
            P("section", ("seq", "wshard"), None),
            P("section", None, ("seq", "wshard")),
        ),
        check_vma=False,
    )
```

```python
import math

import jax
import jax.numpy as jnp
from jax import lax
from jax.experimental import pallas as pl
from jax.experimental.pallas import tpu as pltpu
from jax.sharding import PartitionSpec as P

HEADS = 16
HEAD_DIM = 64
FF = 2624
HALO = 64
FF_PAD = 2688
SEQ_DEV = 16
W_DEV = 4
PAD_ROWS = 48
HIDDEN_BLOCK = 896
QKV_BLOCK = 768

norm_eps = 1e-05
root_half = 1.0 / math.sqrt(2.0)
root_two_pi = 1.0 / math.sqrt(2.0 * math.pi)
score_scale = 1.0 / math.sqrt(HEAD_DIM)

SWAP = [(0, 1), (1, 0)]


def swapped(array):
    return lax.ppermute(array, "section", SWAP)


def norm_parts(rows_in):
    centred = rows_in - jnp.mean(rows_in, axis=1, keepdims=True)
    factor = lax.rsqrt(jnp.mean(centred * centred, axis=1, keepdims=True) + norm_eps)
    return (centred * factor, factor)


def norm_back(grad_norm, normed, factor):
    inner = jnp.mean(grad_norm, axis=1, keepdims=True)
    along = jnp.mean(grad_norm * normed, axis=1, keepdims=True)
    return factor * (grad_norm - inner - normed * along)


def matmul(left, right):
    return jnp.dot(left, right, preferred_element_type=jnp.float32)


def matmul_t(left, right):
    return lax.dot_general(
        left, right, (((1,), (1,)), ((), ())), preferred_element_type=jnp.float32
    )


def inner_rows(left, right):
    return lax.dot_general(
        left, right, (((0,), (0,)), ((), ())), preferred_element_type=jnp.float32
    )


def column_halves(array, on_first):
    even = jnp.concatenate([array[:, 256 * k : 256 * k + 128] for k in range(4)], axis=1)
    odd = jnp.concatenate([array[:, 256 * k + 128 : 256 * k + 256] for k in range(4)], axis=1)
    return (jnp.where(on_first, even, odd), jnp.where(on_first, odd, even))


def from_halves(own, other, on_first):
    even = jnp.where(on_first, own, other)
    odd = jnp.where(on_first, other, own)
    parts = []
    for k in range(4):
        parts += [even[:, 128 * k : 128 * k + 128], odd[:, 128 * k : 128 * k + 128]]
    return jnp.concatenate(parts, axis=1)


def window_allowed(query_seg, key_seg):
    rows, keys = (query_seg.shape[0], key_seg.shape[1])
    offset = lax.broadcasted_iota(jnp.int32, (rows, keys), 1) - lax.broadcasted_iota(
        jnp.int32, (rows, keys), 0
    )
    return (offset >= 0) & (offset <= 2 * HALO) & (query_seg == key_seg)


def attend_kernel(query_seg, key_seg, qkv, mixed, log_total):
    allowed = window_allowed(query_seg[...], key_seg[...])
    width = HEADS * HEAD_DIM
    rows = mixed.shape[0]
    for head in range(HEADS):
        at = head * HEAD_DIM
        q = qkv[HALO : HALO + rows, at : at + HEAD_DIM]
        k = qkv[:, width + at : width + at + HEAD_DIM]
        v = qkv[:, 2 * width + at : 2 * width + at + HEAD_DIM]
        scores = jnp.where(allowed, matmul_t(q, k) * score_scale, -1e30)
        row_max = jnp.max(scores, axis=1, keepdims=True)
        exponent = jnp.exp(scores - row_max)
        total = jnp.sum(exponent, axis=1, keepdims=True)
        probs = (exponent * (1.0 / total)).astype(jnp.bfloat16)
        mixed[:, at : at + HEAD_DIM] = matmul(probs, v).astype(jnp.bfloat16)
        log_total[:, at : at + HEAD_DIM] = jnp.broadcast_to(
            row_max + jnp.log(total), (rows, HEAD_DIM)
        )


def attend_back_kernel(query_seg, key_seg, qkv, log_total, grad_mixed, *refs):
    grad_query, own, before, after = refs[-4:]
    allowed = window_allowed(query_seg[...], key_seg[...])
    width = HEADS * HEAD_DIM
    rows = grad_mixed.shape[0]
    for head in range(HEADS):
        at = head * HEAD_DIM
        q = qkv[HALO : HALO + rows, at : at + HEAD_DIM]
        k = qkv[:, width + at : width + at + HEAD_DIM]
        v = qkv[:, 2 * width + at : 2 * width + at + HEAD_DIM]
        grad = grad_mixed[:, at : at + HEAD_DIM]
        scores = jnp.where(allowed, matmul_t(q, k) * score_scale, -1e30)
        probs = jnp.exp(scores - log_total[:, at : at + 1])
        grad_probs = matmul_t(grad, v)
        inner = jnp.sum(probs * grad_probs, axis=1, keepdims=True)
        grad_scores = (probs * (grad_probs - inner)).astype(jnp.bfloat16)
        grad_query[:, at : at + HEAD_DIM] = (matmul(grad_scores, k) * score_scale).astype(
            jnp.bfloat16
        )
        for place, piece in (
            (at, inner_rows(grad_scores, q) * score_scale),
            (width + at, inner_rows(probs.astype(jnp.bfloat16), grad)),
        ):
            columns = slice(place, place + HEAD_DIM)
            before[:, columns] = piece[:HALO].astype(jnp.bfloat16)
            own[:, columns] = piece[HALO : HALO + rows]
            after[:, columns] = piece[HALO + rows :].astype(jnp.bfloat16)


params = pltpu.CompilerParams(vmem_limit_bytes=56 * 1024 * 1024)


def attend(query_seg, key_seg, qkv):
    rows, width = (query_seg.shape[0], HEADS * HEAD_DIM)
    return pl.pallas_call(
        attend_kernel,
        out_shape=(
            jax.ShapeDtypeStruct((rows, width), jnp.bfloat16),
            jax.ShapeDtypeStruct((rows, width), jnp.float32),
        ),
        compiler_params=params,
        name="attend",
    )(query_seg, key_seg, qkv)


def attend_back(query_seg, key_seg, qkv, log_total, grad_mixed, ready):
    rows, width = (query_seg.shape[0], HEADS * HEAD_DIM)
    return pl.pallas_call(
        attend_back_kernel,
        out_shape=(
            jax.ShapeDtypeStruct((rows, width), jnp.bfloat16),
            jax.ShapeDtypeStruct((rows, 2 * width), jnp.float32),
            jax.ShapeDtypeStruct((HALO, 2 * width), jnp.bfloat16),
            jax.ShapeDtypeStruct((HALO, 2 * width), jnp.bfloat16),
        ),
        in_specs=[pl.BlockSpec(memory_space=pltpu.VMEM)] * 5
        + [pl.BlockSpec(memory_space=pl.ANY)] * len(ready),
        compiler_params=params,
        name="attend_back",
    )(query_seg, key_seg, qkv, log_total, grad_mixed, *ready)


def to_next(array):
    return lax.ppermute(array, "seq", [(i, i + 1) for i in range(SEQ_DEV - 1)])


def to_previous(array):
    return lax.ppermute(array, "seq", [(i + 1, i) for i in range(SEQ_DEV - 1)])


def split_normal(gate):
    cumulative = 0.5 * (1.0 + lax.erf(gate * root_half))
    return cumulative


def grid_call(kernel, name, scalars, grid, in_specs, out_specs, out_shape, scratch, args, aliases=None):
    return pl.pallas_call(
        kernel,
        grid_spec=pltpu.PrefetchScalarGridSpec(
            num_scalar_prefetch=len(scalars),
            grid=grid,
            in_specs=in_specs,
            out_specs=out_specs,
            scratch_shapes=scratch,
        ),
        out_shape=out_shape,
        input_output_aliases=aliases or {},
        compiler_params=params,
        name=name,
    )(*scalars, *args)


def whole(array):
    return pl.BlockSpec(array.shape, lambda n, *_: (0,) * array.ndim)


def columns_at(rows, block, first):
    return pl.BlockSpec((rows, block), lambda n, *_: (0, first + n))


def rows_at(block, columns):
    return pl.BlockSpec((block, columns), lambda n, *_: (n, 0))


def add_to(step, total, value):
    @pl.when(step == 0)
    def _():
        total[...] = value

    @pl.when(step > 0)
    def _():
        total[...] += value


def store_halves(out, own, other, on_first):
    for k in range(4):
        block = slice(128 * k, 128 * k + 128)
        out[:, 256 * k : 256 * k + 128] = jnp.where(on_first, own[:, block], other[:, block])
        out[:, 256 * k + 128 : 256 * k + 256] = jnp.where(on_first, other[:, block], own[:, block])


def qkv_kernel(own, other, weight_own, weight_other, out):
    out[...] = (
        matmul(own[...], weight_own[...]) + matmul(other[...], weight_other[...])
    ).astype(jnp.bfloat16)


def qkv_of(own, other, weights):
    (w_own, at_own), (w_other, at_other) = weights["qkv"]
    width = 3 * HEADS * HEAD_DIM
    depth = own.shape[1]
    return grid_call(
        qkv_kernel,
        "qkv",
        (),
        (width // QKV_BLOCK,),
        [
            whole(own),
            whole(other),
            columns_at(depth, QKV_BLOCK, at_own // QKV_BLOCK),
            columns_at(depth, QKV_BLOCK, at_other // QKV_BLOCK),
        ],
        columns_at(own.shape[0], QKV_BLOCK, 0),
        jax.ShapeDtypeStruct((own.shape[0], width), jnp.bfloat16),
        [],
        (own, other, w_own, w_other),
    )


def qkv_back_kernel(first, grad, weight_own, weight_other, out, total_own, total_other):
    step = pl.program_id(0)
    add_to(step, total_own, matmul_t(grad[...], weight_own[...]))
    add_to(step, total_other, matmul_t(grad[...], weight_other[...]))

    @pl.when(step == pl.num_programs(0) - 1)
    def _():
        store_halves(out, total_own[...], total_other[...], first[0] == 1)


def qkv_back(first, grad, weights):
    (w_own, at_own), (w_other, at_other) = weights["qkv"]
    rows, width = grad.shape
    depth = w_own.shape[0]
    return grid_call(
        qkv_back_kernel,
        "qkv_back",
        (first,),
        (width // QKV_BLOCK,),
        [
            columns_at(rows, QKV_BLOCK, 0),
            columns_at(depth, QKV_BLOCK, at_own // QKV_BLOCK),
            columns_at(depth, QKV_BLOCK, at_other // QKV_BLOCK),
        ],
        pl.BlockSpec((rows, 2 * depth), lambda n, *_: (0, 0)),
        jax.ShapeDtypeStruct((rows, 2 * depth), jnp.float32),
        [pltpu.VMEM((rows, depth), jnp.float32)] * 2,
        (grad, w_own, w_other),
    )


def hidden_kernel(
    first, own, other, gate_own, gate_other, up_own, up_other, down_own, down_other, middle,
    gate_out, up_out, product_out, out, total_own, total_other,
):
    step = pl.program_id(0)
    gate = matmul(own[...], gate_own[...]) + matmul(other[...], gate_other[...])
    up = matmul(own[...], up_own[...]) + matmul(other[...], up_other[...])
    product = (gate * split_normal(gate) * up).astype(jnp.bfloat16)
    gate_out[...] = gate
    up_out[...] = up
    product_out[...] = product
    add_to(step, total_own, matmul(product, down_own[...]))
    add_to(step, total_other, matmul(product, down_other[...]))

    @pl.when(step == pl.num_programs(0) - 1)
    def _():
        half = total_own.shape[1]
        mine, theirs, on_first = (total_own[...], total_other[...], first[0] == 1)
        out[:, :half] = middle[:, :half] + jnp.where(on_first, mine, theirs)
        out[:, half:] = middle[:, half:] + jnp.where(on_first, theirs, mine)


def hidden_specs(weights, depth):
    specs, arrays = ([], [])
    for part in ("gate", "up"):
        for array, at in weights[part]:
            specs.append(columns_at(depth, HIDDEN_BLOCK, at // HIDDEN_BLOCK))
            arrays.append(array)
    for array in weights["down"]:
        specs.append(rows_at(HIDDEN_BLOCK, array.shape[1]))
        arrays.append(array)
    return (specs, arrays)


def hidden_forward(first, own, other, middle, weights):
    rows, depth = own.shape
    width = middle.shape[1]
    specs, arrays = hidden_specs(weights, depth)
    piece = columns_at(rows, HIDDEN_BLOCK, 0)
    return grid_call(
        hidden_kernel,
        "hidden",
        (first,),
        (FF_PAD // HIDDEN_BLOCK,),
        [whole(own), whole(other), *specs, whole(middle)],
        (piece, piece, piece, whole(middle)),
        (
            jax.ShapeDtypeStruct((rows, FF_PAD), jnp.float32),
            jax.ShapeDtypeStruct((rows, FF_PAD), jnp.float32),
            jax.ShapeDtypeStruct((rows, FF_PAD), jnp.bfloat16),
            jax.ShapeDtypeStruct((rows, width), jnp.float32),
        ),
        [pltpu.VMEM((rows, width // 2), jnp.float32)] * 2,
        (own, other, *arrays, middle),
    )


def hidden_back_kernel(
    first, grad_own, grad_other, gate_in, up_in, gate_own, gate_other, up_own, up_other, down_own,
    down_other, grad_gate_out, grad_up_out, out, total_own, total_other,
):
    step = pl.program_id(0)
    gate, up = (gate_in[...], up_in[...])
    grad_product = matmul_t(grad_own[...], down_own[...]) + matmul_t(
        grad_other[...], down_other[...]
    )
    cumulative = split_normal(gate)
    derivative = cumulative + gate * jnp.exp(-0.5 * gate * gate) * root_two_pi
    grad_gate = (grad_product * up * derivative).astype(jnp.bfloat16)
    grad_up = (grad_product * gate * cumulative).astype(jnp.bfloat16)
    grad_gate_out[...] = grad_gate
    grad_up_out[...] = grad_up
    add_to(step, total_own, matmul_t(grad_gate, gate_own[...]) + matmul_t(grad_up, up_own[...]))
    add_to(
        step, total_other, matmul_t(grad_gate, gate_other[...]) + matmul_t(grad_up, up_other[...])
    )

    @pl.when(step == pl.num_programs(0) - 1)
    def _():
        store_halves(out, total_own[...], total_other[...], first[0] == 1)


def hidden_back(first, grad_own, grad_other, gate, up, weights):
    rows, half = grad_own.shape
    depth = half
    specs, arrays = hidden_specs(weights, depth)
    piece = columns_at(rows, HIDDEN_BLOCK, 0)
    return grid_call(
        hidden_back_kernel,
        "hidden_back",
        (first,),
        (FF_PAD // HIDDEN_BLOCK,),
        [whole(grad_own), whole(grad_other), piece, piece, *specs],
        (piece, piece, pl.BlockSpec((rows, 2 * depth), lambda n, *_: (0, 0))),
        (
            jax.ShapeDtypeStruct((rows, FF_PAD), jnp.bfloat16),
            jax.ShapeDtypeStruct((rows, FF_PAD), jnp.bfloat16),
            jax.ShapeDtypeStruct((rows, 2 * depth), jnp.float32),
        ),
        [pltpu.VMEM((rows, depth), jnp.float32)] * 2,
        (grad_own, grad_other, gate, up, *arrays),
    )


def attention_input(rows_in, gain):
    normed, factor = norm_parts(rows_in)
    act_in = (normed * gain).astype(jnp.bfloat16)
    before = to_next(act_in[act_in.shape[0] - HALO :])
    after = to_previous(act_in[:HALO])
    return (normed, factor, act_in, jnp.concatenate([before, act_in, after], axis=0))


def layer_forward(rows_in, entry, gain_pair, weights, segs, on_first, first):
    normed1, factor1, act_in, extended = entry
    qkv = qkv_of(*column_halves(extended, on_first), weights)
    mixed, log_total = attend(*segs, qkv)
    own, other = column_halves(mixed, on_first)
    middle = rows_in + matmul(own, weights["out"][0]) + matmul(other, weights["out"][1])
    normed2, factor2 = norm_parts(middle)
    act_mid = (normed2 * gain_pair[1]).astype(jnp.bfloat16)
    own, other = column_halves(act_mid, on_first)
    gate, up, product, output = hidden_forward(first, own, other, middle, weights)
    acts = (jnp.stack([act_in, mixed, act_mid]), product)
    got = tuple(swapped(act) for act in acts)
    kept = (normed1, factor1, qkv, log_total, normed2, factor2, gate, up, acts, got)
    return (output, kept)


def seq_sum(total):
    return lax.psum_scatter(total, "seq", scatter_dimension=0, tiled=True)


ROW_PIECE = FF // (SEQ_DEV * W_DEV)
ROW_GROUPS = PAD_ROWS // 16


def weight_grads(name, items, grads, total, product=None, gains=None, base=None):
    count, width = items[0][0].shape[1:]
    block = 256
    in_specs, args = ([], [])
    for acts, got, member, *_ in items:
        for array in (acts, got):
            in_specs.append(pl.BlockSpec((1, count, block), lambda n, m=member: (m, 0, n)))
            args.append(array)
    for pair in grads:
        in_specs += [whole(array) for array in pair]
        args += list(pair)
    scratch = [pltpu.VMEM((2 * count, pair[0].shape[1]), jnp.bfloat16) for pair in grads]
    if product is not None:
        in_specs += [whole(array) for array in product[:2]]
        args += list(product[:2])
        half = grads[product[2]][0].shape[1] - product[3]
        scratch += [
            pltpu.VMEM((FF_PAD, half), jnp.float32),
            pltpu.VMEM((width, ROW_GROUPS * half), jnp.bfloat16),
        ]
    if gains is not None:
        in_specs.append(rows_at(block, gains[0].shape[1]))
        args.append(gains[0])
    aliases = {}
    columns = total
    if base is not None:
        aliases = {len(args): 0}
        in_specs.append(pl.BlockSpec(memory_space=pl.ANY))
        args.append(base)
        columns = gains[1] + gains[0].shape[1]

    def kernel(*refs):
        act_refs = refs[: 2 * len(items)]
        grad_refs = refs[2 * len(items) : 2 * (len(items) + len(grads))]
        rest = refs[2 * (len(items) + len(grads)) : len(args)]
        out, token = refs[len(args) : len(args) + 2]
        rows = refs[len(args) + 2 :]
        step = pl.program_id(0)
        token[...] = jnp.zeros(token.shape, token.dtype)

        @pl.when(step == 0)
        def _():
            for k in range(len(grads)):
                rows[k][:count] = grad_refs[2 * k][...]
                rows[k][count:] = grad_refs[2 * k + 1][...]
            if product is not None:
                down, groups = rows[-2:]
                for at in range(0, FF_PAD, 896):
                    part = jnp.concatenate([r[:, at : at + 896] for r in rest[:2]], axis=0)
                    down[at : at + 896] = inner_rows(part, rows[product[2]][:, product[3] :])
                for piece in range(SEQ_DEV * W_DEV):
                    for group in range(ROW_GROUPS):
                        first_row = piece * ROW_PIECE + group * 16
                        groups[
                            16 * piece : 16 * piece + 16, group * half : (group + 1) * half
                        ] = down[first_row : first_row + 16].astype(jnp.bfloat16)

        for k, (_, _, _, which, at, size, place) in enumerate(items):
            acts = jnp.concatenate([act_refs[2 * k][0], act_refs[2 * k + 1][0]], axis=0)
            for part in range(0, size, 512):
                wide = min(512, size - part)
                out[:, place + part : place + part + wide] = inner_rows(
                    acts, rows[which][:, at + part : at + part + wide]
                ).astype(jnp.bfloat16)
        if product is not None:
            place = product[4]
            out[:, place : place + ROW_GROUPS * half] = rows[-1][
                pl.ds(pl.multiple_of(step * block, block), block)
            ]
        if gains is not None:
            out[:, gains[1] : gains[1] + gains[0].shape[1]] = rest[0][...]

    return grid_call(
        kernel,
        name,
        (),
        (width // block,),
        in_specs,
        (rows_at(block, columns), pl.BlockSpec((8, 128), lambda n: (0, 0))),
        (
            jax.ShapeDtypeStruct((width, total), jnp.bfloat16),
            jax.ShapeDtypeStruct((8, 128), jnp.float32),
        ),
        scratch,
        args,
        aliases,
    )


def core_halves(pairs, on_first):
    low, high = [jnp.concatenate([p[k] for p in pairs], axis=1) for k in range(2)]
    return (jnp.where(on_first, low, high), swapped(jnp.where(on_first, high, low)))


def layer_backward(grad_out, kept, gain_pair, weights, segs, on_first, first, ready_of):
    (normed1, factor1, qkv, log_total, normed2, factor2, gate, up, _, _) = kept
    rows, width = normed1.shape
    half = width // 2
    grad_branch = grad_out.astype(jnp.bfloat16)
    low, high = (grad_branch[:, :half], grad_branch[:, half:])
    branch_own, branch_other = (jnp.where(on_first, low, high), jnp.where(on_first, high, low))
    grad_gate, grad_up, grad_norm2 = hidden_back(
        first, branch_own, branch_other, gate, up, weights
    )
    hidden_pair = core_halves(((grad_gate, grad_up), (low, high)), on_first)
    gain_mid = jnp.sum(normed2 * grad_norm2, axis=0)
    grad_middle = grad_out + norm_back(grad_norm2 * gain_pair[1], normed2, factor2)
    grad_attn = grad_middle.astype(jnp.bfloat16)
    mine, theirs = [matmul_t(grad_attn, w) for w in weights["out"]]
    grad_mixed = from_halves(mine, theirs, on_first).astype(jnp.bfloat16)
    grad_query, grad_own, grad_before, grad_after = attend_back(
        *segs, qkv, log_total, grad_mixed, ready_of(hidden_pair)
    )
    from_previous = to_next(grad_after).astype(jnp.float32)
    from_next = to_previous(grad_before).astype(jnp.float32)
    grad_pairs = grad_own + jnp.concatenate([from_previous, from_next], axis=0)
    grad_qkv = jnp.concatenate([grad_query, grad_pairs.astype(jnp.bfloat16)], axis=1)
    attn_pair = core_halves(
        (
            (grad_qkv[:, : 3 * half], grad_qkv[:, 3 * half :]),
            (grad_attn[:, :half], grad_attn[:, half:]),
        ),
        on_first,
    )
    grad_norm1 = qkv_back(first, grad_qkv, weights)
    gain_first = jnp.sum(normed1 * grad_norm1, axis=0)
    grad_inputs = grad_middle + norm_back(grad_norm1 * gain_pair[0], normed1, factor1)
    gains = jnp.stack([gain_first, gain_mid])
    return (grad_inputs, hidden_pair, attn_pair, gains)


def summed_over_w(block, place):
    rows = block.shape[0] // W_DEV
    total = lax.dynamic_slice_in_dim(block, place * rows, rows).astype(jnp.float32)
    for step in range(1, W_DEV):
        part = lax.dynamic_slice_in_dim(block, lax.rem(place + step, W_DEV) * rows, rows)
        got = lax.ppermute(part, "wshard", [(j, (j + step) % W_DEV) for j in range(W_DEV)])
        total = total + got.astype(jnp.float32)
    return total


def summed_by_steps(block, seq_place, w_place):
    side = 4
    columns = block.shape[1]

    def phase(parts, axis, at, place, route):
        size = parts.shape[at]

        def part(step):
            return lax.dynamic_index_in_dim(parts, lax.rem(place + step, size), at, keepdims=False)

        total = part(0).astype(jnp.float32)
        for step in range(1, size):
            total = total + lax.ppermute(part(step), axis, route(step)).astype(jnp.float32)
        return total

    total = phase(
        block.reshape(SEQ_DEV, W_DEV, 16, columns),
        "wshard",
        1,
        w_place,
        lambda step: [(j, (j + step) % W_DEV) for j in range(W_DEV)],
    )
    total = phase(
        total.astype(jnp.bfloat16).reshape(side, side, 16, columns),
        "seq",
        1,
        lax.rem(seq_place, side),
        lambda step: [
            (side * y + x, side * y + (x + step) % side) for y in range(side) for x in range(side)
        ],
    )
    return phase(
        total.astype(jnp.bfloat16),
        "seq",
        0,
        seq_place // side,
        lambda step: [
            (side * y + x, side * ((y + step) % side) + x) for y in range(side) for x in range(side)
        ],
    )


def per_device(
    inputs, cotangent, segments, norm_gains, attend_in, attend_out, hidden_in, hidden_out
):
    on_first = lax.axis_index("section") == 0
    core = lax.axis_index("section")
    seq_place = lax.axis_index("seq")
    w_place = lax.axis_index("wshard")

    def by_core(first, second):
        return jnp.where(on_first, first, second)

    def sections(own, got):
        return (by_core(own, got), by_core(got, own))

    slice_rows = attend_in.shape[1] // (2 * SEQ_DEV)
    pad = jnp.zeros((slice_rows, FF_PAD - FF), jnp.bfloat16)
    width = inputs.shape[3]

    def row_slice(which):
        at = (which * SEQ_DEV + seq_place) * slice_rows
        hidden, qkv, out = [
            lax.dynamic_slice_in_dim(w[0], at, slice_rows)
            for w in (hidden_in, attend_in, attend_out)
        ]
        return jnp.concatenate([hidden[:, :FF], pad, hidden[:, FF:], pad, qkv, out], axis=1)

    row_pieces = sections(row_slice(core), swapped(row_slice(1 - core)))
    hidden_width, qkv_width = (2 * FF_PAD, 3 * width)
    out_at = hidden_width + qkv_width

    def gathered(piece):
        return lax.all_gather(piece, ("wshard", "seq"), axis=0, tiled=True)

    first_own = gathered(row_pieces[0])
    half = hidden_out.shape[2] // 2
    low, high = (hidden_out[0, :, :half], hidden_out[0, :, half:])
    down_pieces = sections(by_core(low, high), swapped(by_core(high, low)))
    w_up = [(j, (j + 1) % W_DEV) for j in range(W_DEV)]
    w_down = [(j, i) for i, j in w_up]
    gain_pairs = sections(norm_gains[0], swapped(norm_gains[0]))

    def neighbours(piece):
        return (lax.ppermute(piece, "wshard", w_up), lax.ppermute(piece, "wshard", w_down))

    def down_of(piece, below, above):
        far = jnp.concatenate(
            [
                lax.ppermute(below[:, : half // 2], "wshard", w_up),
                lax.ppermute(above[:, half // 2 :], "wshard", w_down),
            ],
            axis=1,
        )
        own = jnp.zeros((FF_PAD, half), jnp.bfloat16)
        for step, part in enumerate((piece, above, far, below)):
            own = lax.dynamic_update_slice_in_dim(
                own, part, lax.rem(w_place + step, W_DEV) * piece.shape[0], 0
            )
        return (own, swapped(own))

    rows_in = by_core(inputs[0, 0], inputs[1, 0])
    row_count = rows_in.shape[0]
    segment_row = by_core(segments[0, 0], segments[1, 0])
    padded = jnp.pad(segment_row, (HALO, HALO), constant_values=-1)
    first_row = seq_place * row_count
    segs = (
        lax.dynamic_slice_in_dim(segment_row, first_row, row_count)[:, None],
        lax.dynamic_slice_in_dim(padded, first_row, row_count + 2 * HALO)[None, :],
    )
    entry = attention_input(rows_in, gain_pairs[0][0])
    row_piece, entry = lax.optimization_barrier((row_pieces[1], entry))
    second_own = gathered(row_piece)
    first_own, down_piece, first_down, entry, gain_pairs, segs = lax.optimization_barrier(
        (first_own, down_pieces[1], down_of(down_pieces[0], *neighbours(down_pieces[0])), entry, gain_pairs, segs)
    )
    near = neighbours(down_piece)

    def weights_of(own, other, qkv_other, out_other, down):
        return {
            "qkv": ((own, hidden_width), qkv_other),
            "gate": ((own, 0), (other, 0)),
            "up": ((own, FF_PAD), (other, FF_PAD)),
            "out": (own[:, out_at:], out_other),
            "down": down,
        }

    first = on_first.astype(jnp.int32)[None]
    other = swapped(first_own)
    first_weights = weights_of(
        first_own, other, (other, hidden_width), other[:, out_at:], first_down
    )
    middle, kept0 = layer_forward(
        rows_in, entry, gain_pairs[0], first_weights, segs, on_first, first
    )
    middle, near = lax.optimization_barrier((middle, near))
    second_own, second_down, entry = lax.optimization_barrier(
        (
            second_own, down_of(down_piece, *near), attention_input(middle, gain_pairs[1][0]),
        )
    )
    qkv_other, out_other, second_own = lax.optimization_barrier(
        (
            swapped(second_own[:, hidden_width:out_at]), swapped(second_own[:, out_at:]),
            second_own,
        )
    )
    weights = (
        first_weights,
        weights_of(second_own, swapped(second_own), (qkv_other, 0), out_other, second_down),
    )
    final, kept1 = layer_forward(middle, entry, gain_pairs[1], weights[1], segs, on_first, first)
    upstream = by_core(cotangent[0, 0], cotangent[1, 0])
    attn_cols, out_cols, down_cols = (qkv_width // 2, half, ROW_GROUPS * half)
    hidden_end = FF_PAD + down_cols
    gain_at = attn_cols + out_cols
    second_at = gain_at + 128
    hidden_at = second_at + attn_cols
    total = hidden_at + FF_PAD

    def attn_items(kept, which, at):
        acts, got = (kept[-2][0], kept[-1][0])
        return [
            (acts, got, 0, which, 0, attn_cols, at),
            (acts, got, 1, which, attn_cols, out_cols, at + attn_cols),
        ]

    def hidden_items(kept, which, at, down_at):
        acts, got = (kept[-2], kept[-1])
        return (
            [(acts[0], got[0], 2, which, 0, FF_PAD, at)],
            (acts[1], got[1], which, FF_PAD, down_at),
        )

    early_grads = []

    def make_early(hidden_pair):
        items, product = hidden_items(kept1, 0, 0, FF_PAD)
        early_grads.extend(weight_grads("hidden_grads", items, [hidden_pair], hidden_end, product))
        return early_grads[1:]

    grads1, _, attn_pair1, gains1 = layer_backward(
        upstream, kept1, gain_pairs[1], weights[1], segs, on_first, first, make_early
    )
    early = seq_sum(early_grads[0])
    grads0, hidden_pair0, attn_pair0, gains0 = layer_backward(
        grads1, kept0, gain_pairs[0], weights[0], segs, on_first, first,
        lambda hidden_pair: (hidden_pair[1], *kept0[-1]),
    )
    items, product = hidden_items(kept0, 1, hidden_at, out_cols)
    qkv_item, out_item = attn_items(kept1, 0, 0)
    pairs = [attn_pair1, hidden_pair0]
    side, _ = weight_grads("side_grads", [out_item[:-1] + (0,)], pairs, out_cols + down_cols, product)
    side_total = summed_by_steps(side, seq_place, w_place)
    base, _ = weight_grads("joint_grads", [qkv_item[:-1] + (second_at,)] + items, pairs, total)
    gains = jnp.concatenate([gains0, gains1], axis=0)
    gains = jnp.pad(gains, ((0, 128 - gains.shape[0]), (0, 0))).T.astype(jnp.bfloat16)
    late = seq_sum(
        weight_grads(
            "attn_grads",
            attn_items(kept0, 0, 0),
            [attn_pair0],
            total,
            None,
            (gains, gain_at),
            base,
        )[0]
    )

    def placed(first, second):
        mine, give = (by_core(first, second), by_core(second, first))
        got = swapped(give)
        return jnp.stack([by_core(mine, got), by_core(got, mine)])[None, :, None]

    section_outputs = placed(middle, final)
    section_input_grads = placed(grads0, grads1)

    early_total, late_total = (summed_over_w(early, w_place), summed_over_w(late, w_place))
    of_first = jnp.concatenate(
        [late_total[:, :second_at], late_total[:, hidden_at:], side_total[:, out_cols:]], axis=1
    )
    of_second = jnp.concatenate(
        [
            late_total[:, second_at:hidden_at],
            side_total[:, :out_cols],
            late_total[:, gain_at:second_at],
            early_total,
        ],
        axis=1,
    )
    mine, got = (by_core(of_first, of_second), swapped(by_core(of_second, of_first)))
    low, high = (by_core(mine, got), by_core(got, mine))
    qkv_rows = jnp.concatenate([low[:, :attn_cols], high[:, :attn_cols]], axis=1)
    attn_rows = jnp.concatenate([low[:, attn_cols:gain_at], high[:, attn_cols:gain_at]], axis=1)
    gain_part = (low + high)[:, gain_at:second_at]
    gain_rows = by_core(gain_part[:, :2], gain_part[:, 2:4]).T
    hidden_rows = jnp.concatenate(
        [low[:, second_at : second_at + FF], high[:, second_at : second_at + FF]], axis=1
    )
    down_total = jnp.concatenate(
        [
            jnp.concatenate([h[:, at : at + half] for h in (low, high)], axis=1)
            for at in range(second_at + FF_PAD, low.shape[1], half)
        ],
        axis=0,
    )[:ROW_PIECE]
    return (
        section_outputs,
        section_input_grads,
        qkv_rows[None],
        attn_rows[None],
        hidden_rows[None],
        down_total[None],
        gain_rows[None],
    )


def solution(mesh):
    placed = (
        P(None, "wshard", "seq", None),
        P(None, "wshard", "seq", None),
        P(None, "wshard", None),
        P("section", None, None),
        P("section", "wshard", None),
        P("section", "wshard", None),
        P("section", "wshard", None),
        P("section", "wshard", None),
    )
    return jax.shard_map(
        per_device,
        mesh=mesh,
        in_specs=placed,
        out_specs=(
            P("section", None, "wshard", "seq", None),
            P("section", None, "wshard", "seq", None),
            P("section", ("seq", "wshard"), None),
            P("section", ("seq", "wshard"), None),
            P("section", ("seq", "wshard"), None),
            P("section", ("seq", "wshard"), None),
            P("section", None, ("seq", "wshard")),
        ),
        check_vma=False,
    )
```

```python
import functools
import math

import jax
import jax.numpy as jnp
from jax import lax
from jax.experimental import pallas as pl
from jax.experimental.pallas import tpu as pltpu
from jax.sharding import PartitionSpec as P

HEADS = 16
HEAD_DIM = 64
FF = 2624
HALO = 64
FF_PAD = 2688
SEQ_DEV = 16
W_DEV = 4
PAD_ROWS = 48
HIDDEN_BLOCK = 896
QKV_BLOCK = 768

norm_eps = 1e-05
root_half = 1.0 / math.sqrt(2.0)
root_two_pi = 1.0 / math.sqrt(2.0 * math.pi)
score_scale = 1.0 / math.sqrt(HEAD_DIM)

SWAP = [(0, 1), (1, 0)]


def swapped(array):
    return lax.ppermute(array, "section", SWAP)


def norm_parts(rows_in):
    centred = rows_in - jnp.mean(rows_in, axis=1, keepdims=True)
    factor = lax.rsqrt(jnp.mean(centred * centred, axis=1, keepdims=True) + norm_eps)
    return (centred * factor, factor)


def norm_back(grad_norm, normed, factor):
    inner = jnp.mean(grad_norm, axis=1, keepdims=True)
    along = jnp.mean(grad_norm * normed, axis=1, keepdims=True)
    return factor * (grad_norm - inner - normed * along)


def matmul(left, right):
    return jnp.dot(left, right, preferred_element_type=jnp.float32)


def matmul_t(left, right):
    return lax.dot_general(
        left, right, (((1,), (1,)), ((), ())), preferred_element_type=jnp.float32
    )


def inner_rows(left, right):
    return lax.dot_general(
        left, right, (((0,), (0,)), ((), ())), preferred_element_type=jnp.float32
    )


def column_halves(array, on_first):
    even = jnp.concatenate([array[:, 256 * k : 256 * k + 128] for k in range(4)], axis=1)
    odd = jnp.concatenate([array[:, 256 * k + 128 : 256 * k + 256] for k in range(4)], axis=1)
    return (jnp.where(on_first, even, odd), jnp.where(on_first, odd, even))


def from_halves(own, other, on_first):
    even = jnp.where(on_first, own, other)
    odd = jnp.where(on_first, other, own)
    parts = []
    for k in range(4):
        parts += [even[:, 128 * k : 128 * k + 128], odd[:, 128 * k : 128 * k + 128]]
    return jnp.concatenate(parts, axis=1)


def window_allowed(query_seg, key_seg):
    rows, keys = (query_seg.shape[0], key_seg.shape[1])
    offset = lax.broadcasted_iota(jnp.int32, (rows, keys), 1) - lax.broadcasted_iota(
        jnp.int32, (rows, keys), 0
    )
    return (offset >= 0) & (offset <= 2 * HALO) & (query_seg == key_seg)


def attend_kernel(query_seg, key_seg, qkv, mixed, log_total):
    allowed = window_allowed(query_seg[...], key_seg[...])
    width = HEADS * HEAD_DIM
    rows = mixed.shape[0]
    for head in range(HEADS):
        at = head * HEAD_DIM
        q = qkv[HALO : HALO + rows, at : at + HEAD_DIM]
        k = qkv[:, width + at : width + at + HEAD_DIM]
        v = qkv[:, 2 * width + at : 2 * width + at + HEAD_DIM]
        scores = jnp.where(allowed, matmul_t(q, k) * score_scale, -1e30)
        row_max = jnp.max(scores, axis=1, keepdims=True)
        exponent = jnp.exp(scores - row_max)
        total = jnp.sum(exponent, axis=1, keepdims=True)
        probs = (exponent * (1.0 / total)).astype(jnp.bfloat16)
        mixed[:, at : at + HEAD_DIM] = matmul(probs, v).astype(jnp.bfloat16)
        log_total[:, at : at + HEAD_DIM] = jnp.broadcast_to(
            row_max + jnp.log(total), (rows, HEAD_DIM)
        )


def attend_back_kernel(query_seg, key_seg, qkv, log_total, grad_mixed, *refs):
    grad_query, own, before, after = refs[-4:]
    allowed = window_allowed(query_seg[...], key_seg[...])
    width = HEADS * HEAD_DIM
    rows = grad_mixed.shape[0]
    for head in range(HEADS):
        at = head * HEAD_DIM
        q = qkv[HALO : HALO + rows, at : at + HEAD_DIM]
        k = qkv[:, width + at : width + at + HEAD_DIM]
        v = qkv[:, 2 * width + at : 2 * width + at + HEAD_DIM]
        grad = grad_mixed[:, at : at + HEAD_DIM]
        scores = jnp.where(allowed, matmul_t(q, k) * score_scale, -1e30)
        probs = jnp.exp(scores - log_total[:, at : at + 1])
        grad_probs = matmul_t(grad, v)
        inner = jnp.sum(probs * grad_probs, axis=1, keepdims=True)
        grad_scores = (probs * (grad_probs - inner)).astype(jnp.bfloat16)
        grad_query[:, at : at + HEAD_DIM] = (matmul(grad_scores, k) * score_scale).astype(
            jnp.bfloat16
        )
        for place, piece in (
            (at, inner_rows(grad_scores, q) * score_scale),
            (width + at, inner_rows(probs.astype(jnp.bfloat16), grad)),
        ):
            columns = slice(place, place + HEAD_DIM)
            before[:, columns] = piece[:HALO].astype(jnp.bfloat16)
            own[:, columns] = piece[HALO : HALO + rows]
            after[:, columns] = piece[HALO + rows :].astype(jnp.bfloat16)


params = pltpu.CompilerParams(vmem_limit_bytes=40 * 1024 * 1024)


def attend(query_seg, key_seg, qkv):
    rows, width = (query_seg.shape[0], HEADS * HEAD_DIM)
    return pl.pallas_call(
        attend_kernel,
        out_shape=(
            jax.ShapeDtypeStruct((rows, width), jnp.bfloat16),
            jax.ShapeDtypeStruct((rows, width), jnp.float32),
        ),
        compiler_params=params,
        name="attend",
    )(query_seg, key_seg, qkv)


def attend_back(query_seg, key_seg, qkv, log_total, grad_mixed, ready):
    rows, width = (query_seg.shape[0], HEADS * HEAD_DIM)
    return pl.pallas_call(
        attend_back_kernel,
        out_shape=(
            jax.ShapeDtypeStruct((rows, width), jnp.bfloat16),
            jax.ShapeDtypeStruct((rows, 2 * width), jnp.float32),
            jax.ShapeDtypeStruct((HALO, 2 * width), jnp.bfloat16),
            jax.ShapeDtypeStruct((HALO, 2 * width), jnp.bfloat16),
        ),
        in_specs=[pl.BlockSpec(memory_space=pltpu.VMEM)] * 5
        + [pl.BlockSpec(memory_space=pl.ANY)] * len(ready),
        compiler_params=params,
        name="attend_back",
    )(query_seg, key_seg, qkv, log_total, grad_mixed, *ready)


def to_next(array):
    return lax.ppermute(array, "seq", [(i, i + 1) for i in range(SEQ_DEV - 1)])


def to_previous(array):
    return lax.ppermute(array, "seq", [(i + 1, i) for i in range(SEQ_DEV - 1)])


def split_normal(gate):
    cumulative = 0.5 * (1.0 + lax.erf(gate * root_half))
    return cumulative


def grid_call(kernel, name, scalars, grid, in_specs, out_specs, out_shape, scratch, args, aliases=None):
    return pl.pallas_call(
        kernel,
        grid_spec=pltpu.PrefetchScalarGridSpec(
            num_scalar_prefetch=len(scalars),
            grid=grid,
            in_specs=in_specs,
            out_specs=out_specs,
            scratch_shapes=scratch,
        ),
        out_shape=out_shape,
        input_output_aliases=aliases or {},
        compiler_params=params,
        name=name,
    )(*scalars, *args)


def whole(array):
    return pl.BlockSpec(array.shape, lambda n, *_: (0,) * array.ndim)


def columns_at(rows, block, first):
    return pl.BlockSpec((rows, block), lambda n, *_: (0, first + n))


def rows_at(block, columns):
    return pl.BlockSpec((block, columns), lambda n, *_: (n, 0))


def add_to(step, total, value):
    @pl.when(step == 0)
    def _():
        total[...] = value

    @pl.when(step > 0)
    def _():
        total[...] += value


def store_halves(out, own, other, on_first):
    for k in range(4):
        block = slice(128 * k, 128 * k + 128)
        out[:, 256 * k : 256 * k + 128] = jnp.where(on_first, own[:, block], other[:, block])
        out[:, 256 * k + 128 : 256 * k + 256] = jnp.where(on_first, other[:, block], own[:, block])


def qkv_kernel(own, other, weight_own, weight_other, out):
    out[...] = (
        matmul(own[...], weight_own[...]) + matmul(other[...], weight_other[...])
    ).astype(jnp.bfloat16)


def qkv_of(own, other, weights):
    (w_own, at_own), (w_other, at_other) = weights["qkv"]
    width = 3 * HEADS * HEAD_DIM
    depth = own.shape[1]
    return grid_call(
        qkv_kernel,
        "qkv",
        (),
        (width // QKV_BLOCK,),
        [
            whole(own),
            whole(other),
            columns_at(depth, QKV_BLOCK, at_own // QKV_BLOCK),
            columns_at(depth, QKV_BLOCK, at_other // QKV_BLOCK),
        ],
        columns_at(own.shape[0], QKV_BLOCK, 0),
        jax.ShapeDtypeStruct((own.shape[0], width), jnp.bfloat16),
        [],
        (own, other, w_own, w_other),
    )


def qkv_back_kernel(first, grad, weight_own, weight_other, *refs):
    out, total_own, total_other = refs[-3:]
    step = pl.program_id(0)
    add_to(step, total_own, matmul_t(grad[...], weight_own[...]))
    add_to(step, total_other, matmul_t(grad[...], weight_other[...]))

    @pl.when(step == pl.num_programs(0) - 1)
    def _():
        store_halves(out, total_own[...], total_other[...], first[0] == 1)


def qkv_back(first, grad, weights, ready):
    (w_own, at_own), (w_other, at_other) = weights["qkv"]
    rows, width = grad.shape
    depth = w_own.shape[0]
    return grid_call(
        qkv_back_kernel,
        "qkv_back",
        (first,),
        (width // QKV_BLOCK,),
        [
            columns_at(rows, QKV_BLOCK, 0),
            columns_at(depth, QKV_BLOCK, at_own // QKV_BLOCK),
            columns_at(depth, QKV_BLOCK, at_other // QKV_BLOCK),
            *[pl.BlockSpec(memory_space=pl.ANY)] * len(ready),
        ],
        pl.BlockSpec((rows, 2 * depth), lambda n, *_: (0, 0)),
        jax.ShapeDtypeStruct((rows, 2 * depth), jnp.float32),
        [pltpu.VMEM((rows, depth), jnp.float32)] * 2,
        (grad, w_own, w_other, *ready),
    )


def hidden_kernel(
    first, own, other, gate_own, gate_other, up_own, up_other, down_own, down_other, middle,
    gate_out, up_out, product_out, out, total_own, total_other,
):
    step = pl.program_id(0)
    gate = matmul(own[...], gate_own[...]) + matmul(other[...], gate_other[...])
    up = matmul(own[...], up_own[...]) + matmul(other[...], up_other[...])
    product = (gate * split_normal(gate) * up).astype(jnp.bfloat16)
    gate_out[...] = gate
    up_out[...] = up
    product_out[...] = product
    add_to(step, total_own, matmul(product, down_own[...]))
    add_to(step, total_other, matmul(product, down_other[...]))

    @pl.when(step == pl.num_programs(0) - 1)
    def _():
        half = total_own.shape[1]
        mine, theirs, on_first = (total_own[...], total_other[...], first[0] == 1)
        out[:, :half] = middle[:, :half] + jnp.where(on_first, mine, theirs)
        out[:, half:] = middle[:, half:] + jnp.where(on_first, theirs, mine)


def hidden_specs(weights, depth):
    specs, arrays = ([], [])
    for part in ("gate", "up"):
        for array, at in weights[part]:
            specs.append(columns_at(depth, HIDDEN_BLOCK, at // HIDDEN_BLOCK))
            arrays.append(array)
    for array in weights["down"]:
        specs.append(rows_at(HIDDEN_BLOCK, array.shape[1]))
        arrays.append(array)
    return (specs, arrays)


def hidden_forward(first, own, other, middle, weights):
    rows, depth = own.shape
    width = middle.shape[1]
    specs, arrays = hidden_specs(weights, depth)
    piece = columns_at(rows, HIDDEN_BLOCK, 0)
    return grid_call(
        hidden_kernel,
        "hidden",
        (first,),
        (FF_PAD // HIDDEN_BLOCK,),
        [whole(own), whole(other), *specs, whole(middle)],
        (piece, piece, piece, whole(middle)),
        (
            jax.ShapeDtypeStruct((rows, FF_PAD), jnp.float32),
            jax.ShapeDtypeStruct((rows, FF_PAD), jnp.float32),
            jax.ShapeDtypeStruct((rows, FF_PAD), jnp.bfloat16),
            jax.ShapeDtypeStruct((rows, width), jnp.float32),
        ),
        [pltpu.VMEM((rows, width // 2), jnp.float32)] * 2,
        (own, other, *arrays, middle),
    )


def hidden_back_kernel(
    first, grad_own, grad_other, gate_in, up_in, gate_own, gate_other, up_own, up_other, down_own,
    down_other, grad_gate_out, grad_up_out, out, total_own, total_other,
):
    step = pl.program_id(0)
    gate, up = (gate_in[...], up_in[...])
    grad_product = matmul_t(grad_own[...], down_own[...]) + matmul_t(
        grad_other[...], down_other[...]
    )
    cumulative = split_normal(gate)
    derivative = cumulative + gate * jnp.exp(-0.5 * gate * gate) * root_two_pi
    grad_gate = (grad_product * up * derivative).astype(jnp.bfloat16)
    grad_up = (grad_product * gate * cumulative).astype(jnp.bfloat16)
    grad_gate_out[...] = grad_gate
    grad_up_out[...] = grad_up
    add_to(step, total_own, matmul_t(grad_gate, gate_own[...]) + matmul_t(grad_up, up_own[...]))
    add_to(
        step, total_other, matmul_t(grad_gate, gate_other[...]) + matmul_t(grad_up, up_other[...])
    )

    @pl.when(step == pl.num_programs(0) - 1)
    def _():
        store_halves(out, total_own[...], total_other[...], first[0] == 1)


def hidden_back(first, grad_own, grad_other, gate, up, weights):
    rows, half = grad_own.shape
    depth = half
    specs, arrays = hidden_specs(weights, depth)
    piece = columns_at(rows, HIDDEN_BLOCK, 0)
    return grid_call(
        hidden_back_kernel,
        "hidden_back",
        (first,),
        (FF_PAD // HIDDEN_BLOCK,),
        [whole(grad_own), whole(grad_other), piece, piece, *specs],
        (piece, piece, pl.BlockSpec((rows, 2 * depth), lambda n, *_: (0, 0))),
        (
            jax.ShapeDtypeStruct((rows, FF_PAD), jnp.bfloat16),
            jax.ShapeDtypeStruct((rows, FF_PAD), jnp.bfloat16),
            jax.ShapeDtypeStruct((rows, 2 * depth), jnp.float32),
        ),
        [pltpu.VMEM((rows, depth), jnp.float32)] * 2,
        (grad_own, grad_other, gate, up, *arrays),
    )


def attention_input(rows_in, gain):
    normed, factor = norm_parts(rows_in)
    act_in = (normed * gain).astype(jnp.bfloat16)
    before = to_next(act_in[act_in.shape[0] - HALO :])
    after = to_previous(act_in[:HALO])
    return (normed, factor, act_in, jnp.concatenate([before, act_in, after], axis=0))


def layer_forward(rows_in, entry, gain_pair, weights, segs, on_first, first):
    normed1, factor1, act_in, extended = entry
    qkv = qkv_of(*column_halves(extended, on_first), weights)
    mixed, log_total = attend(*segs, qkv)
    own, other = column_halves(mixed, on_first)
    middle = rows_in + matmul(own, weights["out"][0]) + matmul(other, weights["out"][1])
    normed2, factor2 = norm_parts(middle)
    act_mid = (normed2 * gain_pair[1]).astype(jnp.bfloat16)
    own, other = column_halves(act_mid, on_first)
    gate, up, product, output = hidden_forward(first, own, other, middle, weights)
    acts = (jnp.stack([act_in, mixed, act_mid]), product)
    got = tuple(swapped(act) for act in acts)
    kept = (normed1, factor1, qkv, log_total, normed2, factor2, gate, up, acts, got)
    return (output, kept)


def seq_sum(total):
    return lax.psum_scatter(total, "seq", scatter_dimension=0, tiled=True)


ROW_PIECE = FF // (SEQ_DEV * W_DEV)
ROW_GROUPS = PAD_ROWS // 16


def weight_grads(name, items, grads, total, product=None, gains=None, base=None):
    count, width = items[0][0].shape[1:]
    block = 256
    in_specs, args = ([], [])
    for acts, got, member, *_ in items:
        for array in (acts, got):
            in_specs.append(pl.BlockSpec((1, count, block), lambda n, m=member: (m, 0, n)))
            args.append(array)
    for pair in grads:
        in_specs += [whole(array) for array in pair]
        args += list(pair)
    scratch = [pltpu.VMEM((2 * count, pair[0].shape[1]), jnp.bfloat16) for pair in grads]
    if product is not None:
        in_specs += [whole(array) for array in product[:2]]
        args += list(product[:2])
        half = grads[product[2]][0].shape[1] - product[3]
        scratch += [
            pltpu.VMEM((FF_PAD, half), jnp.float32),
            pltpu.VMEM((width, ROW_GROUPS * half), jnp.bfloat16),
        ]
    if gains is not None:
        in_specs.append(rows_at(block, gains[0].shape[1]))
        args.append(gains[0])
    aliases = {}
    columns = total
    if base is not None:
        aliases = {len(args): 0}
        in_specs.append(pl.BlockSpec(memory_space=pl.ANY))
        args.append(base)
        columns = sum(item[5] for item in items)

    def kernel(*refs):
        act_refs = refs[: 2 * len(items)]
        grad_refs = refs[2 * len(items) : 2 * (len(items) + len(grads))]
        rest = refs[2 * (len(items) + len(grads)) : len(args)]
        out, token = refs[len(args) : len(args) + 2]
        rows = refs[len(args) + 2 :]
        step = pl.program_id(0)
        token[...] = jnp.zeros(token.shape, token.dtype)

        @pl.when(step == 0)
        def _():
            for k in range(len(grads)):
                rows[k][:count] = grad_refs[2 * k][...]
                rows[k][count:] = grad_refs[2 * k + 1][...]
            if product is not None:
                down, groups = rows[-2:]
                for at in range(0, FF_PAD, 896):
                    part = jnp.concatenate([r[:, at : at + 896] for r in rest[:2]], axis=0)
                    down[at : at + 896] = inner_rows(part, rows[product[2]][:, product[3] :])
                for piece in range(SEQ_DEV * W_DEV):
                    for group in range(ROW_GROUPS):
                        first_row = piece * ROW_PIECE + group * 16
                        groups[
                            16 * piece : 16 * piece + 16, group * half : (group + 1) * half
                        ] = down[first_row : first_row + 16].astype(jnp.bfloat16)

        for k, (_, _, _, which, at, size, place) in enumerate(items):
            acts = jnp.concatenate([act_refs[2 * k][0], act_refs[2 * k + 1][0]], axis=0)
            for part in range(0, size, 512):
                wide = min(512, size - part)
                out[:, place + part : place + part + wide] = inner_rows(
                    acts, rows[which][:, at + part : at + part + wide]
                ).astype(jnp.bfloat16)
        if product is not None:
            place = product[4]
            out[:, place : place + ROW_GROUPS * half] = rows[-1][
                pl.ds(pl.multiple_of(step * block, block), block)
            ]
        if gains is not None:
            place = gains[1]
            out[:, place : place + gains[0].shape[1]] = rest[2 if product is not None else 0][...]

    return grid_call(
        kernel,
        name,
        (),
        (width // block,),
        in_specs,
        (rows_at(block, columns), pl.BlockSpec((8, 128), lambda n: (0, 0))),
        (
            jax.ShapeDtypeStruct((width, total), jnp.bfloat16),
            jax.ShapeDtypeStruct((8, 128), jnp.float32),
        ),
        scratch,
        args,
        aliases,
    )


def core_halves(pairs, on_first):
    low, high = [jnp.concatenate([p[k] for p in pairs], axis=1) for k in range(2)]
    return (jnp.where(on_first, low, high), swapped(jnp.where(on_first, high, low)))


def layer_backward(grad_out, kept, gain_pair, weights, segs, on_first, first, ready_of, late_of):
    (normed1, factor1, qkv, log_total, normed2, factor2, gate, up, _, _) = kept
    rows, width = normed1.shape
    half = width // 2
    grad_branch = grad_out.astype(jnp.bfloat16)
    low, high = (grad_branch[:, :half], grad_branch[:, half:])
    branch_own, branch_other = (jnp.where(on_first, low, high), jnp.where(on_first, high, low))
    grad_gate, grad_up, grad_norm2 = hidden_back(
        first, branch_own, branch_other, gate, up, weights
    )
    hidden_pair = core_halves(((grad_gate, grad_up), (low, high)), on_first)
    gain_mid = jnp.sum(normed2 * grad_norm2, axis=0)
    grad_middle = grad_out + norm_back(grad_norm2 * gain_pair[1], normed2, factor2)
    grad_attn = grad_middle.astype(jnp.bfloat16)
    mine, theirs = [matmul_t(grad_attn, w) for w in weights["out"]]
    grad_mixed = from_halves(mine, theirs, on_first).astype(jnp.bfloat16)
    grad_query, grad_own, grad_before, grad_after = attend_back(
        *segs, qkv, log_total, grad_mixed, ready_of(hidden_pair)
    )
    from_previous = to_next(grad_after).astype(jnp.float32)
    from_next = to_previous(grad_before).astype(jnp.float32)
    grad_pairs = grad_own + jnp.concatenate([from_previous, from_next], axis=0)
    grad_qkv = jnp.concatenate([grad_query, grad_pairs.astype(jnp.bfloat16)], axis=1)
    attn_pair = core_halves(
        (
            (grad_qkv[:, : 3 * half], grad_qkv[:, 3 * half :]),
            (grad_attn[:, :half], grad_attn[:, half:]),
        ),
        on_first,
    )
    grad_norm1 = qkv_back(first, grad_qkv, weights, late_of(attn_pair))
    gain_first = jnp.sum(normed1 * grad_norm1, axis=0)
    grad_inputs = grad_middle + norm_back(grad_norm1 * gain_pair[0], normed1, factor1)
    gains = jnp.stack([gain_first, gain_mid])
    return (grad_inputs, hidden_pair, attn_pair, gains)


def summed_over_w(block, place):
    rows = block.shape[0] // W_DEV
    total = lax.dynamic_slice_in_dim(block, place * rows, rows).astype(jnp.float32)
    for step in range(1, W_DEV):
        part = lax.dynamic_slice_in_dim(block, lax.rem(place + step, W_DEV) * rows, rows)
        got = lax.ppermute(part, "wshard", [(j, (j + step) % W_DEV) for j in range(W_DEV)])
        total = total + got.astype(jnp.float32)
    return total


def summed_by_steps(block, seq_place, w_place):
    side = 4
    columns = block.shape[1]

    def phase(parts, axis, at, place, route):
        size = parts.shape[at]

        def part(step):
            return lax.dynamic_index_in_dim(parts, lax.rem(place + step, size), at, keepdims=False)

        total = part(0).astype(jnp.float32)
        for step in range(1, size):
            total = total + lax.ppermute(part(step), axis, route(step)).astype(jnp.float32)
        return total

    total = phase(
        block.reshape(SEQ_DEV, W_DEV, 16, columns),
        "wshard",
        1,
        w_place,
        lambda step: [(j, (j + step) % W_DEV) for j in range(W_DEV)],
    )
    total = phase(
        total.astype(jnp.bfloat16).reshape(side, side, 16, columns),
        "seq",
        1,
        lax.rem(seq_place, side),
        lambda step: [
            (side * y + x, side * y + (x + step) % side) for y in range(side) for x in range(side)
        ],
    )
    return phase(
        total.astype(jnp.bfloat16),
        "seq",
        0,
        seq_place // side,
        lambda step: [
            (side * y + x, side * ((y + step) % side) + x) for y in range(side) for x in range(side)
        ],
    )


def per_device(
    inputs, cotangent, segments, norm_gains, attend_in, attend_out, hidden_in, hidden_out
):
    on_first = lax.axis_index("section") == 0
    core = lax.axis_index("section")
    seq_place = lax.axis_index("seq")
    w_place = lax.axis_index("wshard")

    def by_core(first, second):
        return jnp.where(on_first, first, second)

    def sections(own, got):
        return (by_core(own, got), by_core(got, own))

    slice_rows = attend_in.shape[1] // (2 * SEQ_DEV)
    pad = jnp.zeros((slice_rows, FF_PAD - FF), jnp.bfloat16)
    width = inputs.shape[3]

    def row_slice(which):
        at = (which * SEQ_DEV + seq_place) * slice_rows
        hidden, qkv, out = [
            lax.dynamic_slice_in_dim(w[0], at, slice_rows)
            for w in (hidden_in, attend_in, attend_out)
        ]
        return jnp.concatenate([hidden[:, :FF], pad, hidden[:, FF:], pad, qkv, out], axis=1)

    row_pieces = sections(row_slice(core), swapped(row_slice(1 - core)))
    hidden_width, qkv_width = (2 * FF_PAD, 3 * width)
    out_at = hidden_width + qkv_width

    def gathered(piece):
        return lax.all_gather(piece, ("wshard", "seq"), axis=0, tiled=True)

    first_own = gathered(row_pieces[0])
    half = hidden_out.shape[2] // 2
    low, high = (hidden_out[0, :, :half], hidden_out[0, :, half:])
    down_pieces = sections(by_core(low, high), swapped(by_core(high, low)))
    w_up = [(j, (j + 1) % W_DEV) for j in range(W_DEV)]
    w_down = [(j, i) for i, j in w_up]
    gain_pairs = sections(norm_gains[0], swapped(norm_gains[0]))

    def neighbours(piece):
        return (lax.ppermute(piece, "wshard", w_up), lax.ppermute(piece, "wshard", w_down))

    def down_of(piece, below, above):
        far = jnp.concatenate(
            [
                lax.ppermute(below[:, : half // 2], "wshard", w_up),
                lax.ppermute(above[:, half // 2 :], "wshard", w_down),
            ],
            axis=1,
        )
        own = jnp.zeros((FF_PAD, half), jnp.bfloat16)
        for step, part in enumerate((piece, above, far, below)):
            own = lax.dynamic_update_slice_in_dim(
                own, part, lax.rem(w_place + step, W_DEV) * piece.shape[0], 0
            )
        return (own, swapped(own))

    rows_in = by_core(inputs[0, 0], inputs[1, 0])
    row_count = rows_in.shape[0]
    segment_row = by_core(segments[0, 0], segments[1, 0])
    padded = jnp.pad(segment_row, (HALO, HALO), constant_values=-1)
    first_row = seq_place * row_count
    segs = (
        lax.dynamic_slice_in_dim(segment_row, first_row, row_count)[:, None],
        lax.dynamic_slice_in_dim(padded, first_row, row_count + 2 * HALO)[None, :],
    )
    entry = attention_input(rows_in, gain_pairs[0][0])
    row_piece, entry = lax.optimization_barrier((row_pieces[1], entry))
    second_own = gathered(row_piece)
    first_own, down_piece, first_down, entry, gain_pairs, segs = lax.optimization_barrier(
        (first_own, down_pieces[1], down_of(down_pieces[0], *neighbours(down_pieces[0])), entry, gain_pairs, segs)
    )
    near = neighbours(down_piece)

    def weights_of(own, other, qkv_other, out_other, down):
        return {
            "qkv": ((own, hidden_width), qkv_other),
            "gate": ((own, 0), (other, 0)),
            "up": ((own, FF_PAD), (other, FF_PAD)),
            "out": (own[:, out_at:], out_other),
            "down": down,
        }

    first = on_first.astype(jnp.int32)[None]
    other = swapped(first_own)
    first_weights = weights_of(
        first_own, other, (other, hidden_width), other[:, out_at:], first_down
    )
    middle, kept0 = layer_forward(
        rows_in, entry, gain_pairs[0], first_weights, segs, on_first, first
    )
    middle, near = lax.optimization_barrier((middle, near))
    second_own, second_down, entry = lax.optimization_barrier(
        (
            second_own, down_of(down_piece, *near), attention_input(middle, gain_pairs[1][0]),
        )
    )
    qkv_other, out_other, second_own = lax.optimization_barrier(
        (
            swapped(second_own[:, hidden_width:out_at]), swapped(second_own[:, out_at:]),
            second_own,
        )
    )
    weights = (
        first_weights,
        weights_of(second_own, swapped(second_own), (qkv_other, 0), out_other, second_down),
    )
    final, kept1 = layer_forward(middle, entry, gain_pairs[1], weights[1], segs, on_first, first)
    upstream = by_core(cotangent[0, 0], cotangent[1, 0])
    attn_cols, out_cols, down_cols = (qkv_width // 2, half, ROW_GROUPS * half)
    hidden_end = FF_PAD + down_cols
    second_at = attn_cols + out_cols
    side_at = out_cols + down_cols
    hidden_at = second_at + attn_cols
    total = hidden_at + FF_PAD

    def attn_items(kept, which, at):
        acts, got = (kept[-2][0], kept[-1][0])
        return [
            (acts, got, 0, which, 0, attn_cols, at),
            (acts, got, 1, which, attn_cols, out_cols, at + attn_cols),
        ]

    def hidden_items(kept, which, at, down_at):
        acts, got = (kept[-2], kept[-1])
        return (
            [(acts[0], got[0], 2, which, 0, FF_PAD, at)],
            (acts[1], got[1], which, FF_PAD, down_at),
        )

    early_grads = []

    def make_early(hidden_pair):
        items, product = hidden_items(kept1, 0, 0, FF_PAD)
        early_grads.extend(weight_grads("hidden_grads", items, [hidden_pair], hidden_end, product))
        return early_grads[1:]

    grads1, _, attn_pair1, gains1 = layer_backward(
        upstream, kept1, gain_pairs[1], weights[1], segs, on_first, first, make_early, lambda _: ()
    )
    early = seq_sum(early_grads[0])
    late_grads, side_grads = ([], [])

    def make_joint(hidden_pair):
        items, product = hidden_items(kept0, 1, hidden_at, out_cols)
        qkv_item, out_item = attn_items(kept1, 0, 0)
        pairs = [attn_pair1, hidden_pair]
        late_grads.append(
            weight_grads("joint_grads", [qkv_item[:-1] + (second_at,)] + items, pairs, total)[0]
        )
        side_grads.append(
            functools.partial(
                weight_grads, "side_grads", [out_item[:-1] + (0,)], pairs, side_at + 128, product
            )
        )
        return (hidden_pair[1], attn_pair1[1], *kept0[-1])

    def make_late(attn_pair):
        base = late_grads.pop()
        late_grads.extend(
            weight_grads("attn_grads", attn_items(kept0, 0, 0), [attn_pair], total, base=base)
        )
        return late_grads[1:]

    grads0, _, _, gains0 = layer_backward(
        grads1, kept0, gain_pairs[0], weights[0], segs, on_first, first, make_joint, make_late
    )
    late = seq_sum(late_grads[0])
    gains = jnp.concatenate([gains0, gains1], axis=0)
    gains = jnp.pad(gains, ((0, 128 - gains.shape[0]), (0, 0))).T.astype(jnp.bfloat16)
    side = side_grads[0](gains=(gains, side_at))[0]
    side_total = summed_by_steps(side, seq_place, w_place)

    def placed(first, second):
        mine, give = (by_core(first, second), by_core(second, first))
        got = swapped(give)
        return jnp.stack([by_core(mine, got), by_core(got, mine)])[None, :, None]

    section_outputs = placed(middle, final)
    section_input_grads = placed(grads0, grads1)

    early_total, late_total = (summed_over_w(early, w_place), summed_over_w(late, w_place))
    gain_part = side_total[:, side_at:]
    of_first = jnp.concatenate(
        [
            late_total[:, :second_at], gain_part, late_total[:, hidden_at:],
            side_total[:, out_cols:side_at],
        ],
        axis=1,
    )
    of_second = jnp.concatenate(
        [late_total[:, second_at:hidden_at], side_total[:, :out_cols], gain_part, early_total],
        axis=1,
    )
    mine, got = (by_core(of_first, of_second), swapped(by_core(of_second, of_first)))
    low, high = (by_core(mine, got), by_core(got, mine))
    hidden_at = second_at + 128
    qkv_rows = jnp.concatenate([low[:, :attn_cols], high[:, :attn_cols]], axis=1)
    attn_rows = jnp.concatenate([low[:, attn_cols:second_at], high[:, attn_cols:second_at]], axis=1)
    gain_part = (low + high)[:, second_at:hidden_at]
    gain_rows = by_core(gain_part[:, :2], gain_part[:, 2:4]).T
    hidden_rows = jnp.concatenate(
        [low[:, hidden_at : hidden_at + FF], high[:, hidden_at : hidden_at + FF]], axis=1
    )
    down_total = jnp.concatenate(
        [
            jnp.concatenate([h[:, at : at + half] for h in (low, high)], axis=1)
            for at in range(hidden_at + FF_PAD, low.shape[1], half)
        ],
        axis=0,
    )[:ROW_PIECE]
    return (
        section_outputs,
        section_input_grads,
        qkv_rows[None],
        attn_rows[None],
        hidden_rows[None],
        down_total[None],
        gain_rows[None],
    )


def solution(mesh):
    placed = (
        P(None, "wshard", "seq", None),
        P(None, "wshard", "seq", None),
        P(None, "wshard", None),
        P("section", None, None),
        P("section", "wshard", None),
        P("section", "wshard", None),
        P("section", "wshard", None),
        P("section", "wshard", None),
    )
    return jax.shard_map(
        per_device,
        mesh=mesh,
        in_specs=placed,
        out_specs=(
            P("section", None, "wshard", "seq", None),
            P("section", None, "wshard", "seq", None),
            P("section", ("seq", "wshard"), None),
            P("section", ("seq", "wshard"), None),
            P("section", ("seq", "wshard"), None),
            P("section", ("seq", "wshard"), None),
            P("section", None, ("seq", "wshard")),
        ),
        check_vma=False,
    )
```

```python
import functools
import math

import jax
import jax.numpy as jnp
from jax import lax
from jax.experimental import pallas as pl
from jax.experimental.pallas import tpu as pltpu
from jax.sharding import PartitionSpec as P

HEADS = 16
HEAD_DIM = 64
FF = 2624
HALO = 64
FF_PAD = 2688
SEQ_DEV = 16
W_DEV = 4
PAD_ROWS = 48
HIDDEN_BLOCK = 896
QKV_BLOCK = 768

norm_eps = 1e-05
root_half = 1.0 / math.sqrt(2.0)
root_two_pi = 1.0 / math.sqrt(2.0 * math.pi)
score_scale = 1.0 / math.sqrt(HEAD_DIM)

SWAP = [(0, 1), (1, 0)]


def swapped(array):
    return lax.ppermute(array, "section", SWAP)


def norm_parts(rows_in):
    centred = rows_in - jnp.mean(rows_in, axis=1, keepdims=True)
    factor = lax.rsqrt(jnp.mean(centred * centred, axis=1, keepdims=True) + norm_eps)
    return (centred * factor, factor)


def norm_back(grad_norm, normed, factor):
    inner = jnp.mean(grad_norm, axis=1, keepdims=True)
    along = jnp.mean(grad_norm * normed, axis=1, keepdims=True)
    return factor * (grad_norm - inner - normed * along)


def matmul(left, right):
    return jnp.dot(left, right, preferred_element_type=jnp.float32)


def matmul_t(left, right):
    return lax.dot_general(
        left, right, (((1,), (1,)), ((), ())), preferred_element_type=jnp.float32
    )


def inner_rows(left, right):
    return lax.dot_general(
        left, right, (((0,), (0,)), ((), ())), preferred_element_type=jnp.float32
    )


def column_halves(array, on_first):
    even = jnp.concatenate([array[:, 256 * k : 256 * k + 128] for k in range(4)], axis=1)
    odd = jnp.concatenate([array[:, 256 * k + 128 : 256 * k + 256] for k in range(4)], axis=1)
    return (jnp.where(on_first, even, odd), jnp.where(on_first, odd, even))


def from_halves(own, other, on_first):
    even = jnp.where(on_first, own, other)
    odd = jnp.where(on_first, other, own)
    parts = []
    for k in range(4):
        parts += [even[:, 128 * k : 128 * k + 128], odd[:, 128 * k : 128 * k + 128]]
    return jnp.concatenate(parts, axis=1)


def window_allowed(query_seg, key_seg):
    rows, keys = (query_seg.shape[0], key_seg.shape[1])
    offset = lax.broadcasted_iota(jnp.int32, (rows, keys), 1) - lax.broadcasted_iota(
        jnp.int32, (rows, keys), 0
    )
    return (offset >= 0) & (offset <= 2 * HALO) & (query_seg == key_seg)


def attend_kernel(query_seg, key_seg, qkv, mixed, log_total):
    allowed = window_allowed(query_seg[...], key_seg[...])
    width = HEADS * HEAD_DIM
    rows = mixed.shape[0]
    for head in range(HEADS):
        at = head * HEAD_DIM
        q = qkv[HALO : HALO + rows, at : at + HEAD_DIM]
        k = qkv[:, width + at : width + at + HEAD_DIM]
        v = qkv[:, 2 * width + at : 2 * width + at + HEAD_DIM]
        scores = jnp.where(allowed, matmul_t(q, k) * score_scale, -1e30)
        row_max = jnp.max(scores, axis=1, keepdims=True)
        exponent = jnp.exp(scores - row_max)
        total = jnp.sum(exponent, axis=1, keepdims=True)
        probs = (exponent * (1.0 / total)).astype(jnp.bfloat16)
        mixed[:, at : at + HEAD_DIM] = matmul(probs, v).astype(jnp.bfloat16)
        log_total[:, at : at + HEAD_DIM] = jnp.broadcast_to(
            row_max + jnp.log(total), (rows, HEAD_DIM)
        )


def attend_back_kernel(query_seg, key_seg, qkv, log_total, grad_mixed, *refs):
    grad_query, own, before, after = refs[-4:]
    allowed = window_allowed(query_seg[...], key_seg[...])
    width = HEADS * HEAD_DIM
    rows = grad_mixed.shape[0]
    for head in range(HEADS):
        at = head * HEAD_DIM
        q = qkv[HALO : HALO + rows, at : at + HEAD_DIM]
        k = qkv[:, width + at : width + at + HEAD_DIM]
        v = qkv[:, 2 * width + at : 2 * width + at + HEAD_DIM]
        grad = grad_mixed[:, at : at + HEAD_DIM]
        scores = jnp.where(allowed, matmul_t(q, k) * score_scale, -1e30)
        probs = jnp.exp(scores - log_total[:, at : at + 1])
        grad_probs = matmul_t(grad, v)
        inner = jnp.sum(probs * grad_probs, axis=1, keepdims=True)
        grad_scores = (probs * (grad_probs - inner)).astype(jnp.bfloat16)
        grad_query[:, at : at + HEAD_DIM] = (matmul(grad_scores, k) * score_scale).astype(
            jnp.bfloat16
        )
        for place, piece in (
            (at, inner_rows(grad_scores, q) * score_scale),
            (width + at, inner_rows(probs.astype(jnp.bfloat16), grad)),
        ):
            columns = slice(place, place + HEAD_DIM)
            before[:, columns] = piece[:HALO].astype(jnp.bfloat16)
            own[:, columns] = piece[HALO : HALO + rows]
            after[:, columns] = piece[HALO + rows :].astype(jnp.bfloat16)


params = pltpu.CompilerParams(vmem_limit_bytes=48 * 1024 * 1024)


def attend(query_seg, key_seg, qkv):
    rows, width = (query_seg.shape[0], HEADS * HEAD_DIM)
    return pl.pallas_call(
        attend_kernel,
        out_shape=(
            jax.ShapeDtypeStruct((rows, width), jnp.bfloat16),
            jax.ShapeDtypeStruct((rows, width), jnp.float32),
        ),
        compiler_params=params,
        name="attend",
    )(query_seg, key_seg, qkv)


def attend_back(query_seg, key_seg, qkv, log_total, grad_mixed, ready):
    rows, width = (query_seg.shape[0], HEADS * HEAD_DIM)
    return pl.pallas_call(
        attend_back_kernel,
        out_shape=(
            jax.ShapeDtypeStruct((rows, width), jnp.bfloat16),
            jax.ShapeDtypeStruct((rows, 2 * width), jnp.float32),
            jax.ShapeDtypeStruct((HALO, 2 * width), jnp.bfloat16),
            jax.ShapeDtypeStruct((HALO, 2 * width), jnp.bfloat16),
        ),
        in_specs=[pl.BlockSpec(memory_space=pltpu.VMEM)] * 5
        + [pl.BlockSpec(memory_space=pl.ANY)] * len(ready),
        compiler_params=params,
        name="attend_back",
    )(query_seg, key_seg, qkv, log_total, grad_mixed, *ready)


def to_next(array):
    return lax.ppermute(array, "seq", [(i, i + 1) for i in range(SEQ_DEV - 1)])


def to_previous(array):
    return lax.ppermute(array, "seq", [(i + 1, i) for i in range(SEQ_DEV - 1)])


def split_normal(gate):
    cumulative = 0.5 * (1.0 + lax.erf(gate * root_half))
    return cumulative


def grid_call(kernel, name, scalars, grid, in_specs, out_specs, out_shape, scratch, args, aliases=None):
    return pl.pallas_call(
        kernel,
        grid_spec=pltpu.PrefetchScalarGridSpec(
            num_scalar_prefetch=len(scalars),
            grid=grid,
            in_specs=in_specs,
            out_specs=out_specs,
            scratch_shapes=scratch,
        ),
        out_shape=out_shape,
        input_output_aliases=aliases or {},
        compiler_params=params,
        name=name,
    )(*scalars, *args)


def whole(array):
    return pl.BlockSpec(array.shape, lambda n, *_: (0,) * array.ndim)


def columns_at(rows, block, first):
    return pl.BlockSpec((rows, block), lambda n, *_: (0, first + n))


def rows_at(block, columns):
    return pl.BlockSpec((block, columns), lambda n, *_: (n, 0))


def add_to(step, total, value):
    @pl.when(step == 0)
    def _():
        total[...] = value

    @pl.when(step > 0)
    def _():
        total[...] += value


def store_halves(out, own, other, on_first):
    for k in range(4):
        block = slice(128 * k, 128 * k + 128)
        out[:, 256 * k : 256 * k + 128] = jnp.where(on_first, own[:, block], other[:, block])
        out[:, 256 * k + 128 : 256 * k + 256] = jnp.where(on_first, other[:, block], own[:, block])


def qkv_kernel(own, other, weight_own, weight_other, out):
    out[...] = (
        matmul(own[...], weight_own[...]) + matmul(other[...], weight_other[...])
    ).astype(jnp.bfloat16)


def qkv_of(own, other, weights):
    (w_own, at_own), (w_other, at_other) = weights["qkv"]
    width = 3 * HEADS * HEAD_DIM
    depth = own.shape[1]
    return grid_call(
        qkv_kernel,
        "qkv",
        (),
        (width // QKV_BLOCK,),
        [
            whole(own),
            whole(other),
            columns_at(depth, QKV_BLOCK, at_own // QKV_BLOCK),
            columns_at(depth, QKV_BLOCK, at_other // QKV_BLOCK),
        ],
        columns_at(own.shape[0], QKV_BLOCK, 0),
        jax.ShapeDtypeStruct((own.shape[0], width), jnp.bfloat16),
        [],
        (own, other, w_own, w_other),
    )


def qkv_back_kernel(first, grad, weight_own, weight_other, *refs):
    out, total_own, total_other = refs[-3:]
    step = pl.program_id(0)
    add_to(step, total_own, matmul_t(grad[...], weight_own[...]))
    add_to(step, total_other, matmul_t(grad[...], weight_other[...]))

    @pl.when(step == pl.num_programs(0) - 1)
    def _():
        store_halves(out, total_own[...], total_other[...], first[0] == 1)


def qkv_back(first, grad, weights, ready):
    (w_own, at_own), (w_other, at_other) = weights["qkv"]
    rows, width = grad.shape
    depth = w_own.shape[0]
    return grid_call(
        qkv_back_kernel,
        "qkv_back",
        (first,),
        (width // QKV_BLOCK,),
        [
            columns_at(rows, QKV_BLOCK, 0),
            columns_at(depth, QKV_BLOCK, at_own // QKV_BLOCK),
            columns_at(depth, QKV_BLOCK, at_other // QKV_BLOCK),
            *[pl.BlockSpec(memory_space=pl.ANY)] * len(ready),
        ],
        pl.BlockSpec((rows, 2 * depth), lambda n, *_: (0, 0)),
        jax.ShapeDtypeStruct((rows, 2 * depth), jnp.float32),
        [pltpu.VMEM((rows, depth), jnp.float32)] * 2,
        (grad, w_own, w_other, *ready),
    )


def hidden_kernel(
    first, own, other, gate_own, gate_other, up_own, up_other, down_own, down_other, middle,
    gate_out, up_out, product_out, out, total_own, total_other,
):
    step = pl.program_id(0)
    gate = matmul(own[...], gate_own[...]) + matmul(other[...], gate_other[...])
    up = matmul(own[...], up_own[...]) + matmul(other[...], up_other[...])
    product = (gate * split_normal(gate) * up).astype(jnp.bfloat16)
    gate_out[...] = gate
    up_out[...] = up
    product_out[...] = product
    add_to(step, total_own, matmul(product, down_own[...]))
    add_to(step, total_other, matmul(product, down_other[...]))

    @pl.when(step == pl.num_programs(0) - 1)
    def _():
        half = total_own.shape[1]
        mine, theirs, on_first = (total_own[...], total_other[...], first[0] == 1)
        out[:, :half] = middle[:, :half] + jnp.where(on_first, mine, theirs)
        out[:, half:] = middle[:, half:] + jnp.where(on_first, theirs, mine)


def hidden_specs(weights, depth):
    specs, arrays = ([], [])
    for part in ("gate", "up"):
        for array, at in weights[part]:
            specs.append(columns_at(depth, HIDDEN_BLOCK, at // HIDDEN_BLOCK))
            arrays.append(array)
    for array in weights["down"]:
        specs.append(rows_at(HIDDEN_BLOCK, array.shape[1]))
        arrays.append(array)
    return (specs, arrays)


def hidden_forward(first, own, other, middle, weights):
    rows, depth = own.shape
    width = middle.shape[1]
    specs, arrays = hidden_specs(weights, depth)
    piece = columns_at(rows, HIDDEN_BLOCK, 0)
    return grid_call(
        hidden_kernel,
        "hidden",
        (first,),
        (FF_PAD // HIDDEN_BLOCK,),
        [whole(own), whole(other), *specs, whole(middle)],
        (piece, piece, piece, whole(middle)),
        (
            jax.ShapeDtypeStruct((rows, FF_PAD), jnp.float32),
            jax.ShapeDtypeStruct((rows, FF_PAD), jnp.float32),
            jax.ShapeDtypeStruct((rows, FF_PAD), jnp.bfloat16),
            jax.ShapeDtypeStruct((rows, width), jnp.float32),
        ),
        [pltpu.VMEM((rows, width // 2), jnp.float32)] * 2,
        (own, other, *arrays, middle),
    )


def hidden_back_kernel(
    first, grad_own, grad_other, gate_in, up_in, gate_own, gate_other, up_own, up_other, down_own,
    down_other, grad_gate_out, grad_up_out, out, total_own, total_other,
):
    step = pl.program_id(0)
    gate, up = (gate_in[...], up_in[...])
    grad_product = matmul_t(grad_own[...], down_own[...]) + matmul_t(
        grad_other[...], down_other[...]
    )
    cumulative = split_normal(gate)
    derivative = cumulative + gate * jnp.exp(-0.5 * gate * gate) * root_two_pi
    grad_gate = (grad_product * up * derivative).astype(jnp.bfloat16)
    grad_up = (grad_product * gate * cumulative).astype(jnp.bfloat16)
    grad_gate_out[...] = grad_gate
    grad_up_out[...] = grad_up
    add_to(step, total_own, matmul_t(grad_gate, gate_own[...]) + matmul_t(grad_up, up_own[...]))
    add_to(
        step, total_other, matmul_t(grad_gate, gate_other[...]) + matmul_t(grad_up, up_other[...])
    )

    @pl.when(step == pl.num_programs(0) - 1)
    def _():
        store_halves(out, total_own[...], total_other[...], first[0] == 1)


def hidden_back(first, grad_own, grad_other, gate, up, weights):
    rows, half = grad_own.shape
    depth = half
    specs, arrays = hidden_specs(weights, depth)
    piece = columns_at(rows, HIDDEN_BLOCK, 0)
    return grid_call(
        hidden_back_kernel,
        "hidden_back",
        (first,),
        (FF_PAD // HIDDEN_BLOCK,),
        [whole(grad_own), whole(grad_other), piece, piece, *specs],
        (piece, piece, pl.BlockSpec((rows, 2 * depth), lambda n, *_: (0, 0))),
        (
            jax.ShapeDtypeStruct((rows, FF_PAD), jnp.bfloat16),
            jax.ShapeDtypeStruct((rows, FF_PAD), jnp.bfloat16),
            jax.ShapeDtypeStruct((rows, 2 * depth), jnp.float32),
        ),
        [pltpu.VMEM((rows, depth), jnp.float32)] * 2,
        (grad_own, grad_other, gate, up, *arrays),
    )


def attention_input(rows_in, gain):
    normed, factor = norm_parts(rows_in)
    act_in = (normed * gain).astype(jnp.bfloat16)
    before = to_next(act_in[act_in.shape[0] - HALO :])
    after = to_previous(act_in[:HALO])
    return (normed, factor, act_in, jnp.concatenate([before, act_in, after], axis=0))


def layer_forward(rows_in, entry, gain_pair, weights, segs, on_first, first):
    normed1, factor1, act_in, extended = entry
    qkv = qkv_of(*column_halves(extended, on_first), weights)
    mixed, log_total = attend(*segs, qkv)
    own, other = column_halves(mixed, on_first)
    middle = rows_in + matmul(own, weights["out"][0]) + matmul(other, weights["out"][1])
    normed2, factor2 = norm_parts(middle)
    act_mid = (normed2 * gain_pair[1]).astype(jnp.bfloat16)
    own, other = column_halves(act_mid, on_first)
    gate, up, product, output = hidden_forward(first, own, other, middle, weights)
    acts = (jnp.stack([act_in, mixed, act_mid]), product)
    got = tuple(swapped(act) for act in acts)
    kept = (normed1, factor1, qkv, log_total, normed2, factor2, gate, up, acts, got)
    return (output, kept)


def seq_sum(total):
    return lax.psum_scatter(total, "seq", scatter_dimension=0, tiled=True)


ROW_PIECE = FF // (SEQ_DEV * W_DEV)
ROW_GROUPS = PAD_ROWS // 16


def weight_grads(name, items, grads, total, product=None, base=None):
    count, width = items[0][0].shape[1:]
    block = 256
    in_specs, args = ([], [])
    for acts, got, member, *_ in items:
        for array in (acts, got):
            in_specs.append(pl.BlockSpec((1, count, block), lambda n, m=member: (m, 0, n)))
            args.append(array)
    for pair in grads:
        in_specs += [whole(array) for array in pair]
        args += list(pair)
    scratch = [pltpu.VMEM((2 * count, pair[0].shape[1]), jnp.bfloat16) for pair in grads]
    if product is not None:
        in_specs += [whole(array) for array in product[:2]]
        args += list(product[:2])
        half = grads[product[2]][0].shape[1] - product[3]
        scratch += [
            pltpu.VMEM((FF_PAD, half), jnp.float32),
            pltpu.VMEM((width, ROW_GROUPS * half), jnp.bfloat16),
        ]
    aliases = {}
    columns = total
    if base is not None:
        aliases = {len(args): 0}
        in_specs.append(pl.BlockSpec(memory_space=pl.ANY))
        args.append(base)
        columns = sum(item[5] for item in items)

    def kernel(*refs):
        act_refs = refs[: 2 * len(items)]
        grad_refs = refs[2 * len(items) : 2 * (len(items) + len(grads))]
        rest = refs[2 * (len(items) + len(grads)) : len(args)]
        out, token = refs[len(args) : len(args) + 2]
        rows = refs[len(args) + 2 :]
        step = pl.program_id(0)
        token[...] = jnp.zeros(token.shape, token.dtype)

        @pl.when(step == 0)
        def _():
            for k in range(len(grads)):
                rows[k][:count] = grad_refs[2 * k][...]
                rows[k][count:] = grad_refs[2 * k + 1][...]
            if product is not None:
                down, groups = rows[-2:]
                for at in range(0, FF_PAD, 896):
                    part = jnp.concatenate([r[:, at : at + 896] for r in rest[:2]], axis=0)
                    down[at : at + 896] = inner_rows(part, rows[product[2]][:, product[3] :])
                for piece in range(SEQ_DEV * W_DEV):
                    for group in range(ROW_GROUPS):
                        first_row = piece * ROW_PIECE + group * 16
                        groups[
                            16 * piece : 16 * piece + 16, group * half : (group + 1) * half
                        ] = down[first_row : first_row + 16].astype(jnp.bfloat16)

        for k, (_, _, _, which, at, size, place) in enumerate(items):
            acts = jnp.concatenate([act_refs[2 * k][0], act_refs[2 * k + 1][0]], axis=0)
            for part in range(0, size, 512):
                wide = min(512, size - part)
                out[:, place + part : place + part + wide] = inner_rows(
                    acts, rows[which][:, at + part : at + part + wide]
                ).astype(jnp.bfloat16)
        if product is not None:
            place = product[4]
            out[:, place : place + ROW_GROUPS * half] = rows[-1][
                pl.ds(pl.multiple_of(step * block, block), block)
            ]

    return grid_call(
        kernel,
        name,
        (),
        (width // block,),
        in_specs,
        (rows_at(block, columns), pl.BlockSpec((8, 128), lambda n: (0, 0))),
        (
            jax.ShapeDtypeStruct((width, total), jnp.bfloat16),
            jax.ShapeDtypeStruct((8, 128), jnp.float32),
        ),
        scratch,
        args,
        aliases,
    )


def core_halves(pairs, on_first):
    low, high = [jnp.concatenate([p[k] for p in pairs], axis=1) for k in range(2)]
    return (jnp.where(on_first, low, high), swapped(jnp.where(on_first, high, low)))


def layer_backward(grad_out, kept, gain_pair, weights, segs, on_first, first, ready_of, late_of):
    (normed1, factor1, qkv, log_total, normed2, factor2, gate, up, _, _) = kept
    rows, width = normed1.shape
    half = width // 2
    grad_branch = grad_out.astype(jnp.bfloat16)
    low, high = (grad_branch[:, :half], grad_branch[:, half:])
    branch_own, branch_other = (jnp.where(on_first, low, high), jnp.where(on_first, high, low))
    grad_gate, grad_up, grad_norm2 = hidden_back(
        first, branch_own, branch_other, gate, up, weights
    )
    hidden_pair = core_halves(((grad_gate, grad_up), (low, high)), on_first)
    gain_mid = jnp.sum(normed2 * grad_norm2, axis=0)
    grad_middle = grad_out + norm_back(grad_norm2 * gain_pair[1], normed2, factor2)
    grad_attn = grad_middle.astype(jnp.bfloat16)
    mine, theirs = [matmul_t(grad_attn, w) for w in weights["out"]]
    grad_mixed = from_halves(mine, theirs, on_first).astype(jnp.bfloat16)
    grad_query, grad_own, grad_before, grad_after = attend_back(
        *segs, qkv, log_total, grad_mixed, ready_of(hidden_pair)
    )
    from_previous = to_next(grad_after).astype(jnp.float32)
    from_next = to_previous(grad_before).astype(jnp.float32)
    grad_pairs = grad_own + jnp.concatenate([from_previous, from_next], axis=0)
    grad_qkv = jnp.concatenate([grad_query, grad_pairs.astype(jnp.bfloat16)], axis=1)
    attn_pair = core_halves(
        (
            (grad_qkv[:, : 3 * half], grad_qkv[:, 3 * half :]),
            (grad_attn[:, :half], grad_attn[:, half:]),
        ),
        on_first,
    )
    grad_norm1 = qkv_back(first, grad_qkv, weights, late_of(attn_pair))
    gain_first = jnp.sum(normed1 * grad_norm1, axis=0)
    grad_inputs = grad_middle + norm_back(grad_norm1 * gain_pair[0], normed1, factor1)
    gains = jnp.stack([gain_first, gain_mid])
    return (grad_inputs, hidden_pair, attn_pair, gains)


def summed_over_w(block, place):
    rows = block.shape[0] // W_DEV
    total = lax.dynamic_slice_in_dim(block, place * rows, rows).astype(jnp.float32)
    for step in range(1, W_DEV):
        part = lax.dynamic_slice_in_dim(block, lax.rem(place + step, W_DEV) * rows, rows)
        got = lax.ppermute(part, "wshard", [(j, (j + step) % W_DEV) for j in range(W_DEV)])
        total = total + got.astype(jnp.float32)
    return total


def summed_by_steps(block, seq_place, w_place):
    side = 4
    columns = block.shape[1]

    def phase(parts, axis, at, place, route):
        size = parts.shape[at]

        def part(step):
            return lax.dynamic_index_in_dim(parts, lax.rem(place + step, size), at, keepdims=False)

        total = part(0).astype(jnp.float32)
        for step in range(1, size):
            total = total + lax.ppermute(part(step), axis, route(step)).astype(jnp.float32)
        return total

    total = phase(
        block.reshape(SEQ_DEV, W_DEV, 16, columns),
        "wshard",
        1,
        w_place,
        lambda step: [(j, (j + step) % W_DEV) for j in range(W_DEV)],
    )
    total = phase(
        total.astype(jnp.bfloat16).reshape(side, side, 16, columns),
        "seq",
        1,
        lax.rem(seq_place, side),
        lambda step: [
            (side * y + x, side * y + (x + step) % side) for y in range(side) for x in range(side)
        ],
    )
    return phase(
        total.astype(jnp.bfloat16),
        "seq",
        0,
        seq_place // side,
        lambda step: [
            (side * y + x, side * ((y + step) % side) + x) for y in range(side) for x in range(side)
        ],
    )


def per_device(
    inputs, cotangent, segments, norm_gains, attend_in, attend_out, hidden_in, hidden_out
):
    on_first = lax.axis_index("section") == 0
    core = lax.axis_index("section")
    seq_place = lax.axis_index("seq")
    w_place = lax.axis_index("wshard")

    def by_core(first, second):
        return jnp.where(on_first, first, second)

    def sections(own, got):
        return (by_core(own, got), by_core(got, own))

    slice_rows = attend_in.shape[1] // (2 * SEQ_DEV)
    pad = jnp.zeros((slice_rows, FF_PAD - FF), jnp.bfloat16)
    width = inputs.shape[3]

    def row_slice(which):
        at = (which * SEQ_DEV + seq_place) * slice_rows
        hidden, qkv, out = [
            lax.dynamic_slice_in_dim(w[0], at, slice_rows)
            for w in (hidden_in, attend_in, attend_out)
        ]
        return jnp.concatenate([hidden[:, :FF], pad, hidden[:, FF:], pad, qkv, out], axis=1)

    row_pieces = sections(row_slice(core), swapped(row_slice(1 - core)))
    hidden_width, qkv_width = (2 * FF_PAD, 3 * width)
    out_at = hidden_width + qkv_width

    def gathered(piece):
        return lax.all_gather(piece, ("wshard", "seq"), axis=0, tiled=True)

    first_own = gathered(row_pieces[0])
    half = hidden_out.shape[2] // 2
    low, high = (hidden_out[0, :, :half], hidden_out[0, :, half:])
    down_pieces = sections(by_core(low, high), swapped(by_core(high, low)))
    w_up = [(j, (j + 1) % W_DEV) for j in range(W_DEV)]
    w_down = [(j, i) for i, j in w_up]
    gain_pairs = sections(norm_gains[0], swapped(norm_gains[0]))

    def neighbours(piece):
        return (lax.ppermute(piece, "wshard", w_up), lax.ppermute(piece, "wshard", w_down))

    def down_of(piece, below, above):
        far = jnp.concatenate(
            [
                lax.ppermute(below[:, : half // 2], "wshard", w_up),
                lax.ppermute(above[:, half // 2 :], "wshard", w_down),
            ],
            axis=1,
        )
        own = jnp.zeros((FF_PAD, half), jnp.bfloat16)
        for step, part in enumerate((piece, above, far, below)):
            own = lax.dynamic_update_slice_in_dim(
                own, part, lax.rem(w_place + step, W_DEV) * piece.shape[0], 0
            )
        return (own, swapped(own))

    rows_in = by_core(inputs[0, 0], inputs[1, 0])
    row_count = rows_in.shape[0]
    segment_row = by_core(segments[0, 0], segments[1, 0])
    padded = jnp.pad(segment_row, (HALO, HALO), constant_values=-1)
    first_row = seq_place * row_count
    segs = (
        lax.dynamic_slice_in_dim(segment_row, first_row, row_count)[:, None],
        lax.dynamic_slice_in_dim(padded, first_row, row_count + 2 * HALO)[None, :],
    )
    entry = attention_input(rows_in, gain_pairs[0][0])
    row_piece, entry = lax.optimization_barrier((row_pieces[1], entry))
    second_own = gathered(row_piece)
    first_own, down_piece, first_down, entry, gain_pairs, segs = lax.optimization_barrier(
        (first_own, down_pieces[1], down_of(down_pieces[0], *neighbours(down_pieces[0])), entry, gain_pairs, segs)
    )
    near = neighbours(down_piece)

    def weights_of(own, other, qkv_other, out_other, down):
        return {
            "qkv": ((own, hidden_width), qkv_other),
            "gate": ((own, 0), (other, 0)),
            "up": ((own, FF_PAD), (other, FF_PAD)),
            "out": (own[:, out_at:], out_other),
            "down": down,
        }

    first = on_first.astype(jnp.int32)[None]
    other = swapped(first_own)
    first_weights = weights_of(
        first_own, other, (other, hidden_width), other[:, out_at:], first_down
    )
    middle, kept0 = layer_forward(
        rows_in, entry, gain_pairs[0], first_weights, segs, on_first, first
    )
    middle, near = lax.optimization_barrier((middle, near))
    second_own, second_down, entry = lax.optimization_barrier(
        (
            second_own, down_of(down_piece, *near), attention_input(middle, gain_pairs[1][0]),
        )
    )
    qkv_other, out_other, second_own = lax.optimization_barrier(
        (
            swapped(second_own[:, hidden_width:out_at]), swapped(second_own[:, out_at:]),
            second_own,
        )
    )
    weights = (
        first_weights,
        weights_of(second_own, swapped(second_own), (qkv_other, 0), out_other, second_down),
    )
    final, kept1 = layer_forward(middle, entry, gain_pairs[1], weights[1], segs, on_first, first)
    upstream = by_core(cotangent[0, 0], cotangent[1, 0])
    attn_cols, out_cols, down_cols = (qkv_width // 2, half, ROW_GROUPS * half)
    hidden_end = FF_PAD + down_cols
    second_at = attn_cols + out_cols
    side_at = out_cols + down_cols
    hidden_at = second_at + attn_cols
    total = hidden_at + FF_PAD

    def attn_items(kept, which, at):
        acts, got = (kept[-2][0], kept[-1][0])
        return [
            (acts, got, 0, which, 0, attn_cols, at),
            (acts, got, 1, which, attn_cols, out_cols, at + attn_cols),
        ]

    def hidden_items(kept, which, at, down_at):
        acts, got = (kept[-2], kept[-1])
        return (
            [(acts[0], got[0], 2, which, 0, FF_PAD, at)],
            (acts[1], got[1], which, FF_PAD, down_at),
        )

    early_grads = []

    def make_early(hidden_pair):
        items, product = hidden_items(kept1, 0, 0, FF_PAD)
        early_grads.extend(weight_grads("hidden_grads", items, [hidden_pair], hidden_end, product))
        return early_grads[1:]

    grads1, _, attn_pair1, gains1 = layer_backward(
        upstream, kept1, gain_pairs[1], weights[1], segs, on_first, first, make_early, lambda _: ()
    )
    early = seq_sum(early_grads[0])
    late_grads, side_grads = ([], [])

    def make_joint(hidden_pair):
        items, product = hidden_items(kept0, 1, hidden_at, out_cols)
        qkv_item, out_item = attn_items(kept1, 0, 0)
        pairs = [attn_pair1, hidden_pair]
        late_grads.append(
            weight_grads("joint_grads", [qkv_item[:-1] + (second_at,)] + items, pairs, total)[0]
        )
        side_grads.append(
            functools.partial(
                weight_grads, "side_grads", [out_item[:-1] + (0,)], pairs, side_at, product
            )
        )
        return (hidden_pair[1], attn_pair1[1], *kept0[-1])

    def make_late(attn_pair):
        base = late_grads.pop()
        late_grads.extend(
            weight_grads("attn_grads", attn_items(kept0, 0, 0), [attn_pair], total, base=base)
        )
        side_grads.extend(side_grads.pop()())
        return (late_grads[1], side_grads[1])

    grads0, _, _, gains0 = layer_backward(
        grads1, kept0, gain_pairs[0], weights[0], segs, on_first, first, make_joint, make_late
    )
    late = seq_sum(late_grads[0])
    gains = jnp.concatenate([gains0, gains1], axis=0)
    gains = jnp.pad(gains, ((0, 128 - gains.shape[0]), (0, 0))).T.astype(jnp.bfloat16)
    side_total = summed_by_steps(side_grads[0], seq_place, w_place)
    gain_part = summed_by_steps(gains, seq_place, w_place)

    def placed(first, second):
        mine, give = (by_core(first, second), by_core(second, first))
        got = swapped(give)
        return jnp.stack([by_core(mine, got), by_core(got, mine)])[None, :, None]

    section_outputs = placed(middle, final)
    section_input_grads = placed(grads0, grads1)

    early_total, late_total = (summed_over_w(early, w_place), summed_over_w(late, w_place))
    of_first = jnp.concatenate(
        [
            late_total[:, :second_at], gain_part, late_total[:, hidden_at:],
            side_total[:, out_cols:],
        ],
        axis=1,
    )
    of_second = jnp.concatenate(
        [late_total[:, second_at:hidden_at], side_total[:, :out_cols], gain_part, early_total],
        axis=1,
    )
    mine, got = (by_core(of_first, of_second), swapped(by_core(of_second, of_first)))
    low, high = (by_core(mine, got), by_core(got, mine))
    hidden_at = second_at + 128
    qkv_rows = jnp.concatenate([low[:, :attn_cols], high[:, :attn_cols]], axis=1)
    attn_rows = jnp.concatenate([low[:, attn_cols:second_at], high[:, attn_cols:second_at]], axis=1)
    gain_part = (low + high)[:, second_at:hidden_at]
    gain_rows = by_core(gain_part[:, :2], gain_part[:, 2:4]).T
    hidden_rows = jnp.concatenate(
        [low[:, hidden_at : hidden_at + FF], high[:, hidden_at : hidden_at + FF]], axis=1
    )
    down_total = jnp.concatenate(
        [
            jnp.concatenate([h[:, at : at + half] for h in (low, high)], axis=1)
            for at in range(hidden_at + FF_PAD, low.shape[1], half)
        ],
        axis=0,
    )[:ROW_PIECE]
    return (
        section_outputs,
        section_input_grads,
        qkv_rows[None],
        attn_rows[None],
        hidden_rows[None],
        down_total[None],
        gain_rows[None],
    )


def solution(mesh):
    placed = (
        P(None, "wshard", "seq", None),
        P(None, "wshard", "seq", None),
        P(None, "wshard", None),
        P("section", None, None),
        P("section", "wshard", None),
        P("section", "wshard", None),
        P("section", "wshard", None),
        P("section", "wshard", None),
    )
    return jax.shard_map(
        per_device,
        mesh=mesh,
        in_specs=placed,
        out_specs=(
            P("section", None, "wshard", "seq", None),
            P("section", None, "wshard", "seq", None),
            P("section", ("seq", "wshard"), None),
            P("section", ("seq", "wshard"), None),
            P("section", ("seq", "wshard"), None),
            P("section", ("seq", "wshard"), None),
            P("section", None, ("seq", "wshard")),
        ),
        check_vma=False,
    )
```

```python
import functools
import math

import jax
import jax.numpy as jnp
from jax import lax
from jax.experimental import pallas as pl
from jax.experimental.pallas import tpu as pltpu
from jax.sharding import PartitionSpec as P

HEADS = 16
HEAD_DIM = 64
FF = 2624
HALO = 64
FF_PAD = 2688
SEQ_DEV = 16
W_DEV = 4
PAD_ROWS = 48
HIDDEN_BLOCK = 896
QKV_BLOCK = 768

norm_eps = 1e-05
root_half = 1.0 / math.sqrt(2.0)
root_two_pi = 1.0 / math.sqrt(2.0 * math.pi)
score_scale = 1.0 / math.sqrt(HEAD_DIM)

SWAP = [(0, 1), (1, 0)]


def swapped(array):
    return lax.ppermute(array, "section", SWAP)


def norm_parts(rows_in):
    centred = rows_in - jnp.mean(rows_in, axis=1, keepdims=True)
    factor = lax.rsqrt(jnp.mean(centred * centred, axis=1, keepdims=True) + norm_eps)
    return (centred * factor, factor)


def norm_back(grad_norm, normed, factor):
    inner = jnp.mean(grad_norm, axis=1, keepdims=True)
    along = jnp.mean(grad_norm * normed, axis=1, keepdims=True)
    return factor * (grad_norm - inner - normed * along)


def matmul(left, right):
    return jnp.dot(left, right, preferred_element_type=jnp.float32)


def matmul_t(left, right):
    return lax.dot_general(
        left, right, (((1,), (1,)), ((), ())), preferred_element_type=jnp.float32
    )


def inner_rows(left, right):
    return lax.dot_general(
        left, right, (((0,), (0,)), ((), ())), preferred_element_type=jnp.float32
    )


def column_halves(array, on_first):
    even = jnp.concatenate([array[:, 256 * k : 256 * k + 128] for k in range(4)], axis=1)
    odd = jnp.concatenate([array[:, 256 * k + 128 : 256 * k + 256] for k in range(4)], axis=1)
    return (jnp.where(on_first, even, odd), jnp.where(on_first, odd, even))


def from_halves(own, other, on_first):
    even = jnp.where(on_first, own, other)
    odd = jnp.where(on_first, other, own)
    parts = []
    for k in range(4):
        parts += [even[:, 128 * k : 128 * k + 128], odd[:, 128 * k : 128 * k + 128]]
    return jnp.concatenate(parts, axis=1)


def window_allowed(query_seg, key_seg):
    rows, keys = (query_seg.shape[0], key_seg.shape[1])
    offset = lax.broadcasted_iota(jnp.int32, (rows, keys), 1) - lax.broadcasted_iota(
        jnp.int32, (rows, keys), 0
    )
    return (offset >= 0) & (offset <= 2 * HALO) & (query_seg == key_seg)


def attend_kernel(query_seg, key_seg, qkv, mixed, log_total):
    allowed = window_allowed(query_seg[...], key_seg[...])
    width = HEADS * HEAD_DIM
    rows = mixed.shape[0]
    for head in range(HEADS):
        at = head * HEAD_DIM
        q = qkv[HALO : HALO + rows, at : at + HEAD_DIM]
        k = qkv[:, width + at : width + at + HEAD_DIM]
        v = qkv[:, 2 * width + at : 2 * width + at + HEAD_DIM]
        scores = jnp.where(allowed, matmul_t(q, k) * score_scale, -1e30)
        row_max = jnp.max(scores, axis=1, keepdims=True)
        exponent = jnp.exp(scores - row_max)
        total = jnp.sum(exponent, axis=1, keepdims=True)
        probs = (exponent * (1.0 / total)).astype(jnp.bfloat16)
        mixed[:, at : at + HEAD_DIM] = matmul(probs, v).astype(jnp.bfloat16)
        log_total[:, at : at + HEAD_DIM] = jnp.broadcast_to(
            row_max + jnp.log(total), (rows, HEAD_DIM)
        )


def attend_back_kernel(query_seg, key_seg, qkv, log_total, grad_mixed, *refs):
    grad_query, own, before, after = refs[-4:]
    allowed = window_allowed(query_seg[...], key_seg[...])
    width = HEADS * HEAD_DIM
    rows = grad_mixed.shape[0]
    for head in range(HEADS):
        at = head * HEAD_DIM
        q = qkv[HALO : HALO + rows, at : at + HEAD_DIM]
        k = qkv[:, width + at : width + at + HEAD_DIM]
        v = qkv[:, 2 * width + at : 2 * width + at + HEAD_DIM]
        grad = grad_mixed[:, at : at + HEAD_DIM]
        scores = jnp.where(allowed, matmul_t(q, k) * score_scale, -1e30)
        probs = jnp.exp(scores - log_total[:, at : at + 1])
        grad_probs = matmul_t(grad, v)
        inner = jnp.sum(probs * grad_probs, axis=1, keepdims=True)
        grad_scores = (probs * (grad_probs - inner)).astype(jnp.bfloat16)
        grad_query[:, at : at + HEAD_DIM] = (matmul(grad_scores, k) * score_scale).astype(
            jnp.bfloat16
        )
        for place, piece in (
            (at, inner_rows(grad_scores, q) * score_scale),
            (width + at, inner_rows(probs.astype(jnp.bfloat16), grad)),
        ):
            columns = slice(place, place + HEAD_DIM)
            before[:, columns] = piece[:HALO].astype(jnp.bfloat16)
            own[:, columns] = piece[HALO : HALO + rows]
            after[:, columns] = piece[HALO + rows :].astype(jnp.bfloat16)


params = pltpu.CompilerParams(vmem_limit_bytes=48 * 1024 * 1024)


def attend(query_seg, key_seg, qkv):
    rows, width = (query_seg.shape[0], HEADS * HEAD_DIM)
    return pl.pallas_call(
        attend_kernel,
        out_shape=(
            jax.ShapeDtypeStruct((rows, width), jnp.bfloat16),
            jax.ShapeDtypeStruct((rows, width), jnp.float32),
        ),
        compiler_params=params,
        name="attend",
    )(query_seg, key_seg, qkv)


def attend_back(query_seg, key_seg, qkv, log_total, grad_mixed, ready):
    rows, width = (query_seg.shape[0], HEADS * HEAD_DIM)
    return pl.pallas_call(
        attend_back_kernel,
        out_shape=(
            jax.ShapeDtypeStruct((rows, width), jnp.bfloat16),
            jax.ShapeDtypeStruct((rows, 2 * width), jnp.float32),
            jax.ShapeDtypeStruct((HALO, 2 * width), jnp.bfloat16),
            jax.ShapeDtypeStruct((HALO, 2 * width), jnp.bfloat16),
        ),
        in_specs=[pl.BlockSpec(memory_space=pltpu.VMEM)] * 5
        + [pl.BlockSpec(memory_space=pl.ANY)] * len(ready),
        compiler_params=params,
        name="attend_back",
    )(query_seg, key_seg, qkv, log_total, grad_mixed, *ready)


def to_next(array):
    return lax.ppermute(array, "seq", [(i, i + 1) for i in range(SEQ_DEV - 1)])


def to_previous(array):
    return lax.ppermute(array, "seq", [(i + 1, i) for i in range(SEQ_DEV - 1)])


def split_normal(gate):
    cumulative = 0.5 * (1.0 + lax.erf(gate * root_half))
    return cumulative


def grid_call(kernel, name, scalars, grid, in_specs, out_specs, out_shape, scratch, args, aliases=None):
    return pl.pallas_call(
        kernel,
        grid_spec=pltpu.PrefetchScalarGridSpec(
            num_scalar_prefetch=len(scalars),
            grid=grid,
            in_specs=in_specs,
            out_specs=out_specs,
            scratch_shapes=scratch,
        ),
        out_shape=out_shape,
        input_output_aliases=aliases or {},
        compiler_params=params,
        name=name,
    )(*scalars, *args)


def whole(array):
    return pl.BlockSpec(array.shape, lambda n, *_: (0,) * array.ndim)


def columns_at(rows, block, first):
    return pl.BlockSpec((rows, block), lambda n, *_: (0, first + n))


def rows_at(block, columns):
    return pl.BlockSpec((block, columns), lambda n, *_: (n, 0))


def add_to(step, total, value):
    @pl.when(step == 0)
    def _():
        total[...] = value

    @pl.when(step > 0)
    def _():
        total[...] += value


def store_halves(out, own, other, on_first):
    for k in range(4):
        block = slice(128 * k, 128 * k + 128)
        out[:, 256 * k : 256 * k + 128] = jnp.where(on_first, own[:, block], other[:, block])
        out[:, 256 * k + 128 : 256 * k + 256] = jnp.where(on_first, other[:, block], own[:, block])


def qkv_kernel(own, other, weight_own, weight_other, out):
    out[...] = (
        matmul(own[...], weight_own[...]) + matmul(other[...], weight_other[...])
    ).astype(jnp.bfloat16)


def qkv_of(own, other, weights):
    (w_own, at_own), (w_other, at_other) = weights["qkv"]
    width = 3 * HEADS * HEAD_DIM
    depth = own.shape[1]
    return grid_call(
        qkv_kernel,
        "qkv",
        (),
        (width // QKV_BLOCK,),
        [
            whole(own),
            whole(other),
            columns_at(depth, QKV_BLOCK, at_own // QKV_BLOCK),
            columns_at(depth, QKV_BLOCK, at_other // QKV_BLOCK),
        ],
        columns_at(own.shape[0], QKV_BLOCK, 0),
        jax.ShapeDtypeStruct((own.shape[0], width), jnp.bfloat16),
        [],
        (own, other, w_own, w_other),
    )


def qkv_back_kernel(first, grad, weight_own, weight_other, *refs):
    out, total_own, total_other = refs[-3:]
    step = pl.program_id(0)
    add_to(step, total_own, matmul_t(grad[...], weight_own[...]))
    add_to(step, total_other, matmul_t(grad[...], weight_other[...]))

    @pl.when(step == pl.num_programs(0) - 1)
    def _():
        store_halves(out, total_own[...], total_other[...], first[0] == 1)


def qkv_back(first, grad, weights, ready):
    (w_own, at_own), (w_other, at_other) = weights["qkv"]
    rows, width = grad.shape
    depth = w_own.shape[0]
    return grid_call(
        qkv_back_kernel,
        "qkv_back",
        (first,),
        (width // QKV_BLOCK,),
        [
            columns_at(rows, QKV_BLOCK, 0),
            columns_at(depth, QKV_BLOCK, at_own // QKV_BLOCK),
            columns_at(depth, QKV_BLOCK, at_other // QKV_BLOCK),
            *[pl.BlockSpec(memory_space=pl.ANY)] * len(ready),
        ],
        pl.BlockSpec((rows, 2 * depth), lambda n, *_: (0, 0)),
        jax.ShapeDtypeStruct((rows, 2 * depth), jnp.float32),
        [pltpu.VMEM((rows, depth), jnp.float32)] * 2,
        (grad, w_own, w_other, *ready),
    )


def hidden_kernel(
    first, own, other, gate_own, gate_other, up_own, up_other, down_own, down_other, middle,
    gate_out, up_out, product_out, out, total_own, total_other,
):
    step = pl.program_id(0)
    gate = matmul(own[...], gate_own[...]) + matmul(other[...], gate_other[...])
    up = matmul(own[...], up_own[...]) + matmul(other[...], up_other[...])
    product = (gate * split_normal(gate) * up).astype(jnp.bfloat16)
    gate_out[...] = gate
    up_out[...] = up
    product_out[...] = product
    add_to(step, total_own, matmul(product, down_own[...]))
    add_to(step, total_other, matmul(product, down_other[...]))

    @pl.when(step == pl.num_programs(0) - 1)
    def _():
        half = total_own.shape[1]
        mine, theirs, on_first = (total_own[...], total_other[...], first[0] == 1)
        out[:, :half] = middle[:, :half] + jnp.where(on_first, mine, theirs)
        out[:, half:] = middle[:, half:] + jnp.where(on_first, theirs, mine)


def hidden_specs(weights, depth):
    specs, arrays = ([], [])
    for part in ("gate", "up"):
        for array, at in weights[part]:
            specs.append(columns_at(depth, HIDDEN_BLOCK, at // HIDDEN_BLOCK))
            arrays.append(array)
    for array in weights["down"]:
        specs.append(rows_at(HIDDEN_BLOCK, array.shape[1]))
        arrays.append(array)
    return (specs, arrays)


def hidden_forward(first, own, other, middle, weights):
    rows, depth = own.shape
    width = middle.shape[1]
    specs, arrays = hidden_specs(weights, depth)
    piece = columns_at(rows, HIDDEN_BLOCK, 0)
    return grid_call(
        hidden_kernel,
        "hidden",
        (first,),
        (FF_PAD // HIDDEN_BLOCK,),
        [whole(own), whole(other), *specs, whole(middle)],
        (piece, piece, piece, whole(middle)),
        (
            jax.ShapeDtypeStruct((rows, FF_PAD), jnp.float32),
            jax.ShapeDtypeStruct((rows, FF_PAD), jnp.float32),
            jax.ShapeDtypeStruct((rows, FF_PAD), jnp.bfloat16),
            jax.ShapeDtypeStruct((rows, width), jnp.float32),
        ),
        [pltpu.VMEM((rows, width // 2), jnp.float32)] * 2,
        (own, other, *arrays, middle),
    )


def hidden_back_kernel(
    first, grad_own, grad_other, gate_in, up_in, gate_own, gate_other, up_own, up_other, down_own,
    down_other, grad_gate_out, grad_up_out, out, total_own, total_other,
):
    step = pl.program_id(0)
    gate, up = (gate_in[...], up_in[...])
    grad_product = matmul_t(grad_own[...], down_own[...]) + matmul_t(
        grad_other[...], down_other[...]
    )
    cumulative = split_normal(gate)
    derivative = cumulative + gate * jnp.exp(-0.5 * gate * gate) * root_two_pi
    grad_gate = (grad_product * up * derivative).astype(jnp.bfloat16)
    grad_up = (grad_product * gate * cumulative).astype(jnp.bfloat16)
    grad_gate_out[...] = grad_gate
    grad_up_out[...] = grad_up
    add_to(step, total_own, matmul_t(grad_gate, gate_own[...]) + matmul_t(grad_up, up_own[...]))
    add_to(
        step, total_other, matmul_t(grad_gate, gate_other[...]) + matmul_t(grad_up, up_other[...])
    )

    @pl.when(step == pl.num_programs(0) - 1)
    def _():
        store_halves(out, total_own[...], total_other[...], first[0] == 1)


def hidden_back(first, grad_own, grad_other, gate, up, weights):
    rows, half = grad_own.shape
    depth = half
    specs, arrays = hidden_specs(weights, depth)
    piece = columns_at(rows, HIDDEN_BLOCK, 0)
    return grid_call(
        hidden_back_kernel,
        "hidden_back",
        (first,),
        (FF_PAD // HIDDEN_BLOCK,),
        [whole(grad_own), whole(grad_other), piece, piece, *specs],
        (piece, piece, pl.BlockSpec((rows, 2 * depth), lambda n, *_: (0, 0))),
        (
            jax.ShapeDtypeStruct((rows, FF_PAD), jnp.bfloat16),
            jax.ShapeDtypeStruct((rows, FF_PAD), jnp.bfloat16),
            jax.ShapeDtypeStruct((rows, 2 * depth), jnp.float32),
        ),
        [pltpu.VMEM((rows, depth), jnp.float32)] * 2,
        (grad_own, grad_other, gate, up, *arrays),
    )


def attention_input(rows_in, gain):
    normed, factor = norm_parts(rows_in)
    act_in = (normed * gain).astype(jnp.bfloat16)
    before = to_next(act_in[act_in.shape[0] - HALO :])
    after = to_previous(act_in[:HALO])
    return (normed, factor, act_in, jnp.concatenate([before, act_in, after], axis=0))


def layer_forward(rows_in, entry, gain_pair, weights, segs, on_first, first):
    normed1, factor1, act_in, extended = entry
    qkv = qkv_of(*column_halves(extended, on_first), weights)
    mixed, log_total = attend(*segs, qkv)
    own, other = column_halves(mixed, on_first)
    middle = rows_in + matmul(own, weights["out"][0]) + matmul(other, weights["out"][1])
    normed2, factor2 = norm_parts(middle)
    act_mid = (normed2 * gain_pair[1]).astype(jnp.bfloat16)
    own, other = column_halves(act_mid, on_first)
    gate, up, product, output = hidden_forward(first, own, other, middle, weights)
    acts = (jnp.stack([act_in, mixed, act_mid]), product)
    got = tuple(swapped(act) for act in acts)
    kept = (normed1, factor1, qkv, log_total, normed2, factor2, gate, up, acts, got)
    return (output, kept)


def seq_sum(total):
    return lax.psum_scatter(total, "seq", scatter_dimension=0, tiled=True)


ROW_PIECE = FF // (SEQ_DEV * W_DEV)
ROW_GROUPS = PAD_ROWS // 16


def weight_grads(name, items, grads, total, product=None, base=None):
    count, width, block = (grads[0][0].shape[0], HEADS * HEAD_DIM, 256)
    in_specs, args = ([], [])
    for acts, got, member, *_ in items:
        for array in (acts, got):
            in_specs.append(pl.BlockSpec((1, count, block), lambda n, m=member: (m, 0, n)))
            args.append(array)
    for pair in grads:
        in_specs += [whole(array) for array in pair]
        args += list(pair)
    scratch = [pltpu.VMEM((2 * count, pair[0].shape[1]), jnp.bfloat16) for pair in grads]
    if product is not None:
        in_specs += [whole(array) for array in product[:2]]
        args += list(product[:2])
        half = grads[product[2]][0].shape[1] - product[3]
        scratch += [
            pltpu.VMEM((FF_PAD, half), jnp.float32),
            pltpu.VMEM((width, ROW_GROUPS * half), jnp.bfloat16),
        ]
    aliases = {}
    columns = total
    if base is not None:
        aliases = {len(args): 0}
        in_specs.append(pl.BlockSpec(memory_space=pl.ANY))
        args.append(base)
        columns = sum(item[5] for item in items)

    def kernel(*refs):
        act_refs = refs[: 2 * len(items)]
        grad_refs = refs[2 * len(items) : 2 * (len(items) + len(grads))]
        rest = refs[2 * (len(items) + len(grads)) : len(args)]
        out, token = refs[len(args) : len(args) + 2]
        rows = refs[len(args) + 2 :]
        step = pl.program_id(0)
        token[...] = jnp.zeros(token.shape, token.dtype)

        @pl.when(step == 0)
        def _():
            for k in range(len(grads)):
                rows[k][:count] = grad_refs[2 * k][...]
                rows[k][count:] = grad_refs[2 * k + 1][...]
            if product is not None:
                down, groups = rows[-2:]
                for at in range(0, FF_PAD, 896):
                    part = jnp.concatenate([r[:, at : at + 896] for r in rest[:2]], axis=0)
                    down[at : at + 896] = inner_rows(part, rows[product[2]][:, product[3] :])
                for piece in range(SEQ_DEV * W_DEV):
                    for group in range(ROW_GROUPS):
                        first_row = piece * ROW_PIECE + group * 16
                        groups[
                            16 * piece : 16 * piece + 16, group * half : (group + 1) * half
                        ] = down[first_row : first_row + 16].astype(jnp.bfloat16)

        for k, (_, _, _, which, at, size, place) in enumerate(items):
            acts = jnp.concatenate([act_refs[2 * k][0], act_refs[2 * k + 1][0]], axis=0)
            for part in range(0, size, 512):
                wide = min(512, size - part)
                out[:, place + part : place + part + wide] = inner_rows(
                    acts, rows[which][:, at + part : at + part + wide]
                ).astype(jnp.bfloat16)
        if product is not None:
            place = product[4]
            out[:, place : place + ROW_GROUPS * half] = rows[-1][
                pl.ds(pl.multiple_of(step * block, block), block)
            ]

    return grid_call(
        kernel,
        name,
        (),
        (width // block,),
        in_specs,
        (rows_at(block, columns), pl.BlockSpec((8, 128), lambda n: (0, 0))),
        (
            jax.ShapeDtypeStruct((width, total), jnp.bfloat16),
            jax.ShapeDtypeStruct((8, 128), jnp.float32),
        ),
        scratch,
        args,
        aliases,
    )


def core_halves(pairs, on_first):
    low, high = [jnp.concatenate([p[k] for p in pairs], axis=1) for k in range(2)]
    return (jnp.where(on_first, low, high), swapped(jnp.where(on_first, high, low)))


def layer_backward(grad_out, kept, gain_pair, weights, segs, on_first, first, ready_of, late_of):
    (normed1, factor1, qkv, log_total, normed2, factor2, gate, up, _, _) = kept
    rows, width = normed1.shape
    half = width // 2
    grad_branch = grad_out.astype(jnp.bfloat16)
    low, high = (grad_branch[:, :half], grad_branch[:, half:])
    branch_own, branch_other = (jnp.where(on_first, low, high), jnp.where(on_first, high, low))
    grad_gate, grad_up, grad_norm2 = hidden_back(
        first, branch_own, branch_other, gate, up, weights
    )
    hidden_pair = core_halves(((grad_gate, grad_up), (low, high)), on_first)
    gain_mid = jnp.sum(normed2 * grad_norm2, axis=0)
    grad_middle = grad_out + norm_back(grad_norm2 * gain_pair[1], normed2, factor2)
    grad_attn = grad_middle.astype(jnp.bfloat16)
    mine, theirs = [matmul_t(grad_attn, w) for w in weights["out"]]
    grad_mixed = from_halves(mine, theirs, on_first).astype(jnp.bfloat16)
    grad_query, grad_own, grad_before, grad_after = attend_back(
        *segs, qkv, log_total, grad_mixed, ready_of(hidden_pair)
    )
    from_previous = to_next(grad_after).astype(jnp.float32)
    from_next = to_previous(grad_before).astype(jnp.float32)
    grad_pairs = grad_own + jnp.concatenate([from_previous, from_next], axis=0)
    grad_qkv = jnp.concatenate([grad_query, grad_pairs.astype(jnp.bfloat16)], axis=1)
    attn_pair = core_halves(
        (
            (grad_qkv[:, : 3 * half], grad_qkv[:, 3 * half :]),
            (grad_attn[:, :half], grad_attn[:, half:]),
        ),
        on_first,
    )
    grad_norm1 = qkv_back(first, grad_qkv, weights, late_of(attn_pair))
    gain_first = jnp.sum(normed1 * grad_norm1, axis=0)
    grad_inputs = grad_middle + norm_back(grad_norm1 * gain_pair[0], normed1, factor1)
    gains = jnp.stack([gain_first, gain_mid])
    return (grad_inputs, hidden_pair, attn_pair, gains)


def summed_over_w(block, place):
    rows = block.shape[0] // W_DEV
    total = lax.dynamic_slice_in_dim(block, place * rows, rows).astype(jnp.float32)
    for step in range(1, W_DEV):
        part = lax.dynamic_slice_in_dim(block, lax.rem(place + step, W_DEV) * rows, rows)
        got = lax.ppermute(part, "wshard", [(j, (j + step) % W_DEV) for j in range(W_DEV)])
        total = total + got.astype(jnp.float32)
    return total


def summed_by_steps(block, seq_place, w_place):
    side = 4
    columns = block.shape[1]

    def phase(parts, axis, at, place, route):
        size = parts.shape[at]

        def part(step):
            return lax.dynamic_index_in_dim(parts, lax.rem(place + step, size), at, keepdims=False)

        total = part(0).astype(jnp.float32)
        for step in range(1, size):
            total = total + lax.ppermute(part(step), axis, route(step)).astype(jnp.float32)
        return total

    total = phase(
        block.reshape(SEQ_DEV, W_DEV, 16, columns),
        "wshard",
        1,
        w_place,
        lambda step: [(j, (j + step) % W_DEV) for j in range(W_DEV)],
    )
    total = phase(
        total.astype(jnp.bfloat16).reshape(side, side, 16, columns),
        "seq",
        1,
        lax.rem(seq_place, side),
        lambda step: [
            (side * y + x, side * y + (x + step) % side) for y in range(side) for x in range(side)
        ],
    )
    return phase(
        total.astype(jnp.bfloat16),
        "seq",
        0,
        seq_place // side,
        lambda step: [
            (side * y + x, side * ((y + step) % side) + x) for y in range(side) for x in range(side)
        ],
    )


def per_device(
    inputs, cotangent, segments, norm_gains, attend_in, attend_out, hidden_in, hidden_out
):
    on_first = lax.axis_index("section") == 0
    core = lax.axis_index("section")
    seq_place = lax.axis_index("seq")
    w_place = lax.axis_index("wshard")

    def by_core(first, second):
        return jnp.where(on_first, first, second)

    def sections(own, got):
        return (by_core(own, got), by_core(got, own))

    slice_rows = attend_in.shape[1] // (2 * SEQ_DEV)
    pad = jnp.zeros((slice_rows, FF_PAD - FF), jnp.bfloat16)
    width = inputs.shape[3]

    def row_slice(which):
        at = (which * SEQ_DEV + seq_place) * slice_rows
        hidden, qkv, out = [
            lax.dynamic_slice_in_dim(w[0], at, slice_rows)
            for w in (hidden_in, attend_in, attend_out)
        ]
        return jnp.concatenate([hidden[:, :FF], pad, hidden[:, FF:], pad, qkv, out], axis=1)

    row_pieces = sections(row_slice(core), swapped(row_slice(1 - core)))
    hidden_width, qkv_width = (2 * FF_PAD, 3 * width)
    out_at = hidden_width + qkv_width

    def gathered(piece):
        return lax.all_gather(piece, ("wshard", "seq"), axis=0, tiled=True)

    first_own = gathered(row_pieces[0])
    half = hidden_out.shape[2] // 2
    low, high = (hidden_out[0, :, :half], hidden_out[0, :, half:])
    down_pieces = sections(by_core(low, high), swapped(by_core(high, low)))
    w_up = [(j, (j + 1) % W_DEV) for j in range(W_DEV)]
    w_down = [(j, i) for i, j in w_up]
    gain_pairs = sections(norm_gains[0], swapped(norm_gains[0]))

    def neighbours(piece):
        return (lax.ppermute(piece, "wshard", w_up), lax.ppermute(piece, "wshard", w_down))

    def down_of(piece, below, above):
        far = jnp.concatenate(
            [
                lax.ppermute(below[:, : half // 2], "wshard", w_up),
                lax.ppermute(above[:, half // 2 :], "wshard", w_down),
            ],
            axis=1,
        )
        own = jnp.zeros((FF_PAD, half), jnp.bfloat16)
        for step, part in enumerate((piece, above, far, below)):
            own = lax.dynamic_update_slice_in_dim(
                own, part, lax.rem(w_place + step, W_DEV) * piece.shape[0], 0
            )
        return (own, swapped(own))

    rows_in = by_core(inputs[0, 0], inputs[1, 0])
    row_count = rows_in.shape[0]
    segment_row = by_core(segments[0, 0], segments[1, 0])
    padded = jnp.pad(segment_row, (HALO, HALO), constant_values=-1)
    first_row = seq_place * row_count
    segs = (
        lax.dynamic_slice_in_dim(segment_row, first_row, row_count)[:, None],
        lax.dynamic_slice_in_dim(padded, first_row, row_count + 2 * HALO)[None, :],
    )
    entry = attention_input(rows_in, gain_pairs[0][0])
    row_piece, entry = lax.optimization_barrier((row_pieces[1], entry))
    second_own = gathered(row_piece)
    first_own, down_piece, first_down, entry, gain_pairs, segs = lax.optimization_barrier(
        (first_own, down_pieces[1], down_of(down_pieces[0], *neighbours(down_pieces[0])), entry, gain_pairs, segs)
    )
    near = neighbours(down_piece)

    def weights_of(own, other, qkv_other, out_other, down):
        return {
            "qkv": ((own, hidden_width), qkv_other),
            "gate": ((own, 0), (other, 0)),
            "up": ((own, FF_PAD), (other, FF_PAD)),
            "out": (own[:, out_at:], out_other),
            "down": down,
        }

    first = on_first.astype(jnp.int32)[None]
    other = swapped(first_own)
    first_weights = weights_of(
        first_own, other, (other, hidden_width), other[:, out_at:], first_down
    )
    middle, kept0 = layer_forward(
        rows_in, entry, gain_pairs[0], first_weights, segs, on_first, first
    )
    middle, near = lax.optimization_barrier((middle, near))
    second_own, second_down, entry = lax.optimization_barrier(
        (
            second_own, down_of(down_piece, *near), attention_input(middle, gain_pairs[1][0]),
        )
    )
    qkv_other, out_other, second_own = lax.optimization_barrier(
        (
            swapped(second_own[:, hidden_width:out_at]), swapped(second_own[:, out_at:]),
            second_own,
        )
    )
    weights = (
        first_weights,
        weights_of(second_own, swapped(second_own), (qkv_other, 0), out_other, second_down),
    )
    final, kept1 = layer_forward(middle, entry, gain_pairs[1], weights[1], segs, on_first, first)
    upstream = by_core(cotangent[0, 0], cotangent[1, 0])
    attn_cols, out_cols, down_cols = (qkv_width // 2, half, ROW_GROUPS * half)
    hidden_end = FF_PAD + down_cols
    second_at = attn_cols + out_cols
    hidden_at = 2 * second_at
    total = hidden_at + FF_PAD

    def attn_items(kept, which, at):
        acts, got = (kept[-2][0], kept[-1][0])
        return [
            (acts, got, 0, which, 0, attn_cols, at),
            (acts, got, 1, which, attn_cols, out_cols, at + attn_cols),
        ]

    def hidden_items(kept, which, at, down_at):
        acts, got = (kept[-2], kept[-1])
        return (
            [(acts[0], got[0], 2, which, 0, FF_PAD, at)],
            (acts[1], got[1], which, FF_PAD, down_at),
        )

    early_grads = []

    def make_early(hidden_pair):
        items, product = hidden_items(kept1, 0, 0, FF_PAD)
        early_grads.extend(weight_grads("hidden_grads", items, [hidden_pair], hidden_end, product))
        return early_grads[1:]

    grads1, _, attn_pair1, gains1 = layer_backward(
        upstream, kept1, gain_pairs[1], weights[1], segs, on_first, first, make_early, lambda _: ()
    )
    early = seq_sum(early_grads[0])
    late_grads, side_grads = ([], [])

    def make_joint(hidden_pair):
        items, product = hidden_items(kept0, 1, hidden_at, 0)
        pairs = [attn_pair1, hidden_pair]
        items = attn_items(kept1, 0, second_at) + items
        late_grads.append(weight_grads("joint_grads", items, pairs, total)[0])
        product = (*product[:2], 0, *product[3:])
        side_grads.append(
            functools.partial(weight_grads, "side_grads", [], [hidden_pair], down_cols, product)
        )
        return (hidden_pair[1], attn_pair1[1], *kept0[-1])

    def make_late(attn_pair):
        base = late_grads.pop()
        late_grads.extend(
            weight_grads("attn_grads", attn_items(kept0, 0, 0), [attn_pair], total, base=base)
        )
        side_grads.extend(side_grads.pop()())
        return (late_grads[1], side_grads[1])

    grads0, _, _, gains0 = layer_backward(
        grads1, kept0, gain_pairs[0], weights[0], segs, on_first, first, make_joint, make_late
    )
    late = seq_sum(late_grads[0])
    gains = jnp.concatenate([gains0, gains1], axis=0)
    gains = jnp.pad(gains, ((0, 128 - gains.shape[0]), (0, 0))).T.astype(jnp.bfloat16)
    side_total = summed_by_steps(side_grads[0], seq_place, w_place)
    gain_part = summed_by_steps(gains, seq_place, w_place)

    def placed(first, second):
        mine, give = (by_core(first, second), by_core(second, first))
        got = swapped(give)
        return jnp.stack([by_core(mine, got), by_core(got, mine)])[None, :, None]

    section_outputs = placed(middle, final)
    section_input_grads = placed(grads0, grads1)

    late, early_total, side_total, gain_part, section_outputs, section_input_grads = (
        lax.optimization_barrier(
            (
                late, summed_over_w(early, w_place), side_total, gain_part, section_outputs,
                section_input_grads,
            )
        )
    )
    late_total = summed_over_w(late, w_place)
    of_first = jnp.concatenate(
        [late_total[:, :second_at], gain_part, late_total[:, hidden_at:], side_total], axis=1
    )
    of_second = jnp.concatenate([late_total[:, second_at:hidden_at], gain_part, early_total], axis=1)
    mine, got = (by_core(of_first, of_second), swapped(by_core(of_second, of_first)))
    low, high = (by_core(mine, got), by_core(got, mine))
    hidden_at = second_at + 128
    qkv_rows = jnp.concatenate([low[:, :attn_cols], high[:, :attn_cols]], axis=1)
    attn_rows = jnp.concatenate([low[:, attn_cols:second_at], high[:, attn_cols:second_at]], axis=1)
    gain_part = (low + high)[:, second_at:hidden_at]
    gain_rows = by_core(gain_part[:, :2], gain_part[:, 2:4]).T
    hidden_rows = jnp.concatenate(
        [low[:, hidden_at : hidden_at + FF], high[:, hidden_at : hidden_at + FF]], axis=1
    )
    down_total = jnp.concatenate(
        [
            jnp.concatenate([h[:, at : at + half] for h in (low, high)], axis=1)
            for at in range(hidden_at + FF_PAD, low.shape[1], half)
        ],
        axis=0,
    )[:ROW_PIECE]
    return (
        section_outputs,
        section_input_grads,
        qkv_rows[None],
        attn_rows[None],
        hidden_rows[None],
        down_total[None],
        gain_rows[None],
    )


def solution(mesh):
    placed = (
        P(None, "wshard", "seq", None),
        P(None, "wshard", "seq", None),
        P(None, "wshard", None),
        P("section", None, None),
        P("section", "wshard", None),
        P("section", "wshard", None),
        P("section", "wshard", None),
        P("section", "wshard", None),
    )
    return jax.shard_map(
        per_device,
        mesh=mesh,
        in_specs=placed,
        out_specs=(
            P("section", None, "wshard", "seq", None),
            P("section", None, "wshard", "seq", None),
            P("section", ("seq", "wshard"), None),
            P("section", ("seq", "wshard"), None),
            P("section", ("seq", "wshard"), None),
            P("section", ("seq", "wshard"), None),
            P("section", None, ("seq", "wshard")),
        ),
        check_vma=False,
    )
```

```python
import functools
import math

import jax
import jax.numpy as jnp
from jax import lax
from jax.experimental import pallas as pl
from jax.experimental.pallas import tpu as pltpu
from jax.sharding import PartitionSpec as P

HEADS = 16
HEAD_DIM = 64
FF = 2624
HALO = 64
FF_PAD = 2688
SEQ_DEV = 16
W_DEV = 4
PAD_ROWS = 48
HIDDEN_BLOCK = 896
QKV_BLOCK = 768

norm_eps = 1e-05
root_half = 1.0 / math.sqrt(2.0)
root_two_pi = 1.0 / math.sqrt(2.0 * math.pi)
score_scale = 1.0 / math.sqrt(HEAD_DIM)

SWAP = [(0, 1), (1, 0)]


def swapped(array):
    return lax.ppermute(array, "section", SWAP)


def norm_parts(rows_in):
    centred = rows_in - jnp.mean(rows_in, axis=1, keepdims=True)
    factor = lax.rsqrt(jnp.mean(centred * centred, axis=1, keepdims=True) + norm_eps)
    return (centred * factor, factor)


def norm_back(grad_norm, normed, factor):
    inner = jnp.mean(grad_norm, axis=1, keepdims=True)
    along = jnp.mean(grad_norm * normed, axis=1, keepdims=True)
    return factor * (grad_norm - inner - normed * along)


def matmul(left, right):
    return jnp.dot(left, right, preferred_element_type=jnp.float32)


def matmul_t(left, right):
    return lax.dot_general(
        left, right, (((1,), (1,)), ((), ())), preferred_element_type=jnp.float32
    )


def inner_rows(left, right):
    return lax.dot_general(
        left, right, (((0,), (0,)), ((), ())), preferred_element_type=jnp.float32
    )


def column_halves(array, on_first):
    even = jnp.concatenate([array[:, 256 * k : 256 * k + 128] for k in range(4)], axis=1)
    odd = jnp.concatenate([array[:, 256 * k + 128 : 256 * k + 256] for k in range(4)], axis=1)
    return (jnp.where(on_first, even, odd), jnp.where(on_first, odd, even))


def from_halves(own, other, on_first):
    even = jnp.where(on_first, own, other)
    odd = jnp.where(on_first, other, own)
    parts = []
    for k in range(4):
        parts += [even[:, 128 * k : 128 * k + 128], odd[:, 128 * k : 128 * k + 128]]
    return jnp.concatenate(parts, axis=1)


def window_allowed(query_seg, key_seg):
    rows, keys = (query_seg.shape[0], key_seg.shape[1])
    offset = lax.broadcasted_iota(jnp.int32, (rows, keys), 1) - lax.broadcasted_iota(
        jnp.int32, (rows, keys), 0
    )
    return (offset >= 0) & (offset <= 2 * HALO) & (query_seg == key_seg)


def attend_kernel(query_seg, key_seg, qkv, mixed, log_total):
    allowed = window_allowed(query_seg[...], key_seg[...])
    width = HEADS * HEAD_DIM
    rows = mixed.shape[0]
    for head in range(HEADS):
        at = head * HEAD_DIM
        q = qkv[HALO : HALO + rows, at : at + HEAD_DIM]
        k = qkv[:, width + at : width + at + HEAD_DIM]
        v = qkv[:, 2 * width + at : 2 * width + at + HEAD_DIM]
        scores = jnp.where(allowed, matmul_t(q, k) * score_scale, -1e30)
        row_max = jnp.max(scores, axis=1, keepdims=True)
        exponent = jnp.exp(scores - row_max)
        total = jnp.sum(exponent, axis=1, keepdims=True)
        probs = (exponent * (1.0 / total)).astype(jnp.bfloat16)
        mixed[:, at : at + HEAD_DIM] = matmul(probs, v).astype(jnp.bfloat16)
        log_total[:, at : at + HEAD_DIM] = jnp.broadcast_to(
            row_max + jnp.log(total), (rows, HEAD_DIM)
        )


def attend_back_kernel(query_seg, key_seg, qkv, log_total, grad_mixed, *refs):
    grad_query, own, before, after = refs[-4:]
    allowed = window_allowed(query_seg[...], key_seg[...])
    width = HEADS * HEAD_DIM
    rows = grad_mixed.shape[0]
    for head in range(HEADS):
        at = head * HEAD_DIM
        q = qkv[HALO : HALO + rows, at : at + HEAD_DIM]
        k = qkv[:, width + at : width + at + HEAD_DIM]
        v = qkv[:, 2 * width + at : 2 * width + at + HEAD_DIM]
        grad = grad_mixed[:, at : at + HEAD_DIM]
        scores = jnp.where(allowed, matmul_t(q, k) * score_scale, -1e30)
        probs = jnp.exp(scores - log_total[:, at : at + 1])
        grad_probs = matmul_t(grad, v)
        inner = jnp.sum(probs * grad_probs, axis=1, keepdims=True)
        grad_scores = (probs * (grad_probs - inner)).astype(jnp.bfloat16)
        grad_query[:, at : at + HEAD_DIM] = (matmul(grad_scores, k) * score_scale).astype(
            jnp.bfloat16
        )
        for place, piece in (
            (at, inner_rows(grad_scores, q) * score_scale),
            (width + at, inner_rows(probs.astype(jnp.bfloat16), grad)),
        ):
            columns = slice(place, place + HEAD_DIM)
            before[:, columns] = piece[:HALO].astype(jnp.bfloat16)
            own[:, columns] = piece[HALO : HALO + rows]
            after[:, columns] = piece[HALO + rows :].astype(jnp.bfloat16)


params = pltpu.CompilerParams(vmem_limit_bytes=48 * 1024 * 1024)


def attend(query_seg, key_seg, qkv):
    rows, width = (query_seg.shape[0], HEADS * HEAD_DIM)
    return pl.pallas_call(
        attend_kernel,
        out_shape=(
            jax.ShapeDtypeStruct((rows, width), jnp.bfloat16),
            jax.ShapeDtypeStruct((rows, width), jnp.float32),
        ),
        compiler_params=params,
        name="attend",
    )(query_seg, key_seg, qkv)


def attend_back(query_seg, key_seg, qkv, log_total, grad_mixed, ready):
    rows, width = (query_seg.shape[0], HEADS * HEAD_DIM)
    return pl.pallas_call(
        attend_back_kernel,
        out_shape=(
            jax.ShapeDtypeStruct((rows, width), jnp.bfloat16),
            jax.ShapeDtypeStruct((rows, 2 * width), jnp.float32),
            jax.ShapeDtypeStruct((HALO, 2 * width), jnp.bfloat16),
            jax.ShapeDtypeStruct((HALO, 2 * width), jnp.bfloat16),
        ),
        in_specs=[pl.BlockSpec(memory_space=pltpu.VMEM)] * 5
        + [pl.BlockSpec(memory_space=pl.ANY)] * len(ready),
        compiler_params=params,
        name="attend_back",
    )(query_seg, key_seg, qkv, log_total, grad_mixed, *ready)


def to_next(array):
    return lax.ppermute(array, "seq", [(i, i + 1) for i in range(SEQ_DEV - 1)])


def to_previous(array):
    return lax.ppermute(array, "seq", [(i + 1, i) for i in range(SEQ_DEV - 1)])


def split_normal(gate):
    cumulative = 0.5 * (1.0 + lax.erf(gate * root_half))
    return cumulative


def grid_call(kernel, name, scalars, grid, in_specs, out_specs, out_shape, scratch, args, aliases=None):
    return pl.pallas_call(
        kernel,
        grid_spec=pltpu.PrefetchScalarGridSpec(
            num_scalar_prefetch=len(scalars),
            grid=grid,
            in_specs=in_specs,
            out_specs=out_specs,
            scratch_shapes=scratch,
        ),
        out_shape=out_shape,
        input_output_aliases=aliases or {},
        compiler_params=params,
        name=name,
    )(*scalars, *args)


def whole(array):
    return pl.BlockSpec(array.shape, lambda n, *_: (0,) * array.ndim)


def columns_at(rows, block, first):
    return pl.BlockSpec((rows, block), lambda n, *_: (0, first + n))


def rows_at(block, columns):
    return pl.BlockSpec((block, columns), lambda n, *_: (n, 0))


def add_to(step, total, value):
    @pl.when(step == 0)
    def _():
        total[...] = value

    @pl.when(step > 0)
    def _():
        total[...] += value


def store_halves(out, own, other, on_first):
    for k in range(4):
        block = slice(128 * k, 128 * k + 128)
        out[:, 256 * k : 256 * k + 128] = jnp.where(on_first, own[:, block], other[:, block])
        out[:, 256 * k + 128 : 256 * k + 256] = jnp.where(on_first, other[:, block], own[:, block])


def qkv_kernel(own, other, weight_own, weight_other, out):
    out[...] = (
        matmul(own[...], weight_own[...]) + matmul(other[...], weight_other[...])
    ).astype(jnp.bfloat16)


def qkv_of(own, other, weights):
    (w_own, at_own), (w_other, at_other) = weights["qkv"]
    width = 3 * HEADS * HEAD_DIM
    depth = own.shape[1]
    return grid_call(
        qkv_kernel,
        "qkv",
        (),
        (width // QKV_BLOCK,),
        [
            whole(own),
            whole(other),
            columns_at(depth, QKV_BLOCK, at_own // QKV_BLOCK),
            columns_at(depth, QKV_BLOCK, at_other // QKV_BLOCK),
        ],
        columns_at(own.shape[0], QKV_BLOCK, 0),
        jax.ShapeDtypeStruct((own.shape[0], width), jnp.bfloat16),
        [],
        (own, other, w_own, w_other),
    )


def qkv_back_kernel(first, grad, weight_own, weight_other, *refs):
    out, total_own, total_other = refs[-3:]
    step = pl.program_id(0)
    add_to(step, total_own, matmul_t(grad[...], weight_own[...]))
    add_to(step, total_other, matmul_t(grad[...], weight_other[...]))

    @pl.when(step == pl.num_programs(0) - 1)
    def _():
        store_halves(out, total_own[...], total_other[...], first[0] == 1)


def qkv_back(first, grad, weights, ready):
    (w_own, at_own), (w_other, at_other) = weights["qkv"]
    rows, width = grad.shape
    depth = w_own.shape[0]
    return grid_call(
        qkv_back_kernel,
        "qkv_back",
        (first,),
        (width // QKV_BLOCK,),
        [
            columns_at(rows, QKV_BLOCK, 0),
            columns_at(depth, QKV_BLOCK, at_own // QKV_BLOCK),
            columns_at(depth, QKV_BLOCK, at_other // QKV_BLOCK),
            *[pl.BlockSpec(memory_space=pl.ANY)] * len(ready),
        ],
        pl.BlockSpec((rows, 2 * depth), lambda n, *_: (0, 0)),
        jax.ShapeDtypeStruct((rows, 2 * depth), jnp.float32),
        [pltpu.VMEM((rows, depth), jnp.float32)] * 2,
        (grad, w_own, w_other, *ready),
    )


def hidden_kernel(
    first, own, other, gate_own, gate_other, up_own, up_other, down_own, down_other, middle,
    gate_out, up_out, product_out, out, total_own, total_other,
):
    step = pl.program_id(0)
    gate = matmul(own[...], gate_own[...]) + matmul(other[...], gate_other[...])
    up = matmul(own[...], up_own[...]) + matmul(other[...], up_other[...])
    product = (gate * split_normal(gate) * up).astype(jnp.bfloat16)
    gate_out[...] = gate
    up_out[...] = up
    product_out[...] = product
    add_to(step, total_own, matmul(product, down_own[...]))
    add_to(step, total_other, matmul(product, down_other[...]))

    @pl.when(step == pl.num_programs(0) - 1)
    def _():
        half = total_own.shape[1]
        mine, theirs, on_first = (total_own[...], total_other[...], first[0] == 1)
        out[:, :half] = middle[:, :half] + jnp.where(on_first, mine, theirs)
        out[:, half:] = middle[:, half:] + jnp.where(on_first, theirs, mine)


def hidden_specs(weights, depth):
    specs, arrays = ([], [])
    for part in ("gate", "up"):
        for array, at in weights[part]:
            specs.append(columns_at(depth, HIDDEN_BLOCK, at // HIDDEN_BLOCK))
            arrays.append(array)
    for array in weights["down"]:
        specs.append(rows_at(HIDDEN_BLOCK, array.shape[1]))
        arrays.append(array)
    return (specs, arrays)


def hidden_forward(first, own, other, middle, weights):
    rows, depth = own.shape
    width = middle.shape[1]
    specs, arrays = hidden_specs(weights, depth)
    piece = columns_at(rows, HIDDEN_BLOCK, 0)
    return grid_call(
        hidden_kernel,
        "hidden",
        (first,),
        (FF_PAD // HIDDEN_BLOCK,),
        [whole(own), whole(other), *specs, whole(middle)],
        (piece, piece, piece, whole(middle)),
        (
            jax.ShapeDtypeStruct((rows, FF_PAD), jnp.float32),
            jax.ShapeDtypeStruct((rows, FF_PAD), jnp.float32),
            jax.ShapeDtypeStruct((rows, FF_PAD), jnp.bfloat16),
            jax.ShapeDtypeStruct((rows, width), jnp.float32),
        ),
        [pltpu.VMEM((rows, width // 2), jnp.float32)] * 2,
        (own, other, *arrays, middle),
    )


def hidden_back_kernel(
    first, grad_own, grad_other, gate_in, up_in, gate_own, gate_other, up_own, up_other, down_own,
    down_other, grad_gate_out, grad_up_out, out, total_own, total_other,
):
    step = pl.program_id(0)
    gate, up = (gate_in[...], up_in[...])
    grad_product = matmul_t(grad_own[...], down_own[...]) + matmul_t(
        grad_other[...], down_other[...]
    )
    cumulative = split_normal(gate)
    derivative = cumulative + gate * jnp.exp(-0.5 * gate * gate) * root_two_pi
    grad_gate = (grad_product * up * derivative).astype(jnp.bfloat16)
    grad_up = (grad_product * gate * cumulative).astype(jnp.bfloat16)
    grad_gate_out[...] = grad_gate
    grad_up_out[...] = grad_up
    add_to(step, total_own, matmul_t(grad_gate, gate_own[...]) + matmul_t(grad_up, up_own[...]))
    add_to(
        step, total_other, matmul_t(grad_gate, gate_other[...]) + matmul_t(grad_up, up_other[...])
    )

    @pl.when(step == pl.num_programs(0) - 1)
    def _():
        store_halves(out, total_own[...], total_other[...], first[0] == 1)


def hidden_back(first, grad_own, grad_other, gate, up, weights):
    rows, half = grad_own.shape
    depth = half
    specs, arrays = hidden_specs(weights, depth)
    piece = columns_at(rows, HIDDEN_BLOCK, 0)
    return grid_call(
        hidden_back_kernel,
        "hidden_back",
        (first,),
        (FF_PAD // HIDDEN_BLOCK,),
        [whole(grad_own), whole(grad_other), piece, piece, *specs],
        (piece, piece, pl.BlockSpec((rows, 2 * depth), lambda n, *_: (0, 0))),
        (
            jax.ShapeDtypeStruct((rows, FF_PAD), jnp.bfloat16),
            jax.ShapeDtypeStruct((rows, FF_PAD), jnp.bfloat16),
            jax.ShapeDtypeStruct((rows, 2 * depth), jnp.float32),
        ),
        [pltpu.VMEM((rows, depth), jnp.float32)] * 2,
        (grad_own, grad_other, gate, up, *arrays),
    )


def attention_input(rows_in, gain):
    normed, factor = norm_parts(rows_in)
    act_in = (normed * gain).astype(jnp.bfloat16)
    before = to_next(act_in[act_in.shape[0] - HALO :])
    after = to_previous(act_in[:HALO])
    return (normed, factor, act_in, jnp.concatenate([before, act_in, after], axis=0))


def layer_forward(rows_in, entry, gain_pair, weights, segs, on_first, first):
    normed1, factor1, act_in, extended = entry
    qkv = qkv_of(*column_halves(extended, on_first), weights)
    mixed, log_total = attend(*segs, qkv)
    own, other = column_halves(mixed, on_first)
    middle = rows_in + matmul(own, weights["out"][0]) + matmul(other, weights["out"][1])
    normed2, factor2 = norm_parts(middle)
    act_mid = (normed2 * gain_pair[1]).astype(jnp.bfloat16)
    own, other = column_halves(act_mid, on_first)
    gate, up, product, output = hidden_forward(first, own, other, middle, weights)
    acts = (jnp.stack([act_in, mixed, act_mid]), product)
    got = tuple(swapped(act) for act in acts)
    kept = (normed1, factor1, qkv, log_total, normed2, factor2, gate, up, acts, got)
    return (output, kept)


def seq_sum(total):
    return lax.psum_scatter(total, "seq", scatter_dimension=0, tiled=True)


ROW_PIECE = FF // (SEQ_DEV * W_DEV)
ROW_GROUPS = PAD_ROWS // 16


def weight_grads(name, items, grads, total, product=None, base=None):
    count, width, block = (grads[0][0].shape[0], HEADS * HEAD_DIM, 256)
    in_specs, args = ([], [])
    for acts, got, member, *_ in items:
        for array in (acts, got):
            in_specs.append(pl.BlockSpec((1, count, block), lambda n, m=member: (m, 0, n)))
            args.append(array)
    for pair in grads:
        in_specs += [whole(array) for array in pair]
        args += list(pair)
    scratch = [pltpu.VMEM((2 * count, pair[0].shape[1]), jnp.bfloat16) for pair in grads]
    if product is not None:
        in_specs += [whole(array) for array in product[:2]]
        args += list(product[:2])
        half = grads[product[2]][0].shape[1] - product[3]
        scratch += [
            pltpu.VMEM((FF_PAD, half), jnp.float32),
            pltpu.VMEM((width, ROW_GROUPS * half), jnp.bfloat16),
        ]
    aliases = {}
    columns = total
    if base is not None:
        aliases = {len(args): 0}
        in_specs.append(pl.BlockSpec(memory_space=pl.ANY))
        args.append(base)
        columns = sum(item[5] for item in items)

    def kernel(*refs):
        act_refs = refs[: 2 * len(items)]
        grad_refs = refs[2 * len(items) : 2 * (len(items) + len(grads))]
        rest = refs[2 * (len(items) + len(grads)) : len(args)]
        out, token = refs[len(args) : len(args) + 2]
        rows = refs[len(args) + 2 :]
        step = pl.program_id(0)
        token[...] = jnp.zeros(token.shape, token.dtype)

        @pl.when(step == 0)
        def _():
            for k in range(len(grads)):
                rows[k][:count] = grad_refs[2 * k][...]
                rows[k][count:] = grad_refs[2 * k + 1][...]
            if product is not None:
                down, groups = rows[-2:]
                for at in range(0, FF_PAD, 896):
                    part = jnp.concatenate([r[:, at : at + 896] for r in rest[:2]], axis=0)
                    down[at : at + 896] = inner_rows(part, rows[product[2]][:, product[3] :])
                for piece in range(SEQ_DEV * W_DEV):
                    for group in range(ROW_GROUPS):
                        first_row = piece * ROW_PIECE + group * 16
                        groups[
                            16 * piece : 16 * piece + 16, group * half : (group + 1) * half
                        ] = down[first_row : first_row + 16].astype(jnp.bfloat16)

        for k, (_, _, _, which, at, size, place) in enumerate(items):
            acts = jnp.concatenate([act_refs[2 * k][0], act_refs[2 * k + 1][0]], axis=0)
            for part in range(0, size, 512):
                wide = min(512, size - part)
                out[:, place + part : place + part + wide] = inner_rows(
                    acts, rows[which][:, at + part : at + part + wide]
                ).astype(jnp.bfloat16)
        if product is not None:
            place = product[4]
            out[:, place : place + ROW_GROUPS * half] = rows[-1][
                pl.ds(pl.multiple_of(step * block, block), block)
            ]

    return grid_call(
        kernel,
        name,
        (),
        (width // block,),
        in_specs,
        (rows_at(block, columns), pl.BlockSpec((8, 128), lambda n: (0, 0))),
        (
            jax.ShapeDtypeStruct((width, total), jnp.bfloat16),
            jax.ShapeDtypeStruct((8, 128), jnp.float32),
        ),
        scratch,
        args,
        aliases,
    )


def core_halves(pairs, on_first):
    low, high = [jnp.concatenate([p[k] for p in pairs], axis=1) for k in range(2)]
    return (jnp.where(on_first, low, high), swapped(jnp.where(on_first, high, low)))


def layer_backward(grad_out, kept, gain_pair, weights, segs, on_first, first, ready_of, late_of):
    (normed1, factor1, qkv, log_total, normed2, factor2, gate, up, _, _) = kept
    rows, width = normed1.shape
    half = width // 2
    grad_branch = grad_out.astype(jnp.bfloat16)
    low, high = (grad_branch[:, :half], grad_branch[:, half:])
    branch_own, branch_other = (jnp.where(on_first, low, high), jnp.where(on_first, high, low))
    grad_gate, grad_up, grad_norm2 = hidden_back(
        first, branch_own, branch_other, gate, up, weights
    )
    hidden_pair = core_halves(((grad_gate, grad_up), (low, high)), on_first)
    gain_mid = jnp.sum(normed2 * grad_norm2, axis=0)
    grad_middle = grad_out + norm_back(grad_norm2 * gain_pair[1], normed2, factor2)
    grad_attn = grad_middle.astype(jnp.bfloat16)
    mine, theirs = [matmul_t(grad_attn, w) for w in weights["out"]]
    grad_mixed = from_halves(mine, theirs, on_first).astype(jnp.bfloat16)
    ready, token = ready_of(hidden_pair)
    grad_query, grad_own, grad_before, grad_after = attend_back(
        *segs, qkv, log_total, grad_mixed, ready
    )
    from_previous = to_next(grad_after).astype(jnp.float32) + token
    from_next = to_previous(grad_before).astype(jnp.float32)
    grad_pairs = grad_own + jnp.concatenate([from_previous, from_next], axis=0)
    grad_qkv = jnp.concatenate([grad_query, grad_pairs.astype(jnp.bfloat16)], axis=1)
    attn_pair = core_halves(
        (
            (grad_qkv[:, : 3 * half], grad_qkv[:, 3 * half :]),
            (grad_attn[:, :half], grad_attn[:, half:]),
        ),
        on_first,
    )
    grad_norm1 = qkv_back(first, grad_qkv, weights, late_of(attn_pair))
    gain_first = jnp.sum(normed1 * grad_norm1, axis=0)
    grad_inputs = grad_middle + norm_back(grad_norm1 * gain_pair[0], normed1, factor1)
    gains = jnp.stack([gain_first, gain_mid])
    return (grad_inputs, hidden_pair, attn_pair, gains)


def summed_over_w(block, place):
    rows = block.shape[0] // W_DEV
    total = lax.dynamic_slice_in_dim(block, place * rows, rows).astype(jnp.float32)
    for step in range(1, W_DEV):
        part = lax.dynamic_slice_in_dim(block, lax.rem(place + step, W_DEV) * rows, rows)
        got = lax.ppermute(part, "wshard", [(j, (j + step) % W_DEV) for j in range(W_DEV)])
        total = total + got.astype(jnp.float32)
    return total


def summed_by_steps(block, seq_place, w_place):
    side = 4
    columns = block.shape[1]

    def phase(parts, axis, at, place, route):
        size = parts.shape[at]

        def part(step):
            return lax.dynamic_index_in_dim(parts, lax.rem(place + step, size), at, keepdims=False)

        total = part(0).astype(jnp.float32)
        for step in range(1, size):
            total = total + lax.ppermute(part(step), axis, route(step)).astype(jnp.float32)
        return total

    total = phase(
        block.reshape(SEQ_DEV, W_DEV, 16, columns),
        "wshard",
        1,
        w_place,
        lambda step: [(j, (j + step) % W_DEV) for j in range(W_DEV)],
    )
    total = phase(
        total.astype(jnp.bfloat16).reshape(side, side, 16, columns),
        "seq",
        1,
        lax.rem(seq_place, side),
        lambda step: [
            (side * y + x, side * y + (x + step) % side) for y in range(side) for x in range(side)
        ],
    )
    return phase(
        total.astype(jnp.bfloat16),
        "seq",
        0,
        seq_place // side,
        lambda step: [
            (side * y + x, side * ((y + step) % side) + x) for y in range(side) for x in range(side)
        ],
    )


def per_device(
    inputs, cotangent, segments, norm_gains, attend_in, attend_out, hidden_in, hidden_out
):
    on_first = lax.axis_index("section") == 0
    core = lax.axis_index("section")
    seq_place = lax.axis_index("seq")
    w_place = lax.axis_index("wshard")

    def by_core(first, second):
        return jnp.where(on_first, first, second)

    def sections(own, got):
        return (by_core(own, got), by_core(got, own))

    slice_rows = attend_in.shape[1] // (2 * SEQ_DEV)
    pad = jnp.zeros((slice_rows, FF_PAD - FF), jnp.bfloat16)
    width = inputs.shape[3]

    def row_slice(which):
        at = (which * SEQ_DEV + seq_place) * slice_rows
        hidden, qkv, out = [
            lax.dynamic_slice_in_dim(w[0], at, slice_rows)
            for w in (hidden_in, attend_in, attend_out)
        ]
        return jnp.concatenate([hidden[:, :FF], pad, hidden[:, FF:], pad, qkv, out], axis=1)

    row_pieces = sections(row_slice(core), swapped(row_slice(1 - core)))
    hidden_width, qkv_width = (2 * FF_PAD, 3 * width)
    out_at = hidden_width + qkv_width

    def gathered(piece):
        return lax.all_gather(piece, ("wshard", "seq"), axis=0, tiled=True)

    first_own = gathered(row_pieces[0])
    half = hidden_out.shape[2] // 2
    low, high = (hidden_out[0, :, :half], hidden_out[0, :, half:])
    down_pieces = sections(by_core(low, high), swapped(by_core(high, low)))
    w_up = [(j, (j + 1) % W_DEV) for j in range(W_DEV)]
    w_down = [(j, i) for i, j in w_up]
    gain_pairs = sections(norm_gains[0], swapped(norm_gains[0]))

    def neighbours(piece):
        return (lax.ppermute(piece, "wshard", w_up), lax.ppermute(piece, "wshard", w_down))

    def down_of(piece, below, above):
        far = jnp.concatenate(
            [
                lax.ppermute(below[:, : half // 2], "wshard", w_up),
                lax.ppermute(above[:, half // 2 :], "wshard", w_down),
            ],
            axis=1,
        )
        own = jnp.zeros((FF_PAD, half), jnp.bfloat16)
        for step, part in enumerate((piece, above, far, below)):
            own = lax.dynamic_update_slice_in_dim(
                own, part, lax.rem(w_place + step, W_DEV) * piece.shape[0], 0
            )
        return (own, swapped(own))

    rows_in = by_core(inputs[0, 0], inputs[1, 0])
    row_count = rows_in.shape[0]
    segment_row = by_core(segments[0, 0], segments[1, 0])
    padded = jnp.pad(segment_row, (HALO, HALO), constant_values=-1)
    first_row = seq_place * row_count
    segs = (
        lax.dynamic_slice_in_dim(segment_row, first_row, row_count)[:, None],
        lax.dynamic_slice_in_dim(padded, first_row, row_count + 2 * HALO)[None, :],
    )
    entry = attention_input(rows_in, gain_pairs[0][0])
    row_piece, entry = lax.optimization_barrier((row_pieces[1], entry))
    second_own = gathered(row_piece)
    first_own, down_piece, first_down, entry, gain_pairs, segs = lax.optimization_barrier(
        (first_own, down_pieces[1], down_of(down_pieces[0], *neighbours(down_pieces[0])), entry, gain_pairs, segs)
    )
    near = neighbours(down_piece)

    def weights_of(own, other, qkv_other, out_other, down):
        return {
            "qkv": ((own, hidden_width), qkv_other),
            "gate": ((own, 0), (other, 0)),
            "up": ((own, FF_PAD), (other, FF_PAD)),
            "out": (own[:, out_at:], out_other),
            "down": down,
        }

    first = on_first.astype(jnp.int32)[None]
    other = swapped(first_own)
    first_weights = weights_of(
        first_own, other, (other, hidden_width), other[:, out_at:], first_down
    )
    middle, kept0 = layer_forward(
        rows_in, entry, gain_pairs[0], first_weights, segs, on_first, first
    )
    middle, near = lax.optimization_barrier((middle, near))
    second_own, second_down, entry = lax.optimization_barrier(
        (
            second_own, down_of(down_piece, *near), attention_input(middle, gain_pairs[1][0]),
        )
    )
    qkv_other, out_other, second_own = lax.optimization_barrier(
        (
            swapped(second_own[:, hidden_width:out_at]), swapped(second_own[:, out_at:]),
            second_own,
        )
    )
    weights = (
        first_weights,
        weights_of(second_own, swapped(second_own), (qkv_other, 0), out_other, second_down),
    )
    final, kept1 = layer_forward(middle, entry, gain_pairs[1], weights[1], segs, on_first, first)
    upstream = by_core(cotangent[0, 0], cotangent[1, 0])
    attn_cols, out_cols, down_cols = (qkv_width // 2, half, ROW_GROUPS * half)
    hidden_end = FF_PAD + down_cols
    second_at = attn_cols + out_cols
    hidden_at = 2 * second_at
    total = hidden_at + FF_PAD

    def attn_items(kept, which, at):
        acts, got = (kept[-2][0], kept[-1][0])
        return [
            (acts, got, 0, which, 0, attn_cols, at),
            (acts, got, 1, which, attn_cols, out_cols, at + attn_cols),
        ]

    def hidden_items(kept, which, at, down_at):
        acts, got = (kept[-2], kept[-1])
        return (
            [(acts[0], got[0], 2, which, 0, FF_PAD, at)],
            (acts[1], got[1], which, FF_PAD, down_at),
        )

    early_grads = []

    def make_early(hidden_pair):
        items, product = hidden_items(kept1, 0, 0, FF_PAD)
        early_grads.extend(weight_grads("hidden_grads", items, [hidden_pair], hidden_end, product))
        return (early_grads[1:], 0.0)

    grads1, _, attn_pair1, gains1 = layer_backward(
        upstream, kept1, gain_pairs[1], weights[1], segs, on_first, first, make_early, lambda _: ()
    )
    early = seq_sum(early_grads[0])
    late_grads, side_grads = ([], [])

    def make_joint(hidden_pair):
        items, product = hidden_items(kept0, 1, hidden_at, 0)
        pairs = [attn_pair1, hidden_pair]
        items = attn_items(kept1, 0, second_at) + items
        base, token = weight_grads("joint_grads", items, pairs, total)
        late_grads.append(base)
        product = (*product[:2], 0, *product[3:])
        side_grads.append(
            functools.partial(weight_grads, "side_grads", [], [hidden_pair], down_cols, product)
        )
        return ((hidden_pair[1], attn_pair1[1], *kept0[-1]), token[0, 0])

    def make_late(attn_pair):
        base = late_grads.pop()
        late_grads.extend(
            weight_grads("attn_grads", attn_items(kept0, 0, 0), [attn_pair], total, base=base)
        )
        side_grads.extend(side_grads.pop()())
        return (late_grads[1], side_grads[1])

    grads0, _, _, gains0 = layer_backward(
        grads1, kept0, gain_pairs[0], weights[0], segs, on_first, first, make_joint, make_late
    )
    late = seq_sum(late_grads[0])
    gains = jnp.concatenate([gains0, gains1], axis=0)
    gains = jnp.pad(gains, ((0, 128 - gains.shape[0]), (0, 0))).T.astype(jnp.bfloat16)
    side_total = summed_by_steps(side_grads[0], seq_place, w_place)
    gain_part = summed_by_steps(gains, seq_place, w_place)

    def placed(first, second):
        mine, give = (by_core(first, second), by_core(second, first))
        got = swapped(give)
        return jnp.stack([by_core(mine, got), by_core(got, mine)])[None, :, None]

    section_outputs = placed(middle, final)
    section_input_grads = placed(grads0, grads1)

    late, early_total, side_total, gain_part, section_outputs, section_input_grads = (
        lax.optimization_barrier(
            (
                late, summed_over_w(early, w_place), side_total, gain_part, section_outputs,
                section_input_grads,
            )
        )
    )
    late_total = summed_over_w(late, w_place)
    of_first = jnp.concatenate(
        [late_total[:, :second_at], gain_part, late_total[:, hidden_at:], side_total], axis=1
    )
    of_second = jnp.concatenate([late_total[:, second_at:hidden_at], gain_part, early_total], axis=1)
    mine, got = (by_core(of_first, of_second), swapped(by_core(of_second, of_first)))
    low, high = (by_core(mine, got), by_core(got, mine))
    hidden_at = second_at + 128
    qkv_rows = jnp.concatenate([low[:, :attn_cols], high[:, :attn_cols]], axis=1)
    attn_rows = jnp.concatenate([low[:, attn_cols:second_at], high[:, attn_cols:second_at]], axis=1)
    gain_part = (low + high)[:, second_at:hidden_at]
    gain_rows = by_core(gain_part[:, :2], gain_part[:, 2:4]).T
    hidden_rows = jnp.concatenate(
        [low[:, hidden_at : hidden_at + FF], high[:, hidden_at : hidden_at + FF]], axis=1
    )
    down_total = jnp.concatenate(
        [
            jnp.concatenate([h[:, at : at + half] for h in (low, high)], axis=1)
            for at in range(hidden_at + FF_PAD, low.shape[1], half)
        ],
        axis=0,
    )[:ROW_PIECE]
    return (
        section_outputs,
        section_input_grads,
        qkv_rows[None],
        attn_rows[None],
        hidden_rows[None],
        down_total[None],
        gain_rows[None],
    )


def solution(mesh):
    placed = (
        P(None, "wshard", "seq", None),
        P(None, "wshard", "seq", None),
        P(None, "wshard", None),
        P("section", None, None),
        P("section", "wshard", None),
        P("section", "wshard", None),
        P("section", "wshard", None),
        P("section", "wshard", None),
    )
    return jax.shard_map(
        per_device,
        mesh=mesh,
        in_specs=placed,
        out_specs=(
            P("section", None, "wshard", "seq", None),
            P("section", None, "wshard", "seq", None),
            P("section", ("seq", "wshard"), None),
            P("section", ("seq", "wshard"), None),
            P("section", ("seq", "wshard"), None),
            P("section", ("seq", "wshard"), None),
            P("section", None, ("seq", "wshard")),
        ),
        check_vma=False,
    )
```
